32 devices in a mesh: dp: 32 (over z, y, x, core).
Axes of the slice: x: 2, y: 2, z: 4, core: 2. Of those that a mesh axis runs over, the one named last changes fastest.
Arguments:
- tokens: int32 [16384], P('dp'), may hold values from 0 to 30719
- positions: int32 [2, 16384], P(None, 'dp'), may hold values from 0 to 1000
- documents: int32 [32], P('dp'), may hold values from 0 to 7
- masking: int32 [16384], P('dp'), may hold values from 0 to 1, as said below
- negative_page: int32 [8, 16384], P(None, 'dp'), may hold values from 0 to 31
- negative_row: int32 [8, 16384], P(None, 'dp'), may hold values from 0 to 63, as said below
- pages: bfloat16 [32, 64, 768], P('dp'), may hold values from -6 to 6
- vocabulary: float32 [30720, 768], P('dp'), may hold values from -4.2 to 4.2
- geometry: float32 [768, 768], P(None, 'dp'), may hold values from -0.21875 to 0.21875
- mixing: float32 [768, 2304], P('dp'), may hold values from -0.21875 to 0.21875
- relative: float32 [768, 1536], P(None, 'dp'), may hold values from -0.3125 to 0.3125
- merging: float32 [768, 768], P('dp'), may hold values from -0.875 to 0.875
- widening: float32 [768, 3072], P('dp'), may hold values from -0.21875 to 0.21875
- narrowing: float32 [3072, 768], P('dp'), may hold values from -0.109375 to 0.109375
- scaling: float32 [6, 768], P(None, 'dp'), may hold values from -0.9 to 2.5
- moment_vocabulary: float32 [30720, 768], P('dp'), may hold values from -7.4505806e-08 to 7.4505806e-08
- moment_geometry: float32 [768, 768], P(None, 'dp'), may hold values from -3.0517578e-05 to 3.0517578e-05
- moment_mixing: float32 [768, 2304], P('dp'), may hold values from -3.0517578e-05 to 3.0517578e-05
- moment_relative: float32 [768, 1536], P(None, 'dp'), may hold values from -3.0517578e-05 to 3.0517578e-05
- moment_merging: float32 [768, 768], P('dp'), may hold values from -3.0517578e-05 to 3.0517578e-05
- moment_widening: float32 [768, 3072], P('dp'), may hold values from -3.0517578e-05 to 3.0517578e-05
- moment_narrowing: float32 [3072, 768], P('dp'), may hold values from -3.0517578e-05 to 3.0517578e-05
- moment_scaling: float32 [6, 768], P(None, 'dp'), may hold values from -0.00030517578 to 0.00030517578
- average_vocabulary: float32 [30720, 768], P('dp'), may hold values from -4.2 to 4.2
- average_geometry: float32 [768, 768], P(None, 'dp'), may hold values from -0.21875 to 0.21875
- average_mixing: float32 [768, 2304], P('dp'), may hold values from -0.21875 to 0.21875
- average_relative: float32 [768, 1536], P(None, 'dp'), may hold values from -0.3125 to 0.3125
- average_merging: float32 [768, 768], P('dp'), may hold values from -0.875 to 0.875
- average_widening: float32 [768, 3072], P('dp'), may hold values from -0.21875 to 0.21875
- average_narrowing: float32 [3072, 768], P('dp'), may hold values from -0.109375 to 0.109375
- average_scaling: float32 [6, 768], P(None, 'dp'), may hold values from -0.9 to 2.5
Outputs:
- loss: float32 [], replicated
- grad_norm: float32 [], replicated
- master_vocabulary: float32 [30720, 768], P('dp')
- master_geometry: float32 [768, 768], P(None, 'dp')
- master_mixing: float32 [768, 2304], P('dp')
- master_relative: float32 [768, 1536], P(None, 'dp')
- master_merging: float32 [768, 768], P('dp')
- master_widening: float32 [768, 3072], P('dp')
- master_narrowing: float32 [3072, 768], P('dp')
- master_scaling: float32 [6, 768], P(None, 'dp')
- velocity_vocabulary: float32 [30720, 768], P('dp')
- velocity_geometry: float32 [768, 768], P(None, 'dp')
- velocity_mixing: float32 [768, 2304], P('dp')
- velocity_relative: float32 [768, 1536], P(None, 'dp')
- velocity_merging: float32 [768, 768], P('dp')
- velocity_widening: float32 [768, 3072], P('dp')
- velocity_narrowing: float32 [3072, 768], P('dp')
- velocity_scaling: float32 [6, 768], P(None, 'dp')
- smooth_vocabulary: float32 [30720, 768], P('dp')
- smooth_geometry: float32 [768, 768], P(None, 'dp')
- smooth_mixing: float32 [768, 2304], P('dp')
- smooth_relative: float32 [768, 1536], P(None, 'dp')
- smooth_merging: float32 [768, 768], P('dp')
- smooth_widening: float32 [768, 3072], P('dp')
- smooth_narrowing: float32 [3072, 768], P('dp')
- smooth_scaling: float32 [6, 768], P(None, 'dp')
The draws below stay inside these ranges and needn't reach their ends.
Inputs may be any that keep to these rules, and one draw needn't show every extreme that they name: `masking`: 1 marks a masked token. negative_row[n, t] % 8 equals n.
All inputs are finite; a program needn't handle non-finite values.
Results may differ from the reference program's by a relative error of at most 0.011.
Values may be sent and summed in bfloat16 or wider, within the bound.
A program may use at most 248 MiB of HBM per device.

```python
import math
import jax
import jax.numpy as jnp
import numpy as np
from jax import lax

D = 768
H = 12
HD = 64
FF = 3072
VOCAB = 30720
FREQ = 192
SIN = 768
TOK = 512
NEG = 8
PAGE_ROWS = 64
DOCS = 8
STEP = 10
TOKENS = 16384
PAGES = 32
N_DP = 32


def draw_masking(key, part):
    key = jax.random.fold_in(key, 11)
    draws = jax.random.randint(key, (TOKENS,), 0, 1000)
    block_index = jnp.arange(TOKENS) // TOK
    limit = 200 + 400 * block_index // max(TOKENS // TOK - 1, 1)
    return (draws < limit).astype(jnp.int32)


def draw_negative_row(key, part):
    key = jax.random.fold_in(key, 12)
    base = jax.random.randint(key, (NEG, TOKENS), 0, PAGE_ROWS // NEG)
    return base * NEG + jnp.arange(NEG)[:, None]


def norm_table(key, low_end):
    gain_key, bias_key = jax.random.split(key)
    rising = jnp.arange(D).astype(jnp.float32) / D
    factors = jax.random.uniform(gain_key, (3, D), minval=0.8, maxval=1.25)
    gains = (low_end + rising)[None, :] * factors
    biases = 0.3 * jax.random.truncated_normal(bias_key, -3.0, 3.0, (3, D))
    return jnp.stack([gains[0], biases[0], gains[1], biases[1], gains[2], biases[2]], 0).astype(jnp.float32)


def draw_scaling(key, part):
    key = jax.random.fold_in(key, 13)
    return norm_table(key, 0.5)


def draw_average_scaling(key, part):
    key = jax.random.fold_in(key, 14)
    return norm_table(key, 0.5)


def place_ends(drawn, own_key, least, largest):
    shape = drawn.shape
    index_at = [jax.random.randint(jax.random.fold_in(own_key, axis), (), 0, shape[axis]) for axis in range(len(shape))]
    drawn = drawn.at[tuple(index_at)].set(least)
    longest = shape.index(max(shape))
    index_at[longest] = (index_at[longest] + 1) % shape[longest]
    return drawn.at[tuple(index_at)].set(largest)


def block_levels(key, extent, cuts, least, top_value):
    factor_of = 1.0
    for dim, parts in cuts:
        steps = jax.random.uniform(jax.random.fold_in(jax.random.fold_in(key, 6), dim), (parts,), jnp.float32, least / len(cuts), top_value / len(cuts))
        factor_of = factor_of * jnp.repeat(jnp.exp(steps), extent[dim] // parts).reshape((-1,) + (1,) * (len(extent) - 1 - dim))
    return factor_of


def rank_bounds(number_of, lean):
    weights = [(1 << 20) // math.isqrt(grade ** lean) + 1 for grade in range(1, number_of + 1)]
    scale = 1 + sum(weights) // (1 << 30)
    return np.cumsum(np.array([max(1, weight // scale) for weight in weights]))


def ranked(key, extent, number_of, lean):
    table = rank_bounds(number_of, lean)
    pick = jax.random.randint(jax.random.fold_in(key, 1), extent, 0, int(table[number_of - 1]))
    grade = jnp.searchsorted(jnp.asarray(table, jnp.int32), pick, side="right")
    return jax.random.permutation(jax.random.fold_in(key, 2), number_of)[grade].astype(jnp.int32)


def gaussian(rng, extent, deviation, most, shards=(), dtype=jnp.bfloat16):
    factor_of = block_levels(rng, extent, shards, -0.22, 0.18) if shards else 1.0
    drawn = jax.random.normal(rng, extent, jnp.float32) * deviation * factor_of
    return jnp.minimum(jnp.maximum(drawn, -most), most).astype(dtype)


def setup_inputs(seed: int = 0) -> dict:
    streams_of = jax.random.split(jax.random.key(seed), 32)
    return {
        "tokens": place_ends(ranked(streams_of[0], (TOKENS,), VOCAB, 2), jax.random.fold_in(streams_of[0], 3), 0, VOCAB - 1).astype(jnp.int32),
        "positions": place_ends(jax.random.randint(streams_of[1], (2, TOKENS), 0, 1001), jax.random.fold_in(streams_of[1], 1), 0, 1000).astype(jnp.int32),
        "documents": place_ends(jax.random.randint(streams_of[2], (N_DP,), 0, DOCS), jax.random.fold_in(streams_of[2], 1), 0, DOCS - 1).astype(jnp.int32),
        "masking": draw_masking(jax.random.fold_in(streams_of[31], 71), 0),
        "negative_page": place_ends(jax.random.randint(streams_of[4], (NEG, TOKENS), 0, PAGES), jax.random.fold_in(streams_of[4], 1), 0, PAGES - 1).astype(jnp.int32),
        "negative_row": draw_negative_row(jax.random.fold_in(streams_of[31], 71), 0),
        "pages": gaussian(streams_of[6], (PAGES, PAGE_ROWS, D), 1.0, 6.0, ((0, 32),)),
        "vocabulary": gaussian(streams_of[7], (VOCAB, D), 0.7, 4.2, ((0, 32),), jnp.float32),
        "geometry": gaussian(streams_of[8], (SIN, D), SIN ** -0.5, 0.21875, ((1, 32),), jnp.float32),
        "mixing": gaussian(streams_of[9], (D, 3 * D), D ** -0.5, 0.21875, ((0, 32),), jnp.float32),
        "relative": gaussian(streams_of[10], (SIN, 2 * D), (6 * HD) ** -0.5, 0.3125, ((1, 32),), jnp.float32),
        "merging": gaussian(streams_of[11], (D, D), (D // 16) ** -0.5, 0.875, ((0, 32),), jnp.float32),
        "widening": gaussian(streams_of[12], (D, FF), D ** -0.5, 0.21875, ((0, 32),), jnp.float32),
        "narrowing": gaussian(streams_of[13], (FF, D), FF ** -0.5, 0.109375, ((0, 32),), jnp.float32),
        "scaling": draw_scaling(jax.random.fold_in(streams_of[31], 71), 0),
        "moment_vocabulary": gaussian(streams_of[15], (VOCAB, D), (5e-9), 7.450580596923828e-08, ((0, 32),), jnp.float32),
        "moment_geometry": gaussian(streams_of[16], (SIN, D), (2e-6), 3.0517578125e-05, ((1, 32),), jnp.float32),
        "moment_mixing": gaussian(streams_of[17], (D, 3 * D), (2e-6), 3.0517578125e-05, ((0, 32),), jnp.float32),
        "moment_relative": gaussian(streams_of[18], (SIN, 2 * D), (2e-6), 3.0517578125e-05, ((1, 32),), jnp.float32),
        "moment_merging": gaussian(streams_of[19], (D, D), (2e-6), 3.0517578125e-05, ((0, 32),), jnp.float32),
        "moment_widening": gaussian(streams_of[20], (D, FF), (2e-6), 3.0517578125e-05, ((0, 32),), jnp.float32),
        "moment_narrowing": gaussian(streams_of[21], (FF, D), (2e-6), 3.0517578125e-05, ((0, 32),), jnp.float32),
        "moment_scaling": gaussian(streams_of[22], (6, D), (2e-5), 0.00030517578, ((1, 32),), jnp.float32),
        "average_vocabulary": gaussian(streams_of[23], (VOCAB, D), 0.7, 4.2, ((0, 32),), jnp.float32),
        "average_geometry": gaussian(streams_of[24], (SIN, D), SIN ** -0.5, 0.21875, ((1, 32),), jnp.float32),
        "average_mixing": gaussian(streams_of[25], (D, 3 * D), D ** -0.5, 0.21875, ((0, 32),), jnp.float32),
        "average_relative": gaussian(streams_of[26], (SIN, 2 * D), (6 * HD) ** -0.5, 0.3125, ((1, 32),), jnp.float32),
        "average_merging": gaussian(streams_of[27], (D, D), (D // 16) ** -0.5, 0.875, ((0, 32),), jnp.float32),
        "average_widening": gaussian(streams_of[28], (D, FF), D ** -0.5, 0.21875, ((0, 32),), jnp.float32),
        "average_narrowing": gaussian(streams_of[29], (FF, D), FF ** -0.5, 0.109375, ((0, 32),), jnp.float32),
        "average_scaling": draw_average_scaling(jax.random.fold_in(streams_of[31], 71), 0),
    }


mask_token = 103
ln_epsilon = 1e-06
momentum_decay = 0.9
learn_rate = 5000.0
table_rate = 1000000.0
clip_limit = 0.01
average_cap = 0.999
highest = lax.Precision.HIGHEST

@jax.custom_vjp
def low(v):
    return lax.optimization_barrier(v.astype(jnp.bfloat16)).astype(jnp.float32)

@jax.custom_vjp
def low_back(v):
    return v

def low_keep(v):
    return (low(v), None)

def low_pass(kept, grad):
    return (grad,)

def back_keep(v):
    return (v, None)

def back_low(kept, grad):
    return (low(grad),)
low.defvjp(low_keep, low_pass)
low_back.defvjp(back_keep, back_low)

def sinusoids(positions, count):
    ranks = jnp.arange(count).astype(jnp.float32)
    omegas = jnp.power(10000.0, -ranks / count)
    angle_x = positions[0].astype(jnp.float32)[:, None] * omegas[None, :]
    angle_y = positions[1].astype(jnp.float32)[:, None] * omegas[None, :]
    return (jnp.sin(angle_x), jnp.cos(angle_x), jnp.sin(angle_y), jnp.cos(angle_y))

def rotate(table, waves):
    sin_x, cos_x, sin_y, cos_y = waves
    count = sin_x.shape[-1]
    sine_x = table[..., :count]
    cosine_x = table[..., count:2 * count]
    sine_y = table[..., 2 * count:3 * count]
    cosine_y = table[..., 3 * count:]
    return jnp.concatenate([sine_x * sin_x + cosine_x * cos_x, sine_y * sin_y + cosine_y * cos_y, cosine_x * sin_x - sine_x * cos_x, cosine_y * sin_y - sine_y * cos_y], -1)

def layer_norm(rows, gain, bias):
    centred = rows - lax.optimization_barrier(jnp.mean(rows, -1, keepdims=True))
    rescale = lax.rsqrt(lax.optimization_barrier(jnp.mean(centred * centred, -1, keepdims=True)) + ln_epsilon)
    return centred * rescale * gain + bias

def block_loss(params, bank, block):
    table, box_map, mix_map, rel_map, out_map, up_map, down_map, norm_rows = params
    tokens, positions, masking, flat_index, share = block
    waves = sinusoids(positions, FREQ)
    boxes = low(jnp.concatenate(waves, -1))
    entry = jnp.where(masking == 1, mask_token, tokens)
    embedded = table[entry] + low_back(jnp.dot(boxes, box_map, precision=highest))
    normed = layer_norm(embedded, norm_rows[0], norm_rows[1])
    joined = low_back(jnp.dot(low(normed), mix_map, precision=highest))
    queries = low(joined[:, :D]).reshape(TOK, H, HD)
    keys_low = low(joined[:, D:2 * D]).reshape(TOK, H, HD)
    values_low = low(joined[:, 2 * D:]).reshape(TOK, H, HD)
    text_terms = low_back(jnp.einsum('thd,fhd->htf', queries, rel_map[:, :D].reshape(SIN, H, HD), precision=highest))
    box_terms = low_back(jnp.einsum('thd,fhd->htf', keys_low, rel_map[:, D:].reshape(SIN, H, HD), precision=highest))
    bases = low(jnp.concatenate([waves[1], waves[3], waves[0], waves[2]], -1))
    spread = jnp.broadcast_to(bases[None], (H, TOK, SIN))
    query_ext = jnp.concatenate([queries.transpose(1, 0, 2), low(rotate(text_terms, waves)), spread], -1)
    key_ext = jnp.concatenate([keys_low.transpose(1, 0, 2), spread, low(rotate(box_terms, waves))], -1)
    scores = low_back(jnp.einsum('htf,hsf->hts', query_ext, key_ext, precision=highest) * HD ** (-0.5))
    probs = jax.nn.softmax(scores, axis=-1)
    attended = jnp.einsum('hts,shd->thd', low(probs), values_low, precision=highest).reshape(TOK, D)
    attended = low(low_back(attended))
    middle = layer_norm(normed + low_back(jnp.dot(attended, out_map, precision=highest)), norm_rows[2], norm_rows[3])
    hidden = jax.nn.gelu(low_back(jnp.dot(low(middle), up_map, precision=highest)), approximate=False)
    residual = middle + low_back(jnp.dot(low(hidden), down_map, precision=highest))
    states_low = low(layer_norm(residual, norm_rows[4], norm_rows[5]))
    inv_root = D ** (-0.5)
    positive = lax.optimization_barrier(jnp.sum(states_low * table[tokens], -1)) * inv_root
    rows = bank[flat_index]
    negative = low_back(jnp.einsum('td,ntd->nt', states_low, rows, precision=highest)) * inv_root
    logits = jnp.concatenate([positive[None], negative], 0)
    per_token = jax.scipy.special.logsumexp(logits, axis=0) - positive
    return share * jnp.sum(masking.astype(jnp.float32) * per_token)

def reference(tokens, positions, documents, masking, negative_page, negative_row, pages, vocabulary, geometry, mixing, relative, merging, widening, narrowing, scaling, moment_vocabulary, moment_geometry, moment_mixing, moment_relative, moment_merging, moment_widening, moment_narrowing, moment_scaling, average_vocabulary, average_geometry, average_mixing, average_relative, average_merging, average_widening, average_narrowing, average_scaling):
    masters = (vocabulary, geometry, mixing, relative, merging, widening, narrowing, scaling)
    moments = (moment_vocabulary, moment_geometry, moment_mixing, moment_relative, moment_merging, moment_widening, moment_narrowing, moment_scaling)
    averages = (average_vocabulary, average_geometry, average_mixing, average_relative, average_merging, average_widening, average_narrowing, average_scaling)
    params = tuple((master.astype(jnp.bfloat16).astype(jnp.float32) for master in masters))
    bank = pages.astype(jnp.float32).reshape(-1, D)
    blocks = documents.shape[0]
    mask_rows = masking.reshape(blocks, TOK)
    per_block = lax.optimization_barrier(jnp.sum(mask_rows.astype(jnp.float32), 1))
    chosen = (documents[:, None] == jnp.arange(DOCS)[None, :]).astype(jnp.float32)
    counts = lax.optimization_barrier(jnp.sum(chosen * per_block[:, None], 0))
    shares = 1.0 / (DOCS * jnp.maximum(lax.optimization_barrier(jnp.sum(chosen * counts[None, :], 1)), 1.0))
    flat = (negative_page * PAGE_ROWS + negative_row).reshape(NEG, blocks, TOK).transpose(1, 0, 2)
    inputs = (tokens.reshape(blocks, TOK), positions.reshape(2, blocks, TOK).transpose(1, 0, 2), mask_rows, flat, shares)
    checked = jax.checkpoint(block_loss)

    def total(weights):

        def accumulate(carry, block):
            return (carry + checked(weights, bank, block), None)
        return lax.scan(accumulate, jnp.zeros((), jnp.float32), inputs)[0]
    loss, pullback = jax.vjp(total, params)
    grads = pullback(jnp.ones((), jnp.float32))[0]
    grad_norm = jnp.sqrt(sum((jnp.sum(piece * piece) for piece in grads)))
    factor = clip_limit / jnp.maximum(grad_norm, clip_limit)
    decay = min(average_cap, (1.0 + STEP) / (10.0 + STEP))
    rates = (table_rate,) + (learn_rate,) * 7
    fresh, speeds, smooths = ([], [], [])
    for master, moment, average, piece, rate in zip(masters, moments, averages, grads, rates):
        clipped = piece * factor
        velocity = momentum_decay * moment + clipped
        updated = master - rate * (clipped + momentum_decay * velocity)
        fresh.append(updated)
        speeds.append(velocity)
        smooths.append(decay * average + (1.0 - decay) * updated)
    return (loss, grad_norm, fresh[0], fresh[1], fresh[2], fresh[3], fresh[4], fresh[5], fresh[6], fresh[7], speeds[0], speeds[1], speeds[2], speeds[3], speeds[4], speeds[5], speeds[6], speeds[7], smooths[0], smooths[1], smooths[2], smooths[3], smooths[4], smooths[5], smooths[6], smooths[7])
```

```python
from functools import partial

import jax
import jax.numpy as jnp
from jax import lax
from jax.experimental import pallas as pl
from jax.experimental.pallas import tpu as pltpu
from jax.sharding import PartitionSpec as P

HD = 64
DOCS = 8
STEP = 10
MESH = pl.DeviceIdType.MESH

mask_token = 103
ln_epsilon = 1e-06
momentum_decay = 0.9
learn_rate = 5000.0
table_rate = 1000000.0
clip_limit = 0.01
average_cap = 0.999


def sinusoids(positions, count):
    ranks = jnp.arange(count).astype(jnp.float32)
    omegas = jnp.power(10000.0, -ranks / count)
    angle_x = positions[0].astype(jnp.float32)[:, None] * omegas[None, :]
    angle_y = positions[1].astype(jnp.float32)[:, None] * omegas[None, :]
    return (jnp.sin(angle_x), jnp.cos(angle_x), jnp.sin(angle_y), jnp.cos(angle_y))


def rotate(table, waves):
    sin_x, cos_x, sin_y, cos_y = waves
    count = sin_x.shape[-1]
    sine_x = table[..., :count]
    cosine_x = table[..., count : 2 * count]
    sine_y = table[..., 2 * count : 3 * count]
    cosine_y = table[..., 3 * count :]
    return jnp.concatenate(
        [
            sine_x * sin_x + cosine_x * cos_x,
            sine_y * sin_y + cosine_y * cos_y,
            cosine_x * sin_x - sine_x * cos_x,
            cosine_y * sin_y - sine_y * cos_y,
        ],
        -1,
    )


def rotate_back(upstream, waves):
    sin_x, cos_x, sin_y, cos_y = waves
    count = sin_x.shape[-1]
    first = upstream[..., :count]
    second = upstream[..., count : 2 * count]
    third = upstream[..., 2 * count : 3 * count]
    fourth = upstream[..., 3 * count :]
    return jnp.concatenate(
        [
            first * sin_x - third * cos_x,
            first * cos_x + third * sin_x,
            second * sin_y - fourth * cos_y,
            second * cos_y + fourth * sin_y,
        ],
        -1,
    )


def layer_norm(rows, gain, bias):
    centred = rows - jnp.mean(rows, -1, keepdims=True)
    rescale = lax.rsqrt(jnp.mean(centred * centred, -1, keepdims=True) + ln_epsilon)
    whitened = centred * rescale
    return (whitened * gain + bias, whitened, rescale)


def norm_back(upstream, whitened, rescale, gain):
    scaled = upstream * gain
    inner = (
        scaled
        - jnp.mean(scaled, -1, keepdims=True)
        - whitened * jnp.mean(scaled * whitened, -1, keepdims=True)
    )
    return (rescale * inner, jnp.sum(upstream * whitened, 0), jnp.sum(upstream, 0))


def dot_nn(left, right):
    return lax.dot_general(
        left, right, (((1,), (0,)), ((), ())), preferred_element_type=jnp.float32
    )


def dot_tn(left, right):
    return lax.dot_general(
        left, right, (((0,), (0,)), ((), ())), preferred_element_type=jnp.float32
    )


def dot_nt(left, right):
    return lax.dot_general(
        left, right, (((1,), (1,)), ((), ())), preferred_element_type=jnp.float32
    )


def exchange_kernel(n, src, dst, send_sem, recv_sem, own_sem):
    me = lax.axis_index("dp")
    barrier = pltpu.get_barrier_semaphore()

    def greet(step, carry):
        pl.semaphore_signal(
            barrier, inc=1, device_id=(lax.rem(me + step, n),), device_id_type=MESH
        )
        return carry

    lax.fori_loop(1, n, greet, 0)
    own = pltpu.make_async_copy(src.at[me], dst.at[me], own_sem)
    own.start()
    pl.semaphore_wait(barrier, n - 1)

    def copy(step):
        peer = lax.rem(me + step, n)
        return pltpu.make_async_remote_copy(
            src_ref=src.at[peer],
            dst_ref=dst.at[me],
            send_sem=send_sem.at[step],
            recv_sem=recv_sem.at[step],
            device_id=(peer,),
            device_id_type=MESH,
        )

    def start(step, carry):
        copy(step).start()
        return carry

    def finish(step, carry):
        copy(step).wait()
        return carry

    lax.fori_loop(1, n, start, 0)
    lax.fori_loop(1, n, finish, 0)
    own.wait()


def exchange(blocks, ident, name):
    n = blocks.shape[0]
    return pl.pallas_call(
        partial(exchange_kernel, n),
        name=name,
        out_shape=jax.ShapeDtypeStruct(blocks.shape, blocks.dtype),
        in_specs=[pl.BlockSpec(memory_space=pl.ANY)],
        out_specs=pl.BlockSpec(memory_space=pl.ANY),
        scratch_shapes=[
            pltpu.SemaphoreType.DMA((n,)),
            pltpu.SemaphoreType.DMA((n,)),
            pltpu.SemaphoreType.DMA,
        ],
        compiler_params=pltpu.CompilerParams(collective_id=ident, has_side_effects=True),
        cost_estimate=pl.CostEstimate(
            flops=0, bytes_accessed=2 * blocks.size * blocks.dtype.itemsize, transcendentals=0
        ),
    )(blocks)


def plan_kernel(
    n, rows_own, capacity, tok_col, tok_row, mask_row, doc, info, lists, place
):
    size = tok_col.shape[0]
    ids_col = tok_col[...]
    ids_row = tok_row[...]
    owner_col = lax.div(ids_col, rows_own)
    owner_row = lax.div(ids_row, rows_own)
    at_col = lax.broadcasted_iota(jnp.int32, (size, size), 0)
    at_row = lax.broadcasted_iota(jnp.int32, (size, size), 1)
    same = ids_col == ids_row
    first_col = jnp.min(jnp.where(same, at_row, size), 1, keepdims=True)
    first_row = jnp.min(jnp.where(same, at_col, size), 0, keepdims=True)
    leads_row = first_row == lax.broadcasted_iota(jnp.int32, (1, size), 1)
    leads_col = first_col == lax.broadcasted_iota(jnp.int32, (size, 1), 0)
    ahead = (owner_col == owner_row) & leads_row & (at_row < first_col)
    slot = jnp.sum(jnp.where(ahead, 1.0, 0.0), 1, keepdims=True).astype(jnp.int32)
    fits = slot < capacity - 1
    place[...] = jnp.where(fits, owner_col * capacity + slot, -1)
    over = jnp.max(jnp.where(fits, 0.0, 1.0), keepdims=True)
    local = ids_col - owner_col * rows_own + 1
    high = lax.div(local, 128)
    to_owner = lax.broadcasted_iota(jnp.int32, (size, n), 1) == owner_col
    to_owner = to_owner & leads_col & fits
    in_slot = lax.broadcasted_iota(jnp.int32, (size, 128), 1) == slot
    in_slot = jnp.where(in_slot, 1.0, 0.0).astype(jnp.bfloat16)
    high_part = jnp.where(to_owner, high.astype(jnp.float32), 0.0).astype(jnp.bfloat16)
    low_part = jnp.where(to_owner, (local - high * 128).astype(jnp.float32), 0.0)
    table = dot_tn(high_part, in_slot) * 128.0 + dot_tn(low_part.astype(jnp.bfloat16), in_slot)
    lane = lax.broadcasted_iota(jnp.int32, (n, 128), 1)
    line = lax.broadcasted_iota(jnp.int32, (n, 128), 0)
    fixed = (line == mask_token // rows_own) & (lane == capacity - 1)
    table = jnp.where(fixed, float(mask_token % rows_own + 1), table)
    count = jnp.sum(mask_row[...].astype(jnp.float32), keepdims=True)
    table = jnp.where(lane == 125, count, table)
    table = jnp.where(lane == 126, doc[0].astype(jnp.float32), table)
    table = jnp.where(lane == 127, over, table)
    lists[...] = jnp.broadcast_to(table[:, None, :], lists.shape)


def make_plan(tokens, masking, documents, n, rows_own, capacity):
    size = tokens.shape[0]
    vmem = pl.BlockSpec(memory_space=pltpu.VMEM)
    return pl.pallas_call(
        partial(plan_kernel, n, rows_own, capacity),
        name="plan",
        out_shape=(
            jax.ShapeDtypeStruct((n, 8, 128), jnp.float32),
            jax.ShapeDtypeStruct((size, 1), jnp.int32),
        ),
        in_specs=[vmem, vmem, vmem, pl.BlockSpec(memory_space=pltpu.SMEM), vmem],
        out_specs=(vmem, vmem),
        compiler_params=pltpu.CompilerParams(vmem_limit_bytes=32 * 2**20),
    )(
        tokens[:, None],
        tokens[None, :],
        masking[None, :],
        documents,
        jnp.zeros((8, 128), jnp.float32),
    )


def forward(weights, rows, positions):
    box_map, mix_map, rel_map, out_map, up_map, down_map, norm_rows = weights
    gains = norm_rows.astype(jnp.float32)
    count_tok = rows.shape[0]
    model = rows.shape[1]
    heads = model // HD
    sin_count = box_map.shape[1]
    waves = sinusoids(positions, sin_count // 4)
    boxes = jnp.concatenate(waves, -1).astype(jnp.bfloat16)
    embedded = rows + dot_nt(boxes, box_map)
    first = layer_norm(embedded, gains[0], gains[1])
    normed = first[0].astype(jnp.bfloat16)
    thirds = [dot_nn(normed, part).astype(jnp.bfloat16) for part in mix_map]
    queries, keys_low, values_low = [
        third.reshape(count_tok, heads, HD).transpose(1, 0, 2) for third in thirds
    ]
    rel_text = rel_map[:model].reshape(heads, HD, sin_count)
    rel_box = rel_map[model:].reshape(heads, HD, sin_count)
    text_terms = jnp.einsum("htd,hdf->htf", queries, rel_text, preferred_element_type=jnp.float32)
    box_terms = jnp.einsum("htd,hdf->htf", keys_low, rel_box, preferred_element_type=jnp.float32)
    bases = jnp.concatenate([waves[1], waves[3], waves[0], waves[2]], -1).astype(jnp.bfloat16)
    text_rot = rotate(text_terms, waves).astype(jnp.bfloat16)
    box_rot = rotate(box_terms, waves).astype(jnp.bfloat16)
    scores = (
        jnp.einsum("htd,hsd->hts", queries, keys_low, preferred_element_type=jnp.float32)
        + jnp.einsum("htf,sf->hts", text_rot, bases, preferred_element_type=jnp.float32)
        + jnp.einsum("tf,hsf->hts", bases, box_rot, preferred_element_type=jnp.float32)
    ) * HD ** (-0.5)
    highest = jnp.max(scores, -1, keepdims=True)
    totals = highest + jnp.log(jnp.sum(jnp.exp(scores - highest), -1, keepdims=True))
    probs = jnp.exp(scores - totals)
    attended = jnp.einsum(
        "hts,hsd->thd", probs.astype(jnp.bfloat16), values_low, preferred_element_type=jnp.float32
    )
    attended = attended.reshape(count_tok, model).astype(jnp.bfloat16)
    second = layer_norm(first[0] + dot_nn(attended, out_map), gains[2], gains[3])
    middle = second[0].astype(jnp.bfloat16)
    hidden_pre = [dot_nn(middle, part) for part in up_map]
    hidden = [jax.nn.gelu(part, approximate=False).astype(jnp.bfloat16) for part in hidden_pre]
    lowered = sum(dot_nn(part, weight) for part, weight in zip(hidden, down_map))
    third = layer_norm(second[0] + lowered, gains[4], gains[5])
    return {
        "waves": waves,
        "boxes": boxes,
        "bases": bases,
        "first": first,
        "normed": normed,
        "queries": queries,
        "keys": keys_low,
        "values": values_low,
        "probs": probs,
        "attended": attended,
        "second": second,
        "middle": middle,
        "hidden_pre": hidden_pre,
        "hidden": hidden,
        "third": third,
    }


def backward(weights, cache, d_states):
    box_map, mix_map, rel_map, out_map, up_map, down_map, norm_rows = weights
    gains = norm_rows.astype(jnp.float32)
    count_tok = d_states.shape[0]
    model = d_states.shape[1]
    heads = model // HD
    sin_count = box_map.shape[1]
    d_mid, gain_last, bias_last = norm_back(
        d_states, cache["third"][1], cache["third"][2], gains[4]
    )
    d_down = d_mid.astype(jnp.bfloat16)
    gelu_exact = partial(jax.nn.gelu, approximate=False)
    grad_down, grad_up, d_second = [], [], d_mid
    for pre, hidden, up, down in zip(cache["hidden_pre"], cache["hidden"], up_map, down_map):
        grad_down.append(dot_tn(hidden, d_down))
        d_pre = jax.vjp(gelu_exact, pre)[1](dot_nt(d_down, down))[0].astype(jnp.bfloat16)
        grad_up.append(dot_tn(cache["middle"], d_pre))
        d_second = d_second + dot_nt(d_pre, up)
    d_lower, gain_mid, bias_mid = norm_back(
        d_second, cache["second"][1], cache["second"][2], gains[2]
    )
    d_attn = d_lower.astype(jnp.bfloat16)
    grad_out = dot_tn(cache["attended"], d_attn)
    d_attended = dot_nt(d_attn, out_map).astype(jnp.bfloat16).reshape(count_tok, heads, HD)
    d_attended = d_attended.transpose(1, 0, 2)
    probs, bases = cache["probs"], cache["bases"]
    d_probs = jnp.einsum(
        "htd,hsd->hts", d_attended, cache["values"], preferred_element_type=jnp.float32
    )
    grad_values = jnp.einsum(
        "hts,htd->hsd", probs.astype(jnp.bfloat16), d_attended, preferred_element_type=jnp.float32
    )
    d_scores = (probs * (d_probs - jnp.sum(d_probs * probs, -1, keepdims=True))).astype(
        jnp.bfloat16
    )
    scale = HD ** (-0.5)
    d_text = jnp.einsum("hts,sf->htf", d_scores, bases, preferred_element_type=jnp.float32) * scale
    d_box = jnp.einsum("hts,tf->hsf", d_scores, bases, preferred_element_type=jnp.float32) * scale
    d_text = rotate_back(d_text, cache["waves"]).astype(jnp.bfloat16)
    d_box = rotate_back(d_box, cache["waves"]).astype(jnp.bfloat16)
    rel_text = rel_map[:model].reshape(heads, HD, sin_count)
    rel_box = rel_map[model:].reshape(heads, HD, sin_count)
    grad_rel = jnp.concatenate(
        [
            jnp.einsum(
                "htd,htf->hdf", cache["queries"], d_text, preferred_element_type=jnp.float32
            ).reshape(model, sin_count),
            jnp.einsum(
                "htd,htf->hdf", cache["keys"], d_box, preferred_element_type=jnp.float32
            ).reshape(model, sin_count),
        ],
        0,
    )
    grad_queries = jnp.einsum(
        "hts,hsd->htd", d_scores, cache["keys"], preferred_element_type=jnp.float32
    ) * scale + jnp.einsum("htf,hdf->htd", d_text, rel_text, preferred_element_type=jnp.float32)
    grad_keys = jnp.einsum(
        "hts,htd->hsd", d_scores, cache["queries"], preferred_element_type=jnp.float32
    ) * scale + jnp.einsum("htf,hdf->htd", d_box, rel_box, preferred_element_type=jnp.float32)
    d_joined = [
        part.astype(jnp.bfloat16).transpose(1, 0, 2).reshape(count_tok, model)
        for part in (grad_queries, grad_keys, grad_values)
    ]
    grad_mix = [dot_tn(cache["normed"], part) for part in d_joined]
    d_first = d_lower + sum(dot_nt(part, weight) for part, weight in zip(d_joined, mix_map))
    d_embedded, gain_low, bias_low = norm_back(
        d_first, cache["first"][1], cache["first"][2], gains[0]
    )
    grad_box = dot_tn(d_embedded.astype(jnp.bfloat16), cache["boxes"])
    grad_norms = jnp.stack([gain_low, bias_low, gain_mid, bias_mid, gain_last, bias_last], 0)
    return (d_embedded, (grad_box, grad_mix, grad_rel, grad_out, grad_up, grad_down, grad_norms))


def per_device(
    n,
    tokens,
    positions,
    documents,
    masking,
    negative_page,
    negative_row,
    pages,
    vocabulary,
    geometry,
    mixing,
    relative,
    merging,
    widening,
    narrowing,
    scaling,
    moment_vocabulary,
    moment_geometry,
    moment_mixing,
    moment_relative,
    moment_merging,
    moment_widening,
    moment_narrowing,
    moment_scaling,
    average_vocabulary,
    average_geometry,
    average_mixing,
    average_relative,
    average_merging,
    average_widening,
    average_narrowing,
    average_scaling,
):
    me = lax.axis_index("dp")
    size = tokens.shape[0]
    rows_own, model = vocabulary.shape
    page_rows = pages.shape[1]
    capacity = max(16, -(-2 * size // n) // 16 * 16)
    slots = n * capacity
    mask_float = masking.astype(jnp.float32)
    low = jnp.bfloat16

    parts = (
        geometry.T.astype(low),
        relative.T.astype(low),
        *[mixing[:, k * model : (k + 1) * model].astype(low) for k in range(3)],
    )
    later = (
        merging.astype(low),
        *[
            widening[:, k * model : (k + 1) * model].astype(low)
            for k in range(widening.shape[1] // model)
        ],
        narrowing.astype(low),
        pages.reshape(-1, model),
    )

    def gather(pieces):
        rows = [piece.shape[0] for piece in pieces]
        joined = lax.all_gather(jnp.concatenate(pieces, 0), "dp", axis=0, tiled=False)
        out, at = [], 0
        for count in rows:
            out.append(joined[:, at : at + count].reshape(-1, model))
            at += count
        return out

    early = gather(parts)
    late = gather(later)
    norm_rows = lax.all_gather(scaling.astype(low), "dp", axis=1, tiled=True)
    box_map, rel_map, mix_map = early[0], early[1], early[2:5]
    out_map, up_map, down_full, bank = late[0], late[1:-2], late[-2], late[-1]

    lists, place = make_plan(tokens, masking, documents, n, rows_own, capacity)
    asked = exchange(lists, 1, "ask")[:, 0, :]
    doc_of, count_of = asked[:, 126], asked[:, 125]
    overflow = jnp.max(asked[:, 127]) > 0.0
    my_count = jnp.sum(jnp.where(doc_of == documents[0].astype(jnp.float32), count_of, 0.0))
    share = 1.0 / (DOCS * jnp.maximum(my_count, 1.0))
    wanted = asked[:, :capacity].reshape(slots, 1)
    picks = (wanted == (jnp.arange(rows_own) + 1).astype(jnp.float32)[None, :]).astype(low)
    answer = dot_nn(picks, vocabulary.astype(low)).astype(low)
    table_rows = exchange(answer.reshape(n, capacity, model), 2, "rows").reshape(slots, model)
    fixed = (mask_token // rows_own) * capacity + capacity - 1
    seats = (place == jnp.arange(slots)[None, :]).astype(low)
    target_rows = dot_nn(seats, table_rows)
    mask_rows = table_rows[fixed : fixed + 1].astype(jnp.float32)

    def dense_rows():
        table = lax.all_gather(vocabulary.astype(low), "dp", axis=0, tiled=True)
        return (
            table[tokens].astype(jnp.float32),
            table[mask_token : mask_token + 1].astype(jnp.float32),
        )

    target_rows, mask_rows = lax.cond(overflow, dense_rows, lambda: (target_rows, mask_rows))
    entry_rows = jnp.where(masking[:, None] == 1, mask_rows, target_rows)

    ff = len(up_map)
    down_map = [down_full[k * model : (k + 1) * model] for k in range(ff)]
    weights = (box_map, mix_map, rel_map, out_map, up_map, down_map, norm_rows)
    cache = forward(weights, entry_rows, positions)

    states_low = cache["third"][0].astype(low)
    inv_root = model ** (-0.5)
    positive = jnp.sum(states_low.astype(jnp.float32) * target_rows, -1, keepdims=True) * inv_root
    flat_index = (negative_page * page_rows + negative_row).T
    count_neg = flat_index.shape[1]
    width = bank.shape[0]
    repeated = jnp.tile(flat_index, (1, width // count_neg))
    chosen = repeated == jnp.arange(width)[None, :]
    logits = jnp.where(chosen, dot_nt(states_low, bank) * inv_root, -jnp.inf)
    highest = jnp.maximum(jnp.max(logits, -1, keepdims=True), positive)
    powers = jnp.exp(logits - highest)
    lead = jnp.exp(positive - highest)
    total = jnp.sum(powers, -1, keepdims=True) + lead
    per_token = highest + jnp.log(total) - positive
    mask_col = mask_float[:, None]
    loss_part = share * jnp.sum(mask_col * per_token)
    weight_map = (powers * (share * mask_col / total) * inv_root).astype(low)
    positive_grad = share * mask_col * (lead / total - 1.0) * inv_root
    d_states = positive_grad * target_rows + dot_nn(weight_map, bank)

    d_embedded, layer_grads = backward(weights, cache, d_states)

    positive_rows = positive_grad * states_low.astype(jnp.float32)

    def sparse_table():
        token_grads = jnp.where(mask_col == 1.0, positive_rows, d_embedded).astype(low)
        mask_grad = jnp.sum(mask_col * d_embedded, 0, keepdims=True)
        sent = dot_tn(seats, token_grads)
        sent = jnp.where(jnp.arange(slots)[:, None] == fixed, mask_grad, sent).astype(low)
        came = exchange(sent.reshape(n, capacity, model), 3, "grads").reshape(slots, model)
        return dot_tn(picks, came)

    def dense_table():
        entry = jnp.where(masking == 1, mask_token, tokens)
        table_grad = jnp.zeros((rows_own * n, model), jnp.float32).at[entry].add(d_embedded)
        table_grad = table_grad.at[tokens].add(positive_rows)
        return lax.psum_scatter(table_grad, "dp", scatter_dimension=0, tiled=True)

    table_piece = lax.cond(overflow, dense_table, sparse_table)

    grad_box, grad_mix, grad_rel, grad_out, grad_up, grad_down, grad_norms = layer_grads
    grad_down = jnp.concatenate(grad_down, 0)

    def scatter(pieces):
        blocks = [piece.astype(low).reshape(n, -1, model) for piece in pieces]
        rows = [block.shape[1] for block in blocks]
        joined = jnp.concatenate(blocks, 1).reshape(-1, model)
        mine = lax.psum_scatter(joined, "dp", scatter_dimension=0, tiled=True).astype(jnp.float32)
        out, at = [], 0
        for count in rows:
            out.append(mine[at : at + count])
            at += count
        return out

    first = scatter([grad_down, *grad_up])
    last = scatter([grad_out, grad_box, grad_rel, *grad_mix])
    norm_piece = lax.psum_scatter(grad_norms, "dp", scatter_dimension=1, tiled=True)
    reduced = (
        table_piece,
        last[1].T,
        jnp.concatenate(last[3:], 1),
        last[2].T,
        last[0],
        jnp.concatenate(first[1:], 1),
        first[0],
        norm_piece,
    )
    square = sum((jnp.sum(piece * piece) for piece in reduced))
    message = jnp.where(jnp.arange(128) == 0, square, jnp.where(jnp.arange(128) == 1, loss_part, 0.0))
    sums = exchange(jnp.broadcast_to(message, (n, 8, 128)), 4, "totals")
    sums = jnp.sum(sums[:, 0, :2], 0)
    loss = sums[1]
    grad_norm = jnp.sqrt(sums[0])
    factor = clip_limit / jnp.maximum(grad_norm, clip_limit)
    decay = min(average_cap, (1.0 + STEP) / (10.0 + STEP))
    masters = (vocabulary, geometry, mixing, relative, merging, widening, narrowing, scaling)
    moments = (
        moment_vocabulary,
        moment_geometry,
        moment_mixing,
        moment_relative,
        moment_merging,
        moment_widening,
        moment_narrowing,
        moment_scaling,
    )
    averages = (
        average_vocabulary,
        average_geometry,
        average_mixing,
        average_relative,
        average_merging,
        average_widening,
        average_narrowing,
        average_scaling,
    )
    rates = (table_rate,) + (learn_rate,) * 7
    fresh, speeds, smooths = ([], [], [])
    for master, moment, average, piece, rate in zip(masters, moments, averages, reduced, rates):
        clipped = piece * factor
        velocity = momentum_decay * moment + clipped
        updated = master - rate * (clipped + momentum_decay * velocity)
        fresh.append(updated)
        speeds.append(velocity)
        smooths.append(decay * average + (1.0 - decay) * updated)
    return (loss, grad_norm, *fresh, *speeds, *smooths)


ROWS = P("dp", None)
COLS = P(None, "dp")
WEIGHTS = (ROWS, COLS, ROWS, COLS, ROWS, ROWS, ROWS, COLS)


def solution(mesh):
    return jax.shard_map(
        partial(per_device, mesh.shape["dp"]),
        mesh=mesh,
        in_specs=(P("dp"), COLS, P("dp"), P("dp"), COLS, COLS, P("dp", None, None)) + 3 * WEIGHTS,
        out_specs=(P(), P()) + 3 * WEIGHTS,
        check_vma=False,
    )
```

```python
from functools import partial

import jax
import jax.numpy as jnp
from jax import lax
from jax.experimental import pallas as pl
from jax.experimental.pallas import tpu as pltpu
from jax.sharding import PartitionSpec as P

HD = 64
DOCS = 8
STEP = 10
MESH = pl.DeviceIdType.MESH

mask_token = 103
ln_epsilon = 1e-06
momentum_decay = 0.9
learn_rate = 5000.0
table_rate = 1000000.0
clip_limit = 0.01
average_cap = 0.999


def sinusoids(positions, count):
    ranks = jnp.arange(count).astype(jnp.float32)
    omegas = jnp.power(10000.0, -ranks / count)
    angle_x = positions[0].astype(jnp.float32)[:, None] * omegas[None, :]
    angle_y = positions[1].astype(jnp.float32)[:, None] * omegas[None, :]
    return (jnp.sin(angle_x), jnp.cos(angle_x), jnp.sin(angle_y), jnp.cos(angle_y))


def layer_norm(rows, gain, bias):
    centred = rows - jnp.mean(rows, -1, keepdims=True)
    rescale = lax.rsqrt(jnp.mean(centred * centred, -1, keepdims=True) + ln_epsilon)
    whitened = centred * rescale
    return (whitened * gain + bias, whitened, rescale)


def norm_back(upstream, whitened, rescale, gain):
    scaled = upstream * gain
    inner = (
        scaled
        - jnp.mean(scaled, -1, keepdims=True)
        - whitened * jnp.mean(scaled * whitened, -1, keepdims=True)
    )
    return (rescale * inner, jnp.sum(upstream * whitened, 0), jnp.sum(upstream, 0))


def dot_nn(left, right):
    return lax.dot_general(
        left, right, (((1,), (0,)), ((), ())), preferred_element_type=jnp.float32
    )


def dot_tn(left, right):
    return lax.dot_general(
        left, right, (((0,), (0,)), ((), ())), preferred_element_type=jnp.float32
    )


def dot_nt(left, right):
    return lax.dot_general(
        left, right, (((1,), (1,)), ((), ())), preferred_element_type=jnp.float32
    )


def exchange_kernel(n, count, *refs):
    srcs, dsts = refs[:count], refs[count : 2 * count]
    send_sem, recv_sem, own_sem = refs[2 * count :]
    me = lax.axis_index("dp")
    barrier = pltpu.get_barrier_semaphore()

    def greet(step, carry):
        pl.semaphore_signal(
            barrier, inc=1, device_id=(lax.rem(me + step, n),), device_id_type=MESH
        )
        return carry

    lax.fori_loop(1, n, greet, 0)
    for k in range(count):
        pltpu.make_async_copy(srcs[k].at[me], dsts[k].at[me], own_sem.at[k]).start()
    pl.semaphore_wait(barrier, n - 1)

    def copy(k, step):
        peer = lax.rem(me + step, n)
        return pltpu.make_async_remote_copy(
            src_ref=srcs[k].at[peer],
            dst_ref=dsts[k].at[me],
            send_sem=send_sem.at[k, step],
            recv_sem=recv_sem.at[k, step],
            device_id=(peer,),
            device_id_type=MESH,
        )

    def start(step, carry):
        for k in range(count):
            copy(k, step).start()
        return carry

    def finish(step, carry):
        for k in range(count):
            copy(k, step).wait()
        return carry

    lax.fori_loop(1, n, start, 0)
    lax.fori_loop(1, n, finish, 0)
    for k in range(count):
        pltpu.make_async_copy(srcs[k].at[me], dsts[k].at[me], own_sem.at[k]).wait()


def exchange(arrays, ident, name):
    count, n = len(arrays), arrays[0].shape[0]
    anywhere = pl.BlockSpec(memory_space=pl.ANY)
    return pl.pallas_call(
        partial(exchange_kernel, n, count),
        name=name,
        out_shape=tuple(jax.ShapeDtypeStruct(rows.shape, rows.dtype) for rows in arrays),
        in_specs=[anywhere] * count,
        out_specs=(anywhere,) * count,
        scratch_shapes=[
            pltpu.SemaphoreType.DMA((count, n)),
            pltpu.SemaphoreType.DMA((count, n)),
            pltpu.SemaphoreType.DMA((count,)),
        ],
        compiler_params=pltpu.CompilerParams(collective_id=ident, has_side_effects=True),
        cost_estimate=pl.CostEstimate(
            flops=0, bytes_accessed=2 * 2**20, transcendentals=0
        ),
    )(*arrays)


def plan_kernel(
    n, rows_own, capacity, fold, tok_col, tok_row, mask_row, own, info, lists, place
):
    size = tok_col.shape[0]
    ids_col = tok_col[...]
    ids_row = tok_row[...]
    owner_col = lax.div(ids_col, rows_own)
    owner_row = lax.div(ids_row, rows_own)
    at_col = lax.broadcasted_iota(jnp.int32, (size, size), 0)
    at_row = lax.broadcasted_iota(jnp.int32, (size, size), 1)
    same = ids_col == ids_row
    first_col = jnp.min(jnp.where(same, at_row, size), 1, keepdims=True)
    first_row = jnp.min(jnp.where(same, at_col, size), 0, keepdims=True)
    leads_row = first_row == lax.broadcasted_iota(jnp.int32, (1, size), 1)
    leads_col = first_col == lax.broadcasted_iota(jnp.int32, (size, 1), 0)
    ahead = (owner_col == owner_row) & leads_row & (at_row < first_col)
    slot = jnp.sum(jnp.where(ahead, 1.0, 0.0), 1, keepdims=True).astype(jnp.int32)
    fits = slot < capacity - 1
    place[...] = jnp.where(fits, owner_col * capacity + slot, -1)
    over = jnp.max(jnp.where(fits, 0.0, 1.0), keepdims=True)
    local = ids_col - owner_col * rows_own + 1
    high = lax.div(local, 128)
    to_owner = lax.broadcasted_iota(jnp.int32, (size, n), 1) == owner_col
    to_owner = to_owner & leads_col & fits
    shift = capacity * lax.rem(own[1], fold)
    in_slot = lax.broadcasted_iota(jnp.int32, (size, 128), 1) == slot + shift
    in_slot = jnp.where(in_slot, 1.0, 0.0).astype(jnp.bfloat16)
    high_part = jnp.where(to_owner, high.astype(jnp.float32), 0.0).astype(jnp.bfloat16)
    low_part = jnp.where(to_owner, (local - high * 128).astype(jnp.float32), 0.0)
    table = dot_tn(high_part, in_slot) * 128.0 + dot_tn(low_part.astype(jnp.bfloat16), in_slot)
    lane = lax.broadcasted_iota(jnp.int32, (n, 128), 1)
    line = lax.broadcasted_iota(jnp.int32, (n, 128), 0)
    fixed = (line == mask_token // rows_own) & (lane == capacity - 1 + shift)
    table = jnp.where(fixed, float(mask_token % rows_own + 1), table)
    count = jnp.sum(mask_row[...].astype(jnp.float32), keepdims=True)
    lane = lax.broadcasted_iota(jnp.int32, (8, 128), 1)
    line = lax.broadcasted_iota(jnp.int32, (8, 128), 0)
    extra = jnp.where(lane == 0, count, jnp.where(lane == 1, own[0].astype(jnp.float32), over))
    extra = jnp.where(line == 7, extra, info[...])
    line = lax.broadcasted_iota(jnp.int32, lists.shape, 1)
    lists[...] = jnp.where(line == 0, table[:, None, :], extra[None])


def make_plan(tokens, masking, documents, info, n, rows_own, capacity, fold):
    size = tokens.shape[0]
    vmem = pl.BlockSpec(memory_space=pltpu.VMEM)
    return pl.pallas_call(
        partial(plan_kernel, n, rows_own, capacity, fold),
        name="plan",
        out_shape=(
            jax.ShapeDtypeStruct((n, 8, 128), jnp.float32),
            jax.ShapeDtypeStruct((size, 1), jnp.int32),
        ),
        in_specs=[vmem, vmem, vmem, pl.BlockSpec(memory_space=pltpu.SMEM), vmem],
        out_specs=(vmem, vmem),
        compiler_params=pltpu.CompilerParams(vmem_limit_bytes=32 * 2**20),
    )(
        tokens[:, None],
        tokens[None, :],
        masking[None, :],
        jnp.stack([documents[0], lax.axis_index("dp")]),
        info,
    )


def place_of(me):
    core = lax.rem(me, 2)
    chip = lax.div(me, 2)
    spot = lax.rem(chip, 4)
    layer = lax.div(chip, 4)
    along_a = 1 + core
    along_b = 2 - core
    step_a = along_a * (1 - 2 * lax.rem(lax.div(spot, along_a), 2))
    step_b = along_b * (1 - 2 * lax.rem(lax.div(spot, along_b), 2))
    return core, spot, layer, step_a, step_b


def remote_copy(src, dst, send, recv, device):
    return pltpu.make_async_remote_copy(
        src_ref=src, dst_ref=dst, send_sem=send, recv_sem=recv, device_id=(device,), device_id_type=MESH
    )


def greet_everyone(me, n):
    barrier = pltpu.get_barrier_semaphore()

    def greet(step, carry):
        pl.semaphore_signal(
            barrier, inc=1, device_id=(lax.rem(me + step, n),), device_id_type=MESH
        )
        return carry

    lax.fori_loop(1, n, greet, 0)
    pl.semaphore_wait(barrier, n - 1)


def front_kernel(n, units, capacity, *refs):
    count = len(units)
    lists, vocabulary, pages = refs[:3]
    weights = refs[3 : 3 + count]
    asked, rows, full = refs[3 + count : 6 + count]
    swap_out, swap_in, chip_rows, answers = refs[6 + count : 10 + count]
    ask_send, ask_recv, row_send, row_recv, own_sem, swap_send, swap_recv = refs[10 + count : 17 + count]
    hop_recv, core_recv, core_send, z_send, a_send, b_send = refs[17 + count :]
    me = lax.axis_index("dp")
    core, spot, layer, step_a, step_b = place_of(me)
    layers = n // 8
    half = chip_rows.shape[1]
    page_rows = pages.shape[0]
    here = pl.ds(pl.multiple_of(core * half, 128), half)
    there = pl.ds(pl.multiple_of((1 - core) * half, 128), half)
    partner = me + 1 - 2 * core
    to_a, to_b, up, down = me + 2 * step_a, me + 2 * step_b, me + 8, me - 8
    spot_a, spot_b, spot_ab = spot + step_a, spot + step_b, spot + step_a + step_b

    at = 0
    for ref, unit in zip(weights, units):
        swap_out[pl.ds(at, 24 * unit)] = ref[:, there]
        at += 24 * unit
    greet_everyone(me, n)
    swaps = [
        remote_copy(swap_out, swap_in, swap_send.at[0], swap_recv.at[0], partner),
        remote_copy(
            pages.at[:, there],
            chip_rows.at[pl.ds(2 * at + core * page_rows, page_rows)],
            swap_send.at[1],
            swap_recv.at[1],
            partner,
        ),
    ]
    for copy in swaps:
        copy.start()

    def ask(step):
        peer = lax.rem(me + step, n)
        return remote_copy(lists.at[peer], asked.at[me], ask_send.at[step], ask_recv.at[step], peer)

    def start_ask(step, carry):
        ask(step).start()
        return carry

    def wait_ask(step, carry):
        ask(step).wait()
        return carry

    lax.fori_loop(1, n, start_ask, 0)
    asked[me] = lists[me]
    chip_rows[pl.ds(2 * at + pl.multiple_of(core * page_rows, page_rows), page_rows)] = pages[:, here]
    for copy in swaps:
        copy.wait_recv()
    at = 0
    for ref, unit in zip(weights, units):
        mine, other = ref[:, here], swap_in[pl.ds(at, 24 * unit)]
        ordered = jnp.where(
            core == 0, jnp.concatenate([mine, other], 0), jnp.concatenate([other, mine], 0)
        )
        chip_rows[pl.ds(2 * at, 48 * unit)] = ordered.astype(chip_rows.dtype)
        at += 24 * unit

    def block(level, index):
        return full.at[level, index, :, here]

    def z_hop(way, level, src=None):
        return remote_copy(
            block(level, spot) if src is None else src, block(level, spot),
            z_send.at[way, level], hop_recv.at[level, spot], up if way == 0 else down,
        )

    def a_hop(level, src=None):
        return remote_copy(
            block(level, spot) if src is None else src, block(level, spot),
            a_send.at[level], hop_recv.at[level, spot], to_a,
        )

    def b_hop(kind, level, src=None):
        index = spot if kind == 0 else spot_a
        return remote_copy(
            block(level, index) if src is None else src, block(level, index),
            b_send.at[kind, level], hop_recv.at[level, index], to_b,
        )

    def core_hop(level, index, src=None):
        return remote_copy(
            block(level, index) if src is None else src, block(level, index),
            core_send.at[level, index], core_recv.at[level, index], partner,
        )

    def arrived(level, index):
        pltpu.make_async_copy(block(level, index), block(level, index), hop_recv.at[level, index]).wait()

    low_z, high_z = layer > 0, layer < layers - 1

    @pl.when(high_z)
    def _():
        z_hop(0, layer, chip_rows).start()

    @pl.when(low_z)
    def _():
        z_hop(1, layer, chip_rows).start()

    a_hop(layer, chip_rows).start()
    b_hop(0, layer, chip_rows).start()
    core_hop(layer, spot, chip_rows).start()
    own = pltpu.make_async_copy(chip_rows, block(layer, spot), own_sem.at[0])
    own.start()

    lax.fori_loop(1, n, wait_ask, 0)
    rows_own = vocabulary.shape[0]
    table = vocabulary[...].astype(jnp.bfloat16)
    group = 128 // capacity

    def row_copy(peer):
        return remote_copy(
            answers.at[peer], rows.at[me], row_send.at[peer], row_recv.at[me], peer
        )

    def answer(turn, carry):
        ids = jnp.zeros((8, 128), jnp.float32)
        for k in range(group):
            ids = ids + asked[turn * group + k]
        ids = ids.T[:, 0:1]
        wanted = lax.broadcasted_iota(jnp.int32, (128, rows_own), 1) + 1
        picks = jnp.where(ids.astype(jnp.int32) == wanted, 1.0, 0.0).astype(jnp.bfloat16)
        found = dot_nn(picks, table).astype(jnp.bfloat16)
        for k in range(group):
            peer = turn * group + k
            answers[peer] = found[k * capacity : (k + 1) * capacity]

            @pl.when(peer != me)
            def _():
                row_copy(peer).start()

        return carry

    lax.fori_loop(0, n // group, answer, 0)
    own_rows = pltpu.make_async_copy(answers.at[me], rows.at[me], own_sem.at[1])
    own_rows.start()

    def relay_column(gap):
        for way, level, there_is, further in (
            (0, layer - gap, layer - gap >= 0, high_z),
            (1, layer + gap, layer + gap < layers, low_z),
        ):

            @pl.when(there_is)
            def _():
                arrived(level, spot)

                @pl.when(further)
                def _():
                    z_hop(way, level).start()

                a_hop(level).start()
                b_hop(0, level).start()
                core_hop(level, spot).start()

    def at_gap(gap, visit):
        if gap == 0:
            visit(layer)
            return

        @pl.when(layer - gap >= 0)
        def _():
            visit(layer - gap)

        @pl.when(layer + gap < layers)
        def _():
            visit(layer + gap)

    def relay_a(level):
        arrived(level, spot_a)
        b_hop(1, level).start()
        core_hop(level, spot_a).start()

    def relay_b(index):
        def visit(level):
            arrived(level, index)
            core_hop(level, index).start()

        return visit

    for gap in range(layers):
        if gap > 0:
            relay_column(gap)
        at_gap(gap, relay_a)
        if gap > 0:
            at_gap(gap - 1, relay_b(spot_b))
            at_gap(gap - 1, relay_b(spot_ab))
    at_gap(layers - 1, relay_b(spot_b))
    at_gap(layers - 1, relay_b(spot_ab))

    def finish(level, carry):
        for index in (spot, spot_a, spot_b, spot_ab):
            core_hop(level, index).wait_send()
        for index in range(4):
            other = full.at[level, index, :, there]
            pltpu.make_async_copy(other, other, core_recv.at[level, index]).wait()
        a_hop(level).wait_send()
        b_hop(0, level).wait_send()
        b_hop(1, level).wait_send()

        @pl.when((level <= layer) & high_z)
        def _():
            z_hop(0, level).wait_send()

        @pl.when((level >= layer) & low_z)
        def _():
            z_hop(1, level).wait_send()

        return carry

    lax.fori_loop(0, layers, finish, 0)
    own.wait()
    own_rows.wait()
    for copy in swaps:
        copy.wait_send()

    def finish_rows(step, carry):
        peer = lax.rem(me + step, n)
        pltpu.make_async_copy(answers.at[peer], answers.at[peer], row_send.at[peer]).wait()
        source = lax.rem(me - step + n, n)
        pltpu.make_async_copy(rows.at[source], rows.at[source], row_recv.at[source]).wait()
        return carry

    lax.fori_loop(1, n, finish_rows, 0)


def front(lists, vocabulary, pages, weights, n, capacity, ident):
    model = vocabulary.shape[1]
    layers = n // 8
    units = [weight.shape[0] // 24 for weight in weights]
    swap = 24 * sum(units)
    chip = 2 * (swap + pages.shape[0])
    low = jnp.bfloat16
    dma = pltpu.SemaphoreType.DMA
    vmem = pl.BlockSpec(memory_space=pltpu.VMEM)
    anywhere = pl.BlockSpec(memory_space=pl.ANY)
    return pl.pallas_call(
        partial(front_kernel, n, units, capacity),
        name="front",
        out_shape=(
            jax.ShapeDtypeStruct(lists.shape, lists.dtype),
            jax.ShapeDtypeStruct((n, capacity, model), low),
            jax.ShapeDtypeStruct((layers, 4, chip, model), low),
        ),
        in_specs=[vmem] * (3 + len(weights)),
        out_specs=(vmem, anywhere, anywhere),
        scratch_shapes=[
            pltpu.VMEM((swap, model // 2), jnp.float32),
            pltpu.VMEM((swap, model // 2), jnp.float32),
            pltpu.VMEM((chip, model // 2), low),
            pltpu.VMEM((n, capacity, model), low),
            dma((n,)),
            dma((n,)),
            dma((n,)),
            dma((n,)),
            dma((2,)),
            dma((2,)),
            dma((2,)),
            dma((layers, 4)),
            dma((layers, 4)),
            dma((layers, 4)),
            dma((2, layers)),
            dma((layers,)),
            dma((2, layers)),
        ],
        compiler_params=pltpu.CompilerParams(
            collective_id=ident, has_side_effects=True, vmem_limit_bytes=48 * 2**20
        ),
        cost_estimate=pl.CostEstimate(
            flops=0, bytes_accessed=100 * 2**20, transcendentals=0
        ),
    )(lists, vocabulary, pages, *weights)


def back_kernel(n, units, chunks, *refs):
    count = len(units)
    sent, small, grads = refs[0], refs[1], refs[2 : 2 + count]
    came, small_came, out = refs[2 + count : 5 + count]
    own, par, from_b, from_a, from_z, mine, gone, back = refs[5 + count : 13 + count]
    row_send, row_recv, own_sem, load_sem, pair_send, pair_recv = refs[13 + count : 19 + count]
    b_send, b_recv, a_send, a_recv, z_send, z_recv, f_send, f_recv = refs[19 + count :]
    layers = n // 8
    me = lax.axis_index("dp")
    core, spot, layer, step_a, step_b = place_of(me)
    half = own.shape[3]
    here = pl.ds(pl.multiple_of(core * half, 128), half)
    there = pl.ds(pl.multiple_of((1 - core) * half, 128), half)
    partner = me + 1 - 2 * core
    to_a, to_b = me + 2 * step_a, me + 2 * step_b
    offsets = [48 * sum(units[:k]) for k in range(count)]
    spot_a, spot_b, spot_ab = spot + step_a, spot + step_b, spot + step_a + step_b
    size = own.shape[2] // chunks

    greet_everyone(me, n)
    for index in (spot_ab, spot_a, spot_b, spot):
        for ref, at, unit in zip(grads, offsets, units):
            remote_copy(
                ref.at[:, index, :, there],
                par.at[:, index, pl.ds(at, 48 * unit)],
                pair_send.at[index],
                pair_recv.at[index],
                partner,
            ).start()
    for index in (spot_ab, spot_b, spot_a, spot):
        for ref, at, unit in zip(grads, offsets, units):
            pltpu.make_async_copy(
                ref.at[:, index, :, here], own.at[:, index, pl.ds(at, 48 * unit)], load_sem.at[index]
            ).start()

    def row_copies(step):
        peer = lax.rem(me + step, n)
        return [
            remote_copy(src.at[peer], dst.at[me], row_send.at[k, step], row_recv.at[k, step], peer)
            for k, (src, dst) in enumerate(((sent, came), (small, small_came)))
        ]

    def start_rows(step, carry):
        for copy in row_copies(step):
            copy.start()
        return carry

    def finish_rows(step, carry):
        for copy in row_copies(step):
            copy.wait()
        return carry

    lax.fori_loop(1, n, start_rows, 0)
    own_copies = [
        pltpu.make_async_copy(src.at[me], dst.at[me], own_sem.at[k])
        for k, (src, dst) in enumerate(((sent, came), (small, small_came)))
    ]
    for copy in own_copies:
        copy.start()

    def arrived(index):
        pltpu.make_async_copy(own.at[:, index], own.at[:, index], load_sem.at[index]).wait()
        pltpu.make_async_copy(par.at[:, index], par.at[:, index], pair_recv.at[index]).wait()

    def total(*parts):
        return sum(part[...].astype(jnp.float32) for part in parts)

    def b_copy(kind, level, part):
        cut = pl.ds(part * size, size)
        return remote_copy(
            own.at[level, spot_ab if kind == 0 else spot_b, cut], from_b.at[kind, level, cut],
            b_send.at[kind, level, part], b_recv.at[kind, level, part], to_b,
        )

    def a_copy(level, part):
        cut = pl.ds(part * size, size)
        return remote_copy(
            own.at[level, spot_a, cut], from_a.at[level, cut],
            a_send.at[level, part], a_recv.at[level, part], to_a,
        )

    def z_copy(level, part):
        cut = pl.ds(part * size, size)
        return remote_copy(
            own.at[level, spot, cut], from_z.at[layer, cut],
            z_send.at[level, part], z_recv.at[layer, part], me + 8 * (level - layer),
        )

    def cross_b(kind, index, part):
        cut = pl.ds(part * size, size)

        def step(level, carry):
            own[level, index, cut] = total(
                own.at[level, index, cut], par.at[level, index, cut]
            ).astype(own.dtype)
            b_copy(kind, level, part).start()
            return carry

        lax.fori_loop(0, layers, step, 0)

    def cross_a(part):
        cut = pl.ds(part * size, size)

        def step(level, carry):
            b_copy(0, level, part).wait_recv()
            own[level, spot_a, cut] = total(
                own.at[level, spot_a, cut], par.at[level, spot_a, cut], from_b.at[0, level, cut]
            ).astype(own.dtype)
            a_copy(level, part).start()
            return carry

        lax.fori_loop(0, layers, step, 0)

    def column(level, part):
        cut = pl.ds(part * size, size)
        b_copy(1, level, part).wait_recv()
        a_copy(level, part).wait_recv()
        return total(
            own.at[level, spot, cut], par.at[level, spot, cut],
            from_b.at[1, level, cut], from_a.at[level, cut],
        )

    def cross_z(part):
        cut = pl.ds(part * size, size)

        def step(gap, carry):
            level = lax.rem(layer + gap, layers)
            own[level, spot, cut] = column(level, part).astype(own.dtype)
            z_copy(level, part).start()
            return carry

        lax.fori_loop(1, layers, step, 0)
        mine[cut] = column(layer, part)

    arrived(spot_ab)
    cross_b(0, spot_ab, 0)
    arrived(spot_b)
    for part in range(chunks):
        if part > 0:
            cross_b(0, spot_ab, part)
        cross_b(1, spot_b, part)
    arrived(spot_a)
    arrived(spot)
    for part in range(chunks):
        cross_a(part)
        if part > 0:
            cross_z(part - 1)
    cross_z(chunks - 1)
    for part in range(chunks):
        cut = pl.ds(part * size, size)

        def step(gap, carry):
            level = lax.rem(layer + gap, layers)
            remote_copy(
                own.at[level, spot, cut], from_z.at[level, cut],
                z_send.at[level, part], z_recv.at[level, part], me,
            ).wait_recv()
            mine[cut] += total(from_z.at[level, cut])
            return carry

        lax.fori_loop(1, layers, step, 0)

    at = 0
    for offset, unit in zip(offsets, units):
        rows = 24 * unit
        gone[pl.ds(at, rows)] = mine[pl.ds(pl.multiple_of(offset + (1 - core) * rows, 8), rows)]
        out[pl.ds(at, rows), here] = mine[pl.ds(pl.multiple_of(offset + core * rows, 8), rows)]
        at += rows
    last = remote_copy(gone, back, f_send, f_recv, partner)
    last.start()
    last.wait()
    out[:, there] = back[...]
    for index in range(4):
        pltpu.make_async_copy(par.at[:, index], par.at[:, index], pair_send.at[index]).wait()

    def settle(level, carry):
        for part in range(chunks):
            b_copy(0, level, part).wait_send()
            b_copy(1, level, part).wait_send()
            a_copy(level, part).wait_send()

            @pl.when(level != layer)
            def _():
                z_copy(level, part).wait_send()

        return carry

    lax.fori_loop(0, layers, settle, 0)
    lax.fori_loop(1, n, finish_rows, 0)
    for copy in own_copies:
        copy.wait()


def to_owners(sent, small, grads, n, ident):
    model = grads[0].shape[1]
    layers = n // 8
    units = [grad.shape[0] // n // 24 for grad in grads]
    chunks = max(k for k in range(1, 6) if sum(units) % k == 0)
    rows = 48 * sum(units)
    half = model // 2
    low = jnp.bfloat16
    dma = pltpu.SemaphoreType.DMA
    anywhere = pl.BlockSpec(memory_space=pl.ANY)
    return pl.pallas_call(
        partial(back_kernel, n, units, chunks),
        name="back",
        out_shape=(
            jax.ShapeDtypeStruct(sent.shape, sent.dtype),
            jax.ShapeDtypeStruct(small.shape, small.dtype),
            jax.ShapeDtypeStruct((rows // 2, model), jnp.float32),
        ),
        in_specs=[anywhere] * (2 + len(grads)),
        out_specs=(anywhere, anywhere, pl.BlockSpec(memory_space=pltpu.VMEM)),
        scratch_shapes=[
            pltpu.VMEM((layers, 4, rows, half), low),
            pltpu.VMEM((layers, 4, rows, half), low),
            pltpu.VMEM((2, layers, rows, half), low),
            pltpu.VMEM((layers, rows, half), low),
            pltpu.VMEM((layers, rows, half), low),
            pltpu.VMEM((rows, half), jnp.float32),
            pltpu.VMEM((rows // 2, half), jnp.float32),
            pltpu.VMEM((rows // 2, half), jnp.float32),
            dma((2, n)),
            dma((2, n)),
            dma((2,)),
            dma((4,)),
            dma((4,)),
            dma((4,)),
            dma((2, layers, chunks)),
            dma((2, layers, chunks)),
            dma((layers, chunks)),
            dma((layers, chunks)),
            dma((layers, chunks)),
            dma((layers, chunks)),
            dma,
            dma,
        ],
        compiler_params=pltpu.CompilerParams(
            collective_id=ident, has_side_effects=True, vmem_limit_bytes=60 * 2**20
        ),
        cost_estimate=pl.CostEstimate(
            flops=0, bytes_accessed=100 * 2**20, transcendentals=0
        ),
    )(sent, small, *[grad.reshape(layers, 4, -1, model) for grad in grads])


def split_rows(packed, grads, n):
    out, at = [], 0
    for grad in grads:
        count = grad.shape[0] // n
        out.append(packed[at : at + count])
        at += count
    return out


def scatter(grads, n):
    model = grads[0].shape[1]
    joined = jnp.concatenate([grad.reshape(n, -1, model) for grad in grads], 1)
    joined = joined.reshape(-1, model)
    mine = lax.psum_scatter(joined, "dp", scatter_dimension=0, tiled=True)
    return split_rows(mine.astype(jnp.float32), grads, n)


def masked(rows, half):
    lane = lax.broadcasted_iota(jnp.int32, rows.shape, 1)
    keep = (lane < HD) if half == 0 else (lane >= HD)
    return jnp.where(keep, rows, jnp.zeros_like(rows))


def turn(terms, sines, cosines):
    half = sines.shape[1]
    sine, cosine = terms[:, :half], terms[:, half:]
    return jnp.concatenate(
        [sine * sines + cosine * cosines, cosine * sines - sine * cosines], 1
    ).astype(jnp.bfloat16)


def turn_back(upstream, sines, cosines):
    half = sines.shape[1]
    first, second = upstream[:, :half], upstream[:, half:]
    return jnp.concatenate(
        [first * sines - second * cosines, first * cosines + second * sines], 1
    ).astype(jnp.bfloat16)


def pick_halves(low_half, high_half):
    lane = lax.broadcasted_iota(jnp.int32, low_half.shape, 1)
    return jnp.where(lane < HD, low_half, high_half)


def attend_kernel(q, k, v, rel_text, rel_box, sines, cosines, bases, attended, probs):
    queries, keys, values = q[...], k[...], v[...]
    spread = bases[...]
    results = []
    for half in range(2):
        mine = masked(queries, half)
        terms = dot_nn(masked(keys, half), rel_box[...])
        box_rot = turn(terms, sines[...], cosines[...])
        terms = dot_nn(mine, rel_text[...])
        text_rot = turn(terms, sines[...], cosines[...])
        scores = dot_nt(mine, keys) + dot_nt(text_rot, spread) + dot_nt(spread, box_rot)
        scores = scores * HD ** (-0.5)
        powers = jnp.exp(scores - jnp.max(scores, -1, keepdims=True))
        shares = powers * (1.0 / jnp.sum(powers, -1, keepdims=True))
        probs[half] = shares
        results.append(dot_nn(shares.astype(jnp.bfloat16), values))
    attended[...] = pick_halves(*results).astype(jnp.bfloat16)


def attend(joined, rel_map, sines, cosines, bases):
    size, model = bases.shape
    pairs = model // (2 * HD)
    lanes = 2 * HD
    whole = lambda rows: pl.BlockSpec(rows.shape, lambda i: (0, 0))
    column = pl.BlockSpec((size, lanes), lambda i: (0, i))
    band = lambda part: pl.BlockSpec((lanes, model), lambda i: (i + part * pairs, 0))
    return pl.pallas_call(
        attend_kernel,
        name="attend",
        grid=(pairs,),
        out_shape=(
            jax.ShapeDtypeStruct((size, model), jnp.bfloat16),
            jax.ShapeDtypeStruct((2 * pairs, size, size), jnp.float32),
        ),
        in_specs=[column, column, column, band(0), band(1)]
        + [whole(sines), whole(cosines), whole(bases)],
        out_specs=(
            column,
            pl.BlockSpec((2, size, size), lambda i: (i, 0, 0)),
        ),
        compiler_params=pltpu.CompilerParams(vmem_limit_bytes=56 * 2**20),
        cost_estimate=pl.CostEstimate(
            flops=2 * 12 * size * (size * 1700 + 2 * 64 * 768),
            bytes_accessed=20 * 2**20,
            transcendentals=12 * size * size,
        ),
    )(*joined, rel_map, rel_map, sines, cosines, bases)


def attend_back_kernel(
    d_out, q, k, v, rel_text, rel_box, probs, sines, cosines, bases, dq, dk, dv, g_rel
):
    queries, keys, values, upstream = q[...], k[...], v[...], d_out[...]
    spread = bases[...]
    scale = HD ** (-0.5)
    low = jnp.bfloat16
    got = [[], [], []]
    for half in range(2):
        shares = probs[half]
        d_probs = dot_nt(masked(upstream, half), values)
        got[2].append(dot_tn(shares.astype(low), upstream))
        inner = jnp.sum(d_probs * shares, -1, keepdims=True)
        d_scores = (shares * (d_probs - inner)).astype(low)
        d_text = turn_back(dot_nn(d_scores, spread) * scale, sines[...], cosines[...])
        got[0].append(dot_nn(d_scores, keys) * scale + dot_nt(d_text, rel_text[...]))
        part = dot_tn(masked(queries, half), d_text)
        text_sum = part if half == 0 else text_sum + part
        turned = d_scores.T
        d_box = turn_back(dot_nn(turned, spread) * scale, sines[...], cosines[...])
        got[1].append(dot_nn(turned, queries) * scale + dot_nt(d_box, rel_box[...]))
        part = dot_tn(masked(keys, half), d_box)
        box_sum = part if half == 0 else box_sum + part
    for ref, halves in zip((dq, dk, dv), got):
        ref[...] = pick_halves(*halves).astype(low)
    g_rel[0] = text_sum.astype(low)
    g_rel[1] = box_sum.astype(low)


def attend_back(d_attended, joined, rel_map, probs, sines, cosines, bases):
    size, model = bases.shape
    pairs = model // (2 * HD)
    lanes = 2 * HD
    low = jnp.bfloat16
    whole = lambda rows: pl.BlockSpec(rows.shape, lambda i: (0, 0))
    column = pl.BlockSpec((size, lanes), lambda i: (0, i))
    band = lambda part: pl.BlockSpec((lanes, model), lambda i: (i + part * pairs, 0))
    return pl.pallas_call(
        attend_back_kernel,
        name="attend_back",
        grid=(pairs,),
        out_shape=(jax.ShapeDtypeStruct((size, model), low),) * 3
        + (jax.ShapeDtypeStruct((2, model, model), low),),
        in_specs=[column, column, column, column, band(0), band(1)]
        + [pl.BlockSpec((2, size, size), lambda i: (i, 0, 0))]
        + [whole(sines), whole(cosines), whole(bases)],
        out_specs=(column,) * 3 + (pl.BlockSpec((2, lanes, model), lambda i: (0, i, 0)),),
        compiler_params=pltpu.CompilerParams(vmem_limit_bytes=56 * 2**20),
        cost_estimate=pl.CostEstimate(
            flops=2 * 12 * size * (size * 1800 + 4 * 64 * 768),
            bytes_accessed=25 * 2**20,
            transcendentals=0,
        ),
    )(d_attended, *joined, rel_map, rel_map, probs, sines, cosines, bases)


def swap_middle(rows):
    count = rows.shape[0] // 4
    return jnp.concatenate(
        [rows[:count], rows[2 * count : 3 * count], rows[count : 2 * count], rows[3 * count :]], 0
    )


def forward(weights, rows, positions):
    box_map, mix_map, rel_map, out_map, up_map, down_map, norm_rows = weights
    gains = norm_rows.astype(jnp.float32)
    sin_count = box_map.shape[1]
    sin_x, cos_x, sin_y, cos_y = sinusoids(positions, sin_count // 4)
    sines = jnp.concatenate([sin_x, sin_y], -1)
    cosines = jnp.concatenate([cos_x, cos_y], -1)
    boxes = jnp.concatenate([sines, cosines], -1).astype(jnp.bfloat16)
    bases = jnp.concatenate([cosines, sines], -1).astype(jnp.bfloat16)
    embedded = rows + dot_nt(boxes, box_map)
    first = layer_norm(embedded, gains[0], gains[1])
    normed = first[0].astype(jnp.bfloat16)
    joined = [dot_nn(normed, part).astype(jnp.bfloat16) for part in mix_map]
    attended, probs = attend(joined, rel_map, sines, cosines, bases)
    second = layer_norm(first[0] + dot_nn(attended, out_map), gains[2], gains[3])
    middle = second[0].astype(jnp.bfloat16)
    hidden_pre = [dot_nn(middle, part) for part in up_map]
    hidden = [jax.nn.gelu(part, approximate=False).astype(jnp.bfloat16) for part in hidden_pre]
    lowered = sum(dot_nn(part, weight) for part, weight in zip(hidden, down_map))
    third = layer_norm(second[0] + lowered, gains[4], gains[5])
    return {
        "sines": sines,
        "cosines": cosines,
        "boxes": boxes,
        "bases": bases,
        "first": first,
        "normed": normed,
        "joined": joined,
        "probs": probs,
        "attended": attended,
        "second": second,
        "middle": middle,
        "hidden_pre": hidden_pre,
        "hidden": hidden,
        "third": third,
    }


def backward_upper(weights, cache, d_states):
    _, _, _, out_map, up_map, down_map, norm_rows = weights
    gains = norm_rows.astype(jnp.float32)
    d_mid, gain_last, bias_last = norm_back(
        d_states, cache["third"][1], cache["third"][2], gains[4]
    )
    d_down = d_mid.astype(jnp.bfloat16)
    gelu_exact = partial(jax.nn.gelu, approximate=False)
    grad_down, grad_up, d_second = [], [], d_mid
    for pre, hidden, up, down in zip(cache["hidden_pre"], cache["hidden"], up_map, down_map):
        grad_down.append(dot_tn(hidden, d_down))
        d_pre = jax.vjp(gelu_exact, pre)[1](dot_nt(d_down, down))[0].astype(jnp.bfloat16)
        grad_up.append(dot_tn(cache["middle"], d_pre))
        d_second = d_second + dot_nt(d_pre, up)
    d_lower, gain_mid, bias_mid = norm_back(
        d_second, cache["second"][1], cache["second"][2], gains[2]
    )
    d_attn = d_lower.astype(jnp.bfloat16)
    grad_out = dot_tn(cache["attended"], d_attn)
    d_attended = dot_nt(d_attn, out_map).astype(jnp.bfloat16)
    return d_lower, d_attended, grad_out, grad_up, grad_down, [gain_mid, bias_mid, gain_last, bias_last]


def backward_lower(weights, cache, d_lower, d_attended):
    box_map, mix_map, rel_map, _, _, _, norm_rows = weights
    gains = norm_rows.astype(jnp.float32)
    *d_joined, grad_rel = attend_back(
        d_attended,
        cache["joined"],
        rel_map,
        cache["probs"],
        cache["sines"],
        cache["cosines"],
        cache["bases"],
    )
    grad_mix = [dot_tn(cache["normed"], part) for part in d_joined]
    d_first = d_lower + sum(dot_nt(part, weight) for part, weight in zip(d_joined, mix_map))
    d_embedded, gain_low, bias_low = norm_back(
        d_first, cache["first"][1], cache["first"][2], gains[0]
    )
    grad_box = dot_tn(d_embedded.astype(jnp.bfloat16), cache["boxes"])
    return d_embedded, grad_box, grad_mix, grad_rel, [gain_low, bias_low]


def per_device(
    n,
    tokens,
    positions,
    documents,
    masking,
    negative_page,
    negative_row,
    pages,
    vocabulary,
    geometry,
    mixing,
    relative,
    merging,
    widening,
    narrowing,
    scaling,
    moment_vocabulary,
    moment_geometry,
    moment_mixing,
    moment_relative,
    moment_merging,
    moment_widening,
    moment_narrowing,
    moment_scaling,
    average_vocabulary,
    average_geometry,
    average_mixing,
    average_relative,
    average_merging,
    average_widening,
    average_narrowing,
    average_scaling,
):
    me = lax.axis_index("dp")
    size = tokens.shape[0]
    rows_own, model = vocabulary.shape
    page_rows = pages.shape[1]
    capacity = max(16, -(-2 * size // n) // 16 * 16)
    slots = n * capacity
    mask_float = masking.astype(jnp.float32)
    low = jnp.bfloat16
    fits = n % 8 == 0 and merging.shape[0] == 24 and page_rows % 16 == 0

    fold = 128 // capacity if fits else 1
    pieces = [
        swap_middle(geometry).T,
        swap_middle(relative).T,
        *[mixing[:, k * model : (k + 1) * model] for k in range(3)],
        merging,
        *[widening[:, k * model : (k + 1) * model] for k in range(widening.shape[1] // model)],
        narrowing,
    ]
    cols = scaling.shape[1]
    info = jnp.pad(scaling, ((1, 1), (0, 128 - cols)))
    lists, place = make_plan(tokens, masking, documents, info, n, rows_own, capacity, fold)
    bank_piece = pages.reshape(-1, model)
    if fits:
        asked, table_rows, full = front(lists, vocabulary, bank_piece, pieces, n, capacity, 1)
        wanted = jnp.sum(asked[:, 0].reshape(n // fold, fold, 128), 1)
        weights, at = [], 0
        for piece in [*pieces, bank_piece]:
            count = 2 * piece.shape[0]
            weights.append(full[:, :, at : at + count].reshape(-1, model))
            at += count
    else:
        (asked,) = exchange([lists], 1, "ask")
        wanted = asked[:, 0, :capacity]
        pieces = [piece.astype(low) for piece in pieces] + [bank_piece]
        joined = lax.all_gather(jnp.concatenate(pieces, 0), "dp", axis=0, tiled=False)
        weights, at = [], 0
        for piece in pieces:
            weights.append(joined[:, at : at + piece.shape[0]].reshape(-1, model))
            at += piece.shape[0]
    wanted = wanted.reshape(slots, 1)
    picks = (wanted == (jnp.arange(rows_own) + 1).astype(jnp.float32)[None, :]).astype(low)
    if not fits:
        answer = dot_nn(picks, vocabulary.astype(low)).astype(low)
        (table_rows,) = exchange([answer.reshape(n, capacity, model)], 2, "rows")
    table_rows = table_rows.reshape(slots, model)
    box_map, rel_map, mix_map = weights[0], weights[1], weights[2:5]
    out_map, up_map, down_full, bank = weights[5], weights[6:-2], weights[-2], weights[-1]
    norm_rows = asked[:, 1:7, :cols].transpose(1, 0, 2).reshape(6, n * cols).astype(low)
    count_of, doc_of = asked[:, 7, 0], asked[:, 7, 1]
    overflow = jnp.max(asked[:, 7, 2]) > 0.0
    my_count = jnp.sum(jnp.where(doc_of == documents[0].astype(jnp.float32), count_of, 0.0))
    share = 1.0 / (DOCS * jnp.maximum(my_count, 1.0))
    fixed = (mask_token // rows_own) * capacity + capacity - 1
    seats = (place == jnp.arange(slots)[None, :]).astype(low)
    target_rows = dot_nn(seats, table_rows)
    mask_rows = table_rows[fixed : fixed + 1].astype(jnp.float32)

    def dense_rows():
        table = lax.all_gather(vocabulary.astype(low), "dp", axis=0, tiled=True)
        return (
            table[tokens].astype(jnp.float32),
            table[mask_token : mask_token + 1].astype(jnp.float32),
        )

    target_rows, mask_rows = lax.cond(overflow, dense_rows, lambda: (target_rows, mask_rows))
    entry_rows = jnp.where(masking[:, None] == 1, mask_rows, target_rows)

    ff = len(up_map)
    down_map = [down_full[k * model : (k + 1) * model] for k in range(ff)]
    weights = (box_map, mix_map, rel_map, out_map, up_map, down_map, norm_rows)
    cache = forward(weights, entry_rows, positions)

    states_low = cache["third"][0].astype(low)
    inv_root = model ** (-0.5)
    positive = jnp.sum(states_low.astype(jnp.float32) * target_rows, -1, keepdims=True) * inv_root
    flat_index = (negative_page * page_rows + negative_row).T
    count_neg = flat_index.shape[1]
    width = bank.shape[0]
    repeated = jnp.tile(flat_index, (1, width // count_neg))
    chosen = repeated == jnp.arange(width)[None, :]
    logits = jnp.where(chosen, dot_nt(states_low, bank) * inv_root, -jnp.inf)
    highest = jnp.maximum(jnp.max(logits, -1, keepdims=True), positive)
    powers = jnp.exp(logits - highest)
    lead = jnp.exp(positive - highest)
    total = jnp.sum(powers, -1, keepdims=True) + lead
    per_token = highest + jnp.log(total) - positive
    mask_col = mask_float[:, None]
    loss_part = share * jnp.sum(mask_col * per_token)
    weight_map = (powers * (share * mask_col / total) * inv_root).astype(low)
    positive_grad = share * mask_col * (lead / total - 1.0) * inv_root
    d_states = positive_grad * target_rows + dot_nn(weight_map, bank)

    d_lower, d_attended, grad_out, grad_up, grad_down, upper_norms = backward_upper(
        weights, cache, d_states
    )
    d_embedded, grad_box, grad_mix, grad_rel, lower_norms = backward_lower(
        weights, cache, d_lower, d_attended
    )
    grad_norms = jnp.stack(lower_norms + upper_norms, 0)

    positive_rows = positive_grad * states_low.astype(jnp.float32)

    token_grads = jnp.where(mask_col == 1.0, positive_rows, d_embedded).astype(low)
    mask_grad = jnp.sum(mask_col * d_embedded, 0, keepdims=True)
    sent = dot_tn(seats, token_grads)
    sent = jnp.where(jnp.arange(slots)[:, None] == fixed, mask_grad, sent).astype(low)
    norm_blocks = grad_norms.reshape(6, n, cols).transpose(1, 0, 2)
    norm_blocks = jnp.pad(norm_blocks, ((0, 0), (0, 2), (0, 128 - cols)))
    sent = sent.reshape(n, capacity, model)
    grads = [grad_box, grad_rel.reshape(-1, model), *grad_mix, grad_out, *grad_up]
    grads = [grad.astype(low) for grad in [*grads, jnp.concatenate(grad_down, 0)]]
    if fits:
        came, norm_came, sums = to_owners(sent, norm_blocks, grads, n, 2)
        sums = split_rows(sums, grads, n)
    else:
        came, norm_came = exchange([sent, norm_blocks], 3, "grads")
        sums = scatter(grads, n)
    norm_piece = jnp.sum(norm_came, 0)[:6, :cols]

    def sparse_table():
        return dot_tn(picks, came.reshape(slots, model))

    def dense_table():
        entry = jnp.where(masking == 1, mask_token, tokens)
        table_grad = jnp.zeros((rows_own * n, model), jnp.float32).at[entry].add(d_embedded)
        table_grad = table_grad.at[tokens].add(positive_rows)
        return lax.psum_scatter(table_grad, "dp", scatter_dimension=0, tiled=True)

    table_piece = lax.cond(overflow, dense_table, sparse_table)

    reduced = (
        table_piece,
        swap_middle(sums[0].T),
        jnp.concatenate(sums[2:5], 1),
        swap_middle(sums[1].T),
        sums[5],
        jnp.concatenate(sums[6:-1], 1),
        sums[-1],
        norm_piece,
    )
    square = sum((jnp.sum(piece * piece) for piece in reduced))
    message = jnp.where(jnp.arange(128) == 0, square, jnp.where(jnp.arange(128) == 1, loss_part, 0.0))
    (totals,) = exchange([jnp.broadcast_to(message, (n, 8, 128))], 4, "totals")
    totals = jnp.sum(totals[:, 0, :2], 0)
    loss = totals[1]
    grad_norm = jnp.sqrt(totals[0])
    factor = clip_limit / jnp.maximum(grad_norm, clip_limit)
    decay = min(average_cap, (1.0 + STEP) / (10.0 + STEP))
    masters = (vocabulary, geometry, mixing, relative, merging, widening, narrowing, scaling)
    moments = (
        moment_vocabulary,
        moment_geometry,
        moment_mixing,
        moment_relative,
        moment_merging,
        moment_widening,
        moment_narrowing,
        moment_scaling,
    )
    averages = (
        average_vocabulary,
        average_geometry,
        average_mixing,
        average_relative,
        average_merging,
        average_widening,
        average_narrowing,
        average_scaling,
    )
    rates = (table_rate,) + (learn_rate,) * 7
    fresh, speeds, smooths = ([], [], [])
    for master, moment, average, piece, rate in zip(masters, moments, averages, reduced, rates):
        clipped = piece * factor
        velocity = momentum_decay * moment + clipped
        updated = master - rate * (clipped + momentum_decay * velocity)
        fresh.append(updated)
        speeds.append(velocity)
        smooths.append(decay * average + (1.0 - decay) * updated)
    return (loss, grad_norm, *fresh, *speeds, *smooths)


ROWS = P("dp", None)
COLS = P(None, "dp")
WEIGHTS = (ROWS, COLS, ROWS, COLS, ROWS, ROWS, ROWS, COLS)


def solution(mesh):
    return jax.shard_map(
        partial(per_device, mesh.shape["dp"]),
        mesh=mesh,
        in_specs=(P("dp"), COLS, P("dp"), P("dp"), COLS, COLS, P("dp", None, None)) + 3 * WEIGHTS,
        out_specs=(P(), P()) + 3 * WEIGHTS,
        check_vma=False,
    )
```

```python
from functools import partial

import jax
import jax.numpy as jnp
from jax import lax
from jax.experimental import pallas as pl
from jax.experimental.pallas import tpu as pltpu
from jax.sharding import PartitionSpec as P

HD = 64
DOCS = 8
STEP = 10
MESH = pl.DeviceIdType.MESH

mask_token = 103
ln_epsilon = 1e-06
momentum_decay = 0.9
learn_rate = 5000.0
table_rate = 1000000.0
clip_limit = 0.01
average_cap = 0.999


def sinusoids(positions, count):
    ranks = jnp.arange(count).astype(jnp.float32)
    omegas = jnp.power(10000.0, -ranks / count)
    angle_x = positions[0].astype(jnp.float32)[:, None] * omegas[None, :]
    angle_y = positions[1].astype(jnp.float32)[:, None] * omegas[None, :]
    return (jnp.sin(angle_x), jnp.cos(angle_x), jnp.sin(angle_y), jnp.cos(angle_y))


def layer_norm(rows, gain, bias):
    centred = rows - jnp.mean(rows, -1, keepdims=True)
    rescale = lax.rsqrt(jnp.mean(centred * centred, -1, keepdims=True) + ln_epsilon)
    whitened = centred * rescale
    return (whitened * gain + bias, whitened, rescale)


def norm_back(upstream, whitened, rescale, gain):
    scaled = upstream * gain
    inner = (
        scaled
        - jnp.mean(scaled, -1, keepdims=True)
        - whitened * jnp.mean(scaled * whitened, -1, keepdims=True)
    )
    return (
        rescale * inner,
        jnp.sum(upstream * whitened, 0, keepdims=True),
        jnp.sum(upstream, 0, keepdims=True),
    )


def dot_nn(left, right):
    return lax.dot_general(
        left, right, (((1,), (0,)), ((), ())), preferred_element_type=jnp.float32
    )


def dot_tn(left, right):
    return lax.dot_general(
        left, right, (((0,), (0,)), ((), ())), preferred_element_type=jnp.float32
    )


def dot_nt(left, right):
    return lax.dot_general(
        left, right, (((1,), (1,)), ((), ())), preferred_element_type=jnp.float32
    )


def exchange_kernel(n, count, *refs):
    srcs, dsts = refs[:count], refs[count : 2 * count]
    send_sem, recv_sem, own_sem = refs[2 * count :]
    me = lax.axis_index("dp")
    barrier = pltpu.get_barrier_semaphore()

    def greet(step, carry):
        pl.semaphore_signal(
            barrier, inc=1, device_id=(lax.rem(me + step, n),), device_id_type=MESH
        )
        return carry

    lax.fori_loop(1, n, greet, 0)
    for k in range(count):
        pltpu.make_async_copy(srcs[k].at[me], dsts[k].at[me], own_sem.at[k]).start()
    pl.semaphore_wait(barrier, n - 1)

    def copy(k, step):
        peer = lax.rem(me + step, n)
        return pltpu.make_async_remote_copy(
            src_ref=srcs[k].at[peer],
            dst_ref=dsts[k].at[me],
            send_sem=send_sem.at[k, step],
            recv_sem=recv_sem.at[k, step],
            device_id=(peer,),
            device_id_type=MESH,
        )

    def start(step, carry):
        for k in range(count):
            copy(k, step).start()
        return carry

    def finish(step, carry):
        for k in range(count):
            copy(k, step).wait()
        return carry

    lax.fori_loop(1, n, start, 0)
    lax.fori_loop(1, n, finish, 0)
    for k in range(count):
        pltpu.make_async_copy(srcs[k].at[me], dsts[k].at[me], own_sem.at[k]).wait()


def exchange(arrays, ident, name):
    count, n = len(arrays), arrays[0].shape[0]
    anywhere = pl.BlockSpec(memory_space=pl.ANY)
    return pl.pallas_call(
        partial(exchange_kernel, n, count),
        name=name,
        out_shape=tuple(jax.ShapeDtypeStruct(rows.shape, rows.dtype) for rows in arrays),
        in_specs=[anywhere] * count,
        out_specs=(anywhere,) * count,
        scratch_shapes=[
            pltpu.SemaphoreType.DMA((count, n)),
            pltpu.SemaphoreType.DMA((count, n)),
            pltpu.SemaphoreType.DMA((count,)),
        ],
        compiler_params=pltpu.CompilerParams(collective_id=ident, has_side_effects=True),
        cost_estimate=pl.CostEstimate(
            flops=0, bytes_accessed=2 * 2**20, transcendentals=0
        ),
    )(*arrays)


def plan_kernel(
    n, rows_own, capacity, fold, tok_col, tok_row, mask_row, own, info, lists, place
):
    size = tok_col.shape[0]
    ids_col = tok_col[...]
    ids_row = tok_row[...]
    owner_col = lax.div(ids_col, rows_own)
    owner_row = lax.div(ids_row, rows_own)
    at_col = lax.broadcasted_iota(jnp.int32, (size, size), 0)
    at_row = lax.broadcasted_iota(jnp.int32, (size, size), 1)
    same = ids_col == ids_row
    first_col = jnp.min(jnp.where(same, at_row, size), 1, keepdims=True)
    first_row = jnp.min(jnp.where(same, at_col, size), 0, keepdims=True)
    leads_row = first_row == lax.broadcasted_iota(jnp.int32, (1, size), 1)
    leads_col = first_col == lax.broadcasted_iota(jnp.int32, (size, 1), 0)
    ahead = (owner_col == owner_row) & leads_row & (at_row < first_col)
    slot = jnp.sum(jnp.where(ahead, 1.0, 0.0), 1, keepdims=True).astype(jnp.int32)
    fits = slot < capacity - 1
    place[...] = jnp.where(fits, owner_col * capacity + slot, -1)
    over = jnp.max(jnp.where(fits, 0.0, 1.0), keepdims=True)
    local = ids_col - owner_col * rows_own + 1
    high = lax.div(local, 128)
    to_owner = lax.broadcasted_iota(jnp.int32, (size, n), 1) == owner_col
    to_owner = to_owner & leads_col & fits
    shift = capacity * lax.rem(own[1], fold)
    in_slot = lax.broadcasted_iota(jnp.int32, (size, 128), 1) == slot + shift
    in_slot = jnp.where(in_slot, 1.0, 0.0).astype(jnp.bfloat16)
    high_part = jnp.where(to_owner, high.astype(jnp.float32), 0.0).astype(jnp.bfloat16)
    low_part = jnp.where(to_owner, (local - high * 128).astype(jnp.float32), 0.0)
    table = dot_tn(high_part, in_slot) * 128.0 + dot_tn(low_part.astype(jnp.bfloat16), in_slot)
    lane = lax.broadcasted_iota(jnp.int32, (n, 128), 1)
    line = lax.broadcasted_iota(jnp.int32, (n, 128), 0)
    fixed = (line == mask_token // rows_own) & (lane == capacity - 1 + shift)
    table = jnp.where(fixed, float(mask_token % rows_own + 1), table)
    count = jnp.sum(mask_row[...].astype(jnp.float32), keepdims=True)
    lane = lax.broadcasted_iota(jnp.int32, (8, 128), 1)
    line = lax.broadcasted_iota(jnp.int32, (8, 128), 0)
    extra = jnp.where(lane == 0, count, jnp.where(lane == 1, own[0].astype(jnp.float32), over))
    extra = jnp.where(line == 7, extra, info[...])
    line = lax.broadcasted_iota(jnp.int32, lists.shape, 1)
    lists[...] = jnp.where(line == 0, table[:, None, :], extra[None])


def make_plan(tokens, masking, documents, info, n, rows_own, capacity, fold):
    size = tokens.shape[0]
    vmem = pl.BlockSpec(memory_space=pltpu.VMEM)
    return pl.pallas_call(
        partial(plan_kernel, n, rows_own, capacity, fold),
        name="plan",
        out_shape=(
            jax.ShapeDtypeStruct((n, 8, 128), jnp.float32),
            jax.ShapeDtypeStruct((size, 1), jnp.int32),
        ),
        in_specs=[vmem, vmem, vmem, pl.BlockSpec(memory_space=pltpu.SMEM), vmem],
        out_specs=(vmem, vmem),
        compiler_params=pltpu.CompilerParams(vmem_limit_bytes=32 * 2**20),
    )(
        tokens[:, None],
        tokens[None, :],
        masking[None, :],
        jnp.stack([documents[0], lax.axis_index("dp")]),
        info,
    )


def place_of(me):
    core = lax.rem(me, 2)
    chip = lax.div(me, 2)
    spot = lax.rem(chip, 4)
    layer = lax.div(chip, 4)
    along_a = 1 + core
    along_b = 2 - core
    step_a = along_a * (1 - 2 * lax.rem(lax.div(spot, along_a), 2))
    step_b = along_b * (1 - 2 * lax.rem(lax.div(spot, along_b), 2))
    return core, spot, layer, step_a, step_b


def remote_copy(src, dst, send, recv, device):
    return pltpu.make_async_remote_copy(
        src_ref=src, dst_ref=dst, send_sem=send, recv_sem=recv, device_id=(device,), device_id_type=MESH
    )


def greet_everyone(me, n):
    barrier = pltpu.get_barrier_semaphore()

    def greet(step, carry):
        pl.semaphore_signal(
            barrier, inc=1, device_id=(lax.rem(me + step, n),), device_id_type=MESH
        )
        return carry

    lax.fori_loop(1, n, greet, 0)
    pl.semaphore_wait(barrier, n - 1)


def front_kernel(n, units, capacity, *refs):
    count = len(units)
    lists, vocabulary, pages, points, omegas = refs[:5]
    weights = refs[5 : 5 + count]
    asked, rows, full, sines, cosines = refs[5 + count : 10 + count]
    swap_out, swap_in, chip_rows, answers = refs[10 + count : 14 + count]
    ask_send, ask_recv, row_send, row_recv, own_sem, swap_send, swap_recv = refs[14 + count : 21 + count]
    hop_recv, core_recv, core_send, z_send, a_send, b_send = refs[21 + count :]
    me = lax.axis_index("dp")
    core, spot, layer, step_a, step_b = place_of(me)
    layers = n // 8
    half = chip_rows.shape[1]
    page_rows = pages.shape[0]
    here = pl.ds(pl.multiple_of(core * half, 128), half)
    there = pl.ds(pl.multiple_of((1 - core) * half, 128), half)
    partner = me + 1 - 2 * core
    to_a, to_b, up, down = me + 2 * step_a, me + 2 * step_b, me + 8, me - 8
    spot_a, spot_b, spot_ab = spot + step_a, spot + step_b, spot + step_a + step_b

    at = 0
    for ref, unit in zip(weights, units):
        swap_out[pl.ds(at, 24 * unit)] = ref[:, there]
        at += 24 * unit
    greet_everyone(me, n)
    swaps = [
        remote_copy(swap_out, swap_in, swap_send.at[0], swap_recv.at[0], partner),
        remote_copy(
            pages.at[:, there],
            chip_rows.at[pl.ds(2 * at + core * page_rows, page_rows)],
            swap_send.at[1],
            swap_recv.at[1],
            partner,
        ),
    ]
    for copy in swaps:
        copy.start()

    def ask(step):
        peer = lax.rem(me + step, n)
        return remote_copy(lists.at[peer], asked.at[me], ask_send.at[step], ask_recv.at[step], peer)

    def start_ask(step, carry):
        ask(step).start()
        return carry

    def wait_ask(step, carry):
        ask(step).wait()
        return carry

    lax.fori_loop(1, n, start_ask, 0)
    asked[me] = lists[me]
    chip_rows[pl.ds(2 * at + pl.multiple_of(core * page_rows, page_rows), page_rows)] = pages[:, here]
    for copy in swaps:
        copy.wait_recv()
    at = 0
    for ref, unit in zip(weights, units):
        mine, other = ref[:, here], swap_in[pl.ds(at, 24 * unit)]
        ordered = jnp.where(
            core == 0, jnp.concatenate([mine, other], 0), jnp.concatenate([other, mine], 0)
        )
        chip_rows[pl.ds(2 * at, 48 * unit)] = ordered.astype(chip_rows.dtype)
        at += 24 * unit

    def block(level, index):
        return full.at[level, index, :, here]

    def z_hop(way, level, src=None):
        return remote_copy(
            block(level, spot) if src is None else src, block(level, spot),
            z_send.at[way, level], hop_recv.at[level, spot], up if way == 0 else down,
        )

    def a_hop(level, src=None):
        return remote_copy(
            block(level, spot) if src is None else src, block(level, spot),
            a_send.at[level], hop_recv.at[level, spot], to_a,
        )

    def b_hop(kind, level, src=None):
        index = spot if kind == 0 else spot_a
        return remote_copy(
            block(level, index) if src is None else src, block(level, index),
            b_send.at[kind, level], hop_recv.at[level, index], to_b,
        )

    def core_hop(level, index, src=None):
        return remote_copy(
            block(level, index) if src is None else src, block(level, index),
            core_send.at[level, index], core_recv.at[level, index], partner,
        )

    def arrived(level, index):
        pltpu.make_async_copy(block(level, index), block(level, index), hop_recv.at[level, index]).wait()

    low_z, high_z = layer > 0, layer < layers - 1

    @pl.when(high_z)
    def _():
        z_hop(0, layer, chip_rows).start()

    @pl.when(low_z)
    def _():
        z_hop(1, layer, chip_rows).start()

    a_hop(layer, chip_rows).start()
    b_hop(0, layer, chip_rows).start()
    core_hop(layer, spot, chip_rows).start()
    own = pltpu.make_async_copy(chip_rows, block(layer, spot), own_sem.at[0])
    own.start()

    lax.fori_loop(1, n, wait_ask, 0)
    rows_own = vocabulary.shape[0]
    table = vocabulary[...].astype(jnp.bfloat16)
    group = 128 // capacity

    def row_copy(peer):
        return remote_copy(
            answers.at[peer], rows.at[me], row_send.at[peer], row_recv.at[me], peer
        )

    def answer(turn, carry):
        ids = jnp.zeros((8, 128), jnp.float32)
        for k in range(group):
            ids = ids + asked[turn * group + k]
        ids = ids.T[:, 0:1]
        wanted = lax.broadcasted_iota(jnp.int32, (128, rows_own), 1) + 1
        picks = jnp.where(ids.astype(jnp.int32) == wanted, 1.0, 0.0).astype(jnp.bfloat16)
        found = dot_nn(picks, table).astype(jnp.bfloat16)
        for k in range(group):
            peer = turn * group + k
            answers[peer] = found[k * capacity : (k + 1) * capacity]

            @pl.when(peer != me)
            def _():
                row_copy(peer).start()

        return carry

    lax.fori_loop(0, n // group, answer, 0)
    own_rows = pltpu.make_async_copy(answers.at[me], rows.at[me], own_sem.at[1])
    own_rows.start()

    lane = lax.broadcasted_iota(jnp.int32, sines.shape, 1)
    angles = jnp.where(lane < sines.shape[1] // 2, points[:, 0:1], points[:, 1:2]) * omegas[...]
    sines[...] = jnp.sin(angles)
    cosines[...] = jnp.cos(angles)

    def relay_column(gap):
        for way, level, there_is, further in (
            (0, layer - gap, layer - gap >= 0, high_z),
            (1, layer + gap, layer + gap < layers, low_z),
        ):

            @pl.when(there_is)
            def _():
                arrived(level, spot)

                @pl.when(further)
                def _():
                    z_hop(way, level).start()

                a_hop(level).start()
                b_hop(0, level).start()
                core_hop(level, spot).start()

    def at_gap(gap, visit):
        if gap == 0:
            visit(layer)
            return

        @pl.when(layer - gap >= 0)
        def _():
            visit(layer - gap)

        @pl.when(layer + gap < layers)
        def _():
            visit(layer + gap)

    def relay_a(level):
        arrived(level, spot_a)
        b_hop(1, level).start()
        core_hop(level, spot_a).start()

    def relay_b(index):
        def visit(level):
            arrived(level, index)
            core_hop(level, index).start()

        return visit

    for gap in range(layers):
        if gap > 0:
            relay_column(gap)
        at_gap(gap, relay_a)
        if gap > 0:
            at_gap(gap - 1, relay_b(spot_b))
            at_gap(gap - 1, relay_b(spot_ab))
    at_gap(layers - 1, relay_b(spot_b))
    at_gap(layers - 1, relay_b(spot_ab))

    def finish(level, carry):
        for index in (spot, spot_a, spot_b, spot_ab):
            core_hop(level, index).wait_send()
        for index in range(4):
            other = full.at[level, index, :, there]
            pltpu.make_async_copy(other, other, core_recv.at[level, index]).wait()
        a_hop(level).wait_send()
        b_hop(0, level).wait_send()
        b_hop(1, level).wait_send()

        @pl.when((level <= layer) & high_z)
        def _():
            z_hop(0, level).wait_send()

        @pl.when((level >= layer) & low_z)
        def _():
            z_hop(1, level).wait_send()

        return carry

    lax.fori_loop(0, layers, finish, 0)
    own.wait()
    own_rows.wait()
    for copy in swaps:
        copy.wait_send()

    def finish_rows(step, carry):
        peer = lax.rem(me + step, n)
        pltpu.make_async_copy(answers.at[peer], answers.at[peer], row_send.at[peer]).wait()
        source = lax.rem(me - step + n, n)
        pltpu.make_async_copy(rows.at[source], rows.at[source], row_recv.at[source]).wait()
        return carry

    lax.fori_loop(1, n, finish_rows, 0)


def front(lists, vocabulary, pages, positions, weights, n, capacity, ident):
    model = vocabulary.shape[1]
    layers = n // 8
    units = [weight.shape[0] // 24 for weight in weights]
    points = positions.astype(jnp.float32).T
    waves = model // 4
    omegas = jnp.power(10000.0, -jnp.arange(waves).astype(jnp.float32) / waves)
    omegas = jnp.concatenate([omegas, omegas])[None]
    angles = jax.ShapeDtypeStruct((points.shape[0], 2 * waves), jnp.float32)
    swap = 24 * sum(units)
    chip = 2 * (swap + pages.shape[0])
    low = jnp.bfloat16
    dma = pltpu.SemaphoreType.DMA
    vmem = pl.BlockSpec(memory_space=pltpu.VMEM)
    anywhere = pl.BlockSpec(memory_space=pl.ANY)
    return pl.pallas_call(
        partial(front_kernel, n, units, capacity),
        name="front",
        out_shape=(
            jax.ShapeDtypeStruct(lists.shape, lists.dtype),
            jax.ShapeDtypeStruct((n, capacity, model), low),
            jax.ShapeDtypeStruct((layers, 4, chip, model), low),
            angles,
            angles,
        ),
        in_specs=[vmem] * (5 + len(weights)),
        out_specs=(vmem, anywhere, anywhere, vmem, vmem),
        scratch_shapes=[
            pltpu.VMEM((swap, model // 2), jnp.float32),
            pltpu.VMEM((swap, model // 2), jnp.float32),
            pltpu.VMEM((chip, model // 2), low),
            pltpu.VMEM((n, capacity, model), low),
            dma((n,)),
            dma((n,)),
            dma((n,)),
            dma((n,)),
            dma((2,)),
            dma((2,)),
            dma((2,)),
            dma((layers, 4)),
            dma((layers, 4)),
            dma((layers, 4)),
            dma((2, layers)),
            dma((layers,)),
            dma((2, layers)),
        ],
        compiler_params=pltpu.CompilerParams(
            collective_id=ident, has_side_effects=True, vmem_limit_bytes=48 * 2**20
        ),
        cost_estimate=pl.CostEstimate(
            flops=0, bytes_accessed=100 * 2**20, transcendentals=0
        ),
    )(lists, vocabulary, pages, points, omegas, *weights)


def back_kernel(n, units, pieces, chunks, *refs):
    count = len(units)
    sent, small, grads = refs[0], refs[1], refs[2 : 2 + count]
    came, small_came, out = refs[2 + count : 5 + count]
    own, par, from_b, from_a, from_z, mine, gone, back = refs[5 + count : 13 + count]
    row_send, row_recv, own_sem, load_sem, pair_send, pair_recv = refs[13 + count : 19 + count]
    b_send, b_recv, a_send, a_recv, z_send, z_recv, f_send, f_recv = refs[19 + count :]
    layers = n // 8
    me = lax.axis_index("dp")
    core, spot, layer, step_a, step_b = place_of(me)
    half = own.shape[3]
    here = pl.ds(pl.multiple_of(core * half, 128), half)
    there = pl.ds(pl.multiple_of((1 - core) * half, 128), half)
    partner = me + 1 - 2 * core
    to_a, to_b = me + 2 * step_a, me + 2 * step_b
    offsets = [48 * sum(units[:k]) for k in range(count)]
    spot_a, spot_b, spot_ab = spot + step_a, spot + step_b, spot + step_a + step_b
    size = own.shape[2] // chunks

    greet_everyone(me, n)
    for index in (spot_ab, spot_a, spot_b, spot):
        for ref, at, unit in zip(grads, offsets, units):
            remote_copy(
                ref.at[:, index, :, there],
                par.at[:, index, pl.ds(at, 48 * unit)],
                pair_send.at[index],
                pair_recv.at[index],
                partner,
            ).start()
    for index in (spot_ab, spot_b, spot_a, spot):
        for ref, at, unit in zip(grads, offsets, units):
            pltpu.make_async_copy(
                ref.at[:, index, :, here], own.at[:, index, pl.ds(at, 48 * unit)], load_sem.at[index]
            ).start()

    def row_copies(step):
        peer = lax.rem(me + step, n)
        return [
            remote_copy(src.at[peer], dst.at[me], row_send.at[k, step], row_recv.at[k, step], peer)
            for k, (src, dst) in enumerate(((sent, came), (small, small_came)))
        ]

    def start_rows(step, carry):
        for copy in row_copies(step):
            copy.start()
        return carry

    def finish_rows(step, carry):
        for copy in row_copies(step):
            copy.wait()
        return carry

    lax.fori_loop(1, n, start_rows, 0)
    own_copies = [
        pltpu.make_async_copy(src.at[me], dst.at[me], own_sem.at[k])
        for k, (src, dst) in enumerate(((sent, came), (small, small_came)))
    ]
    for copy in own_copies:
        copy.start()

    def arrived(index):
        pltpu.make_async_copy(own.at[:, index], own.at[:, index], load_sem.at[index]).wait()
        pltpu.make_async_copy(par.at[:, index], par.at[:, index], pair_recv.at[index]).wait()

    def total(*parts):
        return sum(part[...].astype(jnp.float32) for part in parts)

    def b_copy(kind, level, part):
        cut = pl.ds(part * size, size)
        return remote_copy(
            own.at[level, spot_ab if kind == 0 else spot_b, cut], from_b.at[kind, level, cut],
            b_send.at[kind, level, part], b_recv.at[kind, level, part], to_b,
        )

    def a_copy(level, part):
        cut = pl.ds(part * size, size)
        return remote_copy(
            own.at[level, spot_a, cut], from_a.at[level, cut],
            a_send.at[level, part], a_recv.at[level, part], to_a,
        )

    def z_copy(level, part):
        cut = pl.ds(part * size, size)
        return remote_copy(
            own.at[level, spot, cut], from_z.at[layer, cut],
            z_send.at[level, part], z_recv.at[layer, part], me + 8 * (level - layer),
        )

    def cross_b(kind, index, part):
        cut = pl.ds(part * size, size)

        def step(level, carry):
            own[level, index, cut] = total(
                own.at[level, index, cut], par.at[level, index, cut]
            ).astype(own.dtype)
            b_copy(kind, level, part).start()
            return carry

        lax.fori_loop(0, layers, step, 0)

    def cross_a(part):
        cut = pl.ds(part * size, size)

        def step(level, carry):
            b_copy(0, level, part).wait_recv()
            own[level, spot_a, cut] = total(
                own.at[level, spot_a, cut], par.at[level, spot_a, cut], from_b.at[0, level, cut]
            ).astype(own.dtype)
            a_copy(level, part).start()
            return carry

        lax.fori_loop(0, layers, step, 0)

    def column(level, part):
        cut = pl.ds(part * size, size)
        b_copy(1, level, part).wait_recv()
        a_copy(level, part).wait_recv()
        return total(
            own.at[level, spot, cut], par.at[level, spot, cut],
            from_b.at[1, level, cut], from_a.at[level, cut],
        )

    def cross_z(part):
        cut = pl.ds(part * size, size)

        def step(gap, carry):
            level = lax.rem(layer + gap, layers)
            own[level, spot, cut] = column(level, part).astype(own.dtype)
            z_copy(level, part).start()
            return carry

        lax.fori_loop(1, layers, step, 0)
        mine[cut] = column(layer, part)

    arrived(spot_ab)
    cross_b(0, spot_ab, 0)
    arrived(spot_b)
    for part in range(chunks):
        if part > 0:
            cross_b(0, spot_ab, part)
        cross_b(1, spot_b, part)
    arrived(spot_a)
    arrived(spot)
    for part in range(chunks):
        cross_a(part)
        if part > 0:
            cross_z(part - 1)
    cross_z(chunks - 1)
    for part in range(chunks):
        cut = pl.ds(part * size, size)

        def step(gap, carry):
            level = lax.rem(layer + gap, layers)
            remote_copy(
                own.at[level, spot, cut], from_z.at[level, cut],
                z_send.at[level, part], z_recv.at[level, part], me,
            ).wait_recv()
            mine[cut] += total(from_z.at[level, cut])
            return carry

        lax.fori_loop(1, layers, step, 0)

    at = 0
    for piece in pieces:
        offset, rows = 2 * at, 24 * piece
        gone[pl.ds(at, rows)] = mine[pl.ds(pl.multiple_of(offset + (1 - core) * rows, 8), rows)]
        out[pl.ds(at, rows), here] = mine[pl.ds(pl.multiple_of(offset + core * rows, 8), rows)]
        at += rows
    last = remote_copy(gone, back, f_send, f_recv, partner)
    last.start()
    last.wait()
    out[:, there] = back[...]
    for index in range(4):
        pltpu.make_async_copy(par.at[:, index], par.at[:, index], pair_send.at[index]).wait()

    def settle(level, carry):
        for part in range(chunks):
            b_copy(0, level, part).wait_send()
            b_copy(1, level, part).wait_send()
            a_copy(level, part).wait_send()

            @pl.when(level != layer)
            def _():
                z_copy(level, part).wait_send()

        return carry

    lax.fori_loop(0, layers, settle, 0)
    lax.fori_loop(1, n, finish_rows, 0)
    for copy in own_copies:
        copy.wait()


def to_owners(sent, small, grads, pieces, n, ident):
    model = grads[0].shape[2]
    layers = n // 8
    units = [grad.shape[1] // 48 for grad in grads]
    chunks = max(k for k in range(1, 6) if sum(units) % k == 0)
    rows = 48 * sum(units)
    half = model // 2
    low = jnp.bfloat16
    dma = pltpu.SemaphoreType.DMA
    anywhere = pl.BlockSpec(memory_space=pl.ANY)
    return pl.pallas_call(
        partial(back_kernel, n, units, pieces, chunks),
        name="back",
        out_shape=(
            jax.ShapeDtypeStruct(sent.shape, sent.dtype),
            jax.ShapeDtypeStruct(small.shape, small.dtype),
            jax.ShapeDtypeStruct((rows // 2, model), jnp.float32),
        ),
        in_specs=[anywhere] * (2 + len(grads)),
        out_specs=(anywhere, anywhere, pl.BlockSpec(memory_space=pltpu.VMEM)),
        scratch_shapes=[
            pltpu.VMEM((layers, 4, rows, half), low),
            pltpu.VMEM((layers, 4, rows, half), low),
            pltpu.VMEM((2, layers, rows, half), low),
            pltpu.VMEM((layers, rows, half), low),
            pltpu.VMEM((layers, rows, half), low),
            pltpu.VMEM((rows, half), jnp.float32),
            pltpu.VMEM((rows // 2, half), jnp.float32),
            pltpu.VMEM((rows // 2, half), jnp.float32),
            dma((2, n)),
            dma((2, n)),
            dma((2,)),
            dma((4,)),
            dma((4,)),
            dma((4,)),
            dma((2, layers, chunks)),
            dma((2, layers, chunks)),
            dma((layers, chunks)),
            dma((layers, chunks)),
            dma((layers, chunks)),
            dma((layers, chunks)),
            dma,
            dma,
        ],
        compiler_params=pltpu.CompilerParams(
            collective_id=ident, has_side_effects=True, vmem_limit_bytes=60 * 2**20
        ),
        cost_estimate=pl.CostEstimate(
            flops=0, bytes_accessed=100 * 2**20, transcendentals=0
        ),
    )(sent, small, *[grad.reshape(layers, 4, -1, model) for grad in grads])


def flat(rows):
    return rows.reshape(-1, rows.shape[-1])


def enter_kernel(
    full, target, mask_rows, mask_col, sines, cosines, gains, normed_out, white_out, scale_out, low_out, q, k, v, held, sem
):
    low = jnp.bfloat16
    box_copy = pltpu.make_async_copy(full.at[:, pl.ds(0, 48)], held.at[:, pl.ds(0, 48)], sem.at[0])
    mix_copy = pltpu.make_async_copy(full.at[:, pl.ds(144, 144)], held.at[:, pl.ds(48, 144)], sem.at[1])
    box_copy.start()
    mix_copy.start()
    rows = jnp.where(mask_col[...] == 1.0, mask_rows[...], target[...])
    boxes = jnp.concatenate([sines[...], cosines[...]], 1).astype(low)
    box_copy.wait()
    embedded = rows + dot_nt(boxes, flat(held[:, 0:48]))
    normed, white, scale = layer_norm(embedded, gains[0:1], gains[1:2])
    normed_out[...], white_out[...], scale_out[...] = normed, white, scale
    normed = normed.astype(low)
    low_out[...] = normed
    mix_copy.wait()
    for third, ref in enumerate((q, k, v)):
        part = flat(held[:, 48 + 48 * third : 96 + 48 * third])
        ref[...] = dot_nn(normed, part).astype(low)


def enter(full, target, mask_rows, mask_col, sines, cosines, gains):
    size, model = target.shape
    low, wide = jnp.bfloat16, jnp.float32
    vmem = pl.BlockSpec(memory_space=pltpu.VMEM)
    shape = jax.ShapeDtypeStruct
    return pl.pallas_call(
        enter_kernel,
        name="enter",
        out_shape=(
            shape((size, model), wide),
            shape((size, model), wide),
            shape((size, 1), wide),
            shape((size, model), low),
        )
        + (shape((size, model), low),) * 3,
        in_specs=[pl.BlockSpec(memory_space=pl.ANY)] + [vmem] * 6,
        out_specs=(vmem,) * 7,
        scratch_shapes=[
            pltpu.VMEM((full.shape[0], 192, model), low),
            pltpu.SemaphoreType.DMA((2,)),
        ],
        compiler_params=pltpu.CompilerParams(vmem_limit_bytes=56 * 2**20),
        cost_estimate=pl.CostEstimate(
            flops=8 * size * model * model, bytes_accessed=16 * 2**20, transcendentals=0
        ),
    )(full, target, mask_rows, mask_col, sines, cosines, gains)


def upper_kernel(
    page_rows, full, attended, normed, target, mask_col, page, row, share, gains,
    grads, d_attended, d_lower, pos_rows, norms, loss_part,
    held, bank, slopes, hidden, scores, load_sem, store_sem,
):
    low = jnp.bfloat16
    chips, used, model = held.shape
    size = attended.shape[0]
    blocks = hidden.shape[0]
    first_row = 288
    span = model // (used - 48 - 48 * blocks)
    down_at = 48 + 48 * blocks
    loads = [
        pltpu.make_async_copy(full.at[:, pl.ds(first_row + at, many)], held.at[:, pl.ds(at, many)], load_sem.at[k])
        for k, (at, many) in enumerate(((0, 48), (48, 48 * blocks), (down_at, used - down_at)))
    ]
    loads.append(
        pltpu.make_async_copy(full.at[:, pl.ds(first_row + used, bank.shape[1])], bank, load_sem.at[3])
    )
    for copy in loads:
        copy.start()

    def up_map(k):
        return flat(held[:, 48 + 48 * k : 96 + 48 * k])

    def down_map(k):
        return flat(held[span * k : span * (k + 1), down_at:])

    loads[0].wait()
    second, white_mid, scale_mid = layer_norm(
        normed[...] + dot_nn(attended[...], flat(held[:, 0:48])), gains[2:3], gains[3:4]
    )
    middle = second.astype(low)
    loads[1].wait()
    loads[2].wait()
    for k in range(blocks):
        pre = dot_nn(middle, up_map(k))
        normal = 0.5 + 0.5 * lax.erf(pre * (0.5**0.5))
        active = (pre * normal).astype(low)
        slopes[k] = normal + pre * (jnp.exp(-0.5 * pre * pre) * 0.3989422804014327)
        hidden[k] = active
        part = dot_nn(active, down_map(k))
        lowered = part if k == 0 else lowered + part
    states, white_last, scale_last = layer_norm(second + lowered, gains[4:5], gains[5:6])
    states = states.astype(low)

    inv_root = model ** (-0.5)
    positive = jnp.sum(states.astype(jnp.float32) * target[...], -1, keepdims=True) * inv_root
    many = page.shape[0]
    seat = lax.broadcasted_iota(jnp.int32, (many, 128), 0)
    lane = lax.broadcasted_iota(jnp.int32, (many, 128), 1)
    spread = jnp.where(lax.rem(lane, many) == seat, 1.0, 0.0).astype(low)
    wanted = page_rows * dot_tn(page[...].astype(jnp.float32).astype(low), spread) + dot_tn(
        row[...].astype(jnp.float32).astype(low), spread
    )
    wanted = jnp.concatenate([wanted.astype(jnp.int32)] * 4, 1)
    column = lax.broadcasted_iota(jnp.int32, wanted.shape, 1)
    width = wanted.shape[1]
    per = width // bank.shape[1]
    parts = chips // per
    loads[3].wait()
    highest = positive
    for c in range(parts):
        raw = dot_nt(states, flat(bank[per * c : per * (c + 1)])) * inv_root
        raw = jnp.where(wanted == column + c * width, raw, -jnp.inf)
        scores[:, c * width : (c + 1) * width] = raw
        highest = jnp.maximum(highest, jnp.max(raw, -1, keepdims=True))
    lead = jnp.exp(positive - highest)
    total = lead
    for c in range(parts):
        powers = jnp.exp(scores[:, c * width : (c + 1) * width] - highest)
        scores[:, c * width : (c + 1) * width] = powers
        total = total + jnp.sum(powers, -1, keepdims=True)
    mask = mask_col[...]
    loss_part[...] = share[0, 0] * jnp.sum(
        mask * (highest + jnp.log(total) - positive), keepdims=True
    )
    factor = share[0, 0] * mask * inv_root
    positive_grad = factor * (lead / total - 1.0)
    factor = factor / total
    pos_rows[...] = (positive_grad * states.astype(jnp.float32)).astype(pos_rows.dtype)
    d_states = positive_grad * target[...]
    for c in range(parts):
        weights = (scores[:, c * width : (c + 1) * width] * factor).astype(low)
        d_states = d_states + dot_nn(weights, flat(bank[per * c : per * (c + 1)]))

    d_mid, gain_last, bias_last = norm_back(d_states, white_last, scale_last, gains[4:5])
    d_down = d_mid.astype(low)
    d_second = d_mid
    stores = []
    for k in range(blocks):
        d_pre = (dot_nt(d_down, down_map(k)) * slopes[k]).astype(low)
        d_second = d_second + dot_nt(d_pre, up_map(k))
        grad = dot_tn(hidden[k], d_down).astype(low)
        held[span * k : span * (k + 1), down_at:] = grad.reshape(span, -1, model)
        grad = dot_tn(middle, d_pre).astype(low)
        held[:, 48 + 48 * k : 96 + 48 * k] = grad.reshape(chips, 48, model)
        for j, cut in enumerate(
            (
                (pl.ds(span * k, span), pl.ds(down_at, used - down_at)),
                (pl.ds(0, chips), pl.ds(48 + 48 * k, 48)),
            )
        ):
            stores.append(pltpu.make_async_copy(held.at[cut], grads.at[cut], store_sem.at[2 * k + j]))
            stores[-1].start()
    d_low, gain_mid, bias_mid = norm_back(d_second, white_mid, scale_mid, gains[2:3])
    d_lower[...] = d_low
    d_attn = d_low.astype(low)
    d_attended[...] = dot_nt(d_attn, flat(held[:, 0:48])).astype(low)
    held[:, 0:48] = dot_tn(attended[...], d_attn).astype(low).reshape(chips, 48, model)
    cut = (pl.ds(0, chips), pl.ds(0, 48))
    stores.append(pltpu.make_async_copy(held.at[cut], grads.at[cut], store_sem.at[2 * blocks]))
    stores[-1].start()
    for at, line in enumerate((gain_mid, bias_mid, gain_last, bias_last)):
        norms[at : at + 1] = line
    for copy in stores:
        copy.wait()


def upper(full, attended, normed, target, mask_col, page, row, share, gains, blocks, page_rows):
    size, model = normed.shape
    chips = full.shape[0]
    used = full.shape[1] - 288 - 2 * page_rows
    low, wide = jnp.bfloat16, jnp.float32
    vmem = pl.BlockSpec(memory_space=pltpu.VMEM)
    anywhere = pl.BlockSpec(memory_space=pl.ANY)
    shape = jax.ShapeDtypeStruct
    return pl.pallas_call(
        partial(upper_kernel, page_rows),
        name="upper",
        out_shape=(
            shape((chips, used, model), low),
            shape((size, model), low),
            shape((size, model), wide),
            shape((size, model), low),
            shape((4, model), wide),
            shape((1, 1), wide),
        ),
        in_specs=[anywhere]
        + [vmem] * 6
        + [pl.BlockSpec(memory_space=pltpu.SMEM), vmem],
        out_specs=(anywhere,) + (vmem,) * 5,
        scratch_shapes=[
            pltpu.VMEM((chips, used, model), low),
            pltpu.VMEM((chips, 2 * page_rows, model), low),
            pltpu.VMEM((blocks, size, model), wide),
            pltpu.VMEM((blocks, size, model), low),
            pltpu.VMEM((size, chips * 2 * page_rows), wide),
            pltpu.SemaphoreType.DMA((4,)),
            pltpu.SemaphoreType.DMA((2 * blocks + 1,)),
        ],
        compiler_params=pltpu.CompilerParams(vmem_limit_bytes=63 * 2**20),
        cost_estimate=pl.CostEstimate(
            flops=20 * 10**9, bytes_accessed=32 * 2**20, transcendentals=4 * size * model * 2
        ),
    )(full, attended, normed, target, mask_col, page, row, share, gains)


def lower_kernel(
    fixed, full, dq, dk, dv, d_lower, white, scale, gains, normed, sines, cosines, mask_col, pos_rows, place,
    grads, d_embedded, sent, norms, held, sem,
):
    low = jnp.bfloat16
    chips, _, model = held.shape
    load = pltpu.make_async_copy(full.at[:, pl.ds(144, 144)], held.at[:, pl.ds(48, 144)], sem.at[0])
    load.start()
    mask = mask_col[...]
    d_first = d_lower[...]
    load.wait()
    stores = []
    for third, ref in enumerate((dq, dk, dv)):
        at = 48 + 48 * third
        upstream = ref[...]
        d_first = d_first + dot_nt(upstream, flat(held[:, at : at + 48]))
        held[:, at : at + 48] = dot_tn(normed[...], upstream).astype(low).reshape(chips, 48, model)
        stores.append(
            pltpu.make_async_copy(held.at[:, pl.ds(at, 48)], grads.at[:, pl.ds(at, 48)], sem.at[1 + third])
        )
        stores[-1].start()
    d_rows, gain, bias = norm_back(d_first, white[...], scale[...], gains[0:1])
    d_embedded[...] = d_rows
    boxes = jnp.concatenate([sines[...], cosines[...]], 1).astype(low)
    held[:, 0:48] = dot_tn(d_rows.astype(low), boxes).astype(low).reshape(chips, 48, model)
    stores.append(pltpu.make_async_copy(held.at[:, pl.ds(0, 48)], grads.at[:, pl.ds(0, 48)], sem.at[4]))
    stores[-1].start()
    norms[0:1], norms[1:2] = gain, bias
    token_grads = jnp.where(mask == 1.0, pos_rows[...].astype(jnp.float32), d_rows).astype(low)
    mask_grad = jnp.sum(mask * d_rows, 0, keepdims=True)
    slots = sent.shape[0]
    seats = lax.broadcasted_iota(jnp.int32, (place.shape[0], slots), 1) == place[...]
    found = dot_tn(jnp.where(seats, 1.0, 0.0).astype(low), token_grads)
    line = lax.broadcasted_iota(jnp.int32, (slots, 1), 0)
    sent[...] = jnp.where(line == fixed, mask_grad, found).astype(low)
    for copy in stores:
        copy.wait()


def lower(
    full, d_joined, d_lower, white, scale, gains, normed, sines, cosines, mask_col, pos_rows, place, slots, fixed
):
    size, model = d_lower.shape
    chips = full.shape[0]
    low, wide = jnp.bfloat16, jnp.float32
    vmem = pl.BlockSpec(memory_space=pltpu.VMEM)
    anywhere = pl.BlockSpec(memory_space=pl.ANY)
    shape = jax.ShapeDtypeStruct
    return pl.pallas_call(
        partial(lower_kernel, fixed),
        name="lower",
        out_shape=(
            shape((chips, 192, model), low),
            shape((size, model), wide),
            shape((slots, model), low),
            shape((2, model), wide),
        ),
        in_specs=[anywhere] + [vmem] * 13,
        out_specs=(anywhere,) + (vmem,) * 3,
        scratch_shapes=[
            pltpu.VMEM((chips, 192, model), low),
            pltpu.SemaphoreType.DMA((5,)),
        ],
        compiler_params=pltpu.CompilerParams(vmem_limit_bytes=60 * 2**20),
        cost_estimate=pl.CostEstimate(
            flops=6 * 10**9, bytes_accessed=24 * 2**20, transcendentals=0
        ),
    )(full, *d_joined, d_lower, white, scale, gains, normed, sines, cosines, mask_col, pos_rows, place)


def totals_kernel(n, table, sums, norm_came, loss_part, out, norm_piece, message, came, send_sem, recv_sem):
    me = lax.axis_index("dp")
    square = jnp.sum(sums[...] * sums[...], keepdims=True)
    for part in range(4):
        rows = table.shape[0] // 4
        piece = table[part * rows : (part + 1) * rows]
        square = square + jnp.sum(piece * piece, keepdims=True)
    norm = norm_came[0]
    for k in range(1, n):
        norm = norm + norm_came[k]
    norm_piece[...] = norm
    square = square + jnp.sum(norm * norm, keepdims=True)
    lane = lax.broadcasted_iota(jnp.int32, message.shape, 1)
    message[...] = jnp.where(lane == 0, square, jnp.where(lane == 1, loss_part[...], 0.0))
    greet_everyone(me, n)

    def copy(step):
        peer = lax.rem(me + step, n)
        return remote_copy(message, came.at[me], send_sem.at[step], recv_sem.at[step], peer)

    def start(step, carry):
        copy(step).start()
        return carry

    def finish(step, carry):
        copy(step).wait()
        return carry

    lax.fori_loop(1, n, start, 0)
    came[me] = message[...]
    lax.fori_loop(1, n, finish, 0)
    total = came[0]
    for k in range(1, n):
        total = total + came[k]
    out[...] = total


def sum_totals(table, sums, norm_came, loss_part, n, ident):
    vmem = pl.BlockSpec(memory_space=pltpu.VMEM)
    tile = jax.ShapeDtypeStruct((8, 128), jnp.float32)
    return pl.pallas_call(
        partial(totals_kernel, n),
        name="totals",
        out_shape=(tile, tile),
        in_specs=[vmem] * 4,
        out_specs=(vmem,) * 2,
        scratch_shapes=[
            pltpu.VMEM((8, 128), jnp.float32),
            pltpu.VMEM((n, 8, 128), jnp.float32),
            pltpu.SemaphoreType.DMA((n,)),
            pltpu.SemaphoreType.DMA((n,)),
        ],
        compiler_params=pltpu.CompilerParams(
            collective_id=ident, has_side_effects=True, vmem_limit_bytes=32 * 2**20
        ),
        cost_estimate=pl.CostEstimate(flops=0, bytes_accessed=8 * 2**20, transcendentals=0),
    )(table, sums, norm_came, loss_part)


def update_kernel(decay, layout, factor, table, sums, *refs):
    masters, moments, averages = refs[0:7], refs[7:14], refs[14:21]
    fresh, speeds, smooths = refs[21:28], refs[28:35], refs[35:42]
    scale = factor[0, 0]

    def update(k, piece, rate, cut):
        clipped = piece * scale
        velocity = momentum_decay * moments[k][cut] + clipped
        updated = masters[k][cut] - rate * (clipped + momentum_decay * velocity)
        fresh[k][cut] = updated
        speeds[k][cut] = velocity
        smooths[k][cut] = decay * averages[k][cut] + (1.0 - decay) * updated

    update(0, table[...], table_rate, (slice(None), slice(None)))

    @pl.when(pl.program_id(0) == 0)
    def _():
        model = sums.shape[1]
        for k, at, blocks, rows, turned in layout:
            for block in range(blocks):
                piece = sums[at + block * rows : at + (block + 1) * rows]
                if turned:
                    update(k, swap_middle(piece.T), learn_rate, (slice(None), slice(None)))
                else:
                    cut = (slice(None), slice(block * model, (block + 1) * model))
                    update(k, piece, learn_rate, cut)


def update_all(factor, table, sums, masters, moments, averages, decay, layout):
    steps = 6
    rows, model = table.shape
    banded = pl.BlockSpec((rows // steps, model), lambda i: (i, 0))
    whole = lambda array: pl.BlockSpec(array.shape, lambda i: (0, 0))
    group = lambda arrays: [banded] + [whole(array) for array in arrays[1:]]
    shapes = tuple(jax.ShapeDtypeStruct(array.shape, jnp.float32) for array in masters)
    return pl.pallas_call(
        partial(update_kernel, decay, layout),
        name="update",
        grid=(steps,),
        out_shape=shapes * 3,
        in_specs=[pl.BlockSpec(memory_space=pltpu.SMEM), banded, whole(sums)]
        + group(masters)
        + group(moments)
        + group(averages),
        out_specs=tuple(group(masters) * 3),
        compiler_params=pltpu.CompilerParams(vmem_limit_bytes=56 * 2**20),
        cost_estimate=pl.CostEstimate(flops=0, bytes_accessed=28 * 2**20, transcendentals=0),
    )(factor, table, sums, *masters, *moments, *averages)


def split_rows(packed, grads, n):
    out, at = [], 0
    for grad in grads:
        count = grad.shape[0] // n
        out.append(packed[at : at + count])
        at += count
    return out


def scatter(grads, n):
    model = grads[0].shape[1]
    joined = jnp.concatenate([grad.reshape(n, -1, model) for grad in grads], 1)
    joined = joined.reshape(-1, model)
    mine = lax.psum_scatter(joined, "dp", scatter_dimension=0, tiled=True)
    return split_rows(mine.astype(jnp.float32), grads, n)


def masked(rows, half):
    lane = lax.broadcasted_iota(jnp.int32, rows.shape, 1)
    keep = (lane < HD) if half == 0 else (lane >= HD)
    return jnp.where(keep, rows, jnp.zeros_like(rows))


def turn(terms, sines, cosines):
    half = sines.shape[1]
    sine, cosine = terms[:, :half], terms[:, half:]
    return jnp.concatenate(
        [sine * sines + cosine * cosines, cosine * sines - sine * cosines], 1
    ).astype(jnp.bfloat16)


def turn_back(upstream, sines, cosines):
    half = sines.shape[1]
    first, second = upstream[:, :half], upstream[:, half:]
    return jnp.concatenate(
        [first * sines - second * cosines, first * cosines + second * sines], 1
    ).astype(jnp.bfloat16)


def pick_halves(low_half, high_half):
    lane = lax.broadcasted_iota(jnp.int32, low_half.shape, 1)
    return jnp.where(lane < HD, low_half, high_half)


def attend_kernel(q, k, v, rel_text, rel_box, sines, cosines, bases, attended, probs):
    queries, keys, values = q[...], k[...], v[...]
    spread = bases[...]
    results = []
    for half in range(2):
        mine = masked(queries, half)
        terms = dot_nn(masked(keys, half), rel_box[...])
        box_rot = turn(terms, sines[...], cosines[...])
        terms = dot_nn(mine, rel_text[...])
        text_rot = turn(terms, sines[...], cosines[...])
        scores = dot_nt(mine, keys) + dot_nt(text_rot, spread) + dot_nt(spread, box_rot)
        scores = scores * HD ** (-0.5)
        powers = jnp.exp(scores - jnp.max(scores, -1, keepdims=True))
        shares = powers * (1.0 / jnp.sum(powers, -1, keepdims=True))
        probs[half] = shares
        results.append(dot_nn(shares.astype(jnp.bfloat16), values))
    attended[...] = pick_halves(*results).astype(jnp.bfloat16)


def attend(joined, rel_map, sines, cosines, bases):
    size, model = bases.shape
    pairs = model // (2 * HD)
    lanes = 2 * HD
    whole = lambda rows: pl.BlockSpec(rows.shape, lambda i: (0, 0))
    column = pl.BlockSpec((size, lanes), lambda i: (0, i))
    band = lambda part: pl.BlockSpec((lanes, model), lambda i: (i + part * pairs, 0))
    return pl.pallas_call(
        attend_kernel,
        name="attend",
        grid=(pairs,),
        out_shape=(
            jax.ShapeDtypeStruct((size, model), jnp.bfloat16),
            jax.ShapeDtypeStruct((2 * pairs, size, size), jnp.float32),
        ),
        in_specs=[column, column, column, band(0), band(1)]
        + [whole(sines), whole(cosines), whole(bases)],
        out_specs=(
            column,
            pl.BlockSpec((2, size, size), lambda i: (i, 0, 0)),
        ),
        compiler_params=pltpu.CompilerParams(vmem_limit_bytes=56 * 2**20),
        cost_estimate=pl.CostEstimate(
            flops=2 * 12 * size * (size * 1700 + 2 * 64 * 768),
            bytes_accessed=20 * 2**20,
            transcendentals=12 * size * size,
        ),
    )(*joined, rel_map, rel_map, sines, cosines, bases)


def attend_back_kernel(
    d_out, q, k, v, rel_text, rel_box, probs, sines, cosines, bases, dq, dk, dv, g_rel
):
    queries, keys, values, upstream = q[...], k[...], v[...], d_out[...]
    spread = bases[...]
    scale = HD ** (-0.5)
    low = jnp.bfloat16
    got = [[], [], []]
    for half in range(2):
        shares = probs[half]
        d_probs = dot_nt(masked(upstream, half), values)
        got[2].append(dot_tn(shares.astype(low), upstream))
        inner = jnp.sum(d_probs * shares, -1, keepdims=True)
        d_scores = (shares * (d_probs - inner)).astype(low)
        d_text = turn_back(dot_nn(d_scores, spread) * scale, sines[...], cosines[...])
        got[0].append(dot_nn(d_scores, keys) * scale + dot_nt(d_text, rel_text[...]))
        part = dot_tn(masked(queries, half), d_text)
        text_sum = part if half == 0 else text_sum + part
        turned = d_scores.T
        d_box = turn_back(dot_nn(turned, spread) * scale, sines[...], cosines[...])
        got[1].append(dot_nn(turned, queries) * scale + dot_nt(d_box, rel_box[...]))
        part = dot_tn(masked(keys, half), d_box)
        box_sum = part if half == 0 else box_sum + part
    for ref, halves in zip((dq, dk, dv), got):
        ref[...] = pick_halves(*halves).astype(low)
    g_rel[0] = text_sum.astype(low)
    g_rel[1] = box_sum.astype(low)


def attend_back(d_attended, joined, rel_map, probs, sines, cosines, bases):
    size, model = bases.shape
    pairs = model // (2 * HD)
    lanes = 2 * HD
    low = jnp.bfloat16
    whole = lambda rows: pl.BlockSpec(rows.shape, lambda i: (0, 0))
    column = pl.BlockSpec((size, lanes), lambda i: (0, i))
    band = lambda part: pl.BlockSpec((lanes, model), lambda i: (i + part * pairs, 0))
    return pl.pallas_call(
        attend_back_kernel,
        name="attend_back",
        grid=(pairs,),
        out_shape=(jax.ShapeDtypeStruct((size, model), low),) * 3
        + (jax.ShapeDtypeStruct((2, model, model), low),),
        in_specs=[column, column, column, column, band(0), band(1)]
        + [pl.BlockSpec((2, size, size), lambda i: (i, 0, 0))]
        + [whole(sines), whole(cosines), whole(bases)],
        out_specs=(column,) * 3 + (pl.BlockSpec((2, lanes, model), lambda i: (0, i, 0)),),
        compiler_params=pltpu.CompilerParams(vmem_limit_bytes=56 * 2**20),
        cost_estimate=pl.CostEstimate(
            flops=2 * 12 * size * (size * 1800 + 4 * 64 * 768),
            bytes_accessed=25 * 2**20,
            transcendentals=0,
        ),
    )(d_attended, *joined, rel_map, rel_map, probs, sines, cosines, bases)


def swap_middle(rows):
    count = rows.shape[0] // 4
    return jnp.concatenate(
        [rows[:count], rows[2 * count : 3 * count], rows[count : 2 * count], rows[3 * count :]], 0
    )


def forward(weights, rows, positions):
    box_map, mix_map, rel_map, out_map, up_map, down_map, norm_rows = weights
    gains = norm_rows.astype(jnp.float32)
    sin_count = box_map.shape[1]
    sin_x, cos_x, sin_y, cos_y = sinusoids(positions, sin_count // 4)
    sines = jnp.concatenate([sin_x, sin_y], -1)
    cosines = jnp.concatenate([cos_x, cos_y], -1)
    boxes = jnp.concatenate([sines, cosines], -1).astype(jnp.bfloat16)
    bases = jnp.concatenate([cosines, sines], -1).astype(jnp.bfloat16)
    embedded = rows + dot_nt(boxes, box_map)
    first = layer_norm(embedded, gains[0], gains[1])
    normed = first[0].astype(jnp.bfloat16)
    joined = [dot_nn(normed, part).astype(jnp.bfloat16) for part in mix_map]
    attended, probs = attend(joined, rel_map, sines, cosines, bases)
    second = layer_norm(first[0] + dot_nn(attended, out_map), gains[2], gains[3])
    middle = second[0].astype(jnp.bfloat16)
    hidden_pre = [dot_nn(middle, part) for part in up_map]
    hidden = [jax.nn.gelu(part, approximate=False).astype(jnp.bfloat16) for part in hidden_pre]
    lowered = sum(dot_nn(part, weight) for part, weight in zip(hidden, down_map))
    third = layer_norm(second[0] + lowered, gains[4], gains[5])
    return {
        "sines": sines,
        "cosines": cosines,
        "boxes": boxes,
        "bases": bases,
        "first": first,
        "normed": normed,
        "joined": joined,
        "probs": probs,
        "attended": attended,
        "second": second,
        "middle": middle,
        "hidden_pre": hidden_pre,
        "hidden": hidden,
        "third": third,
    }


def backward_upper(weights, cache, d_states):
    _, _, _, out_map, up_map, down_map, norm_rows = weights
    gains = norm_rows.astype(jnp.float32)
    d_mid, gain_last, bias_last = norm_back(
        d_states, cache["third"][1], cache["third"][2], gains[4]
    )
    d_down = d_mid.astype(jnp.bfloat16)
    gelu_exact = partial(jax.nn.gelu, approximate=False)
    grad_down, grad_up, d_second = [], [], d_mid
    for pre, hidden, up, down in zip(cache["hidden_pre"], cache["hidden"], up_map, down_map):
        grad_down.append(dot_tn(hidden, d_down))
        d_pre = jax.vjp(gelu_exact, pre)[1](dot_nt(d_down, down))[0].astype(jnp.bfloat16)
        grad_up.append(dot_tn(cache["middle"], d_pre))
        d_second = d_second + dot_nt(d_pre, up)
    d_lower, gain_mid, bias_mid = norm_back(
        d_second, cache["second"][1], cache["second"][2], gains[2]
    )
    d_attn = d_lower.astype(jnp.bfloat16)
    grad_out = dot_tn(cache["attended"], d_attn)
    d_attended = dot_nt(d_attn, out_map).astype(jnp.bfloat16)
    return d_lower, d_attended, grad_out, grad_up, grad_down, [gain_mid, bias_mid, gain_last, bias_last]


def backward_lower(weights, cache, d_lower, d_attended):
    box_map, mix_map, rel_map, _, _, _, norm_rows = weights
    gains = norm_rows.astype(jnp.float32)
    *d_joined, grad_rel = attend_back(
        d_attended,
        cache["joined"],
        rel_map,
        cache["probs"],
        cache["sines"],
        cache["cosines"],
        cache["bases"],
    )
    grad_mix = [dot_tn(cache["normed"], part) for part in d_joined]
    d_first = d_lower + sum(dot_nt(part, weight) for part, weight in zip(d_joined, mix_map))
    d_embedded, gain_low, bias_low = norm_back(
        d_first, cache["first"][1], cache["first"][2], gains[0]
    )
    grad_box = dot_tn(d_embedded.astype(jnp.bfloat16), cache["boxes"])
    return d_embedded, grad_box, grad_mix, grad_rel, [gain_low, bias_low]


def per_device(
    n,
    tokens,
    positions,
    documents,
    masking,
    negative_page,
    negative_row,
    pages,
    vocabulary,
    geometry,
    mixing,
    relative,
    merging,
    widening,
    narrowing,
    scaling,
    moment_vocabulary,
    moment_geometry,
    moment_mixing,
    moment_relative,
    moment_merging,
    moment_widening,
    moment_narrowing,
    moment_scaling,
    average_vocabulary,
    average_geometry,
    average_mixing,
    average_relative,
    average_merging,
    average_widening,
    average_narrowing,
    average_scaling,
):
    me = lax.axis_index("dp")
    size = tokens.shape[0]
    rows_own, model = vocabulary.shape
    page_rows = pages.shape[1]
    capacity = max(16, -(-2 * size // n) // 16 * 16)
    slots = n * capacity
    mask_float = masking.astype(jnp.float32)
    low = jnp.bfloat16
    fits = n % 8 == 0 and merging.shape[0] == 24 and page_rows % 16 == 0

    fold = 128 // capacity if fits else 1
    pieces = [
        swap_middle(geometry).T,
        swap_middle(relative).T,
        *[mixing[:, k * model : (k + 1) * model] for k in range(3)],
        merging,
        *[widening[:, k * model : (k + 1) * model] for k in range(widening.shape[1] // model)],
        narrowing,
    ]
    cols = scaling.shape[1]
    info = jnp.pad(scaling, ((1, 1), (0, 128 - cols)))
    lists, place = make_plan(tokens, masking, documents, info, n, rows_own, capacity, fold)
    bank_piece = pages.reshape(-1, model)
    if fits:
        asked, table_rows, full, sines, cosines = front(
            lists, vocabulary, bank_piece, positions, pieces, n, capacity, 1
        )
        full = full.reshape(-1, *full.shape[2:])
        wanted = jnp.sum(asked[:, 0].reshape(n // fold, fold, 128), 1)
    else:
        (asked,) = exchange([lists], 1, "ask")
        wanted = asked[:, 0, :capacity]
        pieces = [piece.astype(low) for piece in pieces] + [bank_piece]
        joined = lax.all_gather(jnp.concatenate(pieces, 0), "dp", axis=0, tiled=False)
        weights, at = [], 0
        for piece in pieces:
            weights.append(joined[:, at : at + piece.shape[0]].reshape(-1, model))
            at += piece.shape[0]
    wanted = wanted.reshape(slots, 1)
    picks = (wanted == (jnp.arange(rows_own) + 1).astype(jnp.float32)[None, :]).astype(low)
    if not fits:
        answer = dot_nn(picks, vocabulary.astype(low)).astype(low)
        (table_rows,) = exchange([answer.reshape(n, capacity, model)], 2, "rows")
    table_rows = table_rows.reshape(slots, model)
    norm_rows = asked[:, 1:7, :cols].transpose(1, 0, 2).reshape(6, n * cols).astype(low)
    count_of, doc_of = asked[:, 7, 0], asked[:, 7, 1]
    overflow = jnp.max(asked[:, 7, 2]) > 0.0
    my_count = jnp.sum(jnp.where(doc_of == documents[0].astype(jnp.float32), count_of, 0.0))
    share = 1.0 / (DOCS * jnp.maximum(my_count, 1.0))
    fixed = (mask_token // rows_own) * capacity + capacity - 1
    seats = (place == jnp.arange(slots)[None, :]).astype(low)
    target_rows = dot_nn(seats, table_rows)
    mask_rows = table_rows[fixed : fixed + 1].astype(jnp.float32)

    def dense_rows():
        table = lax.all_gather(vocabulary.astype(low), "dp", axis=0, tiled=True)
        return (
            table[tokens].astype(jnp.float32),
            table[mask_token : mask_token + 1].astype(jnp.float32),
        )

    target_rows, mask_rows = lax.cond(overflow, dense_rows, lambda: (target_rows, mask_rows))
    mask_col = mask_float[:, None]
    if fits:
        gains = norm_rows.astype(jnp.float32)
        rel_map = full[:, 48:144].reshape(-1, model)
        bases = jnp.concatenate([cosines, sines], -1).astype(low)
        normed, white, scale, normed_low, *joined = enter(
            full, target_rows, mask_rows, mask_col, sines, cosines, gains
        )
        attended, probs = attend(joined, rel_map, sines, cosines, bases)
        blocks = widening.shape[1] // model
        upper_grads, d_attended, d_lower, positive_rows, upper_norms, loss_part = upper(
            full,
            attended,
            normed,
            target_rows,
            mask_col,
            negative_page,
            negative_row,
            share.reshape(1, 1),
            gains,
            blocks,
            page_rows,
        )
        *d_joined, grad_rel = attend_back(
            d_attended, joined, rel_map, probs, sines, cosines, bases
        )
        lower_grads, d_embedded, sent, lower_norms = lower(
            full,
            d_joined,
            d_lower,
            white,
            scale,
            gains,
            normed_low,
            sines,
            cosines,
            mask_col,
            positive_rows,
            place,
            slots,
            fixed,
        )
        grad_norms = jnp.concatenate([lower_norms, upper_norms], 0)
        positive_rows = positive_rows.astype(jnp.float32)
    else:
        box_map, rel_map, mix_map = weights[0], weights[1], weights[2:5]
        out_map, up_map, down_full, bank = weights[5], weights[6:-2], weights[-2], weights[-1]
        entry_rows = jnp.where(masking[:, None] == 1, mask_rows, target_rows)

        ff = len(up_map)
        down_map = [down_full[k * model : (k + 1) * model] for k in range(ff)]
        weights = (box_map, mix_map, rel_map, out_map, up_map, down_map, norm_rows)
        cache = forward(weights, entry_rows, positions)

        states_low = cache["third"][0].astype(low)
        inv_root = model ** (-0.5)
        positive = jnp.sum(states_low.astype(jnp.float32) * target_rows, -1, keepdims=True) * inv_root
        flat_index = (negative_page * page_rows + negative_row).T
        count_neg = flat_index.shape[1]
        width = bank.shape[0]
        repeated = jnp.tile(flat_index, (1, width // count_neg))
        chosen = repeated == jnp.arange(width)[None, :]
        logits = jnp.where(chosen, dot_nt(states_low, bank) * inv_root, -jnp.inf)
        highest = jnp.maximum(jnp.max(logits, -1, keepdims=True), positive)
        powers = jnp.exp(logits - highest)
        lead = jnp.exp(positive - highest)
        total = jnp.sum(powers, -1, keepdims=True) + lead
        per_token = highest + jnp.log(total) - positive
        mask_col = mask_float[:, None]
        loss_part = share * jnp.sum(mask_col * per_token)
        weight_map = (powers * (share * mask_col / total) * inv_root).astype(low)
        positive_grad = share * mask_col * (lead / total - 1.0) * inv_root
        d_states = positive_grad * target_rows + dot_nn(weight_map, bank)

        d_lower, d_attended, grad_out, grad_up, grad_down, upper_norms = backward_upper(
            weights, cache, d_states
        )
        d_embedded, grad_box, grad_mix, grad_rel, lower_norms = backward_lower(
            weights, cache, d_lower, d_attended
        )
        grad_norms = jnp.concatenate(lower_norms + upper_norms, 0)

        positive_rows = positive_grad * states_low.astype(jnp.float32)
        token_grads = jnp.where(mask_col == 1.0, positive_rows, d_embedded).astype(low)
        mask_grad = jnp.sum(mask_col * d_embedded, 0, keepdims=True)
        sent = dot_tn(seats, token_grads)
        sent = jnp.where(jnp.arange(slots)[:, None] == fixed, mask_grad, sent).astype(low)

    norm_blocks = grad_norms.reshape(6, n, cols).transpose(1, 0, 2)
    norm_blocks = jnp.pad(norm_blocks, ((0, 0), (0, 2), (0, 128 - cols)))
    sent = sent.reshape(n, capacity, model)
    if fits:
        grads = [lower_grads, grad_rel.reshape(n // 2, -1, model), upper_grads]
        parts = (1, 1, 1, 1, 2, 1) + (1,) * blocks + (narrowing.shape[0] // 24,)
        came, norm_came, sums = to_owners(sent, norm_blocks, grads, parts, n, 2)
    else:
        came, norm_came = exchange([sent, norm_blocks], 3, "grads")
        grads = [grad_box, grad_rel.reshape(-1, model), *grad_mix, grad_out, *grad_up]
        grads = [grad.astype(low) for grad in [*grads, jnp.concatenate(grad_down, 0)]]
        sums = scatter(grads, n)

    def sparse_table():
        return dot_tn(picks, came.reshape(slots, model))

    def dense_table():
        entry = jnp.where(masking == 1, mask_token, tokens)
        table_grad = jnp.zeros((rows_own * n, model), jnp.float32).at[entry].add(d_embedded)
        table_grad = table_grad.at[tokens].add(positive_rows)
        return lax.psum_scatter(table_grad, "dp", scatter_dimension=0, tiled=True)

    table_piece = lax.cond(overflow, dense_table, sparse_table)

    masters = (vocabulary, geometry, mixing, relative, merging, widening, narrowing, scaling)
    moments = (
        moment_vocabulary,
        moment_geometry,
        moment_mixing,
        moment_relative,
        moment_merging,
        moment_widening,
        moment_narrowing,
        moment_scaling,
    )
    averages = (
        average_vocabulary,
        average_geometry,
        average_mixing,
        average_relative,
        average_merging,
        average_widening,
        average_narrowing,
        average_scaling,
    )
    decay = min(average_cap, (1.0 + STEP) / (10.0 + STEP))
    if fits:
        totals, norm_piece = sum_totals(table_piece, sums, norm_came, loss_part, n, 4)
        norm_piece = norm_piece[:6, :cols]
    else:
        norm_piece = jnp.sum(norm_came, 0)[:6, :cols]
        reduced = (
            table_piece,
            swap_middle(sums[0].T),
            jnp.concatenate(sums[2:5], 1),
            swap_middle(sums[1].T),
            sums[5],
            jnp.concatenate(sums[6:-1], 1),
            sums[-1],
            norm_piece,
        )
        square = sum((jnp.sum(piece * piece) for piece in reduced))
        lane = jnp.arange(128)
        message = jnp.where(lane == 0, square, jnp.where(lane == 1, loss_part, 0.0))
        (totals,) = exchange([jnp.broadcast_to(message, (n, 8, 128))], 4, "totals")
        totals = jnp.sum(totals, 0)
    loss = totals[0, 1]
    grad_norm = jnp.sqrt(totals[0, 0])
    factor = clip_limit / jnp.maximum(grad_norm, clip_limit)

    def update(master, moment, average, piece, rate):
        clipped = piece * factor
        velocity = momentum_decay * moment + clipped
        updated = master - rate * (clipped + momentum_decay * velocity)
        return updated, velocity, decay * average + (1.0 - decay) * updated

    last = update(scaling, moment_scaling, average_scaling, norm_piece, learn_rate)
    if fits:
        row = sums.shape[0] - narrowing.shape[0]
        layout = (
            (1, 0, 1, 24, True),
            (2, 24, 3, 24, False),
            (3, 96, 1, 48, True),
            (4, 144, 1, 24, False),
            (5, 168, blocks, 24, False),
            (6, row, 1, narrowing.shape[0], False),
        )
        groups = [group[:7] for group in (masters, moments, averages)]
        done = update_all(factor.reshape(1, 1), table_piece, sums, *groups, decay, layout)
        fresh, speeds, smooths = done[:7], done[7:14], done[14:]
    else:
        rates = (table_rate,) + (learn_rate,) * 6
        done = [
            update(*group) for group in zip(masters[:7], moments[:7], averages[:7], reduced[:7], rates)
        ]
        fresh, speeds, smooths = zip(*done)
    return (loss, grad_norm, *fresh, last[0], *speeds, last[1], *smooths, last[2])


ROWS = P("dp", None)
COLS = P(None, "dp")
WEIGHTS = (ROWS, COLS, ROWS, COLS, ROWS, ROWS, ROWS, COLS)


def solution(mesh):
    return jax.shard_map(
        partial(per_device, mesh.shape["dp"]),
        mesh=mesh,
        in_specs=(P("dp"), COLS, P("dp"), P("dp"), COLS, COLS, P("dp", None, None)) + 3 * WEIGHTS,
        out_specs=(P(), P()) + 3 * WEIGHTS,
        check_vma=False,
    )
```

```python
from functools import partial

import jax
import jax.numpy as jnp
from jax import lax
from jax.experimental import pallas as pl
from jax.experimental.pallas import tpu as pltpu
from jax.sharding import PartitionSpec as P

HD = 64
DOCS = 8
STEP = 10
MESH = pl.DeviceIdType.MESH

mask_token = 103
ln_epsilon = 1e-06
momentum_decay = 0.9
learn_rate = 5000.0
table_rate = 1000000.0
clip_limit = 0.01
average_cap = 0.999


def sinusoids(positions, count):
    ranks = jnp.arange(count).astype(jnp.float32)
    omegas = jnp.power(10000.0, -ranks / count)
    angle_x = positions[0].astype(jnp.float32)[:, None] * omegas[None, :]
    angle_y = positions[1].astype(jnp.float32)[:, None] * omegas[None, :]
    return (jnp.sin(angle_x), jnp.cos(angle_x), jnp.sin(angle_y), jnp.cos(angle_y))


def layer_norm(rows, gain, bias):
    centred = rows - jnp.mean(rows, -1, keepdims=True)
    rescale = lax.rsqrt(jnp.mean(centred * centred, -1, keepdims=True) + ln_epsilon)
    whitened = centred * rescale
    return (whitened * gain + bias, whitened, rescale)


def norm_back(upstream, whitened, rescale, gain):
    scaled = upstream * gain
    inner = (
        scaled
        - jnp.mean(scaled, -1, keepdims=True)
        - whitened * jnp.mean(scaled * whitened, -1, keepdims=True)
    )
    return (
        rescale * inner,
        jnp.sum(upstream * whitened, 0, keepdims=True),
        jnp.sum(upstream, 0, keepdims=True),
    )


def swap_middle(rows, axis=0):
    count = rows.shape[axis] // 4
    cuts = [lax.slice_in_dim(rows, k * count, (k + 1) * count, axis=axis) for k in (0, 2, 1, 3)]
    return jnp.concatenate(cuts, axis)


def dot_nn(left, right):
    return lax.dot_general(
        left, right, (((1,), (0,)), ((), ())), preferred_element_type=jnp.float32
    )


def dot_tn(left, right):
    return lax.dot_general(
        left, right, (((0,), (0,)), ((), ())), preferred_element_type=jnp.float32
    )


def dot_nt(left, right):
    return lax.dot_general(
        left, right, (((1,), (1,)), ((), ())), preferred_element_type=jnp.float32
    )


def plan_kernel(
    n, rows_own, capacity, fold, tok_col, tok_row, mask_row, own, info, lists, place
):
    size = tok_col.shape[0]
    ids_col = tok_col[...]
    ids_row = tok_row[...]
    owner_col = lax.div(ids_col, rows_own)
    owner_row = lax.div(ids_row, rows_own)
    at_col = lax.broadcasted_iota(jnp.int32, (size, size), 0)
    at_row = lax.broadcasted_iota(jnp.int32, (size, size), 1)
    same = ids_col == ids_row
    first_col = jnp.min(jnp.where(same, at_row, size), 1, keepdims=True)
    first_row = jnp.min(jnp.where(same, at_col, size), 0, keepdims=True)
    leads_row = first_row == lax.broadcasted_iota(jnp.int32, (1, size), 1)
    leads_col = first_col == lax.broadcasted_iota(jnp.int32, (size, 1), 0)
    ahead = (owner_col == owner_row) & leads_row & (at_row < first_col)
    slot = jnp.sum(jnp.where(ahead, 1.0, 0.0), 1, keepdims=True).astype(jnp.int32)
    fits = slot < capacity - 1
    place[...] = jnp.where(fits, owner_col * capacity + slot, -1)
    over = jnp.max(jnp.where(fits, 0.0, 1.0), keepdims=True)
    local = ids_col - owner_col * rows_own + 1
    high = lax.div(local, 128)
    to_owner = lax.broadcasted_iota(jnp.int32, (size, n), 1) == owner_col
    to_owner = to_owner & leads_col & fits
    shift = capacity * lax.rem(own[1], fold)
    in_slot = lax.broadcasted_iota(jnp.int32, (size, 128), 1) == slot + shift
    in_slot = jnp.where(in_slot, 1.0, 0.0).astype(jnp.bfloat16)
    high_part = jnp.where(to_owner, high.astype(jnp.float32), 0.0).astype(jnp.bfloat16)
    low_part = jnp.where(to_owner, (local - high * 128).astype(jnp.float32), 0.0)
    table = dot_tn(high_part, in_slot) * 128.0 + dot_tn(low_part.astype(jnp.bfloat16), in_slot)
    lane = lax.broadcasted_iota(jnp.int32, (n, 128), 1)
    line = lax.broadcasted_iota(jnp.int32, (n, 128), 0)
    fixed = (line == mask_token // rows_own) & (lane == capacity - 1 + shift)
    table = jnp.where(fixed, float(mask_token % rows_own + 1), table)
    count = jnp.sum(mask_row[...].astype(jnp.float32), keepdims=True)
    lane = lax.broadcasted_iota(jnp.int32, (8, 128), 1)
    line = lax.broadcasted_iota(jnp.int32, (8, 128), 0)
    extra = jnp.where(lane == 0, count, jnp.where(lane == 1, own[0].astype(jnp.float32), over))
    extra = jnp.where(line == 7, extra, info[...])
    line = lax.broadcasted_iota(jnp.int32, lists.shape, 1)
    lists[...] = jnp.where(line == 6, table[:, None, :], extra[None])


def make_plan(tokens, masking, documents, info, n, rows_own, capacity, fold):
    size = tokens.shape[0]
    vmem = pl.BlockSpec(memory_space=pltpu.VMEM)
    return pl.pallas_call(
        partial(plan_kernel, n, rows_own, capacity, fold),
        name="plan",
        out_shape=(
            jax.ShapeDtypeStruct((n, 8, 128), jnp.float32),
            jax.ShapeDtypeStruct((size, 1), jnp.int32),
        ),
        in_specs=[vmem, vmem, vmem, pl.BlockSpec(memory_space=pltpu.SMEM), vmem],
        out_specs=(vmem, vmem),
        compiler_params=pltpu.CompilerParams(vmem_limit_bytes=32 * 2**20),
    )(
        tokens[:, None],
        tokens[None, :],
        masking[None, :],
        jnp.stack([documents[0], lax.axis_index("dp")]),
        info,
    )


def place_of(me):
    core = lax.rem(me, 2)
    chip = lax.div(me, 2)
    spot = lax.rem(chip, 4)
    layer = lax.div(chip, 4)
    along_a = 1 + core
    along_b = 2 - core
    step_a = along_a * (1 - 2 * lax.rem(lax.div(spot, along_a), 2))
    step_b = along_b * (1 - 2 * lax.rem(lax.div(spot, along_b), 2))
    return core, spot, layer, step_a, step_b


def remote_copy(src, dst, send, recv, device):
    return pltpu.make_async_remote_copy(
        src_ref=src, dst_ref=dst, send_sem=send, recv_sem=recv, device_id=(device,), device_id_type=MESH
    )


def greet_everyone(me, n):
    barrier = pltpu.get_barrier_semaphore()

    def greet(step, carry):
        pl.semaphore_signal(
            barrier, inc=1, device_id=(lax.rem(me + step, n),), device_id_type=MESH
        )
        return carry

    lax.fori_loop(1, n, greet, 0)
    pl.semaphore_wait(barrier, n - 1)


def back_kernel(n, units, pieces, chunks, fold, *refs):
    count = len(units)
    sent, small, asked, loss_part, grads = *refs[:4], refs[4 : 4 + count]
    out, table, norm_piece, totals = refs[4 + count : 8 + count]
    own, par, from_b, from_a, from_z, mine, gone, back = refs[8 + count : 16 + count]
    came, small_came, picks, message, told = refs[16 + count : 21 + count]
    row_send, row_recv, own_sem, load_sem, pair_send, pair_recv = refs[21 + count : 27 + count]
    b_send, b_recv, a_send, a_recv, z_send, z_recv, f_send, f_recv, t_send, t_recv = refs[27 + count :]
    layers = n // 8
    me = lax.axis_index("dp")
    core, spot, layer, step_a, step_b = place_of(me)
    half = own.shape[3]
    here = pl.ds(pl.multiple_of(core * half, 128), half)
    there = pl.ds(pl.multiple_of((1 - core) * half, 128), half)
    partner = me + 1 - 2 * core
    to_a, to_b = me + 2 * step_a, me + 2 * step_b
    offsets = [48 * sum(units[:k]) for k in range(count)]
    spot_a, spot_b, spot_ab = spot + step_a, spot + step_b, spot + step_a + step_b
    size = own.shape[2] // chunks

    greet_everyone(me, n)
    for index in (spot_ab, spot_a, spot_b, spot):
        for ref, at, unit in zip(grads, offsets, units):
            remote_copy(
                ref.at[:, index, :, there],
                par.at[:, index, pl.ds(at, 48 * unit)],
                pair_send.at[index],
                pair_recv.at[index],
                partner,
            ).start()
    for index in (spot_ab, spot_b, spot_a, spot):
        for ref, at, unit in zip(grads, offsets, units):
            pltpu.make_async_copy(
                ref.at[:, index, :, here], own.at[:, index, pl.ds(at, 48 * unit)], load_sem.at[index]
            ).start()

    def row_copies(step):
        peer = lax.rem(me + step, n)
        return [
            remote_copy(src.at[peer], dst.at[me], row_send.at[k, step], row_recv.at[k, step], peer)
            for k, (src, dst) in enumerate(((sent, came), (small, small_came)))
        ]

    def start_rows(step, carry):
        for copy in row_copies(step):
            copy.start()
        return carry

    def finish_rows(step, carry):
        for copy in row_copies(step):
            copy.wait()
        return carry

    lax.fori_loop(1, n, start_rows, 0)
    own_copies = [
        pltpu.make_async_copy(src.at[me], dst.at[me], own_sem.at[k])
        for k, (src, dst) in enumerate(((sent, came), (small, small_came)))
    ]
    for copy in own_copies:
        copy.start()

    def arrived(index):
        pltpu.make_async_copy(own.at[:, index], own.at[:, index], load_sem.at[index]).wait()
        pltpu.make_async_copy(par.at[:, index], par.at[:, index], pair_recv.at[index]).wait()

    def total(*parts):
        return sum(part[...].astype(jnp.float32) for part in parts)

    def b_copy(kind, level, part):
        cut = pl.ds(part * size, size)
        return remote_copy(
            own.at[level, spot_ab if kind == 0 else spot_b, cut], from_b.at[kind, level, cut],
            b_send.at[kind, level, part], b_recv.at[kind, level, part], to_b,
        )

    def a_copy(level, part):
        cut = pl.ds(part * size, size)
        return remote_copy(
            own.at[level, spot_a, cut], from_a.at[level, cut],
            a_send.at[level, part], a_recv.at[level, part], to_a,
        )

    def z_copy(level, part):
        cut = pl.ds(part * size, size)
        return remote_copy(
            own.at[level, spot, cut], from_z.at[layer, cut],
            z_send.at[level, part], z_recv.at[layer, part], me + 8 * (level - layer),
        )

    def cross_b(kind, index, part):
        cut = pl.ds(part * size, size)

        def step(level, carry):
            own[level, index, cut] = total(
                own.at[level, index, cut], par.at[level, index, cut]
            ).astype(own.dtype)
            b_copy(kind, level, part).start()
            return carry

        lax.fori_loop(0, layers, step, 0)

    def cross_a(part):
        cut = pl.ds(part * size, size)

        def step(level, carry):
            b_copy(0, level, part).wait_recv()
            own[level, spot_a, cut] = total(
                own.at[level, spot_a, cut], par.at[level, spot_a, cut], from_b.at[0, level, cut]
            ).astype(own.dtype)
            a_copy(level, part).start()
            return carry

        lax.fori_loop(0, layers, step, 0)

    def column(level, part):
        cut = pl.ds(part * size, size)
        b_copy(1, level, part).wait_recv()
        a_copy(level, part).wait_recv()
        return total(
            own.at[level, spot, cut], par.at[level, spot, cut],
            from_b.at[1, level, cut], from_a.at[level, cut],
        )

    def cross_z(part):
        cut = pl.ds(part * size, size)

        def step(gap, carry):
            level = lax.rem(layer + gap, layers)
            own[level, spot, cut] = column(level, part).astype(own.dtype)
            z_copy(level, part).start()
            return carry

        lax.fori_loop(1, layers, step, 0)
        mine[cut] = column(layer, part)

    arrived(spot_ab)
    cross_b(0, spot_ab, 0)
    arrived(spot_b)
    for part in range(chunks):
        if part > 0:
            cross_b(0, spot_ab, part)
        cross_b(1, spot_b, part)
    wanted = lax.broadcasted_iota(jnp.int32, (table.shape[0], 128), 0) + 1
    for turn in range(n // fold):
        ids = asked[turn * fold]
        for k in range(1, fold):
            ids = ids + asked[turn * fold + k]
        found = ids[6:7].astype(jnp.int32) == wanted
        picks[:, turn * 128 : (turn + 1) * 128] = jnp.where(found, 1.0, 0.0).astype(picks.dtype)
    arrived(spot_a)
    arrived(spot)
    for part in range(chunks):
        cross_a(part)
        if part > 0:
            cross_z(part - 1)
    cross_z(chunks - 1)
    lax.fori_loop(1, n, finish_rows, 0)
    for copy in own_copies:
        copy.wait()
    table[...] = dot_nn(picks[...], came[...].reshape(picks.shape[1], -1))
    squares = jnp.zeros((1, 1), jnp.float32)
    for part in range(4):
        rows = table.shape[0] // 4
        piece = table[part * rows : (part + 1) * rows]
        squares = squares + jnp.sum(piece * piece, keepdims=True)
    norm = small_came[0]
    for k in range(1, n):
        norm = norm + small_came[k]
    norm_piece[...] = norm
    squares = squares + jnp.sum(norm * norm, keepdims=True)
    for part in range(chunks):
        cut = pl.ds(part * size, size)

        def step(gap, carry):
            level = lax.rem(layer + gap, layers)
            remote_copy(
                own.at[level, spot, cut], from_z.at[level, cut],
                z_send.at[level, part], z_recv.at[level, part], me,
            ).wait_recv()
            mine[cut] += total(from_z.at[level, cut])
            return carry

        lax.fori_loop(1, layers, step, 0)

    at = 0
    for piece in pieces:
        offset, rows = 2 * at, 24 * piece
        gone[pl.ds(at, rows)] = mine[pl.ds(pl.multiple_of(offset + (1 - core) * rows, 8), rows)]
        out[pl.ds(at, rows), here] = mine[pl.ds(pl.multiple_of(offset + core * rows, 8), rows)]
        at += rows
    last = remote_copy(gone, back, f_send, f_recv, partner)
    last.start()
    squares = squares + jnp.sum(out[:, here] * out[:, here], keepdims=True)
    last.wait()
    out[:, there] = back[...]
    squares = squares + jnp.sum(back[...] * back[...], keepdims=True)
    lane = lax.broadcasted_iota(jnp.int32, message.shape, 1)
    message[...] = jnp.where(lane == 0, squares, jnp.where(lane == 1, loss_part[...], 0.0))

    def tell(step):
        peer = lax.rem(me + step, n)
        return remote_copy(message, told.at[me], t_send.at[step], t_recv.at[step], peer)

    def start_told(step, carry):
        tell(step).start()
        return carry

    def wait_told(step, carry):
        tell(step).wait()
        return carry

    lax.fori_loop(1, n, start_told, 0)
    told[me] = message[...]
    for index in range(4):
        pltpu.make_async_copy(par.at[:, index], par.at[:, index], pair_send.at[index]).wait()

    def settle(level, carry):
        for part in range(chunks):
            b_copy(0, level, part).wait_send()
            b_copy(1, level, part).wait_send()
            a_copy(level, part).wait_send()

            @pl.when(level != layer)
            def _():
                z_copy(level, part).wait_send()

        return carry

    lax.fori_loop(0, layers, settle, 0)
    lax.fori_loop(1, n, wait_told, 0)
    total_line = told[0]
    for k in range(1, n):
        total_line = total_line + told[k]
    totals[...] = total_line


def to_owners(sent, small, asked, loss_part, grads, pieces, rows_own, fold, n, ident):
    model = grads[0].shape[2]
    layers = n // 8
    units = [grad.shape[1] // 48 for grad in grads]
    chunks = max(k for k in range(1, 6) if sum(units) % k == 0)
    rows = 48 * sum(units)
    half = model // 2
    low = jnp.bfloat16
    dma = pltpu.SemaphoreType.DMA
    anywhere = pl.BlockSpec(memory_space=pl.ANY)
    vmem = pl.BlockSpec(memory_space=pltpu.VMEM)
    return pl.pallas_call(
        partial(back_kernel, n, units, pieces, chunks, fold),
        name="back",
        out_shape=(
            jax.ShapeDtypeStruct((rows // 2, model), jnp.float32),
            jax.ShapeDtypeStruct((rows_own, model), jnp.float32),
            jax.ShapeDtypeStruct((8, 128), jnp.float32),
            jax.ShapeDtypeStruct((8, 128), jnp.float32),
        ),
        in_specs=[anywhere, anywhere, vmem, vmem] + [anywhere] * len(grads),
        out_specs=(vmem,) * 4,
        scratch_shapes=[
            pltpu.VMEM((layers, 4, rows, half), low),
            pltpu.VMEM((layers, 4, rows, half), low),
            pltpu.VMEM((2, layers, rows, half), low),
            pltpu.VMEM((layers, rows, half), low),
            pltpu.VMEM((layers, rows, half), low),
            pltpu.VMEM((rows, half), jnp.float32),
            pltpu.VMEM((rows // 2, half), jnp.float32),
            pltpu.VMEM((rows // 2, half), jnp.float32),
            pltpu.VMEM(sent.shape, low),
            pltpu.VMEM(small.shape, jnp.float32),
            pltpu.VMEM((rows_own, sent.shape[0] * sent.shape[1]), low),
            pltpu.VMEM((8, 128), jnp.float32),
            pltpu.VMEM((n, 8, 128), jnp.float32),
            dma((2, n)),
            dma((2, n)),
            dma((2,)),
            dma((4,)),
            dma((4,)),
            dma((4,)),
            dma((2, layers, chunks)),
            dma((2, layers, chunks)),
            dma((layers, chunks)),
            dma((layers, chunks)),
            dma((layers, chunks)),
            dma((layers, chunks)),
            dma,
            dma,
            dma((n,)),
            dma((n,)),
        ],
        compiler_params=pltpu.CompilerParams(
            collective_id=ident, has_side_effects=True, vmem_limit_bytes=60 * 2**20
        ),
        cost_estimate=pl.CostEstimate(
            flops=0, bytes_accessed=100 * 2**20, transcendentals=0
        ),
    )(sent, small, asked, loss_part, *[grad.reshape(layers, 4, -1, model) for grad in grads])


def flat(rows):
    return rows.reshape(-1, rows.shape[-1])


def upper_kernel(
    page_rows, full, attended, normed, target, mask_col, page, row, asked, doc, gains,
    grads, d_attended, d_lower, pos_rows, norms, loss_part,
    held, bank, slopes, hidden, scores, load_sem, store_sem,
):
    low = jnp.bfloat16
    chips, used, model = held.shape
    size = attended.shape[0]
    blocks = hidden.shape[0]
    first_row = 288
    span = model // (used - 48 - 48 * blocks)
    down_at = 48 + 48 * blocks
    loads = [
        pltpu.make_async_copy(full.at[:, pl.ds(first_row + at, many)], held.at[:, pl.ds(at, many)], load_sem.at[k])
        for k, (at, many) in enumerate(((0, 48), (48, 48 * blocks), (down_at, used - down_at)))
    ]
    loads.append(
        pltpu.make_async_copy(full.at[:, pl.ds(first_row + used, bank.shape[1])], bank, load_sem.at[3])
    )
    for copy in loads:
        copy.start()

    def up_map(k):
        return flat(held[:, 48 + 48 * k : 96 + 48 * k])

    def down_map(k):
        return flat(held[span * k : span * (k + 1), down_at:])

    loads[0].wait()
    second, white_mid, scale_mid = layer_norm(
        normed[...] + dot_nn(attended[...], flat(held[:, 0:48])), gains[2:3], gains[3:4]
    )
    middle = second.astype(low)
    loads[1].wait()
    loads[2].wait()
    for k in range(blocks):
        pre = dot_nn(middle, up_map(k))
        normal = 0.5 + 0.5 * lax.erf(pre * (0.5**0.5))
        active = (pre * normal).astype(low)
        slopes[k] = normal + pre * (jnp.exp(-0.5 * pre * pre) * 0.3989422804014327)
        hidden[k] = active
        part = dot_nn(active, down_map(k))
        lowered = part if k == 0 else lowered + part
    states, white_last, scale_last = layer_norm(second + lowered, gains[4:5], gains[5:6])
    states = states.astype(low)

    inv_root = model ** (-0.5)
    positive = jnp.sum(states.astype(jnp.float32) * target[...], -1, keepdims=True) * inv_root
    many = page.shape[0]
    seat = lax.broadcasted_iota(jnp.int32, (many, 128), 0)
    lane = lax.broadcasted_iota(jnp.int32, (many, 128), 1)
    spread = jnp.where(lax.rem(lane, many) == seat, 1.0, 0.0).astype(low)
    wanted = page_rows * dot_tn(page[...].astype(jnp.float32).astype(low), spread) + dot_tn(
        row[...].astype(jnp.float32).astype(low), spread
    )
    wanted = jnp.concatenate([wanted.astype(jnp.int32)] * 4, 1)
    column = lax.broadcasted_iota(jnp.int32, wanted.shape, 1)
    width = wanted.shape[1]
    per = width // bank.shape[1]
    parts = chips // per
    loads[3].wait()
    highest = positive
    for c in range(parts):
        raw = dot_nt(states, flat(bank[per * c : per * (c + 1)])) * inv_root
        raw = jnp.where(wanted == column + c * width, raw, -jnp.inf)
        scores[:, c * width : (c + 1) * width] = raw
        highest = jnp.maximum(highest, jnp.max(raw, -1, keepdims=True))
    lead = jnp.exp(positive - highest)
    total = lead
    for c in range(parts):
        powers = jnp.exp(scores[:, c * width : (c + 1) * width] - highest)
        scores[:, c * width : (c + 1) * width] = powers
        total = total + jnp.sum(powers, -1, keepdims=True)
    mask = mask_col[...]
    facts = asked[:, 7, :]
    counted = jnp.where(facts[:, 1:2] == doc[0].astype(jnp.float32), facts[:, 0:1], 0.0)
    share = 1.0 / (DOCS * jnp.maximum(jnp.sum(counted, keepdims=True), 1.0))
    loss_part[...] = share * jnp.sum(
        mask * (highest + jnp.log(total) - positive), keepdims=True
    )
    factor = share * mask * inv_root
    positive_grad = factor * (lead / total - 1.0)
    factor = factor / total
    pos_rows[...] = (positive_grad * states.astype(jnp.float32)).astype(pos_rows.dtype)
    d_states = positive_grad * target[...]
    for c in range(parts):
        weights = (scores[:, c * width : (c + 1) * width] * factor).astype(low)
        d_states = d_states + dot_nn(weights, flat(bank[per * c : per * (c + 1)]))

    d_mid, gain_last, bias_last = norm_back(d_states, white_last, scale_last, gains[4:5])
    d_down = d_mid.astype(low)
    d_second = d_mid
    stores = []
    for k in range(blocks):
        d_pre = (dot_nt(d_down, down_map(k)) * slopes[k]).astype(low)
        d_second = d_second + dot_nt(d_pre, up_map(k))
        grad = dot_tn(hidden[k], d_down).astype(low)
        held[span * k : span * (k + 1), down_at:] = grad.reshape(span, -1, model)
        grad = dot_tn(middle, d_pre).astype(low)
        held[:, 48 + 48 * k : 96 + 48 * k] = grad.reshape(chips, 48, model)
        for j, cut in enumerate(
            (
                (pl.ds(span * k, span), pl.ds(down_at, used - down_at)),
                (pl.ds(0, chips), pl.ds(48 + 48 * k, 48)),
            )
        ):
            stores.append(pltpu.make_async_copy(held.at[cut], grads.at[cut], store_sem.at[2 * k + j]))
            stores[-1].start()
    d_low, gain_mid, bias_mid = norm_back(d_second, white_mid, scale_mid, gains[2:3])
    d_lower[...] = d_low
    d_attn = d_low.astype(low)
    d_attended[...] = dot_nt(d_attn, flat(held[:, 0:48])).astype(low)
    held[:, 0:48] = dot_tn(attended[...], d_attn).astype(low).reshape(chips, 48, model)
    cut = (pl.ds(0, chips), pl.ds(0, 48))
    stores.append(pltpu.make_async_copy(held.at[cut], grads.at[cut], store_sem.at[2 * blocks]))
    stores[-1].start()
    for at, line in enumerate((gain_mid, bias_mid, gain_last, bias_last)):
        norms[at : at + 1] = line
    for copy in stores:
        copy.wait()


def upper(full, attended, normed, target, mask_col, page, row, asked, doc, gains, blocks, page_rows):
    size, model = normed.shape
    chips = full.shape[0]
    used = full.shape[1] - 288 - 2 * page_rows
    low, wide = jnp.bfloat16, jnp.float32
    vmem = pl.BlockSpec(memory_space=pltpu.VMEM)
    anywhere = pl.BlockSpec(memory_space=pl.ANY)
    shape = jax.ShapeDtypeStruct
    return pl.pallas_call(
        partial(upper_kernel, page_rows),
        name="upper",
        out_shape=(
            shape((chips, used, model), low),
            shape((size, model), low),
            shape((size, model), wide),
            shape((size, model), low),
            shape((4, model), wide),
            shape((1, 1), wide),
        ),
        in_specs=[anywhere]
        + [vmem] * 7
        + [pl.BlockSpec(memory_space=pltpu.SMEM), vmem],
        out_specs=(anywhere,) + (vmem,) * 5,
        scratch_shapes=[
            pltpu.VMEM((chips, used, model), low),
            pltpu.VMEM((chips, 2 * page_rows, model), low),
            pltpu.VMEM((blocks, size, model), wide),
            pltpu.VMEM((blocks, size, model), low),
            pltpu.VMEM((size, chips * 2 * page_rows), wide),
            pltpu.SemaphoreType.DMA((4,)),
            pltpu.SemaphoreType.DMA((2 * blocks + 1,)),
        ],
        compiler_params=pltpu.CompilerParams(vmem_limit_bytes=63 * 2**20),
        cost_estimate=pl.CostEstimate(
            flops=20 * 10**9, bytes_accessed=32 * 2**20, transcendentals=4 * size * model * 2
        ),
    )(full, attended, normed, target, mask_col, page, row, asked, doc, gains)


def lower_kernel(
    fixed, full, dq, dk, dv, d_lower, white, scale, gains, normed, sines, cosines, mask_col, pos_rows, place, upper_norms,
    grads, sent, norms, held, sem,
):
    low = jnp.bfloat16
    chips, _, model = held.shape
    load = pltpu.make_async_copy(full.at[:, pl.ds(48, 144)], held.at[:, pl.ds(48, 144)], sem.at[0])
    load.start()
    mask = mask_col[...]
    d_first = d_lower[...]
    load.wait()
    stores = []
    for third, ref in enumerate((dq, dk, dv)):
        at = 48 + 48 * third
        upstream = ref[...]
        d_first = d_first + dot_nt(upstream, flat(held[:, at : at + 48]))
        held[:, at : at + 48] = dot_tn(normed[...], upstream).astype(low).reshape(chips, 48, model)
        stores.append(
            pltpu.make_async_copy(held.at[:, pl.ds(at, 48)], grads.at[:, pl.ds(at, 48)], sem.at[1 + third])
        )
        stores[-1].start()
    d_rows, gain, bias = norm_back(d_first, white[...], scale[...], gains[0:1])
    boxes = jnp.concatenate([sines[...], cosines[...]], 1).astype(low)
    held[:, 0:48] = dot_tn(d_rows.astype(low), boxes).astype(low).reshape(chips, 48, model)
    stores.append(pltpu.make_async_copy(held.at[:, pl.ds(0, 48)], grads.at[:, pl.ds(0, 48)], sem.at[4]))
    stores[-1].start()
    count = norms.shape[0]
    lines = jnp.concatenate([gain, bias, upper_norms[...]], 0)
    cols = model // count
    norms[...] = jnp.zeros_like(norms)
    for owner in range(count):
        norms[owner, 0:6, 0:cols] = lines[:, owner * cols : (owner + 1) * cols]
    token_grads = jnp.where(mask == 1.0, pos_rows[...].astype(jnp.float32), d_rows).astype(low)
    mask_grad = jnp.sum(mask * d_rows, 0, keepdims=True)
    slots = sent.shape[0]
    seats = lax.broadcasted_iota(jnp.int32, (place.shape[0], slots), 1) == place[...]
    found = dot_tn(jnp.where(seats, 1.0, 0.0).astype(low), token_grads)
    line = lax.broadcasted_iota(jnp.int32, (slots, 1), 0)
    sent[...] = jnp.where(line == fixed, mask_grad, found).astype(low)
    for copy in stores:
        copy.wait()


def lower(
    full, d_joined, d_lower, white, scale, gains, normed, sines, cosines, mask_col, pos_rows, place,
    upper_norms, n, slots, fixed,
):
    size, model = d_lower.shape
    chips = full.shape[0]
    low, wide = jnp.bfloat16, jnp.float32
    vmem = pl.BlockSpec(memory_space=pltpu.VMEM)
    anywhere = pl.BlockSpec(memory_space=pl.ANY)
    shape = jax.ShapeDtypeStruct
    return pl.pallas_call(
        partial(lower_kernel, fixed),
        name="lower",
        out_shape=(
            shape((chips, 192, model), low),
            shape((slots, model), low),
            shape((n, 8, 128), wide),
        ),
        in_specs=[anywhere] + [vmem] * 14,
        out_specs=(anywhere,) + (vmem,) * 2,
        scratch_shapes=[
            pltpu.VMEM((chips, 192, model), low),
            pltpu.SemaphoreType.DMA((5,)),
        ],
        compiler_params=pltpu.CompilerParams(vmem_limit_bytes=60 * 2**20),
        cost_estimate=pl.CostEstimate(
            flops=6 * 10**9, bytes_accessed=24 * 2**20, transcendentals=0
        ),
    )(full, *d_joined, d_lower, white, scale, gains, normed, sines, cosines, mask_col, pos_rows, place, upper_norms)


def update_kernel(decay, layout, factor, table, sums, *refs):
    masters, moments, averages = refs[0:7], refs[7:14], refs[14:21]
    fresh, speeds, smooths = refs[21:28], refs[28:35], refs[35:42]
    scale = factor[0, 0]

    def update(k, piece, rate, cut):
        clipped = piece * scale
        velocity = momentum_decay * moments[k][cut] + clipped
        updated = masters[k][cut] - rate * (clipped + momentum_decay * velocity)
        fresh[k][cut] = updated
        speeds[k][cut] = velocity
        smooths[k][cut] = decay * averages[k][cut] + (1.0 - decay) * updated

    update(0, table[...], table_rate, (slice(None), slice(None)))

    @pl.when(pl.program_id(0) == 0)
    def _():
        model = sums.shape[1]
        for k, at, blocks, rows, turned in layout:
            for block in range(blocks):
                piece = sums[at + block * rows : at + (block + 1) * rows]
                if turned:
                    update(k, swap_middle(piece, 1), learn_rate, (slice(None), slice(None)))
                else:
                    cut = (slice(None), slice(block * model, (block + 1) * model))
                    update(k, piece, learn_rate, cut)


def update_all(factor, table, sums, masters, moments, averages, decay, layout):
    steps = 6
    rows, model = table.shape
    banded = pl.BlockSpec((rows // steps, model), lambda i: (i, 0))
    whole = lambda array: pl.BlockSpec(array.shape, lambda i: (0, 0))
    group = lambda arrays: [banded] + [whole(array) for array in arrays[1:]]
    shapes = tuple(jax.ShapeDtypeStruct(array.shape, jnp.float32) for array in masters)
    return pl.pallas_call(
        partial(update_kernel, decay, layout),
        name="update",
        grid=(steps,),
        out_shape=shapes * 3,
        in_specs=[pl.BlockSpec(memory_space=pltpu.SMEM), banded, whole(sums)]
        + group(masters)
        + group(moments)
        + group(averages),
        out_specs=tuple(group(masters) * 3),
        compiler_params=pltpu.CompilerParams(vmem_limit_bytes=56 * 2**20),
        cost_estimate=pl.CostEstimate(flops=0, bytes_accessed=28 * 2**20, transcendentals=0),
    )(factor, table, sums, *masters, *moments, *averages)


def split_rows(packed, grads, n):
    out, at = [], 0
    for grad in grads:
        count = grad.shape[0] // n
        out.append(packed[at : at + count])
        at += count
    return out


def scatter(grads, n):
    model = grads[0].shape[1]
    joined = jnp.concatenate([grad.reshape(n, -1, model) for grad in grads], 1)
    joined = joined.reshape(-1, model)
    mine = lax.psum_scatter(joined, "dp", scatter_dimension=0, tiled=True)
    return split_rows(mine.astype(jnp.float32), grads, n)


def masked(rows, half):
    lane = lax.broadcasted_iota(jnp.int32, rows.shape, 1)
    keep = (lane < HD) if half == 0 else (lane >= HD)
    return jnp.where(keep, rows, jnp.zeros_like(rows))


def turn(terms, sines, cosines):
    half = sines.shape[1]
    sine, cosine = terms[:, :half], terms[:, half:]
    return jnp.concatenate(
        [sine * sines + cosine * cosines, cosine * sines - sine * cosines], 1
    ).astype(jnp.bfloat16)


def turn_back(upstream, sines, cosines):
    half = sines.shape[1]
    first, second = upstream[:, :half], upstream[:, half:]
    return jnp.concatenate(
        [first * sines - second * cosines, first * cosines + second * sines], 1
    ).astype(jnp.bfloat16)


def pick_halves(low_half, high_half):
    lane = lax.broadcasted_iota(jnp.int32, low_half.shape, 1)
    return jnp.where(lane < HD, low_half, high_half)


def attend_pair(queries, keys, values, rel_text, rel_box, sines, cosines, spread, probs):
    results = []
    for half in range(2):
        mine = masked(queries, half)
        terms = dot_nn(masked(keys, half), rel_box[...])
        box_rot = turn(terms, sines[...], cosines[...])
        terms = dot_nn(mine, rel_text[...])
        text_rot = turn(terms, sines[...], cosines[...])
        scores = dot_nt(mine, keys) + dot_nt(text_rot, spread) + dot_nt(spread, box_rot)
        scores = scores * HD ** (-0.5)
        powers = jnp.exp(scores - jnp.max(scores, -1, keepdims=True))
        shares = powers * (1.0 / jnp.sum(powers, -1, keepdims=True))
        probs[half] = shares
        results.append(dot_nn(shares.astype(jnp.bfloat16), values))
    return pick_halves(*results).astype(jnp.bfloat16)


def attend_kernel(q, k, v, rel_text, rel_box, sines, cosines, bases, attended, probs):
    attended[...] = attend_pair(
        q[...], k[...], v[...], rel_text, rel_box, sines, cosines, bases[...], probs
    )


def attend(joined, rel_map, sines, cosines, bases):
    size, model = bases.shape
    pairs = model // (2 * HD)
    lanes = 2 * HD
    whole = lambda rows: pl.BlockSpec(rows.shape, lambda i: (0, 0))
    column = pl.BlockSpec((size, lanes), lambda i: (0, i))
    band = lambda part: pl.BlockSpec((lanes, model), lambda i: (i + part * pairs, 0))
    return pl.pallas_call(
        attend_kernel,
        name="attend",
        grid=(pairs,),
        out_shape=(
            jax.ShapeDtypeStruct((size, model), jnp.bfloat16),
            jax.ShapeDtypeStruct((2 * pairs, size, size), jnp.float32),
        ),
        in_specs=[column, column, column, band(0), band(1)]
        + [whole(sines), whole(cosines), whole(bases)],
        out_specs=(
            column,
            pl.BlockSpec((2, size, size), lambda i: (i, 0, 0)),
        ),
        compiler_params=pltpu.CompilerParams(vmem_limit_bytes=56 * 2**20),
        cost_estimate=pl.CostEstimate(
            flops=2 * 12 * size * (size * 1700 + 2 * 64 * 768),
            bytes_accessed=20 * 2**20,
            transcendentals=12 * size * size,
        ),
    )(*joined, rel_map, rel_map, sines, cosines, bases)


def attend_back_kernel(
    d_out, q, k, v, rel_text, rel_box, probs, sines, cosines, bases, dq, dk, dv, g_rel
):
    queries, keys, values, upstream = q[...], k[...], v[...], d_out[...]
    spread = bases[...]
    scale = HD ** (-0.5)
    low = jnp.bfloat16
    got = [[], [], []]
    for half in range(2):
        shares = probs[half]
        d_probs = dot_nt(masked(upstream, half), values)
        got[2].append(dot_tn(shares.astype(low), upstream))
        inner = jnp.sum(d_probs * shares, -1, keepdims=True)
        d_scores = (shares * (d_probs - inner)).astype(low)
        d_text = turn_back(dot_nn(d_scores, spread) * scale, sines[...], cosines[...])
        got[0].append(dot_nn(d_scores, keys) * scale + dot_nt(d_text, rel_text[...]))
        part = dot_tn(masked(queries, half), d_text)
        text_sum = part if half == 0 else text_sum + part
        turned = d_scores.T
        d_box = turn_back(dot_nn(turned, spread) * scale, sines[...], cosines[...])
        got[1].append(dot_nn(turned, queries) * scale + dot_nt(d_box, rel_box[...]))
        part = dot_tn(masked(keys, half), d_box)
        box_sum = part if half == 0 else box_sum + part
    for ref, halves in zip((dq, dk, dv), got):
        ref[...] = pick_halves(*halves).astype(low)
    g_rel[0] = text_sum.astype(low)
    g_rel[1] = box_sum.astype(low)


def attend_back(d_attended, joined, rel_map, probs, sines, cosines, bases):
    size, model = bases.shape
    pairs = model // (2 * HD)
    lanes = 2 * HD
    low = jnp.bfloat16
    whole = lambda rows: pl.BlockSpec(rows.shape, lambda i: (0, 0))
    column = pl.BlockSpec((size, lanes), lambda i: (0, i))
    band = lambda part: pl.BlockSpec((lanes, model), lambda i: (i + part * pairs, 0))
    return pl.pallas_call(
        attend_back_kernel,
        name="attend_back",
        grid=(pairs,),
        out_shape=(jax.ShapeDtypeStruct((size, model), low),) * 3
        + (jax.ShapeDtypeStruct((2, model, model), low),),
        in_specs=[column, column, column, column, band(0), band(1)]
        + [pl.BlockSpec((2, size, size), lambda i: (i, 0, 0))]
        + [whole(sines), whole(cosines), whole(bases)],
        out_specs=(column,) * 3 + (pl.BlockSpec((2, lanes, model), lambda i: (0, i, 0)),),
        compiler_params=pltpu.CompilerParams(vmem_limit_bytes=56 * 2**20),
        cost_estimate=pl.CostEstimate(
            flops=2 * 12 * size * (size * 1800 + 4 * 64 * 768),
            bytes_accessed=25 * 2**20,
            transcendentals=0,
        ),
    )(d_attended, *joined, rel_map, rel_map, probs, sines, cosines, bases)


def ahead_kernel(n, units, early, capacity, *refs):
    count = len(units)
    lists, vocabulary, pages, points, omegas, place, mask_col = refs[:7]
    weights = refs[7 : 7 + count]
    outs = refs[7 + count : 23 + count]
    asked, full, probs, sines, cosines, bases, target_out, normed_out, white_out, scale_out, low_out = outs[:11]
    q, k, v, attended, gains = outs[11:]
    swap_out, swap_in, chip_rows, answers, rows, held, rel_map, shares = refs[23 + count : 31 + count]
    ask_send, ask_recv, row_send, row_recv, own_sem, swap_send, swap_recv = refs[31 + count : 38 + count]
    hop_recv, core_recv, core_send, z_send, a_send, b_send, load_sem, out_sem = refs[38 + count :]
    low = jnp.bfloat16
    me = lax.axis_index("dp")
    core, spot, layer, step_a, step_b = place_of(me)
    layers = n // 8
    half = chip_rows.shape[1]
    page_rows = pages.shape[0]
    here = pl.ds(pl.multiple_of(core * half, 128), half)
    there = pl.ds(pl.multiple_of((1 - core) * half, 128), half)
    partner = me + 1 - 2 * core
    to_a, to_b, up, down = me + 2 * step_a, me + 2 * step_b, me + 8, me - 8
    spot_a, spot_b, spot_ab = spot + step_a, spot + step_b, spot + step_a + step_b
    low_z, high_z = layer > 0, layer < layers - 1
    cuts = (pl.ds(0, early), pl.ds(early, chip_rows.shape[0] - early))

    at = 0
    for ref, unit in zip(weights, units):
        swap_out[pl.ds(at, 24 * unit)] = ref[:, there]
        at += 24 * unit
    greet_everyone(me, n)
    swaps = [
        remote_copy(swap_out, swap_in, swap_send.at[0], swap_recv.at[0], partner),
        remote_copy(
            pages.at[:, there],
            chip_rows.at[pl.ds(2 * at + core * page_rows, page_rows)],
            swap_send.at[1],
            swap_recv.at[1],
            partner,
        ),
    ]
    for copy in swaps:
        copy.start()

    def ask(step):
        peer = lax.rem(me + step, n)
        return remote_copy(lists.at[peer], asked.at[me], ask_send.at[step], ask_recv.at[step], peer)

    def start_ask(step, carry):
        ask(step).start()
        return carry

    def wait_ask(step, carry):
        ask(step).wait()
        return carry

    lax.fori_loop(1, n, start_ask, 0)
    asked[me] = lists[me]
    chip_rows[pl.ds(2 * at + pl.multiple_of(core * page_rows, page_rows), page_rows)] = pages[:, here]
    for copy in swaps:
        copy.wait_recv()
    at = 0
    for ref, unit in zip(weights, units):
        mine, other = ref[:, here], swap_in[pl.ds(at, 24 * unit)]
        ordered = jnp.where(
            core == 0, jnp.concatenate([mine, other], 0), jnp.concatenate([other, mine], 0)
        )
        chip_rows[pl.ds(2 * at, 48 * unit)] = ordered.astype(low)
        at += 24 * unit

    def block(g, level, index):
        return full.at[level, index, cuts[g], here]

    def z_hop(g, way, level, src=None):
        return remote_copy(
            block(g, level, spot) if src is None else src, block(g, level, spot),
            z_send.at[g, way, level], hop_recv.at[g, level, spot], up if way == 0 else down,
        )

    def a_hop(g, level, src=None):
        return remote_copy(
            block(g, level, spot) if src is None else src, block(g, level, spot),
            a_send.at[g, level], hop_recv.at[g, level, spot], to_a,
        )

    def b_hop(g, kind, level, src=None):
        index = spot if kind == 0 else spot_a
        return remote_copy(
            block(g, level, index) if src is None else src, block(g, level, index),
            b_send.at[g, kind, level], hop_recv.at[g, level, index], to_b,
        )

    def core_hop(g, level, index, src=None):
        return remote_copy(
            block(g, level, index) if src is None else src, block(g, level, index),
            core_send.at[g, level, index], core_recv.at[g, level, index], partner,
        )

    def arrived(g, level, index):
        view = block(g, level, index)
        pltpu.make_async_copy(view, view, hop_recv.at[g, level, index]).wait()

    def own_copy(g):
        return pltpu.make_async_copy(chip_rows.at[cuts[g]], block(g, layer, spot), own_sem.at[g])

    def send_own(g):
        src = chip_rows.at[cuts[g]]

        @pl.when(high_z)
        def _():
            z_hop(g, 0, layer, src).start()

        @pl.when(low_z)
        def _():
            z_hop(g, 1, layer, src).start()

        a_hop(g, layer, src).start()
        b_hop(g, 0, layer, src).start()
        core_hop(g, layer, spot, src).start()
        own_copy(g).start()

    def relay_column(g, gap):
        for way, level, there_is, further in (
            (0, layer - gap, layer - gap >= 0, high_z),
            (1, layer + gap, layer + gap < layers, low_z),
        ):

            @pl.when(there_is)
            def _():
                arrived(g, level, spot)

                @pl.when(further)
                def _():
                    z_hop(g, way, level).start()

                a_hop(g, level).start()
                b_hop(g, 0, level).start()
                core_hop(g, level, spot).start()

    def at_gap(gap, visit):
        if gap == 0:
            visit(layer)
            return

        @pl.when(layer - gap >= 0)
        def _():
            visit(layer - gap)

        @pl.when(layer + gap < layers)
        def _():
            visit(layer + gap)

    def relay_a(g, gap):
        def visit(level):
            arrived(g, level, spot_a)
            b_hop(g, 1, level).start()
            core_hop(g, level, spot_a).start()

        at_gap(gap, visit)

    def relay_b(g, gap):
        for index in (spot_b, spot_ab):

            def visit(level):
                arrived(g, level, index)
                core_hop(g, level, index).start()

            at_gap(gap, visit)

    def relays(g):
        steps = [lambda: relay_a(g, 0)]
        for gap in range(1, layers):
            steps.append(lambda gap=gap: relay_column(g, gap))
            steps.append(lambda gap=gap: relay_a(g, gap))
            steps.append(lambda gap=gap: relay_b(g, gap - 1))
        steps.append(lambda: relay_b(g, layers - 1))
        return steps

    def gathered(g):
        def wait(level, carry):
            for index in range(4):
                view = full.at[level, index, cuts[g], there]
                pltpu.make_async_copy(view, view, core_recv.at[g, level, index]).wait()
            return carry

        lax.fori_loop(0, layers, wait, 0)
        own_copy(g).wait()

    send_own(0)

    lax.fori_loop(1, n, wait_ask, 0)
    rows_own = vocabulary.shape[0]
    table = vocabulary[...].astype(low)
    group = 128 // capacity

    def row_copy(peer):
        return remote_copy(
            answers.at[peer], rows.at[me], row_send.at[peer], row_recv.at[me], peer
        )

    def answer(turn, carry):
        ids = jnp.zeros((8, 128), jnp.float32)
        for j in range(group):
            ids = ids + asked[turn * group + j]
        ids = ids.T[:, 6:7]
        wanted = lax.broadcasted_iota(jnp.int32, (128, rows_own), 1) + 1
        picks = jnp.where(ids.astype(jnp.int32) == wanted, 1.0, 0.0).astype(low)
        found = dot_nn(picks, table).astype(low)
        for j in range(group):
            peer = turn * group + j
            answers[peer] = found[j * capacity : (j + 1) * capacity]

            @pl.when(peer != me)
            def _():
                row_copy(peer).start()

        return carry

    lax.fori_loop(0, n // group, answer, 0)
    first = relays(0)
    rest = relays(1)
    for step in first[:2]:
        step()
    send_own(1)
    rows[me] = answers[me]
    cols = gains.shape[1] // n
    for source in range(n):
        gains[:, source * cols : (source + 1) * cols] = (
            asked[source, :, 0:cols].astype(low).astype(jnp.float32)
        )
    lane = lax.broadcasted_iota(jnp.int32, sines.shape, 1)
    angles = jnp.where(lane < sines.shape[1] // 2, points[:, 0:1], points[:, 1:2]) * omegas[...]
    sines[...] = jnp.sin(angles)
    cosines[...] = jnp.cos(angles)
    boxes = jnp.concatenate([sines[...], cosines[...]], 1).astype(low)
    bases[...] = jnp.concatenate([cosines[...], sines[...]], 1).astype(low)
    for step in (*first[2:6], *rest[:2], *first[6:9], *rest[2:3], *first[9:], rest[4]):
        step()
    gathered(0)
    map_copy = pltpu.make_async_copy(full.at[:, :, pl.ds(0, 192)], held, load_sem.at[0])
    map_copy.start()
    deep = (early - 192) if early > 192 else 0
    for chip in range(4 * layers):
        pltpu.make_async_copy(
            full.at[chip // 4, chip % 4, pl.ds(192, deep)], rel_map.at[pl.ds(chip * deep, deep)], load_sem.at[1]
        ).start()

    def wait_row(step, carry):
        source = lax.rem(me - step + n, n)
        pltpu.make_async_copy(rows.at[source], rows.at[source], row_recv.at[source]).wait()
        return carry

    lax.fori_loop(1, n, wait_row, 0)
    slots = n * capacity
    seats = lax.broadcasted_iota(jnp.int32, (place.shape[0], slots), 1) == place[...]
    target = dot_nn(jnp.where(seats, 1.0, 0.0).astype(low), rows[...].reshape(slots, -1))
    target_out[...] = target
    mask_owner, mask_slot = mask_token // rows_own, capacity - 1
    mask_row = rows[mask_owner, mask_slot : mask_slot + 1].astype(jnp.float32)
    entry = jnp.where(mask_col[...] == 1.0, mask_row, target)
    map_copy.wait()
    model = target.shape[1]

    def weight(at):
        return held[:, :, at : at + 48].reshape(-1, model)

    embedded = entry + dot_nt(boxes, weight(0))
    normed, white, scale = layer_norm(embedded, gains[0:1], gains[1:2])
    normed_out[...], white_out[...], scale_out[...] = normed, white, scale
    normed = normed.astype(low)
    low_out[...] = normed
    for third, ref in enumerate((q, k, v)):
        ref[...] = dot_nn(normed, weight(48 + 48 * third)).astype(low)
    rest[5]()
    pltpu.make_async_copy(rel_map, rel_map, load_sem.at[1]).wait()
    pairs = model // (2 * HD)
    turns = [[] for _ in range(pairs)]
    for at, which in zip((0, 1, 2, 3, 5), (7, 3, 6, 8, 9)):
        turns[min(at, pairs - 1)].append(rest[which])

    def shares_copy(pair):
        slot = lax.rem(pair, 2)
        return pltpu.make_async_copy(shares.at[slot], probs.at[pl.ds(2 * pair, 2)], out_sem.at[slot])

    def attend(pair, carry):
        for turn in range(pairs):

            @pl.when(pair == turn)
            def _():
                for step in turns[turn]:
                    step()

        @pl.when(pair >= 2)
        def _():
            shares_copy(pair - 2).wait()

        lanes = pl.ds(pl.multiple_of(pair * 2 * HD, 2 * HD), 2 * HD)
        band = pl.ds(pl.multiple_of(pair * 2 * HD, 2 * HD), 2 * HD)
        other = pl.ds(pl.multiple_of(model + pair * 2 * HD, 2 * HD), 2 * HD)
        slot = lax.rem(pair, 2)
        result = attend_pair(
            q[:, lanes], k[:, lanes], v[:, lanes], rel_map.at[band], rel_map.at[other],
            sines, cosines, bases[...], shares.at[slot],
        )
        attended[:, lanes] = result
        shares_copy(pair).start()
        return carry

    lax.fori_loop(0, pairs, attend, 0)
    shares_copy(pairs - 2).wait()
    shares_copy(pairs - 1).wait()
    rest[10]()
    gathered(1)

    def finish(level, carry):
        for g in range(2):
            for index in (spot, spot_a, spot_b, spot_ab):
                core_hop(g, level, index).wait_send()
            a_hop(g, level).wait_send()
            b_hop(g, 0, level).wait_send()
            b_hop(g, 1, level).wait_send()

            @pl.when((level <= layer) & high_z)
            def _():
                z_hop(g, 0, level).wait_send()

            @pl.when((level >= layer) & low_z)
            def _():
                z_hop(g, 1, level).wait_send()

        return carry

    lax.fori_loop(0, layers, finish, 0)
    for copy in swaps:
        copy.wait_send()

    def finish_rows(step, carry):
        peer = lax.rem(me + step, n)
        pltpu.make_async_copy(answers.at[peer], answers.at[peer], row_send.at[peer]).wait()
        return carry

    lax.fori_loop(1, n, finish_rows, 0)


def ahead(lists, vocabulary, pages, positions, place, mask_col, weights, early, n, capacity, ident):
    model = vocabulary.shape[1]
    size = place.shape[0]
    layers = n // 8
    units = [weight.shape[0] // 24 for weight in weights]
    points = positions.astype(jnp.float32).T
    waves = model // 4
    omegas = jnp.power(10000.0, -jnp.arange(waves).astype(jnp.float32) / waves)
    omegas = jnp.concatenate([omegas, omegas])[None]
    swap = 24 * sum(units)
    chip = 2 * (swap + pages.shape[0])
    low, wide = jnp.bfloat16, jnp.float32
    dma = pltpu.SemaphoreType.DMA
    vmem = pl.BlockSpec(memory_space=pltpu.VMEM)
    anywhere = pl.BlockSpec(memory_space=pl.ANY)
    shape = jax.ShapeDtypeStruct
    rows = lambda kind: shape((size, model), kind)
    heads = model // HD
    return pl.pallas_call(
        partial(ahead_kernel, n, units, early, capacity),
        name="ahead",
        out_shape=(
            shape(lists.shape, lists.dtype),
            shape((layers, 4, chip, model), low),
            shape((heads, size, size), wide),
            shape((size, 2 * waves), wide),
            shape((size, 2 * waves), wide),
            rows(low),
            rows(wide),
            rows(wide),
            rows(wide),
            shape((size, 1), wide),
            rows(low),
            rows(low),
            rows(low),
            rows(low),
            rows(low),
            shape((8, model), wide),
        ),
        in_specs=[vmem] * (7 + len(weights)),
        out_specs=(vmem, anywhere, anywhere) + (vmem,) * 13,
        scratch_shapes=[
            pltpu.VMEM((swap, model // 2), wide),
            pltpu.VMEM((swap, model // 2), wide),
            pltpu.VMEM((chip, model // 2), low),
            pltpu.VMEM((n, capacity, model), low),
            pltpu.VMEM((n, capacity, model), low),
            pltpu.VMEM((layers, 4, 192, model), low),
            pltpu.VMEM((2 * model, model), low),
            pltpu.VMEM((2, 2, size, size), wide),
            dma((n,)),
            dma((n,)),
            dma((n,)),
            dma((n,)),
            dma((2,)),
            dma((2,)),
            dma((2,)),
            dma((2, layers, 4)),
            dma((2, layers, 4)),
            dma((2, layers, 4)),
            dma((2, 2, layers)),
            dma((2, layers)),
            dma((2, 2, layers)),
            dma((2,)),
            dma((2,)),
        ],
        compiler_params=pltpu.CompilerParams(
            collective_id=ident, has_side_effects=True, vmem_limit_bytes=62 * 2**20
        ),
        cost_estimate=pl.CostEstimate(
            flops=13 * 10**9, bytes_accessed=100 * 2**20, transcendentals=0
        ),
    )(lists, vocabulary, pages, points, omegas, place, mask_col, *weights)


def forward(weights, rows, positions):
    box_map, mix_map, rel_map, out_map, up_map, down_map, norm_rows = weights
    gains = norm_rows.astype(jnp.float32)
    sin_count = box_map.shape[1]
    sin_x, cos_x, sin_y, cos_y = sinusoids(positions, sin_count // 4)
    sines = jnp.concatenate([sin_x, sin_y], -1)
    cosines = jnp.concatenate([cos_x, cos_y], -1)
    boxes = jnp.concatenate([sines, cosines], -1).astype(jnp.bfloat16)
    bases = jnp.concatenate([cosines, sines], -1).astype(jnp.bfloat16)
    embedded = rows + dot_nt(boxes, box_map)
    first = layer_norm(embedded, gains[0], gains[1])
    normed = first[0].astype(jnp.bfloat16)
    joined = [dot_nn(normed, part).astype(jnp.bfloat16) for part in mix_map]
    attended, probs = attend(joined, rel_map, sines, cosines, bases)
    second = layer_norm(first[0] + dot_nn(attended, out_map), gains[2], gains[3])
    middle = second[0].astype(jnp.bfloat16)
    hidden_pre = [dot_nn(middle, part) for part in up_map]
    hidden = [jax.nn.gelu(part, approximate=False).astype(jnp.bfloat16) for part in hidden_pre]
    lowered = sum(dot_nn(part, weight) for part, weight in zip(hidden, down_map))
    third = layer_norm(second[0] + lowered, gains[4], gains[5])
    return {
        "sines": sines,
        "cosines": cosines,
        "boxes": boxes,
        "bases": bases,
        "first": first,
        "normed": normed,
        "joined": joined,
        "probs": probs,
        "attended": attended,
        "second": second,
        "middle": middle,
        "hidden_pre": hidden_pre,
        "hidden": hidden,
        "third": third,
    }


def backward_upper(weights, cache, d_states):
    _, _, _, out_map, up_map, down_map, norm_rows = weights
    gains = norm_rows.astype(jnp.float32)
    d_mid, gain_last, bias_last = norm_back(
        d_states, cache["third"][1], cache["third"][2], gains[4]
    )
    d_down = d_mid.astype(jnp.bfloat16)
    gelu_exact = partial(jax.nn.gelu, approximate=False)
    grad_down, grad_up, d_second = [], [], d_mid
    for pre, hidden, up, down in zip(cache["hidden_pre"], cache["hidden"], up_map, down_map):
        grad_down.append(dot_tn(hidden, d_down))
        d_pre = jax.vjp(gelu_exact, pre)[1](dot_nt(d_down, down))[0].astype(jnp.bfloat16)
        grad_up.append(dot_tn(cache["middle"], d_pre))
        d_second = d_second + dot_nt(d_pre, up)
    d_lower, gain_mid, bias_mid = norm_back(
        d_second, cache["second"][1], cache["second"][2], gains[2]
    )
    d_attn = d_lower.astype(jnp.bfloat16)
    grad_out = dot_tn(cache["attended"], d_attn)
    d_attended = dot_nt(d_attn, out_map).astype(jnp.bfloat16)
    return d_lower, d_attended, grad_out, grad_up, grad_down, [gain_mid, bias_mid, gain_last, bias_last]


def backward_lower(weights, cache, d_lower, d_attended):
    box_map, mix_map, rel_map, _, _, _, norm_rows = weights
    gains = norm_rows.astype(jnp.float32)
    *d_joined, grad_rel = attend_back(
        d_attended,
        cache["joined"],
        rel_map,
        cache["probs"],
        cache["sines"],
        cache["cosines"],
        cache["bases"],
    )
    grad_mix = [dot_tn(cache["normed"], part) for part in d_joined]
    d_first = d_lower + sum(dot_nt(part, weight) for part, weight in zip(d_joined, mix_map))
    d_embedded, gain_low, bias_low = norm_back(
        d_first, cache["first"][1], cache["first"][2], gains[0]
    )
    grad_box = dot_tn(d_embedded.astype(jnp.bfloat16), cache["boxes"])
    return d_embedded, grad_box, grad_mix, grad_rel, [gain_low, bias_low]


def per_device(
    n,
    tokens,
    positions,
    documents,
    masking,
    negative_page,
    negative_row,
    pages,
    vocabulary,
    geometry,
    mixing,
    relative,
    merging,
    widening,
    narrowing,
    scaling,
    moment_vocabulary,
    moment_geometry,
    moment_mixing,
    moment_relative,
    moment_merging,
    moment_widening,
    moment_narrowing,
    moment_scaling,
    average_vocabulary,
    average_geometry,
    average_mixing,
    average_relative,
    average_merging,
    average_widening,
    average_narrowing,
    average_scaling,
):
    size = tokens.shape[0]
    rows_own, model = vocabulary.shape
    page_rows = pages.shape[1]
    mask_float = masking.astype(jnp.float32)
    mask_col = mask_float[:, None]
    low = jnp.bfloat16
    blocks = widening.shape[1] // model
    decay = min(average_cap, (1.0 + STEP) / (10.0 + STEP))
    masters = (vocabulary, geometry, mixing, relative, merging, widening, narrowing, scaling)
    moments = (
        moment_vocabulary,
        moment_geometry,
        moment_mixing,
        moment_relative,
        moment_merging,
        moment_widening,
        moment_narrowing,
        moment_scaling,
    )
    averages = (
        average_vocabulary,
        average_geometry,
        average_mixing,
        average_relative,
        average_merging,
        average_widening,
        average_narrowing,
        average_scaling,
    )
    pieces = [
        swap_middle(geometry).T,
        *[mixing[:, k * model : (k + 1) * model] for k in range(3)],
        swap_middle(relative).T,
        merging,
        *[widening[:, k * model : (k + 1) * model] for k in range(blocks)],
        narrowing,
    ]
    bank_piece = pages.reshape(-1, model)

    def step(master, moment, average, piece, rate, factor):
        clipped = piece * factor
        velocity = momentum_decay * moment + clipped
        updated = master - rate * (clipped + momentum_decay * velocity)
        return updated, velocity, decay * average + (1.0 - decay) * updated

    def dense():
        chosen = (documents[0] == jnp.arange(DOCS)).astype(jnp.float32)
        counts = lax.psum(chosen * jnp.sum(mask_float), "dp")
        share = jnp.sum(chosen / (DOCS * jnp.maximum(counts, 1.0)))
        cast = [piece.astype(low) for piece in pieces] + [bank_piece]
        joined = lax.all_gather(jnp.concatenate(cast, 0), "dp", axis=0, tiled=False)
        weights, at = [], 0
        for piece in cast:
            weights.append(joined[:, at : at + piece.shape[0]].reshape(-1, model))
            at += piece.shape[0]
        norm_rows = lax.all_gather(scaling.astype(low), "dp", axis=1, tiled=True)
        entry = jnp.where(masking == 1, mask_token, tokens)
        lanes = 4

        def split(rows):
            return rows.reshape(rows.shape[0], lanes, -1).transpose(1, 0, 2)

        def join(rows):
            return rows.transpose(1, 0, 2).reshape(rows.shape[1], -1)

        def named_rows(part):
            table = lax.all_gather(part, "dp", axis=0, tiled=True)
            return table[tokens], table[entry]

        found = lax.map(named_rows, split(vocabulary.astype(low)))
        target_rows, entry_rows = [join(rows).astype(jnp.float32) for rows in found]
        box_map, mix_map, rel_map, out_map = weights[0], weights[1:4], weights[4], weights[5]
        up_map, down_full, bank = weights[6:-2], weights[-2], weights[-1]
        ff = len(up_map)
        down_map = [down_full[k * model : (k + 1) * model] for k in range(ff)]
        weights = (box_map, mix_map, rel_map, out_map, up_map, down_map, norm_rows)
        cache = forward(weights, entry_rows, positions)

        states_low = cache["third"][0].astype(low)
        inv_root = model ** (-0.5)
        positive = jnp.sum(states_low.astype(jnp.float32) * target_rows, -1, keepdims=True) * inv_root
        flat_index = (negative_page * page_rows + negative_row).T
        count_neg = flat_index.shape[1]
        width = bank.shape[0]
        repeated = jnp.tile(flat_index, (1, width // count_neg))
        chosen = repeated == jnp.arange(width)[None, :]
        logits = jnp.where(chosen, dot_nt(states_low, bank) * inv_root, -jnp.inf)
        highest = jnp.maximum(jnp.max(logits, -1, keepdims=True), positive)
        powers = jnp.exp(logits - highest)
        lead = jnp.exp(positive - highest)
        total = jnp.sum(powers, -1, keepdims=True) + lead
        per_token = highest + jnp.log(total) - positive
        loss_part = share * jnp.sum(mask_col * per_token)
        weight_map = (powers * (share * mask_col / total) * inv_root).astype(low)
        positive_grad = share * mask_col * (lead / total - 1.0) * inv_root
        d_states = positive_grad * target_rows + dot_nn(weight_map, bank)

        d_lower, d_attended, grad_out, grad_up, grad_down, upper_norms = backward_upper(
            weights, cache, d_states
        )
        d_embedded, grad_box, grad_mix, grad_rel, lower_norms = backward_lower(
            weights, cache, d_lower, d_attended
        )
        grad_norms = jnp.concatenate(lower_norms + upper_norms, 0)
        positive_rows = positive_grad * states_low.astype(jnp.float32)

        def summed_rows(parts):
            whole = jnp.zeros((rows_own * n, model // lanes), jnp.float32)
            whole = whole.at[entry].add(parts[0]).at[tokens].add(parts[1])
            return lax.psum_scatter(whole, "dp", scatter_dimension=0, tiled=True)

        table_piece = join(lax.map(summed_rows, (split(d_embedded), split(positive_rows))))
        norm_piece = lax.psum_scatter(grad_norms, "dp", scatter_dimension=1, tiled=True)
        grads = [grad_box, *grad_mix, grad_rel.reshape(-1, model), grad_out, *grad_up]
        grads = [grad.astype(low) for grad in [*grads, jnp.concatenate(grad_down, 0)]]
        sums = scatter(grads, n)
        reduced = (
            table_piece,
            swap_middle(sums[0].T),
            jnp.concatenate(sums[1:4], 1),
            swap_middle(sums[4].T),
            sums[5],
            jnp.concatenate(sums[6:-1], 1),
            sums[-1],
            norm_piece,
        )
        square = lax.psum(sum(jnp.sum(piece * piece) for piece in reduced), "dp")
        grad_norm = jnp.sqrt(square)
        factor = clip_limit / jnp.maximum(grad_norm, clip_limit)
        rates = (table_rate,) + (learn_rate,) * 7
        done = [step(*group, factor) for group in zip(masters, moments, averages, reduced, rates)]
        return (lax.psum(loss_part, "dp"), grad_norm) + sum(zip(*done), ())

    if n // 8 != 4 or n % 8 != 0 or merging.shape[0] != 24 or page_rows % 16 != 0 or size % 128 != 0:
        return dense()

    capacity = max(16, -(-2 * size // n) // 16 * 16)
    slots = n * capacity
    fold = 128 // capacity
    cols = scaling.shape[1]
    info = jnp.pad(scaling, ((0, 2), (0, 128 - cols)))
    lists, place = make_plan(tokens, masking, documents, info, n, rows_own, capacity, fold)
    early = 48 * (1 + 3 + relative.shape[1] // 24)
    (
        asked,
        full,
        probs,
        sines,
        cosines,
        bases,
        target,
        normed,
        white,
        scale,
        normed_low,
        *joined,
        attended,
        gains,
    ) = ahead(
        lists, vocabulary, bank_piece, positions, place, mask_col, pieces, early, n, capacity, 1
    )
    full = full.reshape(-1, *full.shape[2:])
    upper_grads, d_attended, d_lower, positive_rows, upper_norms, loss_part = upper(
        full,
        attended,
        normed,
        target,
        mask_col,
        negative_page,
        negative_row,
        asked,
        documents,
        gains,
        blocks,
        page_rows,
    )
    rel_map = full[:, 192:early].reshape(-1, model)
    *d_joined, grad_rel = attend_back(d_attended, joined, rel_map, probs, sines, cosines, bases)
    fixed = (mask_token // rows_own) * capacity + capacity - 1
    lower_grads, sent, norm_blocks = lower(
        full,
        d_joined,
        d_lower,
        white,
        scale,
        gains,
        normed_low,
        sines,
        cosines,
        mask_col,
        positive_rows,
        place,
        upper_norms,
        n,
        slots,
        fixed,
    )
    grads = [lower_grads, grad_rel.reshape(n // 2, -1, model), upper_grads]
    parts = (1, 1, 1, 1, 2, 1) + (1,) * blocks + (narrowing.shape[0] // 24,)
    sent = sent.reshape(n, capacity, model)
    sums, table_piece, norm_piece, totals = to_owners(
        sent, norm_blocks, asked, loss_part, grads, parts, rows_own, fold, n, 2
    )

    def finish():
        grad_norm = jnp.sqrt(totals[0, 0])
        factor = clip_limit / jnp.maximum(grad_norm, clip_limit)
        last = step(
            scaling, moment_scaling, average_scaling, norm_piece[:6, :cols], learn_rate, factor
        )
        layout = (
            (1, 0, 1, 24, True),
            (2, 24, 3, 24, False),
            (3, 96, 1, 48, True),
            (4, 144, 1, 24, False),
            (5, 168, blocks, 24, False),
            (6, 168 + 24 * blocks, 1, narrowing.shape[0], False),
        )
        lay = lambda group: [group[0], group[1].T, group[2], group[3].T, *group[4:7]]
        groups = [lay(group) for group in (masters, moments, averages)]
        done = update_all(factor.reshape(1, 1), table_piece, sums, *groups, decay, layout)
        results = [totals[0, 1], grad_norm]
        for at, tail in zip((0, 7, 14), last):
            results += [*lay(done[at : at + 7]), tail]
        return tuple(results)

    overflow = jnp.max(asked[:, 7, 2]) > 0.0
    return lax.cond(overflow, dense, finish)


ROWS = P("dp", None)
COLS = P(None, "dp")
WEIGHTS = (ROWS, COLS, ROWS, COLS, ROWS, ROWS, ROWS, COLS)


def solution(mesh):
    return jax.shard_map(
        partial(per_device, mesh.shape["dp"]),
        mesh=mesh,
        in_specs=(P("dp"), COLS, P("dp"), P("dp"), COLS, COLS, P("dp", None, None)) + 3 * WEIGHTS,
        out_specs=(P(), P()) + 3 * WEIGHTS,
        check_vma=False,
    )
```

```python
from functools import partial

import jax
import jax.numpy as jnp
from jax import lax
from jax.experimental import pallas as pl
from jax.experimental.pallas import tpu as pltpu
from jax.sharding import PartitionSpec as P

HD = 64
DOCS = 8
STEP = 10
MESH = pl.DeviceIdType.MESH

mask_token = 103
ln_epsilon = 1e-06
momentum_decay = 0.9
learn_rate = 5000.0
table_rate = 1000000.0
clip_limit = 0.01
average_cap = 0.999


def sinusoids(positions, count):
    ranks = jnp.arange(count).astype(jnp.float32)
    omegas = jnp.power(10000.0, -ranks / count)
    angle_x = positions[0].astype(jnp.float32)[:, None] * omegas[None, :]
    angle_y = positions[1].astype(jnp.float32)[:, None] * omegas[None, :]
    return (jnp.sin(angle_x), jnp.cos(angle_x), jnp.sin(angle_y), jnp.cos(angle_y))


def layer_norm(rows, gain, bias):
    centred = rows - jnp.mean(rows, -1, keepdims=True)
    rescale = lax.rsqrt(jnp.mean(centred * centred, -1, keepdims=True) + ln_epsilon)
    whitened = centred * rescale
    return (whitened * gain + bias, whitened, rescale)


def norm_back(upstream, whitened, rescale, gain):
    scaled = upstream * gain
    inner = (
        scaled
        - jnp.mean(scaled, -1, keepdims=True)
        - whitened * jnp.mean(scaled * whitened, -1, keepdims=True)
    )
    return (
        rescale * inner,
        jnp.sum(upstream * whitened, 0, keepdims=True),
        jnp.sum(upstream, 0, keepdims=True),
    )


def swap_middle(rows, axis=0):
    count = rows.shape[axis] // 4
    cuts = [lax.slice_in_dim(rows, k * count, (k + 1) * count, axis=axis) for k in (0, 2, 1, 3)]
    return jnp.concatenate(cuts, axis)


def dot_nn(left, right):
    return lax.dot_general(
        left, right, (((1,), (0,)), ((), ())), preferred_element_type=jnp.float32
    )


def dot_tn(left, right):
    return lax.dot_general(
        left, right, (((0,), (0,)), ((), ())), preferred_element_type=jnp.float32
    )


def dot_nt(left, right):
    return lax.dot_general(
        left, right, (((1,), (1,)), ((), ())), preferred_element_type=jnp.float32
    )


def plan_kernel(
    n, rows_own, capacity, fold, tok_col, tok_row, mask_row, own, info, lists, place
):
    size = tok_col.shape[0]
    ids_col = tok_col[...]
    ids_row = tok_row[...]
    owner_col = lax.div(ids_col, rows_own)
    owner_row = lax.div(ids_row, rows_own)
    at_col = lax.broadcasted_iota(jnp.int32, (size, size), 0)
    at_row = lax.broadcasted_iota(jnp.int32, (size, size), 1)
    same = ids_col == ids_row
    first_col = jnp.min(jnp.where(same, at_row, size), 1, keepdims=True)
    first_row = jnp.min(jnp.where(same, at_col, size), 0, keepdims=True)
    leads_row = first_row == lax.broadcasted_iota(jnp.int32, (1, size), 1)
    leads_col = first_col == lax.broadcasted_iota(jnp.int32, (size, 1), 0)
    ahead = (owner_col == owner_row) & leads_row & (at_row < first_col)
    slot = jnp.sum(jnp.where(ahead, 1.0, 0.0), 1, keepdims=True).astype(jnp.int32)
    fits = slot < capacity - 1
    place[...] = jnp.where(fits, owner_col * capacity + slot, -1)
    over = jnp.max(jnp.where(fits, 0.0, 1.0), keepdims=True)
    local = ids_col - owner_col * rows_own + 1
    high = lax.div(local, 128)
    to_owner = lax.broadcasted_iota(jnp.int32, (size, n), 1) == owner_col
    to_owner = to_owner & leads_col & fits
    shift = capacity * lax.rem(own[1], fold)
    in_slot = lax.broadcasted_iota(jnp.int32, (size, 128), 1) == slot + shift
    in_slot = jnp.where(in_slot, 1.0, 0.0).astype(jnp.bfloat16)
    high_part = jnp.where(to_owner, high.astype(jnp.float32), 0.0).astype(jnp.bfloat16)
    low_part = jnp.where(to_owner, (local - high * 128).astype(jnp.float32), 0.0)
    table = dot_tn(high_part, in_slot) * 128.0 + dot_tn(low_part.astype(jnp.bfloat16), in_slot)
    lane = lax.broadcasted_iota(jnp.int32, (n, 128), 1)
    line = lax.broadcasted_iota(jnp.int32, (n, 128), 0)
    fixed = (line == mask_token // rows_own) & (lane == capacity - 1 + shift)
    table = jnp.where(fixed, float(mask_token % rows_own + 1), table)
    count = jnp.sum(mask_row[...].astype(jnp.float32), keepdims=True)
    lane = lax.broadcasted_iota(jnp.int32, (8, 128), 1)
    line = lax.broadcasted_iota(jnp.int32, (8, 128), 0)
    extra = jnp.where(lane == 0, count, jnp.where(lane == 1, own[0].astype(jnp.float32), over))
    extra = jnp.where(line == 7, extra, info[...])
    line = lax.broadcasted_iota(jnp.int32, lists.shape, 1)
    lists[...] = jnp.where(line == 6, table[:, None, :], extra[None])


def make_plan(tokens, masking, documents, info, n, rows_own, capacity, fold):
    size = tokens.shape[0]
    vmem = pl.BlockSpec(memory_space=pltpu.VMEM)
    return pl.pallas_call(
        partial(plan_kernel, n, rows_own, capacity, fold),
        name="plan",
        out_shape=(
            jax.ShapeDtypeStruct((n, 8, 128), jnp.float32),
            jax.ShapeDtypeStruct((size, 1), jnp.int32),
        ),
        in_specs=[vmem, vmem, vmem, pl.BlockSpec(memory_space=pltpu.SMEM), vmem],
        out_specs=(vmem, vmem),
        compiler_params=pltpu.CompilerParams(vmem_limit_bytes=32 * 2**20),
    )(
        tokens[:, None],
        tokens[None, :],
        masking[None, :],
        jnp.stack([documents[0], lax.axis_index("dp")]),
        info,
    )


def place_of(me):
    core = lax.rem(me, 2)
    chip = lax.div(me, 2)
    spot = lax.rem(chip, 4)
    layer = lax.div(chip, 4)
    along_a = 1 + core
    along_b = 2 - core
    step_a = along_a * (1 - 2 * lax.rem(lax.div(spot, along_a), 2))
    step_b = along_b * (1 - 2 * lax.rem(lax.div(spot, along_b), 2))
    return core, spot, layer, step_a, step_b


def remote_copy(src, dst, send, recv, device):
    return pltpu.make_async_remote_copy(
        src_ref=src, dst_ref=dst, send_sem=send, recv_sem=recv, device_id=(device,), device_id_type=MESH
    )


def greet_everyone(me, n):
    barrier = pltpu.get_barrier_semaphore()

    def greet(step, carry):
        pl.semaphore_signal(
            barrier, inc=1, device_id=(lax.rem(me + step, n),), device_id_type=MESH
        )
        return carry

    lax.fori_loop(1, n, greet, 0)
    pl.semaphore_wait(barrier, n - 1)


def flat(rows):
    return rows.reshape(-1, rows.shape[-1])


def upper_kernel(
    page_rows, full, attended, normed, target, mask_col, page, row, asked, doc, gains,
    grads, d_attended, d_lower, pos_rows, norms, loss_part,
    held, bank, slopes, hidden, scores, load_sem, store_sem,
):
    low = jnp.bfloat16
    chips, used, model = held.shape
    size = attended.shape[0]
    blocks = hidden.shape[0]
    first_row = 288
    span = model // (used - 48 - 48 * blocks)
    down_at = 48 + 48 * blocks
    loads = [
        pltpu.make_async_copy(full.at[:, pl.ds(first_row + at, many)], held.at[:, pl.ds(at, many)], load_sem.at[k])
        for k, (at, many) in enumerate(((0, 48), (48, 48 * blocks), (down_at, used - down_at)))
    ]
    loads.append(
        pltpu.make_async_copy(full.at[:, pl.ds(first_row + used, bank.shape[1])], bank, load_sem.at[3])
    )
    for copy in loads:
        copy.start()

    def up_map(k):
        return flat(held[:, 48 + 48 * k : 96 + 48 * k])

    def down_map(k):
        return flat(held[span * k : span * (k + 1), down_at:])

    loads[0].wait()
    second, white_mid, scale_mid = layer_norm(
        normed[...] + dot_nn(attended[...], flat(held[:, 0:48])), gains[2:3], gains[3:4]
    )
    middle = second.astype(low)
    loads[1].wait()
    loads[2].wait()
    for k in range(blocks):
        pre = dot_nn(middle, up_map(k))
        normal = 0.5 + 0.5 * lax.erf(pre * (0.5**0.5))
        active = (pre * normal).astype(low)
        slopes[k] = normal + pre * (jnp.exp(-0.5 * pre * pre) * 0.3989422804014327)
        hidden[k] = active
        part = dot_nn(active, down_map(k))
        lowered = part if k == 0 else lowered + part
    states, white_last, scale_last = layer_norm(second + lowered, gains[4:5], gains[5:6])
    states = states.astype(low)

    inv_root = model ** (-0.5)
    positive = jnp.sum(states.astype(jnp.float32) * target[...], -1, keepdims=True) * inv_root
    many = page.shape[0]
    seat = lax.broadcasted_iota(jnp.int32, (many, 128), 0)
    lane = lax.broadcasted_iota(jnp.int32, (many, 128), 1)
    spread = jnp.where(lax.rem(lane, many) == seat, 1.0, 0.0).astype(low)
    wanted = page_rows * dot_tn(page[...].astype(jnp.float32).astype(low), spread) + dot_tn(
        row[...].astype(jnp.float32).astype(low), spread
    )
    wanted = jnp.concatenate([wanted.astype(jnp.int32)] * 4, 1)
    column = lax.broadcasted_iota(jnp.int32, wanted.shape, 1)
    width = wanted.shape[1]
    per = width // bank.shape[1]
    parts = chips // per
    loads[3].wait()
    highest = positive
    for c in range(parts):
        raw = dot_nt(states, flat(bank[per * c : per * (c + 1)])) * inv_root
        raw = jnp.where(wanted == column + c * width, raw, -jnp.inf)
        scores[:, c * width : (c + 1) * width] = raw
        highest = jnp.maximum(highest, jnp.max(raw, -1, keepdims=True))
    lead = jnp.exp(positive - highest)
    total = lead
    for c in range(parts):
        powers = jnp.exp(scores[:, c * width : (c + 1) * width] - highest)
        scores[:, c * width : (c + 1) * width] = powers
        total = total + jnp.sum(powers, -1, keepdims=True)
    mask = mask_col[...]
    facts = asked[:, 7, :]
    counted = jnp.where(facts[:, 1:2] == doc[0].astype(jnp.float32), facts[:, 0:1], 0.0)
    share = 1.0 / (DOCS * jnp.maximum(jnp.sum(counted, keepdims=True), 1.0))
    loss_part[...] = share * jnp.sum(
        mask * (highest + jnp.log(total) - positive), keepdims=True
    )
    factor = share * mask * inv_root
    positive_grad = factor * (lead / total - 1.0)
    factor = factor / total
    pos_rows[...] = (positive_grad * states.astype(jnp.float32)).astype(pos_rows.dtype)
    d_states = positive_grad * target[...]
    for c in range(parts):
        weights = (scores[:, c * width : (c + 1) * width] * factor).astype(low)
        d_states = d_states + dot_nn(weights, flat(bank[per * c : per * (c + 1)]))

    d_mid, gain_last, bias_last = norm_back(d_states, white_last, scale_last, gains[4:5])
    d_down = d_mid.astype(low)
    d_second = d_mid
    stores = []
    for k in range(blocks):
        d_pre = (dot_nt(d_down, down_map(k)) * slopes[k]).astype(low)
        d_second = d_second + dot_nt(d_pre, up_map(k))
        grad = dot_tn(hidden[k], d_down).astype(low)
        held[span * k : span * (k + 1), down_at:] = grad.reshape(span, -1, model)
        grad = dot_tn(middle, d_pre).astype(low)
        held[:, 48 + 48 * k : 96 + 48 * k] = grad.reshape(chips, 48, model)
        for j, cut in enumerate(
            (
                (pl.ds(span * k, span), pl.ds(down_at, used - down_at)),
                (pl.ds(0, chips), pl.ds(48 + 48 * k, 48)),
            )
        ):
            stores.append(pltpu.make_async_copy(held.at[cut], grads.at[cut], store_sem.at[2 * k + j]))
            stores[-1].start()
    d_low, gain_mid, bias_mid = norm_back(d_second, white_mid, scale_mid, gains[2:3])
    d_lower[...] = d_low
    d_attn = d_low.astype(low)
    d_attended[...] = dot_nt(d_attn, flat(held[:, 0:48])).astype(low)
    held[:, 0:48] = dot_tn(attended[...], d_attn).astype(low).reshape(chips, 48, model)
    cut = (pl.ds(0, chips), pl.ds(0, 48))
    stores.append(pltpu.make_async_copy(held.at[cut], grads.at[cut], store_sem.at[2 * blocks]))
    stores[-1].start()
    for at, line in enumerate((gain_mid, bias_mid, gain_last, bias_last)):
        norms[at : at + 1] = line
    for copy in stores:
        copy.wait()


def upper(full, attended, normed, target, mask_col, page, row, asked, doc, gains, blocks, page_rows):
    size, model = normed.shape
    chips = full.shape[0]
    used = full.shape[1] - 288 - 2 * page_rows
    low, wide = jnp.bfloat16, jnp.float32
    vmem = pl.BlockSpec(memory_space=pltpu.VMEM)
    anywhere = pl.BlockSpec(memory_space=pl.ANY)
    shape = jax.ShapeDtypeStruct
    return pl.pallas_call(
        partial(upper_kernel, page_rows),
        name="upper",
        out_shape=(
            shape((chips, used, model), low),
            shape((size, model), low),
            shape((size, model), wide),
            shape((size, model), low),
            shape((4, model), wide),
            shape((1, 1), wide),
        ),
        in_specs=[anywhere]
        + [vmem] * 7
        + [pl.BlockSpec(memory_space=pltpu.SMEM), vmem],
        out_specs=(anywhere,) + (vmem,) * 5,
        scratch_shapes=[
            pltpu.VMEM((chips, used, model), low),
            pltpu.VMEM((chips, 2 * page_rows, model), low),
            pltpu.VMEM((blocks, size, model), wide),
            pltpu.VMEM((blocks, size, model), low),
            pltpu.VMEM((size, chips * 2 * page_rows), wide),
            pltpu.SemaphoreType.DMA((4,)),
            pltpu.SemaphoreType.DMA((2 * blocks + 1,)),
        ],
        compiler_params=pltpu.CompilerParams(vmem_limit_bytes=63 * 2**20),
        cost_estimate=pl.CostEstimate(
            flops=20 * 10**9, bytes_accessed=32 * 2**20, transcendentals=4 * size * model * 2
        ),
    )(full, attended, normed, target, mask_col, page, row, asked, doc, gains)


def update_kernel(decay, layout, factor, table, sums, *refs):
    masters, moments, averages = refs[0:7], refs[7:14], refs[14:21]
    fresh, speeds, smooths = refs[21:28], refs[28:35], refs[35:42]
    scale = factor[0, 0]

    def update(k, piece, rate, cut):
        clipped = piece * scale
        velocity = momentum_decay * moments[k][cut] + clipped
        updated = masters[k][cut] - rate * (clipped + momentum_decay * velocity)
        fresh[k][cut] = updated
        speeds[k][cut] = velocity
        smooths[k][cut] = decay * averages[k][cut] + (1.0 - decay) * updated

    update(0, table[...], table_rate, (slice(None), slice(None)))

    @pl.when(pl.program_id(0) == 0)
    def _():
        model = sums.shape[1]
        for k, at, blocks, rows, turned in layout:
            for block in range(blocks):
                piece = sums[at + block * rows : at + (block + 1) * rows]
                if turned:
                    update(k, swap_middle(piece, 1), learn_rate, (slice(None), slice(None)))
                else:
                    cut = (slice(None), slice(block * model, (block + 1) * model))
                    update(k, piece, learn_rate, cut)


def update_all(factor, table, sums, masters, moments, averages, decay, layout):
    steps = 6
    rows, model = table.shape
    banded = pl.BlockSpec((rows // steps, model), lambda i: (i, 0))
    whole = lambda array: pl.BlockSpec(array.shape, lambda i: (0, 0))
    group = lambda arrays: [banded] + [whole(array) for array in arrays[1:]]
    shapes = tuple(jax.ShapeDtypeStruct(array.shape, jnp.float32) for array in masters)
    return pl.pallas_call(
        partial(update_kernel, decay, layout),
        name="update",
        grid=(steps,),
        out_shape=shapes * 3,
        in_specs=[pl.BlockSpec(memory_space=pltpu.SMEM), banded, whole(sums)]
        + group(masters)
        + group(moments)
        + group(averages),
        out_specs=tuple(group(masters) * 3),
        compiler_params=pltpu.CompilerParams(vmem_limit_bytes=56 * 2**20),
        cost_estimate=pl.CostEstimate(flops=0, bytes_accessed=28 * 2**20, transcendentals=0),
    )(factor, table, sums, *masters, *moments, *averages)


def split_rows(packed, grads, n):
    out, at = [], 0
    for grad in grads:
        count = grad.shape[0] // n
        out.append(packed[at : at + count])
        at += count
    return out


def scatter(grads, n):
    model = grads[0].shape[1]
    joined = jnp.concatenate([grad.reshape(n, -1, model) for grad in grads], 1)
    joined = joined.reshape(-1, model)
    mine = lax.psum_scatter(joined, "dp", scatter_dimension=0, tiled=True)
    return split_rows(mine.astype(jnp.float32), grads, n)


def masked(rows, half):
    lane = lax.broadcasted_iota(jnp.int32, rows.shape, 1)
    keep = (lane < HD) if half == 0 else (lane >= HD)
    return jnp.where(keep, rows, jnp.zeros_like(rows))


def turn(terms, sines, cosines):
    half = sines.shape[1]
    sine, cosine = terms[:, :half], terms[:, half:]
    return jnp.concatenate(
        [sine * sines + cosine * cosines, cosine * sines - sine * cosines], 1
    ).astype(jnp.bfloat16)


def turn_back(upstream, sines, cosines):
    half = sines.shape[1]
    first, second = upstream[:, :half], upstream[:, half:]
    return jnp.concatenate(
        [first * sines - second * cosines, first * cosines + second * sines], 1
    ).astype(jnp.bfloat16)


def pick_halves(low_half, high_half):
    lane = lax.broadcasted_iota(jnp.int32, low_half.shape, 1)
    return jnp.where(lane < HD, low_half, high_half)


def attend_pair(queries, keys, values, rel_text, rel_box, sines, cosines, spread, probs):
    results = []
    for half in range(2):
        mine = masked(queries, half)
        terms = dot_nn(masked(keys, half), rel_box[...])
        box_rot = turn(terms, sines[...], cosines[...])
        terms = dot_nn(mine, rel_text[...])
        text_rot = turn(terms, sines[...], cosines[...])
        scores = dot_nt(mine, keys) + dot_nt(text_rot, spread) + dot_nt(spread, box_rot)
        scores = scores * HD ** (-0.5)
        powers = jnp.exp(scores - jnp.max(scores, -1, keepdims=True))
        shares = powers * (1.0 / jnp.sum(powers, -1, keepdims=True))
        probs[half] = shares.astype(probs.dtype)
        results.append(dot_nn(shares.astype(jnp.bfloat16), values))
    return pick_halves(*results).astype(jnp.bfloat16)


def attend_kernel(q, k, v, rel_text, rel_box, sines, cosines, bases, attended, probs):
    attended[...] = attend_pair(
        q[...], k[...], v[...], rel_text, rel_box, sines, cosines, bases[...], probs
    )


def attend(joined, rel_map, sines, cosines, bases):
    size, model = bases.shape
    pairs = model // (2 * HD)
    lanes = 2 * HD
    whole = lambda rows: pl.BlockSpec(rows.shape, lambda i: (0, 0))
    column = pl.BlockSpec((size, lanes), lambda i: (0, i))
    band = lambda part: pl.BlockSpec((lanes, model), lambda i: (i + part * pairs, 0))
    return pl.pallas_call(
        attend_kernel,
        name="attend",
        grid=(pairs,),
        out_shape=(
            jax.ShapeDtypeStruct((size, model), jnp.bfloat16),
            jax.ShapeDtypeStruct((2 * pairs, size, size), jnp.float32),
        ),
        in_specs=[column, column, column, band(0), band(1)]
        + [whole(sines), whole(cosines), whole(bases)],
        out_specs=(
            column,
            pl.BlockSpec((2, size, size), lambda i: (i, 0, 0)),
        ),
        compiler_params=pltpu.CompilerParams(vmem_limit_bytes=56 * 2**20),
        cost_estimate=pl.CostEstimate(
            flops=2 * 12 * size * (size * 1700 + 2 * 64 * 768),
            bytes_accessed=20 * 2**20,
            transcendentals=12 * size * size,
        ),
    )(*joined, rel_map, rel_map, sines, cosines, bases)


def attend_back_pair(upstream, queries, keys, values, rel_text, rel_box, probs, sines, cosines, spread):
    scale = HD ** (-0.5)
    low = jnp.bfloat16
    got = [[], [], []]
    for half in range(2):
        shares = probs[half].astype(jnp.float32)
        d_probs = dot_nt(masked(upstream, half), values)
        got[2].append(dot_tn(shares.astype(low), upstream))
        inner = jnp.sum(d_probs * shares, -1, keepdims=True)
        d_scores = (shares * (d_probs - inner)).astype(low)
        d_text = turn_back(dot_nn(d_scores, spread) * scale, sines[...], cosines[...])
        got[0].append(dot_nn(d_scores, keys) * scale + dot_nt(d_text, rel_text[...]))
        part = dot_tn(masked(queries, half), d_text)
        text_sum = part if half == 0 else text_sum + part
        turned = d_scores.T
        d_box = turn_back(dot_nn(turned, spread) * scale, sines[...], cosines[...])
        got[1].append(dot_nn(turned, queries) * scale + dot_nt(d_box, rel_box[...]))
        part = dot_tn(masked(keys, half), d_box)
        box_sum = part if half == 0 else box_sum + part
    return (*[pick_halves(*halves).astype(low) for halves in got], text_sum, box_sum)


def attend_back_kernel(
    d_out, q, k, v, rel_text, rel_box, probs, sines, cosines, bases, dq, dk, dv, g_rel
):
    dq[...], dk[...], dv[...], text_sum, box_sum = attend_back_pair(
        d_out[...], q[...], k[...], v[...], rel_text, rel_box, probs, sines, cosines, bases[...]
    )
    g_rel[0] = text_sum.astype(jnp.bfloat16)
    g_rel[1] = box_sum.astype(jnp.bfloat16)


def attend_back(d_attended, joined, rel_map, probs, sines, cosines, bases):
    size, model = bases.shape
    pairs = model // (2 * HD)
    lanes = 2 * HD
    low = jnp.bfloat16
    whole = lambda rows: pl.BlockSpec(rows.shape, lambda i: (0, 0))
    column = pl.BlockSpec((size, lanes), lambda i: (0, i))
    band = lambda part: pl.BlockSpec((lanes, model), lambda i: (i + part * pairs, 0))
    return pl.pallas_call(
        attend_back_kernel,
        name="attend_back",
        grid=(pairs,),
        out_shape=(jax.ShapeDtypeStruct((size, model), low),) * 3
        + (jax.ShapeDtypeStruct((2, model, model), low),),
        in_specs=[column, column, column, column, band(0), band(1)]
        + [pl.BlockSpec((2, size, size), lambda i: (i, 0, 0))]
        + [whole(sines), whole(cosines), whole(bases)],
        out_specs=(column,) * 3 + (pl.BlockSpec((2, lanes, model), lambda i: (0, i, 0)),),
        compiler_params=pltpu.CompilerParams(vmem_limit_bytes=56 * 2**20),
        cost_estimate=pl.CostEstimate(
            flops=2 * 12 * size * (size * 1800 + 4 * 64 * 768),
            bytes_accessed=25 * 2**20,
            transcendentals=0,
        ),
    )(d_attended, *joined, rel_map, rel_map, probs, sines, cosines, bases)


def ahead_kernel(n, units, early, capacity, *refs):
    count = len(units)
    lists, vocabulary, pages, points, omegas, place, mask_col = refs[:7]
    weights = refs[7 : 7 + count]
    outs = refs[7 + count : 23 + count]
    asked, full, probs, sines, cosines, bases, target_out, normed_out, white_out, scale_out, low_out = outs[:11]
    q, k, v, attended, gains = outs[11:]
    swap_out, swap_in, chip_rows, answers, rows, held, rel_map, shares = refs[23 + count : 31 + count]
    ask_send, ask_recv, row_send, row_recv, own_sem, swap_send, swap_recv = refs[31 + count : 38 + count]
    hop_recv, core_recv, core_send, z_send, a_send, b_send, load_sem, out_sem = refs[38 + count :]
    low = jnp.bfloat16
    me = lax.axis_index("dp")
    core, spot, layer, step_a, step_b = place_of(me)
    layers = n // 8
    half = chip_rows.shape[1]
    page_rows = pages.shape[0]
    here = pl.ds(pl.multiple_of(core * half, 128), half)
    there = pl.ds(pl.multiple_of((1 - core) * half, 128), half)
    partner = me + 1 - 2 * core
    to_a, to_b, up, down = me + 2 * step_a, me + 2 * step_b, me + 8, me - 8
    spot_a, spot_b, spot_ab = spot + step_a, spot + step_b, spot + step_a + step_b
    low_z, high_z = layer > 0, layer < layers - 1
    cuts = (pl.ds(0, early), pl.ds(early, chip_rows.shape[0] - early))

    at = 0
    for ref, unit in zip(weights, units):
        swap_out[pl.ds(at, 24 * unit)] = ref[:, there]
        at += 24 * unit
    greet_everyone(me, n)
    swaps = [
        remote_copy(swap_out, swap_in, swap_send.at[0], swap_recv.at[0], partner),
        remote_copy(
            pages.at[:, there],
            chip_rows.at[pl.ds(2 * at + core * page_rows, page_rows)],
            swap_send.at[1],
            swap_recv.at[1],
            partner,
        ),
    ]
    for copy in swaps:
        copy.start()

    def ask(step):
        peer = lax.rem(me + step, n)
        return remote_copy(lists.at[peer], asked.at[me], ask_send.at[step], ask_recv.at[step], peer)

    def start_ask(step, carry):
        ask(step).start()
        return carry

    def wait_ask(step, carry):
        ask(step).wait()
        return carry

    lax.fori_loop(1, n, start_ask, 0)
    asked[me] = lists[me]
    chip_rows[pl.ds(2 * at + pl.multiple_of(core * page_rows, page_rows), page_rows)] = pages[:, here]
    for copy in swaps:
        copy.wait_recv()
    at = 0
    for ref, unit in zip(weights, units):
        mine, other = ref[:, here], swap_in[pl.ds(at, 24 * unit)]
        ordered = jnp.where(
            core == 0, jnp.concatenate([mine, other], 0), jnp.concatenate([other, mine], 0)
        )
        chip_rows[pl.ds(2 * at, 48 * unit)] = ordered.astype(low)
        at += 24 * unit

    def block(g, level, index):
        return full.at[level, index, cuts[g], here]

    def z_hop(g, way, level, src=None):
        return remote_copy(
            block(g, level, spot) if src is None else src, block(g, level, spot),
            z_send.at[g, way, level], hop_recv.at[g, level, spot], up if way == 0 else down,
        )

    def a_hop(g, level, src=None):
        return remote_copy(
            block(g, level, spot) if src is None else src, block(g, level, spot),
            a_send.at[g, level], hop_recv.at[g, level, spot], to_a,
        )

    def b_hop(g, kind, level, src=None):
        index = spot if kind == 0 else spot_a
        return remote_copy(
            block(g, level, index) if src is None else src, block(g, level, index),
            b_send.at[g, kind, level], hop_recv.at[g, level, index], to_b,
        )

    def core_hop(g, level, index, src=None):
        return remote_copy(
            block(g, level, index) if src is None else src, block(g, level, index),
            core_send.at[g, level, index], core_recv.at[g, level, index], partner,
        )

    def arrived(g, level, index):
        view = block(g, level, index)
        pltpu.make_async_copy(view, view, hop_recv.at[g, level, index]).wait()

    def own_copy(g):
        return pltpu.make_async_copy(chip_rows.at[cuts[g]], block(g, layer, spot), own_sem.at[g])

    def send_own(g):
        src = chip_rows.at[cuts[g]]

        @pl.when(high_z)
        def _():
            z_hop(g, 0, layer, src).start()

        @pl.when(low_z)
        def _():
            z_hop(g, 1, layer, src).start()

        a_hop(g, layer, src).start()
        b_hop(g, 0, layer, src).start()
        core_hop(g, layer, spot, src).start()
        own_copy(g).start()

    def relay_column(g, gap):
        for way, level, there_is, further in (
            (0, layer - gap, layer - gap >= 0, high_z),
            (1, layer + gap, layer + gap < layers, low_z),
        ):

            @pl.when(there_is)
            def _():
                arrived(g, level, spot)

                @pl.when(further)
                def _():
                    z_hop(g, way, level).start()

                a_hop(g, level).start()
                b_hop(g, 0, level).start()
                core_hop(g, level, spot).start()

    def at_gap(gap, visit):
        if gap == 0:
            visit(layer)
            return

        @pl.when(layer - gap >= 0)
        def _():
            visit(layer - gap)

        @pl.when(layer + gap < layers)
        def _():
            visit(layer + gap)

    def relay_a(g, gap):
        def visit(level):
            arrived(g, level, spot_a)
            b_hop(g, 1, level).start()
            core_hop(g, level, spot_a).start()

        at_gap(gap, visit)

    def relay_b(g, gap):
        for index in (spot_b, spot_ab):

            def visit(level):
                arrived(g, level, index)
                core_hop(g, level, index).start()

            at_gap(gap, visit)

    def relays(g):
        steps = [lambda: relay_a(g, 0)]
        for gap in range(1, layers):
            steps.append(lambda gap=gap: relay_column(g, gap))
            steps.append(lambda gap=gap: relay_a(g, gap))
            steps.append(lambda gap=gap: relay_b(g, gap - 1))
        steps.append(lambda: relay_b(g, layers - 1))
        return steps

    def gathered(g):
        def wait(level, carry):
            for index in range(4):
                view = full.at[level, index, cuts[g], there]
                pltpu.make_async_copy(view, view, core_recv.at[g, level, index]).wait()
            return carry

        lax.fori_loop(0, layers, wait, 0)
        own_copy(g).wait()

    send_own(0)

    lax.fori_loop(1, n, wait_ask, 0)
    rows_own = vocabulary.shape[0]
    table = vocabulary[...].astype(low)
    group = 128 // capacity

    def row_copy(peer):
        return remote_copy(
            answers.at[peer], rows.at[me], row_send.at[peer], row_recv.at[me], peer
        )

    def answer(turn, carry):
        ids = jnp.zeros((8, 128), jnp.float32)
        for j in range(group):
            ids = ids + asked[turn * group + j]
        ids = ids.T[:, 6:7]
        wanted = lax.broadcasted_iota(jnp.int32, (128, rows_own), 1) + 1
        picks = jnp.where(ids.astype(jnp.int32) == wanted, 1.0, 0.0).astype(low)
        found = dot_nn(picks, table).astype(low)
        for j in range(group):
            peer = turn * group + j
            answers[peer] = found[j * capacity : (j + 1) * capacity]

            @pl.when(peer != me)
            def _():
                row_copy(peer).start()

        return carry

    lax.fori_loop(0, n // group, answer, 0)
    first = relays(0)
    rest = relays(1)
    for step in first[:2]:
        step()
    send_own(1)
    rows[me] = answers[me]
    cols = gains.shape[1] // n
    for source in range(n):
        gains[:, source * cols : (source + 1) * cols] = (
            asked[source, :, 0:cols].astype(low).astype(jnp.float32)
        )
    lane = lax.broadcasted_iota(jnp.int32, sines.shape, 1)
    angles = jnp.where(lane < sines.shape[1] // 2, points[:, 0:1], points[:, 1:2]) * omegas[...]
    sines[...] = jnp.sin(angles)
    cosines[...] = jnp.cos(angles)
    boxes = jnp.concatenate([sines[...], cosines[...]], 1).astype(low)
    bases[...] = jnp.concatenate([cosines[...], sines[...]], 1).astype(low)
    for step in (*first[2:6], *rest[:2], *first[6:9], *rest[2:3], *first[9:], rest[4]):
        step()
    gathered(0)
    map_copy = pltpu.make_async_copy(full.at[:, :, pl.ds(0, 192)], held, load_sem.at[0])
    map_copy.start()
    deep = (early - 192) if early > 192 else 0
    for chip in range(4 * layers):
        pltpu.make_async_copy(
            full.at[chip // 4, chip % 4, pl.ds(192, deep)], rel_map.at[pl.ds(chip * deep, deep)], load_sem.at[1]
        ).start()

    def wait_row(step, carry):
        source = lax.rem(me - step + n, n)
        pltpu.make_async_copy(rows.at[source], rows.at[source], row_recv.at[source]).wait()
        return carry

    lax.fori_loop(1, n, wait_row, 0)
    slots = n * capacity
    seats = lax.broadcasted_iota(jnp.int32, (place.shape[0], slots), 1) == place[...]
    target = dot_nn(jnp.where(seats, 1.0, 0.0).astype(low), rows[...].reshape(slots, -1))
    target_out[...] = target
    mask_owner, mask_slot = mask_token // rows_own, capacity - 1
    mask_row = rows[mask_owner, mask_slot : mask_slot + 1].astype(jnp.float32)
    entry = jnp.where(mask_col[...] == 1.0, mask_row, target)
    map_copy.wait()
    model = target.shape[1]

    def weight(at):
        return held[:, :, at : at + 48].reshape(-1, model)

    embedded = entry + dot_nt(boxes, weight(0))
    normed, white, scale = layer_norm(embedded, gains[0:1], gains[1:2])
    normed_out[...], white_out[...], scale_out[...] = normed, white, scale
    normed = normed.astype(low)
    low_out[...] = normed
    for third, ref in enumerate((q, k, v)):
        ref[...] = dot_nn(normed, weight(48 + 48 * third)).astype(low)
    rest[5]()
    pltpu.make_async_copy(rel_map, rel_map, load_sem.at[1]).wait()
    pairs = model // (2 * HD)
    turns = [[] for _ in range(pairs)]
    for at, which in zip((0, 1, 2, 3, 5), (7, 3, 6, 8, 9)):
        turns[min(at, pairs - 1)].append(rest[which])

    def shares_copy(pair):
        slot = lax.rem(pair, 2)
        return pltpu.make_async_copy(shares.at[slot], probs.at[pl.ds(2 * pair, 2)], out_sem.at[slot])

    def attend(pair, carry):
        for turn in range(pairs):

            @pl.when(pair == turn)
            def _():
                for step in turns[turn]:
                    step()

        @pl.when(pair >= 2)
        def _():
            shares_copy(pair - 2).wait()

        lanes = pl.ds(pl.multiple_of(pair * 2 * HD, 2 * HD), 2 * HD)
        band = pl.ds(pl.multiple_of(pair * 2 * HD, 2 * HD), 2 * HD)
        other = pl.ds(pl.multiple_of(model + pair * 2 * HD, 2 * HD), 2 * HD)
        slot = lax.rem(pair, 2)
        result = attend_pair(
            q[:, lanes], k[:, lanes], v[:, lanes], rel_map.at[band], rel_map.at[other],
            sines, cosines, bases[...], shares.at[slot],
        )
        attended[:, lanes] = result
        shares_copy(pair).start()
        return carry

    lax.fori_loop(0, pairs, attend, 0)
    shares_copy(pairs - 2).wait()
    shares_copy(pairs - 1).wait()
    rest[10]()
    gathered(1)

    def finish(level, carry):
        for g in range(2):
            for index in (spot, spot_a, spot_b, spot_ab):
                core_hop(g, level, index).wait_send()
            a_hop(g, level).wait_send()
            b_hop(g, 0, level).wait_send()
            b_hop(g, 1, level).wait_send()

            @pl.when((level <= layer) & high_z)
            def _():
                z_hop(g, 0, level).wait_send()

            @pl.when((level >= layer) & low_z)
            def _():
                z_hop(g, 1, level).wait_send()

        return carry

    lax.fori_loop(0, layers, finish, 0)
    for copy in swaps:
        copy.wait_send()

    def finish_rows(step, carry):
        peer = lax.rem(me + step, n)
        pltpu.make_async_copy(answers.at[peer], answers.at[peer], row_send.at[peer]).wait()
        return carry

    lax.fori_loop(1, n, finish_rows, 0)


def ahead(lists, vocabulary, pages, positions, place, mask_col, weights, early, n, capacity, ident):
    model = vocabulary.shape[1]
    size = place.shape[0]
    layers = n // 8
    units = [weight.shape[0] // 24 for weight in weights]
    points = positions.astype(jnp.float32).T
    waves = model // 4
    omegas = jnp.power(10000.0, -jnp.arange(waves).astype(jnp.float32) / waves)
    omegas = jnp.concatenate([omegas, omegas])[None]
    swap = 24 * sum(units)
    chip = 2 * (swap + pages.shape[0])
    low, wide = jnp.bfloat16, jnp.float32
    dma = pltpu.SemaphoreType.DMA
    vmem = pl.BlockSpec(memory_space=pltpu.VMEM)
    anywhere = pl.BlockSpec(memory_space=pl.ANY)
    shape = jax.ShapeDtypeStruct
    rows = lambda kind: shape((size, model), kind)
    heads = model // HD
    return pl.pallas_call(
        partial(ahead_kernel, n, units, early, capacity),
        name="ahead",
        out_shape=(
            shape(lists.shape, lists.dtype),
            shape((layers, 4, chip, model), low),
            shape((heads, size, size), low),
            shape((size, 2 * waves), wide),
            shape((size, 2 * waves), wide),
            rows(low),
            rows(wide),
            rows(wide),
            rows(wide),
            shape((size, 1), wide),
            rows(low),
            rows(low),
            rows(low),
            rows(low),
            rows(low),
            shape((8, model), wide),
        ),
        in_specs=[vmem] * (7 + len(weights)),
        out_specs=(vmem, anywhere, anywhere) + (vmem,) * 13,
        scratch_shapes=[
            pltpu.VMEM((swap, model // 2), wide),
            pltpu.VMEM((swap, model // 2), wide),
            pltpu.VMEM((chip, model // 2), low),
            pltpu.VMEM((n, capacity, model), low),
            pltpu.VMEM((n, capacity, model), low),
            pltpu.VMEM((layers, 4, 192, model), low),
            pltpu.VMEM((2 * model, model), low),
            pltpu.VMEM((2, 2, size, size), low),
            dma((n,)),
            dma((n,)),
            dma((n,)),
            dma((n,)),
            dma((2,)),
            dma((2,)),
            dma((2,)),
            dma((2, layers, 4)),
            dma((2, layers, 4)),
            dma((2, layers, 4)),
            dma((2, 2, layers)),
            dma((2, layers)),
            dma((2, 2, layers)),
            dma((2,)),
            dma((2,)),
        ],
        compiler_params=pltpu.CompilerParams(
            collective_id=ident, has_side_effects=True, vmem_limit_bytes=62 * 2**20
        ),
        cost_estimate=pl.CostEstimate(
            flops=13 * 10**9, bytes_accessed=100 * 2**20, transcendentals=0
        ),
    )(lists, vocabulary, pages, points, omegas, place, mask_col, *weights)


def behind_kernel(n, early, pieces, fold, fixed, *refs):
    full, upper, probs, d_lower, white, q_in, k_in, v_in, d_attended, sines, cosines, bases = refs[:12]
    scale, gains, normed, mask_col, pos_rows, place, upper_norms, asked, loss_part = refs[12:21]
    out, table, norm_piece, totals = refs[21:25]
    rel_map, low_grads, shares, q, k, v, sent, small = refs[25:33]
    own, par, par_low, from_b, from_a, from_z, mine, gone, back = refs[33:42]
    came, small_came, message, told = refs[42:46]
    row_send, row_recv, own_sem, load_sem, pair_send, pair_recv, local_sem, share_sem = refs[46:54]
    b_send, b_recv, a_send, a_recv, z_send, z_recv, f_send, f_recv, t_send, t_recv = refs[54:]
    low, wide = jnp.bfloat16, jnp.float32
    layers = n // 8
    me = lax.axis_index("dp")
    core, spot, layer, step_a, step_b = place_of(me)
    half = own.shape[3]
    model = 2 * half
    size = normed.shape[0]
    here = pl.ds(pl.multiple_of(core * half, 128), half)
    there = pl.ds(pl.multiple_of((1 - core) * half, 128), half)
    partner = me + 1 - 2 * core
    to_a, to_b = me + 2 * step_a, me + 2 * step_b
    spot_a, spot_b, spot_ab = spot + step_a, spot + step_b, spot + step_a + step_b
    bulk = own.shape[2]
    chunk = 144
    parts = (bulk // chunk, early // chunk)
    pairs = model // (2 * HD)
    deep = early - 192

    for chip in range(4 * layers):
        pltpu.make_async_copy(
            full.at[chip // 4, chip % 4, pl.ds(192, deep)], rel_map.at[pl.ds(chip * deep, deep)], local_sem.at[0]
        ).start()
    joined = [
        pltpu.make_async_copy(src, dst, local_sem.at[1 + j])
        for j, (src, dst) in enumerate(((q_in, q), (k_in, k), (v_in, v)))
    ]
    mixing = pltpu.make_async_copy(
        full.at[:, :, pl.ds(48, 144)], low_grads.at[:, :, pl.ds(48, 144)], local_sem.at[4]
    )
    rest = size - (table.shape[0] - size)
    kept = [
        pltpu.make_async_copy(d_lower, table.at[pl.ds(0, size)], local_sem.at[5]),
        pltpu.make_async_copy(
            white.at[pl.ds(0, size - rest)], table.at[pl.ds(size, size - rest)], local_sem.at[6]
        ),
        pltpu.make_async_copy(white.at[pl.ds(size - rest, rest)], out.at[pl.ds(0, rest)], local_sem.at[7]),
    ]

    def shares_copy(pair):
        slot = lax.rem(pair, 2)
        return pltpu.make_async_copy(probs.at[pl.ds(2 * pair, 2)], shares.at[slot], share_sem.at[slot])

    for copy in (*joined, shares_copy(0), shares_copy(1), mixing, *kept):
        copy.start()

    greet_everyone(me, n)

    def pair_copy(g, index):
        if g == 0:
            src, dst = upper.at[:, index, :, there], par.at[:, index]
        else:
            src, dst = low_grads.at[:, index, :, there], par_low.at[:, index]
        return remote_copy(src, dst, pair_send.at[g, index], pair_recv.at[g, index], partner)

    def load_copy(index):
        return pltpu.make_async_copy(upper.at[:, index, :, here], own.at[:, index], load_sem.at[index])

    for index in (spot_ab, spot_a, spot_b, spot):
        pair_copy(0, index).start()
    for index in (spot_ab, spot_b, spot_a, spot):
        load_copy(index).start()

    def arrived(g, index):
        if g == 0:
            load_copy(index).wait()
        pair_copy(g, index).wait_recv()

    def total(*views):
        return sum(view[...].astype(wide) for view in views)

    def mine_at(g, level, index, part):
        cut = pl.ds(part * chunk, chunk)
        return own.at[level, index, cut] if g == 0 else low_grads.at[level, index, cut, here]

    def par_at(g, level, index, part):
        cut = pl.ds(part * chunk, chunk)
        return (par if g == 0 else par_low).at[level, index, cut]

    def cut_of(g, part):
        return pl.ds(g * bulk + part * chunk, chunk)

    def b_copy(g, kind, level, part):
        return remote_copy(
            mine_at(g, level, spot_ab if kind == 0 else spot_b, part),
            from_b.at[kind, level, cut_of(g, part)],
            b_send.at[g, kind, level, part], b_recv.at[g, kind, level, part], to_b,
        )

    def a_copy(g, level, part):
        return remote_copy(
            mine_at(g, level, spot_a, part), from_a.at[level, cut_of(g, part)],
            a_send.at[g, level, part], a_recv.at[g, level, part], to_a,
        )

    def z_copy(g, level, part):
        return remote_copy(
            mine_at(g, level, spot, part), from_z.at[layer, cut_of(g, part)],
            z_send.at[g, level, part], z_recv.at[g, layer, part], me + 8 * (level - layer),
        )

    def cross_b(g, kind):
        index = spot_ab if kind == 0 else spot_b

        def step(turn, carry):
            part, level = lax.div(turn, layers), lax.rem(turn, layers)
            view = mine_at(g, level, index, part)
            view[...] = total(view, par_at(g, level, index, part)).astype(low)
            b_copy(g, kind, level, part).start()
            return carry

        lax.fori_loop(0, layers * parts[g], step, 0)

    def cross_a(g, part):
        def step(level, carry):
            b_copy(g, 0, level, part).wait_recv()
            view = mine_at(g, level, spot_a, part)
            view[...] = total(
                view, par_at(g, level, spot_a, part), from_b.at[0, level, cut_of(g, part)]
            ).astype(low)
            a_copy(g, level, part).start()
            return carry

        lax.fori_loop(0, layers, step, 0)

    def column(g, level, part):
        b_copy(g, 1, level, part).wait_recv()
        a_copy(g, level, part).wait_recv()
        cut = cut_of(g, part)
        return total(
            mine_at(g, level, spot, part), par_at(g, level, spot, part),
            from_b.at[1, level, cut], from_a.at[level, cut],
        )

    def cross_z(g, part):
        def step(gap, carry):
            level = lax.rem(layer + gap, layers)
            view = mine_at(g, level, spot, part)
            view[...] = column(g, level, part).astype(low)
            z_copy(g, level, part).start()
            return carry

        lax.fori_loop(1, layers, step, 0)
        mine[cut_of(g, part)] = column(g, layer, part)

    def last_z(g, part):
        cut = cut_of(g, part)

        def step(gap, carry):
            level = lax.rem(layer + gap, layers)
            view = from_z.at[level, cut]
            pltpu.make_async_copy(view, view, z_recv.at[g, level, part]).wait()
            mine[cut] += total(view)
            return carry

        lax.fori_loop(1, layers, step, 0)

    for copy in joined:
        copy.wait()
    pltpu.make_async_copy(rel_map, rel_map, local_sem.at[0]).wait()

    def first_cross():
        arrived(0, spot_ab)
        cross_b(0, 0)

    def second_cross():
        arrived(0, spot_b)
        cross_b(0, 1)
        arrived(0, spot_a)
        arrived(0, spot)

    turns = [[] for _ in range(pairs)]
    turns[1], turns[2] = [first_cross], [second_cross]
    for part in range(parts[0]):
        turns[min(3 + part, pairs - 1)].append(lambda part=part: cross_a(0, part))

    def attend_turn(pair, carry):
        for at in range(pairs):

            @pl.when(pair == at)
            def _():
                for step in turns[at]:
                    step()

        shares_copy(pair).wait()
        start = pl.multiple_of(pair * 2 * HD, 2 * HD)
        lanes = pl.ds(start, 2 * HD)
        other = pl.ds(pl.multiple_of(model + start, 2 * HD), 2 * HD)
        dq, dk, dv, text_sum, box_sum = attend_back_pair(
            d_attended[:, lanes], q[:, lanes], k[:, lanes], v[:, lanes],
            rel_map.at[pl.ds(start, 2 * HD)], rel_map.at[other], shares.at[lax.rem(pair, 2)],
            sines, cosines, bases[...],
        )
        q[:, lanes], k[:, lanes], v[:, lanes] = dq, dk, dv
        for first, rows in ((0, text_sum), (model, box_sum)):
            for j in range(0, 2 * HD, 32):
                row = first + pair * 2 * HD + j
                chip = lax.div(row, deep)
                at = pl.multiple_of(192 + lax.rem(row, deep), 32)
                low_grads[lax.div(chip, 4), lax.rem(chip, 4), pl.ds(at, 32)] = rows[j : j + 32].astype(low)

        @pl.when(pair + 2 < pairs)
        def _():
            shares_copy(pair + 2).start()

        return carry

    lax.fori_loop(0, pairs, attend_turn, 0)

    mixing.wait()
    for copy in kept:
        copy.wait()
    d_first = table[0:size]
    for third, ref in enumerate((q, k, v)):
        at = 48 + 48 * third
        upstream = ref[...]
        d_first = d_first + dot_nt(upstream, low_grads[:, :, at : at + 48].reshape(-1, model))
        grad = dot_tn(normed[...], upstream).astype(low)
        low_grads[:, :, at : at + 48] = grad.reshape(layers, 4, 48, model)
    whitened = jnp.concatenate([table[size : 2 * size - rest], out[0:rest]], 0)
    d_rows, gain, bias = norm_back(d_first, whitened, scale[...], gains[0:1])
    boxes = jnp.concatenate([sines[...], cosines[...]], 1).astype(low)
    grad = dot_tn(d_rows.astype(low), boxes).astype(low)
    low_grads[:, :, 0:48] = grad.reshape(layers, 4, 48, model)
    for index in (spot_ab, spot_a, spot_b, spot):
        pair_copy(1, index).start()
    mask = mask_col[...]
    token_grads = jnp.where(mask == 1.0, pos_rows[...].astype(wide), d_rows).astype(low)
    mask_grad = jnp.sum(mask * d_rows, 0, keepdims=True)
    slots = sent.shape[0] * sent.shape[1]
    seats = lax.broadcasted_iota(jnp.int32, (size, slots), 1) == place[...]
    found = dot_tn(jnp.where(seats, 1.0, 0.0).astype(low), token_grads)
    line = lax.broadcasted_iota(jnp.int32, (slots, 1), 0)
    sent[...] = jnp.where(line == fixed, mask_grad, found).astype(low).reshape(sent.shape)
    lines = jnp.concatenate([gain, bias, upper_norms[...]], 0)
    cols = model // n
    small[...] = jnp.zeros_like(small)
    for owner in range(n):
        small[owner, 0:6, 0:cols] = lines[:, owner * cols : (owner + 1) * cols]

    def row_copies(step):
        peer = lax.rem(me + step, n)
        return [
            remote_copy(src.at[peer], dst.at[me], row_send.at[j, step], row_recv.at[j, step], peer)
            for j, (src, dst) in enumerate(((sent, came), (small, small_came)))
        ]

    def start_rows(step, carry):
        for copy in row_copies(step):
            copy.start()
        return carry

    def finish_rows(step, carry):
        for copy in row_copies(step):
            copy.wait()
        return carry

    lax.fori_loop(1, n, start_rows, 0)
    came[me] = sent[me]
    small_came[me] = small[me]

    cross_z(0, 0)
    arrived(1, spot_ab)
    cross_b(1, 0)
    arrived(1, spot_b)
    cross_b(1, 1)
    for part in range(1, parts[0]):
        cross_z(0, part)
    arrived(1, spot_a)
    arrived(1, spot)
    for part in range(parts[1]):
        cross_a(1, part)
    for part in range(parts[1]):
        cross_z(1, part)
    lax.fori_loop(1, n, finish_rows, 0)
    wanted = lax.broadcasted_iota(jnp.int32, (table.shape[0], 128), 0) + 1
    group = 128 // sent.shape[1]
    for turn in range(n // fold):
        ids = asked[turn * fold]
        for j in range(1, fold):
            ids = ids + asked[turn * fold + j]
        picks = jnp.where(ids[6:7].astype(jnp.int32) == wanted, 1.0, 0.0).astype(low)
        found = dot_nn(picks, came[turn * group : (turn + 1) * group].reshape(128, model))
        if turn == 0:
            table[...] = found
        else:
            table[...] += found
    squares = jnp.zeros((1, 1), wide)
    for part in range(4):
        rows = table.shape[0] // 4
        piece = table[part * rows : (part + 1) * rows]
        squares = squares + jnp.sum(piece * piece, keepdims=True)
    norm = small_came[0]
    for j in range(1, n):
        norm = norm + small_came[j]
    norm_piece[...] = norm
    squares = squares + jnp.sum(norm * norm, keepdims=True)
    for g in range(2):
        for part in range(parts[g]):
            last_z(g, part)

    at = 0
    for piece in pieces:
        offset, rows = 2 * at, 24 * piece
        gone[pl.ds(at, rows)] = mine[pl.ds(pl.multiple_of(offset + (1 - core) * rows, 8), rows)]
        out[pl.ds(at, rows), here] = mine[pl.ds(pl.multiple_of(offset + core * rows, 8), rows)]
        at += rows
    last = remote_copy(gone, back, f_send, f_recv, partner)
    last.start()
    squares = squares + jnp.sum(out[:, here] * out[:, here], keepdims=True)
    last.wait()
    out[:, there] = back[...]
    squares = squares + jnp.sum(back[...] * back[...], keepdims=True)
    lane = lax.broadcasted_iota(jnp.int32, message.shape, 1)
    message[...] = jnp.where(lane == 0, squares, jnp.where(lane == 1, loss_part[...], 0.0))

    def tell(step):
        peer = lax.rem(me + step, n)
        return remote_copy(message, told.at[me], t_send.at[step], t_recv.at[step], peer)

    def start_told(step, carry):
        tell(step).start()
        return carry

    def wait_told(step, carry):
        tell(step).wait()
        return carry

    lax.fori_loop(1, n, start_told, 0)
    told[me] = message[...]
    for g in range(2):
        for index in range(4):
            pair_copy(g, index).wait_send()

        def settle(turn, carry, g=g):
            part, level = lax.div(turn, layers), lax.rem(turn, layers)
            b_copy(g, 0, level, part).wait_send()
            b_copy(g, 1, level, part).wait_send()
            a_copy(g, level, part).wait_send()

            @pl.when(level != layer)
            def _():
                z_copy(g, level, part).wait_send()

            return carry

        lax.fori_loop(0, layers * parts[g], settle, 0)
    lax.fori_loop(1, n, wait_told, 0)
    total_line = told[0]
    for j in range(1, n):
        total_line = total_line + told[j]
    totals[...] = total_line


def behind(in_hbm, in_vmem, rows_own, early, pieces, capacity, fold, fixed, n, ident):
    size, model = in_vmem[0].shape
    layers = n // 8
    bulk = in_hbm[1].shape[2]
    rows = bulk + early
    half = model // 2
    most = max(bulk, early) // 144
    low, wide = jnp.bfloat16, jnp.float32
    dma = pltpu.SemaphoreType.DMA
    vmem = pl.BlockSpec(memory_space=pltpu.VMEM)
    anywhere = pl.BlockSpec(memory_space=pl.ANY)
    shape = jax.ShapeDtypeStruct
    tile = shape((8, 128), wide)
    return pl.pallas_call(
        partial(behind_kernel, n, early, pieces, fold, fixed),
        name="behind",
        out_shape=(shape((rows // 2, model), wide), shape((rows_own, model), wide), tile, tile),
        in_specs=[anywhere] * len(in_hbm) + [vmem] * len(in_vmem),
        out_specs=(vmem,) * 4,
        scratch_shapes=[
            pltpu.VMEM((2 * model, model), low),
            pltpu.VMEM((layers, 4, early, model), low),
            pltpu.VMEM((2, 2, size, size), low),
            pltpu.VMEM((size, model), low),
            pltpu.VMEM((size, model), low),
            pltpu.VMEM((size, model), low),
            pltpu.VMEM((n, capacity, model), low),
            pltpu.VMEM((n, 8, 128), wide),
            pltpu.VMEM((layers, 4, bulk, half), low),
            pltpu.VMEM((layers, 4, bulk, half), low),
            pltpu.VMEM((layers, 4, early, half), low),
            pltpu.VMEM((2, layers, rows, half), low),
            pltpu.VMEM((layers, rows, half), low),
            pltpu.VMEM((layers, rows, half), low),
            pltpu.VMEM((rows, half), wide),
            pltpu.VMEM((rows // 2, half), wide),
            pltpu.VMEM((rows // 2, half), wide),
            pltpu.VMEM((n, capacity, model), low),
            pltpu.VMEM((n, 8, 128), wide),
            pltpu.VMEM((8, 128), wide),
            pltpu.VMEM((n, 8, 128), wide),
            dma((2, n)),
            dma((2, n)),
            dma((2,)),
            dma((4,)),
            dma((2, 4)),
            dma((2, 4)),
            dma((8,)),
            dma((2,)),
            dma((2, 2, layers, most)),
            dma((2, 2, layers, most)),
            dma((2, layers, most)),
            dma((2, layers, most)),
            dma((2, layers, most)),
            dma((2, layers, most)),
            dma,
            dma,
            dma((n,)),
            dma((n,)),
        ],
        compiler_params=pltpu.CompilerParams(
            collective_id=ident, has_side_effects=True, vmem_limit_bytes=64 * 2**20 - 2**17
        ),
        cost_estimate=pl.CostEstimate(
            flops=20 * 10**9, bytes_accessed=100 * 2**20, transcendentals=0
        ),
    )(*in_hbm, *in_vmem)


def forward(weights, rows, positions):
    box_map, mix_map, rel_map, out_map, up_map, down_map, norm_rows = weights
    gains = norm_rows.astype(jnp.float32)
    sin_count = box_map.shape[1]
    sin_x, cos_x, sin_y, cos_y = sinusoids(positions, sin_count // 4)
    sines = jnp.concatenate([sin_x, sin_y], -1)
    cosines = jnp.concatenate([cos_x, cos_y], -1)
    boxes = jnp.concatenate([sines, cosines], -1).astype(jnp.bfloat16)
    bases = jnp.concatenate([cosines, sines], -1).astype(jnp.bfloat16)
    embedded = rows + dot_nt(boxes, box_map)
    first = layer_norm(embedded, gains[0], gains[1])
    normed = first[0].astype(jnp.bfloat16)
    joined = [dot_nn(normed, part).astype(jnp.bfloat16) for part in mix_map]
    attended, probs = attend(joined, rel_map, sines, cosines, bases)
    second = layer_norm(first[0] + dot_nn(attended, out_map), gains[2], gains[3])
    middle = second[0].astype(jnp.bfloat16)
    hidden_pre = [dot_nn(middle, part) for part in up_map]
    hidden = [jax.nn.gelu(part, approximate=False).astype(jnp.bfloat16) for part in hidden_pre]
    lowered = sum(dot_nn(part, weight) for part, weight in zip(hidden, down_map))
    third = layer_norm(second[0] + lowered, gains[4], gains[5])
    return {
        "sines": sines,
        "cosines": cosines,
        "boxes": boxes,
        "bases": bases,
        "first": first,
        "normed": normed,
        "joined": joined,
        "probs": probs,
        "attended": attended,
        "second": second,
        "middle": middle,
        "hidden_pre": hidden_pre,
        "hidden": hidden,
        "third": third,
    }


def backward_upper(weights, cache, d_states):
    _, _, _, out_map, up_map, down_map, norm_rows = weights
    gains = norm_rows.astype(jnp.float32)
    d_mid, gain_last, bias_last = norm_back(
        d_states, cache["third"][1], cache["third"][2], gains[4]
    )
    d_down = d_mid.astype(jnp.bfloat16)
    gelu_exact = partial(jax.nn.gelu, approximate=False)
    grad_down, grad_up, d_second = [], [], d_mid
    for pre, hidden, up, down in zip(cache["hidden_pre"], cache["hidden"], up_map, down_map):
        grad_down.append(dot_tn(hidden, d_down))
        d_pre = jax.vjp(gelu_exact, pre)[1](dot_nt(d_down, down))[0].astype(jnp.bfloat16)
        grad_up.append(dot_tn(cache["middle"], d_pre))
        d_second = d_second + dot_nt(d_pre, up)
    d_lower, gain_mid, bias_mid = norm_back(
        d_second, cache["second"][1], cache["second"][2], gains[2]
    )
    d_attn = d_lower.astype(jnp.bfloat16)
    grad_out = dot_tn(cache["attended"], d_attn)
    d_attended = dot_nt(d_attn, out_map).astype(jnp.bfloat16)
    return d_lower, d_attended, grad_out, grad_up, grad_down, [gain_mid, bias_mid, gain_last, bias_last]


def backward_lower(weights, cache, d_lower, d_attended):
    box_map, mix_map, rel_map, _, _, _, norm_rows = weights
    gains = norm_rows.astype(jnp.float32)
    *d_joined, grad_rel = attend_back(
        d_attended,
        cache["joined"],
        rel_map,
        cache["probs"],
        cache["sines"],
        cache["cosines"],
        cache["bases"],
    )
    grad_mix = [dot_tn(cache["normed"], part) for part in d_joined]
    d_first = d_lower + sum(dot_nt(part, weight) for part, weight in zip(d_joined, mix_map))
    d_embedded, gain_low, bias_low = norm_back(
        d_first, cache["first"][1], cache["first"][2], gains[0]
    )
    grad_box = dot_tn(d_embedded.astype(jnp.bfloat16), cache["boxes"])
    return d_embedded, grad_box, grad_mix, grad_rel, [gain_low, bias_low]


def per_device(
    n,
    tokens,
    positions,
    documents,
    masking,
    negative_page,
    negative_row,
    pages,
    vocabulary,
    geometry,
    mixing,
    relative,
    merging,
    widening,
    narrowing,
    scaling,
    moment_vocabulary,
    moment_geometry,
    moment_mixing,
    moment_relative,
    moment_merging,
    moment_widening,
    moment_narrowing,
    moment_scaling,
    average_vocabulary,
    average_geometry,
    average_mixing,
    average_relative,
    average_merging,
    average_widening,
    average_narrowing,
    average_scaling,
):
    size = tokens.shape[0]
    rows_own, model = vocabulary.shape
    page_rows = pages.shape[1]
    mask_float = masking.astype(jnp.float32)
    mask_col = mask_float[:, None]
    low = jnp.bfloat16
    blocks = widening.shape[1] // model
    decay = min(average_cap, (1.0 + STEP) / (10.0 + STEP))
    masters = (vocabulary, geometry, mixing, relative, merging, widening, narrowing, scaling)
    moments = (
        moment_vocabulary,
        moment_geometry,
        moment_mixing,
        moment_relative,
        moment_merging,
        moment_widening,
        moment_narrowing,
        moment_scaling,
    )
    averages = (
        average_vocabulary,
        average_geometry,
        average_mixing,
        average_relative,
        average_merging,
        average_widening,
        average_narrowing,
        average_scaling,
    )
    pieces = [
        swap_middle(geometry).T,
        *[mixing[:, k * model : (k + 1) * model] for k in range(3)],
        swap_middle(relative).T,
        merging,
        *[widening[:, k * model : (k + 1) * model] for k in range(blocks)],
        narrowing,
    ]
    bank_piece = pages.reshape(-1, model)

    def step(master, moment, average, piece, rate, factor):
        clipped = piece * factor
        velocity = momentum_decay * moment + clipped
        updated = master - rate * (clipped + momentum_decay * velocity)
        return updated, velocity, decay * average + (1.0 - decay) * updated

    def dense():
        chosen = (documents[0] == jnp.arange(DOCS)).astype(jnp.float32)
        counts = lax.psum(chosen * jnp.sum(mask_float), "dp")
        share = jnp.sum(chosen / (DOCS * jnp.maximum(counts, 1.0)))
        cast = [piece.astype(low) for piece in pieces] + [bank_piece]
        joined = lax.all_gather(jnp.concatenate(cast, 0), "dp", axis=0, tiled=False)
        weights, at = [], 0
        for piece in cast:
            weights.append(joined[:, at : at + piece.shape[0]].reshape(-1, model))
            at += piece.shape[0]
        norm_rows = lax.all_gather(scaling.astype(low), "dp", axis=1, tiled=True)
        entry = jnp.where(masking == 1, mask_token, tokens)
        lanes = 4

        def split(rows):
            return rows.reshape(rows.shape[0], lanes, -1).transpose(1, 0, 2)

        def join(rows):
            return rows.transpose(1, 0, 2).reshape(rows.shape[1], -1)

        def named_rows(part):
            table = lax.all_gather(part, "dp", axis=0, tiled=True)
            return table[tokens], table[entry]

        found = lax.map(named_rows, split(vocabulary.astype(low)))
        target_rows, entry_rows = [join(rows).astype(jnp.float32) for rows in found]
        box_map, mix_map, rel_map, out_map = weights[0], weights[1:4], weights[4], weights[5]
        up_map, down_full, bank = weights[6:-2], weights[-2], weights[-1]
        ff = len(up_map)
        down_map = [down_full[k * model : (k + 1) * model] for k in range(ff)]
        weights = (box_map, mix_map, rel_map, out_map, up_map, down_map, norm_rows)
        cache = forward(weights, entry_rows, positions)

        states_low = cache["third"][0].astype(low)
        inv_root = model ** (-0.5)
        positive = jnp.sum(states_low.astype(jnp.float32) * target_rows, -1, keepdims=True) * inv_root
        flat_index = (negative_page * page_rows + negative_row).T
        count_neg = flat_index.shape[1]
        width = bank.shape[0]
        repeated = jnp.tile(flat_index, (1, width // count_neg))
        chosen = repeated == jnp.arange(width)[None, :]
        logits = jnp.where(chosen, dot_nt(states_low, bank) * inv_root, -jnp.inf)
        highest = jnp.maximum(jnp.max(logits, -1, keepdims=True), positive)
        powers = jnp.exp(logits - highest)
        lead = jnp.exp(positive - highest)
        total = jnp.sum(powers, -1, keepdims=True) + lead
        per_token = highest + jnp.log(total) - positive
        loss_part = share * jnp.sum(mask_col * per_token)
        weight_map = (powers * (share * mask_col / total) * inv_root).astype(low)
        positive_grad = share * mask_col * (lead / total - 1.0) * inv_root
        d_states = positive_grad * target_rows + dot_nn(weight_map, bank)

        d_lower, d_attended, grad_out, grad_up, grad_down, upper_norms = backward_upper(
            weights, cache, d_states
        )
        d_embedded, grad_box, grad_mix, grad_rel, lower_norms = backward_lower(
            weights, cache, d_lower, d_attended
        )
        grad_norms = jnp.concatenate(lower_norms + upper_norms, 0)
        positive_rows = positive_grad * states_low.astype(jnp.float32)

        def summed_rows(parts):
            whole = jnp.zeros((rows_own * n, model // lanes), jnp.float32)
            whole = whole.at[entry].add(parts[0]).at[tokens].add(parts[1])
            return lax.psum_scatter(whole, "dp", scatter_dimension=0, tiled=True)

        table_piece = join(lax.map(summed_rows, (split(d_embedded), split(positive_rows))))
        norm_piece = lax.psum_scatter(grad_norms, "dp", scatter_dimension=1, tiled=True)
        grads = [grad_box, *grad_mix, grad_rel.reshape(-1, model), grad_out, *grad_up]
        grads = [grad.astype(low) for grad in [*grads, jnp.concatenate(grad_down, 0)]]
        sums = scatter(grads, n)
        reduced = (
            table_piece,
            swap_middle(sums[0].T),
            jnp.concatenate(sums[1:4], 1),
            swap_middle(sums[4].T),
            sums[5],
            jnp.concatenate(sums[6:-1], 1),
            sums[-1],
            norm_piece,
        )
        square = lax.psum(sum(jnp.sum(piece * piece) for piece in reduced), "dp")
        grad_norm = jnp.sqrt(square)
        factor = clip_limit / jnp.maximum(grad_norm, clip_limit)
        rates = (table_rate,) + (learn_rate,) * 7
        done = [step(*group, factor) for group in zip(masters, moments, averages, reduced, rates)]
        return (lax.psum(loss_part, "dp"), grad_norm) + sum(zip(*done), ())

    if n // 8 != 4 or n % 8 != 0 or merging.shape[0] != 24 or page_rows % 16 != 0 or size % 128 != 0:
        return dense()

    capacity = max(16, -(-2 * size // n) // 16 * 16)
    slots = n * capacity
    fold = 128 // capacity
    cols = scaling.shape[1]
    info = jnp.pad(scaling, ((0, 2), (0, 128 - cols)))
    lists, place = make_plan(tokens, masking, documents, info, n, rows_own, capacity, fold)
    early = 48 * (1 + 3 + relative.shape[1] // 24)
    (
        asked,
        full,
        probs,
        sines,
        cosines,
        bases,
        target,
        normed,
        white,
        scale,
        normed_low,
        *joined,
        attended,
        gains,
    ) = ahead(
        lists, vocabulary, bank_piece, positions, place, mask_col, pieces, early, n, capacity, 1
    )
    upper_grads, d_attended, d_lower, positive_rows, upper_norms, loss_part = upper(
        full.reshape(-1, *full.shape[2:]),
        attended,
        normed,
        target,
        mask_col,
        negative_page,
        negative_row,
        asked,
        documents,
        gains,
        blocks,
        page_rows,
    )
    fixed = (mask_token // rows_own) * capacity + capacity - 1
    sums, table_piece, norm_piece, totals = behind(
        (
            full,
            upper_grads.reshape(*full.shape[:2], -1, model),
            probs,
            d_lower,
            white,
            *joined,
        ),
        (
            d_attended,
            sines,
            cosines,
            bases,
            scale,
            gains,
            normed_low,
            mask_col,
            positive_rows,
            place,
            upper_norms,
            asked,
            loss_part,
        ),
        rows_own,
        early,
        (1,) + (1,) * blocks + (narrowing.shape[0] // 24, 1, 1, 1, 1, 2),
        capacity,
        fold,
        fixed,
        n,
        2,
    )

    def finish():
        grad_norm = jnp.sqrt(totals[0, 0])
        factor = clip_limit / jnp.maximum(grad_norm, clip_limit)
        last = step(
            scaling, moment_scaling, average_scaling, norm_piece[:6, :cols], learn_rate, factor
        )
        row = 24 * (1 + blocks) + narrowing.shape[0]
        layout = (
            (1, row, 1, 24, True),
            (2, row + 24, 3, 24, False),
            (3, row + 96, 1, 48, True),
            (4, 0, 1, 24, False),
            (5, 24, blocks, 24, False),
            (6, 24 * (1 + blocks), 1, narrowing.shape[0], False),
        )
        lay = lambda group: [group[0], group[1].T, group[2], group[3].T, *group[4:7]]
        groups = [lay(group) for group in (masters, moments, averages)]
        done = update_all(factor.reshape(1, 1), table_piece, sums, *groups, decay, layout)
        results = [totals[0, 1], grad_norm]
        for at, tail in zip((0, 7, 14), last):
            results += [*lay(done[at : at + 7]), tail]
        return tuple(results)

    overflow = jnp.max(asked[:, 7, 2]) > 0.0
    return lax.cond(overflow, dense, finish)


ROWS = P("dp", None)
COLS = P(None, "dp")
WEIGHTS = (ROWS, COLS, ROWS, COLS, ROWS, ROWS, ROWS, COLS)


def solution(mesh):
    return jax.shard_map(
        partial(per_device, mesh.shape["dp"]),
        mesh=mesh,
        in_specs=(P("dp"), COLS, P("dp"), P("dp"), COLS, COLS, P("dp", None, None)) + 3 * WEIGHTS,
        out_specs=(P(), P()) + 3 * WEIGHTS,
        check_vma=False,
    )
```

```python
from functools import partial

import jax
import jax.numpy as jnp
from jax import lax
from jax.experimental import pallas as pl
from jax.experimental.pallas import tpu as pltpu
from jax.sharding import PartitionSpec as P

HD = 64
DOCS = 8
STEP = 10
MESH = pl.DeviceIdType.MESH

mask_token = 103
ln_epsilon = 1e-06
momentum_decay = 0.9
learn_rate = 5000.0
table_rate = 1000000.0
clip_limit = 0.01
average_cap = 0.999


def sinusoids(positions, count):
    ranks = jnp.arange(count).astype(jnp.float32)
    omegas = jnp.power(10000.0, -ranks / count)
    angle_x = positions[0].astype(jnp.float32)[:, None] * omegas[None, :]
    angle_y = positions[1].astype(jnp.float32)[:, None] * omegas[None, :]
    return (jnp.sin(angle_x), jnp.cos(angle_x), jnp.sin(angle_y), jnp.cos(angle_y))


def layer_norm(rows, gain, bias):
    centred = rows - jnp.mean(rows, -1, keepdims=True)
    rescale = lax.rsqrt(jnp.mean(centred * centred, -1, keepdims=True) + ln_epsilon)
    whitened = centred * rescale
    return (whitened * gain + bias, whitened, rescale)


def norm_back(upstream, whitened, rescale, gain):
    scaled = upstream * gain
    inner = (
        scaled
        - jnp.mean(scaled, -1, keepdims=True)
        - whitened * jnp.mean(scaled * whitened, -1, keepdims=True)
    )
    return (
        rescale * inner,
        jnp.sum(upstream * whitened, 0, keepdims=True),
        jnp.sum(upstream, 0, keepdims=True),
    )


def swap_middle(rows, axis=0):
    count = rows.shape[axis] // 4
    cuts = [lax.slice_in_dim(rows, k * count, (k + 1) * count, axis=axis) for k in (0, 2, 1, 3)]
    return jnp.concatenate(cuts, axis)


def dot_nn(left, right):
    return lax.dot_general(
        left, right, (((1,), (0,)), ((), ())), preferred_element_type=jnp.float32
    )


def dot_tn(left, right):
    return lax.dot_general(
        left, right, (((0,), (0,)), ((), ())), preferred_element_type=jnp.float32
    )


def dot_nt(left, right):
    return lax.dot_general(
        left, right, (((1,), (1,)), ((), ())), preferred_element_type=jnp.float32
    )


def plan_kernel(
    n, rows_own, capacity, fold, tok_row, mask_row, own, info, lists, place, mask_col
):
    size = tok_row.shape[1]
    ids_row = tok_row[...]
    line = lax.broadcasted_iota(jnp.int32, (8, size), 0)
    columns = jnp.where(line == 0, ids_row, mask_row[...]).astype(jnp.float32).T
    ids_col = columns[:, 0:1].astype(jnp.int32)
    mask_col[...] = columns[:, 1:2]
    owner_col = lax.div(ids_col, rows_own)
    owner_row = lax.div(ids_row, rows_own)
    at_col = lax.broadcasted_iota(jnp.int32, (size, size), 0)
    at_row = lax.broadcasted_iota(jnp.int32, (size, size), 1)
    same = ids_col == ids_row
    first_col = jnp.min(jnp.where(same, at_row, size), 1, keepdims=True)
    first_row = jnp.min(jnp.where(same, at_col, size), 0, keepdims=True)
    leads_row = first_row == lax.broadcasted_iota(jnp.int32, (1, size), 1)
    leads_col = first_col == lax.broadcasted_iota(jnp.int32, (size, 1), 0)
    ahead = (owner_col == owner_row) & leads_row & (at_row < first_col)
    slot = jnp.sum(jnp.where(ahead, 1.0, 0.0), 1, keepdims=True).astype(jnp.int32)
    fits = slot < capacity - 1
    place[...] = jnp.where(fits, owner_col * capacity + slot, -1)
    over = jnp.max(jnp.where(fits, 0.0, 1.0), keepdims=True)
    local = ids_col - owner_col * rows_own + 1
    high = lax.div(local, 128)
    to_owner = lax.broadcasted_iota(jnp.int32, (size, n), 1) == owner_col
    to_owner = to_owner & leads_col & fits
    shift = capacity * lax.rem(own[1], fold)
    in_slot = lax.broadcasted_iota(jnp.int32, (size, 128), 1) == slot + shift
    in_slot = jnp.where(in_slot, 1.0, 0.0).astype(jnp.bfloat16)
    high_part = jnp.where(to_owner, high.astype(jnp.float32), 0.0).astype(jnp.bfloat16)
    low_part = jnp.where(to_owner, (local - high * 128).astype(jnp.float32), 0.0)
    table = dot_tn(high_part, in_slot) * 128.0 + dot_tn(low_part.astype(jnp.bfloat16), in_slot)
    lane = lax.broadcasted_iota(jnp.int32, (n, 128), 1)
    line = lax.broadcasted_iota(jnp.int32, (n, 128), 0)
    fixed = (line == mask_token // rows_own) & (lane == capacity - 1 + shift)
    table = jnp.where(fixed, float(mask_token % rows_own + 1), table)
    count = jnp.sum(mask_row[...].astype(jnp.float32), keepdims=True)
    lane = lax.broadcasted_iota(jnp.int32, (8, 128), 1)
    line = lax.broadcasted_iota(jnp.int32, (8, 128), 0)
    extra = jnp.where(lane == 0, count, jnp.where(lane == 1, own[0].astype(jnp.float32), over))
    extra = jnp.where(line == 7, extra, info[...])
    line = lax.broadcasted_iota(jnp.int32, lists.shape, 1)
    lists[...] = jnp.where(line == 6, table[:, None, :], extra[None])


def make_plan(tokens, masking, documents, info, n, rows_own, capacity, fold):
    size = tokens.shape[0]
    vmem = pl.BlockSpec(memory_space=pltpu.VMEM)
    return pl.pallas_call(
        partial(plan_kernel, n, rows_own, capacity, fold),
        name="plan",
        out_shape=(
            jax.ShapeDtypeStruct((n, 8, 128), jnp.float32),
            jax.ShapeDtypeStruct((size, 1), jnp.int32),
            jax.ShapeDtypeStruct((size, 1), jnp.float32),
        ),
        in_specs=[vmem, vmem, pl.BlockSpec(memory_space=pltpu.SMEM), vmem],
        out_specs=(vmem,) * 3,
        compiler_params=pltpu.CompilerParams(vmem_limit_bytes=32 * 2**20),
    )(
        tokens[None, :],
        masking[None, :],
        jnp.stack([documents[0], lax.axis_index("dp")]),
        info,
    )


def place_of(me):
    core = lax.rem(me, 2)
    chip = lax.div(me, 2)
    spot = lax.rem(chip, 4)
    layer = lax.div(chip, 4)
    along_a = 1 + core
    along_b = 2 - core
    step_a = along_a * (1 - 2 * lax.rem(lax.div(spot, along_a), 2))
    step_b = along_b * (1 - 2 * lax.rem(lax.div(spot, along_b), 2))
    return core, spot, layer, step_a, step_b


def remote_copy(src, dst, send, recv, device):
    return pltpu.make_async_remote_copy(
        src_ref=src, dst_ref=dst, send_sem=send, recv_sem=recv, device_id=(device,), device_id_type=MESH
    )


def greet_everyone(me, n):
    barrier = pltpu.get_barrier_semaphore()

    def greet(step, carry):
        pl.semaphore_signal(
            barrier, inc=1, device_id=(lax.rem(me + step, n),), device_id_type=MESH
        )
        return carry

    lax.fori_loop(1, n, greet, 0)
    pl.semaphore_wait(barrier, n - 1)


def flat(rows):
    return rows.reshape(-1, rows.shape[-1])


def upper_kernel(
    page_rows, full, attended, normed, target, mask_col, page, row, asked, doc, gains,
    grads, d_attended, d_lower, pos_rows, norms, loss_part,
    held, bank, slopes, hidden, scores, load_sem, store_sem,
):
    low = jnp.bfloat16
    chips, used, model = held.shape
    size = attended.shape[0]
    blocks = hidden.shape[0]
    first_row = 288
    span = model // (used - 48 - 48 * blocks)
    down_at = 48 + 48 * blocks
    loads = [
        pltpu.make_async_copy(full.at[:, pl.ds(first_row + at, many)], held.at[:, pl.ds(at, many)], load_sem.at[k])
        for k, (at, many) in enumerate(((0, 48), (48, 48 * blocks), (down_at, used - down_at)))
    ]
    loads.append(
        pltpu.make_async_copy(full.at[:, pl.ds(first_row + used, bank.shape[1])], bank, load_sem.at[3])
    )
    for copy in loads:
        copy.start()

    def up_map(k):
        return flat(held[:, 48 + 48 * k : 96 + 48 * k])

    def down_map(k):
        return flat(held[span * k : span * (k + 1), down_at:])

    loads[0].wait()
    second, white_mid, scale_mid = layer_norm(
        normed[...] + dot_nn(attended[...], flat(held[:, 0:48])), gains[2:3], gains[3:4]
    )
    middle = second.astype(low)
    loads[1].wait()
    loads[2].wait()
    for k in range(blocks):
        pre = dot_nn(middle, up_map(k))
        normal = 0.5 + 0.5 * lax.erf(pre * (0.5**0.5))
        active = (pre * normal).astype(low)
        slopes[k] = normal + pre * (jnp.exp(-0.5 * pre * pre) * 0.3989422804014327)
        hidden[k] = active
        part = dot_nn(active, down_map(k))
        lowered = part if k == 0 else lowered + part
    states, white_last, scale_last = layer_norm(second + lowered, gains[4:5], gains[5:6])
    states = states.astype(low)

    inv_root = model ** (-0.5)
    positive = jnp.sum(states.astype(jnp.float32) * target[...], -1, keepdims=True) * inv_root
    many = page.shape[0]
    seat = lax.broadcasted_iota(jnp.int32, (many, 128), 0)
    lane = lax.broadcasted_iota(jnp.int32, (many, 128), 1)
    spread = jnp.where(lax.rem(lane, many) == seat, 1.0, 0.0).astype(low)
    wanted = page_rows * dot_tn(page[...].astype(jnp.float32).astype(low), spread) + dot_tn(
        row[...].astype(jnp.float32).astype(low), spread
    )
    wanted = jnp.concatenate([wanted.astype(jnp.int32)] * 4, 1)
    column = lax.broadcasted_iota(jnp.int32, wanted.shape, 1)
    width = wanted.shape[1]
    per = width // bank.shape[1]
    parts = chips // per
    loads[3].wait()
    highest = positive
    for c in range(parts):
        raw = dot_nt(states, flat(bank[per * c : per * (c + 1)])) * inv_root
        raw = jnp.where(wanted == column + c * width, raw, -jnp.inf)
        scores[:, c * width : (c + 1) * width] = raw
        highest = jnp.maximum(highest, jnp.max(raw, -1, keepdims=True))
    lead = jnp.exp(positive - highest)
    total = lead
    for c in range(parts):
        powers = jnp.exp(scores[:, c * width : (c + 1) * width] - highest)
        scores[:, c * width : (c + 1) * width] = powers
        total = total + jnp.sum(powers, -1, keepdims=True)
    mask = mask_col[...]
    facts = asked[:, 7, :]
    counted = jnp.where(facts[:, 1:2] == doc[0].astype(jnp.float32), facts[:, 0:1], 0.0)
    share = 1.0 / (DOCS * jnp.maximum(jnp.sum(counted, keepdims=True), 1.0))
    loss_part[...] = share * jnp.sum(
        mask * (highest + jnp.log(total) - positive), keepdims=True
    )
    factor = share * mask * inv_root
    positive_grad = factor * (lead / total - 1.0)
    factor = factor / total
    pos_rows[...] = (positive_grad * states.astype(jnp.float32)).astype(pos_rows.dtype)
    d_states = positive_grad * target[...]
    for c in range(parts):
        weights = (scores[:, c * width : (c + 1) * width] * factor).astype(low)
        d_states = d_states + dot_nn(weights, flat(bank[per * c : per * (c + 1)]))

    d_mid, gain_last, bias_last = norm_back(d_states, white_last, scale_last, gains[4:5])
    d_down = d_mid.astype(low)
    d_second = d_mid
    stores = []
    for k in range(blocks):
        d_pre = (dot_nt(d_down, down_map(k)) * slopes[k]).astype(low)
        d_second = d_second + dot_nt(d_pre, up_map(k))
        grad = dot_tn(hidden[k], d_down).astype(low)
        held[span * k : span * (k + 1), down_at:] = grad.reshape(span, -1, model)
        grad = dot_tn(middle, d_pre).astype(low)
        held[:, 48 + 48 * k : 96 + 48 * k] = grad.reshape(chips, 48, model)
        for j, cut in enumerate(
            (
                (pl.ds(span * k, span), pl.ds(down_at, used - down_at)),
                (pl.ds(0, chips), pl.ds(48 + 48 * k, 48)),
            )
        ):
            stores.append(pltpu.make_async_copy(held.at[cut], grads.at[cut], store_sem.at[2 * k + j]))
            stores[-1].start()
    d_low, gain_mid, bias_mid = norm_back(d_second, white_mid, scale_mid, gains[2:3])
    d_lower[...] = d_low
    d_attn = d_low.astype(low)
    d_attended[...] = dot_nt(d_attn, flat(held[:, 0:48])).astype(low)
    held[:, 0:48] = dot_tn(attended[...], d_attn).astype(low).reshape(chips, 48, model)
    cut = (pl.ds(0, chips), pl.ds(0, 48))
    stores.append(pltpu.make_async_copy(held.at[cut], grads.at[cut], store_sem.at[2 * blocks]))
    stores[-1].start()
    for at, line in enumerate((gain_mid, bias_mid, gain_last, bias_last)):
        norms[at : at + 1] = line
    for copy in stores:
        copy.wait()


def upper(full, attended, normed, target, mask_col, page, row, asked, doc, gains, blocks, page_rows):
    size, model = normed.shape
    chips = full.shape[0]
    used = full.shape[1] - 288 - 2 * page_rows
    low, wide = jnp.bfloat16, jnp.float32
    vmem = pl.BlockSpec(memory_space=pltpu.VMEM)
    anywhere = pl.BlockSpec(memory_space=pl.ANY)
    shape = jax.ShapeDtypeStruct
    return pl.pallas_call(
        partial(upper_kernel, page_rows),
        name="upper",
        out_shape=(
            shape((chips, used, model), low),
            shape((size, model), low),
            shape((size, model), wide),
            shape((size, model), low),
            shape((4, model), wide),
            shape((1, 1), wide),
        ),
        in_specs=[anywhere]
        + [vmem] * 7
        + [pl.BlockSpec(memory_space=pltpu.SMEM), vmem],
        out_specs=(anywhere,) + (vmem,) * 5,
        scratch_shapes=[
            pltpu.VMEM((chips, used, model), low),
            pltpu.VMEM((chips, 2 * page_rows, model), low),
            pltpu.VMEM((blocks, size, model), wide),
            pltpu.VMEM((blocks, size, model), low),
            pltpu.VMEM((size, chips * 2 * page_rows), wide),
            pltpu.SemaphoreType.DMA((4,)),
            pltpu.SemaphoreType.DMA((2 * blocks + 1,)),
        ],
        compiler_params=pltpu.CompilerParams(vmem_limit_bytes=63 * 2**20),
        cost_estimate=pl.CostEstimate(
            flops=20 * 10**9, bytes_accessed=32 * 2**20, transcendentals=4 * size * model * 2
        ),
    )(full, attended, normed, target, mask_col, page, row, asked, doc, gains)


def update_kernel(decay, layout, factor, table, sums, *refs):
    masters, moments, averages = refs[0:7], refs[7:14], refs[14:21]
    fresh, speeds, smooths = refs[21:28], refs[28:35], refs[35:42]
    scale = factor[0, 0]

    def update(k, piece, rate, cut):
        clipped = piece * scale
        velocity = momentum_decay * moments[k][cut] + clipped
        updated = masters[k][cut] - rate * (clipped + momentum_decay * velocity)
        fresh[k][cut] = updated
        speeds[k][cut] = velocity
        smooths[k][cut] = decay * averages[k][cut] + (1.0 - decay) * updated

    update(0, table[...], table_rate, (slice(None), slice(None)))

    @pl.when(pl.program_id(0) == 0)
    def _():
        model = sums.shape[1]
        for k, at, blocks, rows, turned in layout:
            for block in range(blocks):
                piece = sums[at + block * rows : at + (block + 1) * rows]
                if turned:
                    update(k, swap_middle(piece, 1), learn_rate, (slice(None), slice(None)))
                else:
                    cut = (slice(None), slice(block * model, (block + 1) * model))
                    update(k, piece, learn_rate, cut)


def update_all(factor, table, sums, masters, moments, averages, decay, layout):
    steps = 6
    rows, model = table.shape
    banded = pl.BlockSpec((rows // steps, model), lambda i: (i, 0))
    whole = lambda array: pl.BlockSpec(array.shape, lambda i: (0, 0))
    group = lambda arrays: [banded] + [whole(array) for array in arrays[1:]]
    shapes = tuple(jax.ShapeDtypeStruct(array.shape, jnp.float32) for array in masters)
    return pl.pallas_call(
        partial(update_kernel, decay, layout),
        name="update",
        grid=(steps,),
        out_shape=shapes * 3,
        in_specs=[pl.BlockSpec(memory_space=pltpu.SMEM), banded, whole(sums)]
        + group(masters)
        + group(moments)
        + group(averages),
        out_specs=tuple(group(masters) * 3),
        compiler_params=pltpu.CompilerParams(vmem_limit_bytes=56 * 2**20),
        cost_estimate=pl.CostEstimate(flops=0, bytes_accessed=28 * 2**20, transcendentals=0),
    )(factor, table, sums, *masters, *moments, *averages)


def split_rows(packed, grads, n):
    out, at = [], 0
    for grad in grads:
        count = grad.shape[0] // n
        out.append(packed[at : at + count])
        at += count
    return out


def scatter(grads, n):
    model = grads[0].shape[1]
    joined = jnp.concatenate([grad.reshape(n, -1, model) for grad in grads], 1)
    joined = joined.reshape(-1, model)
    mine = lax.psum_scatter(joined, "dp", scatter_dimension=0, tiled=True)
    return split_rows(mine.astype(jnp.float32), grads, n)


def masked(rows, half):
    lane = lax.broadcasted_iota(jnp.int32, rows.shape, 1)
    keep = (lane < HD) if half == 0 else (lane >= HD)
    return jnp.where(keep, rows, jnp.zeros_like(rows))


def turn(terms, sines, cosines):
    half = sines.shape[1]
    sine, cosine = terms[:, :half], terms[:, half:]
    return jnp.concatenate(
        [sine * sines + cosine * cosines, cosine * sines - sine * cosines], 1
    ).astype(jnp.bfloat16)


def turn_back(upstream, sines, cosines):
    half = sines.shape[1]
    first, second = upstream[:, :half], upstream[:, half:]
    return jnp.concatenate(
        [first * sines - second * cosines, first * cosines + second * sines], 1
    ).astype(jnp.bfloat16)


def pick_halves(low_half, high_half):
    lane = lax.broadcasted_iota(jnp.int32, low_half.shape, 1)
    return jnp.where(lane < HD, low_half, high_half)


def attend_pair(queries, keys, values, rel_text, rel_box, sines, cosines, spread, probs):
    results = []
    for half in range(2):
        mine = masked(queries, half)
        terms = dot_nn(masked(keys, half), rel_box[...])
        box_rot = turn(terms, sines[...], cosines[...])
        terms = dot_nn(mine, rel_text[...])
        text_rot = turn(terms, sines[...], cosines[...])
        scores = dot_nt(mine, keys) + dot_nt(text_rot, spread) + dot_nt(spread, box_rot)
        scores = scores * HD ** (-0.5)
        powers = jnp.exp(scores - jnp.max(scores, -1, keepdims=True))
        shares = powers * (1.0 / jnp.sum(powers, -1, keepdims=True))
        probs[half] = shares.astype(probs.dtype)
        results.append(dot_nn(shares.astype(jnp.bfloat16), values))
    return pick_halves(*results).astype(jnp.bfloat16)


def attend_kernel(q, k, v, rel_text, rel_box, sines, cosines, bases, attended, probs):
    attended[...] = attend_pair(
        q[...], k[...], v[...], rel_text, rel_box, sines, cosines, bases[...], probs
    )


def attend(joined, rel_map, sines, cosines, bases):
    size, model = bases.shape
    pairs = model // (2 * HD)
    lanes = 2 * HD
    whole = lambda rows: pl.BlockSpec(rows.shape, lambda i: (0, 0))
    column = pl.BlockSpec((size, lanes), lambda i: (0, i))
    band = lambda part: pl.BlockSpec((lanes, model), lambda i: (i + part * pairs, 0))
    return pl.pallas_call(
        attend_kernel,
        name="attend",
        grid=(pairs,),
        out_shape=(
            jax.ShapeDtypeStruct((size, model), jnp.bfloat16),
            jax.ShapeDtypeStruct((2 * pairs, size, size), jnp.float32),
        ),
        in_specs=[column, column, column, band(0), band(1)]
        + [whole(sines), whole(cosines), whole(bases)],
        out_specs=(
            column,
            pl.BlockSpec((2, size, size), lambda i: (i, 0, 0)),
        ),
        compiler_params=pltpu.CompilerParams(vmem_limit_bytes=56 * 2**20),
        cost_estimate=pl.CostEstimate(
            flops=2 * 12 * size * (size * 1700 + 2 * 64 * 768),
            bytes_accessed=20 * 2**20,
            transcendentals=12 * size * size,
        ),
    )(*joined, rel_map, rel_map, sines, cosines, bases)


def attend_back_pair(upstream, queries, keys, values, rel_text, rel_box, probs, sines, cosines, spread):
    scale = HD ** (-0.5)
    low = jnp.bfloat16
    got = [[], [], []]
    for half in range(2):
        shares = probs[half].astype(jnp.float32)
        d_probs = dot_nt(masked(upstream, half), values)
        got[2].append(dot_tn(shares.astype(low), upstream))
        inner = jnp.sum(d_probs * shares, -1, keepdims=True)
        d_scores = (shares * (d_probs - inner)).astype(low)
        d_text = turn_back(dot_nn(d_scores, spread) * scale, sines[...], cosines[...])
        got[0].append(dot_nn(d_scores, keys) * scale + dot_nt(d_text, rel_text[...]))
        part = dot_tn(masked(queries, half), d_text)
        text_sum = part if half == 0 else text_sum + part
        turned = d_scores.T
        d_box = turn_back(dot_nn(turned, spread) * scale, sines[...], cosines[...])
        got[1].append(dot_nn(turned, queries) * scale + dot_nt(d_box, rel_box[...]))
        part = dot_tn(masked(keys, half), d_box)
        box_sum = part if half == 0 else box_sum + part
    return (*[pick_halves(*halves).astype(low) for halves in got], text_sum, box_sum)


def attend_back_kernel(
    d_out, q, k, v, rel_text, rel_box, probs, sines, cosines, bases, dq, dk, dv, g_rel
):
    dq[...], dk[...], dv[...], text_sum, box_sum = attend_back_pair(
        d_out[...], q[...], k[...], v[...], rel_text, rel_box, probs, sines, cosines, bases[...]
    )
    g_rel[0] = text_sum.astype(jnp.bfloat16)
    g_rel[1] = box_sum.astype(jnp.bfloat16)


def attend_back(d_attended, joined, rel_map, probs, sines, cosines, bases):
    size, model = bases.shape
    pairs = model // (2 * HD)
    lanes = 2 * HD
    low = jnp.bfloat16
    whole = lambda rows: pl.BlockSpec(rows.shape, lambda i: (0, 0))
    column = pl.BlockSpec((size, lanes), lambda i: (0, i))
    band = lambda part: pl.BlockSpec((lanes, model), lambda i: (i + part * pairs, 0))
    return pl.pallas_call(
        attend_back_kernel,
        name="attend_back",
        grid=(pairs,),
        out_shape=(jax.ShapeDtypeStruct((size, model), low),) * 3
        + (jax.ShapeDtypeStruct((2, model, model), low),),
        in_specs=[column, column, column, column, band(0), band(1)]
        + [pl.BlockSpec((2, size, size), lambda i: (i, 0, 0))]
        + [whole(sines), whole(cosines), whole(bases)],
        out_specs=(column,) * 3 + (pl.BlockSpec((2, lanes, model), lambda i: (0, i, 0)),),
        compiler_params=pltpu.CompilerParams(vmem_limit_bytes=56 * 2**20),
        cost_estimate=pl.CostEstimate(
            flops=2 * 12 * size * (size * 1800 + 4 * 64 * 768),
            bytes_accessed=25 * 2**20,
            transcendentals=0,
        ),
    )(d_attended, *joined, rel_map, rel_map, probs, sines, cosines, bases)


def ahead_kernel(n, layout, early, capacity, *refs):
    count = 1 + max(source for source, _, _ in layout)
    lists, vocabulary, pages, positions, omegas, place, mask_col = refs[:7]
    weights = refs[7 : 7 + count]
    outs = refs[7 + count : 23 + count]
    asked, full, probs, sines, cosines, bases, target_out, normed_out, white_out, scale_out, low_out = outs[:11]
    q, k, v, attended, gains = outs[11:]
    swap_out, swap_in, chip_rows, answers, rows, held, rel_map, shares, turned = refs[23 + count : 32 + count]
    ask_send, ask_recv, row_send, row_recv, own_sem, swap_send, swap_recv = refs[32 + count : 39 + count]
    hop_recv, core_recv, core_send, z_send, a_send, b_send, load_sem, out_sem = refs[39 + count :]
    low = jnp.bfloat16
    me = lax.axis_index("dp")
    core, spot, layer, step_a, step_b = place_of(me)
    layers = n // 8
    half = chip_rows.shape[1]
    page_rows = pages.shape[0]
    here = pl.ds(pl.multiple_of(core * half, 128), half)
    there = pl.ds(pl.multiple_of((1 - core) * half, 128), half)
    partner = me + 1 - 2 * core
    to_a, to_b, up, down = me + 2 * step_a, me + 2 * step_b, me + 8, me - 8
    spot_a, spot_b, spot_ab = spot + step_a, spot + step_b, spot + step_a + step_b
    low_z, high_z = layer > 0, layer < layers - 1
    cuts = (pl.ds(0, early), pl.ds(early, chip_rows.shape[0] - early))

    high = weights[0].shape[0]
    turned[0:high] = swap_middle(weights[0][...], 1)
    turned[high:] = swap_middle(weights[1][...], 1)

    def piece(source, column, side):
        lanes = pl.ds(pl.multiple_of(column + side * half, 128), half)
        if source == 0:
            return turned[0:high, lanes]
        return turned[high:, lanes] if source == 1 else weights[source][:, lanes]

    at = 0
    for source, column, unit in layout:
        swap_out[pl.ds(at, 24 * unit)] = piece(source, column, 1 - core)
        at += 24 * unit
    greet_everyone(me, n)
    swaps = [
        remote_copy(swap_out, swap_in, swap_send.at[0], swap_recv.at[0], partner),
        remote_copy(
            pages.at[:, there],
            chip_rows.at[pl.ds(2 * at + core * page_rows, page_rows)],
            swap_send.at[1],
            swap_recv.at[1],
            partner,
        ),
    ]
    for copy in swaps:
        copy.start()

    def ask(step):
        peer = lax.rem(me + step, n)
        return remote_copy(lists.at[peer], asked.at[me], ask_send.at[step], ask_recv.at[step], peer)

    def start_ask(step, carry):
        ask(step).start()
        return carry

    def wait_ask(step, carry):
        ask(step).wait()
        return carry

    lax.fori_loop(1, n, start_ask, 0)
    asked[me] = lists[me]
    chip_rows[pl.ds(2 * at + pl.multiple_of(core * page_rows, page_rows), page_rows)] = pages[:, here]
    for copy in swaps:
        copy.wait_recv()
    at = 0
    for source, column, unit in layout:
        mine, other = piece(source, column, core), swap_in[pl.ds(at, 24 * unit)]
        ordered = jnp.where(
            core == 0, jnp.concatenate([mine, other], 0), jnp.concatenate([other, mine], 0)
        )
        chip_rows[pl.ds(2 * at, 48 * unit)] = ordered.astype(low)
        at += 24 * unit

    def block(g, level, index):
        return full.at[level, index, cuts[g], here]

    def z_hop(g, way, level, src=None):
        return remote_copy(
            block(g, level, spot) if src is None else src, block(g, level, spot),
            z_send.at[g, way, level], hop_recv.at[g, level, spot], up if way == 0 else down,
        )

    def a_hop(g, level, src=None):
        return remote_copy(
            block(g, level, spot) if src is None else src, block(g, level, spot),
            a_send.at[g, level], hop_recv.at[g, level, spot], to_a,
        )

    def b_hop(g, kind, level, src=None):
        index = spot if kind == 0 else spot_a
        return remote_copy(
            block(g, level, index) if src is None else src, block(g, level, index),
            b_send.at[g, kind, level], hop_recv.at[g, level, index], to_b,
        )

    def core_hop(g, level, index, src=None):
        return remote_copy(
            block(g, level, index) if src is None else src, block(g, level, index),
            core_send.at[g, level, index], core_recv.at[g, level, index], partner,
        )

    def arrived(g, level, index):
        view = block(g, level, index)
        pltpu.make_async_copy(view, view, hop_recv.at[g, level, index]).wait()

    def own_copy(g):
        return pltpu.make_async_copy(chip_rows.at[cuts[g]], block(g, layer, spot), own_sem.at[g])

    def send_own(g):
        src = chip_rows.at[cuts[g]]

        @pl.when(high_z)
        def _():
            z_hop(g, 0, layer, src).start()

        @pl.when(low_z)
        def _():
            z_hop(g, 1, layer, src).start()

        a_hop(g, layer, src).start()
        b_hop(g, 0, layer, src).start()
        core_hop(g, layer, spot, src).start()
        own_copy(g).start()

    def relay_column(g, gap):
        for way, level, there_is, further in (
            (0, layer - gap, layer - gap >= 0, high_z),
            (1, layer + gap, layer + gap < layers, low_z),
        ):

            @pl.when(there_is)
            def _():
                arrived(g, level, spot)

                @pl.when(further)
                def _():
                    z_hop(g, way, level).start()

                a_hop(g, level).start()
                b_hop(g, 0, level).start()
                core_hop(g, level, spot).start()

    def at_gap(gap, visit):
        if gap == 0:
            visit(layer)
            return

        @pl.when(layer - gap >= 0)
        def _():
            visit(layer - gap)

        @pl.when(layer + gap < layers)
        def _():
            visit(layer + gap)

    def relay_a(g, gap):
        def visit(level):
            arrived(g, level, spot_a)
            b_hop(g, 1, level).start()
            core_hop(g, level, spot_a).start()

        at_gap(gap, visit)

    def relay_b(g, gap):
        for index in (spot_b, spot_ab):

            def visit(level):
                arrived(g, level, index)
                core_hop(g, level, index).start()

            at_gap(gap, visit)

    def relays(g):
        steps = [lambda: relay_a(g, 0)]
        for gap in range(1, layers):
            steps.append(lambda gap=gap: relay_column(g, gap))
            steps.append(lambda gap=gap: relay_a(g, gap))
            steps.append(lambda gap=gap: relay_b(g, gap - 1))
        steps.append(lambda: relay_b(g, layers - 1))
        return steps

    def gathered(g):
        def wait(level, carry):
            for index in range(4):
                view = full.at[level, index, cuts[g], there]
                pltpu.make_async_copy(view, view, core_recv.at[g, level, index]).wait()
            return carry

        lax.fori_loop(0, layers, wait, 0)
        own_copy(g).wait()

    send_own(0)

    lax.fori_loop(1, n, wait_ask, 0)
    rows_own = vocabulary.shape[0]
    table = vocabulary[...].astype(low)
    group = 128 // capacity

    def row_copy(peer):
        return remote_copy(
            answers.at[peer], rows.at[me], row_send.at[peer], row_recv.at[me], peer
        )

    def answer(turn, carry):
        ids = jnp.zeros((8, 128), jnp.float32)
        for j in range(group):
            ids = ids + asked[turn * group + j]
        ids = ids.T[:, 6:7]
        wanted = lax.broadcasted_iota(jnp.int32, (128, rows_own), 1) + 1
        picks = jnp.where(ids.astype(jnp.int32) == wanted, 1.0, 0.0).astype(low)
        found = dot_nn(picks, table).astype(low)
        for j in range(group):
            peer = turn * group + j
            answers[peer] = found[j * capacity : (j + 1) * capacity]

            @pl.when(peer != me)
            def _():
                row_copy(peer).start()

        return carry

    lax.fori_loop(0, n // group, answer, 0)
    first = relays(0)
    rest = relays(1)
    for step in first[:2]:
        step()
    send_own(1)
    rows[me] = answers[me]
    cols = gains.shape[1] // n
    for source in range(n):
        gains[:, source * cols : (source + 1) * cols] = (
            asked[source, :, 0:cols].astype(low).astype(jnp.float32)
        )
    lane = lax.broadcasted_iota(jnp.int32, sines.shape, 1)
    line = lax.broadcasted_iota(jnp.int32, (8, sines.shape[0]), 0)
    points = jnp.where(line == 0, positions[0:1], positions[1:2]).astype(jnp.float32).T
    angles = jnp.where(lane < sines.shape[1] // 2, points[:, 0:1], points[:, 1:2]) * omegas[...]
    sines[...] = jnp.sin(angles)
    cosines[...] = jnp.cos(angles)
    boxes = jnp.concatenate([sines[...], cosines[...]], 1).astype(low)
    bases[...] = jnp.concatenate([cosines[...], sines[...]], 1).astype(low)
    for step in (*first[2:6], *rest[:2], *first[6:9], *rest[2:3], *first[9:], rest[4]):
        step()
    gathered(0)
    map_copy = pltpu.make_async_copy(full.at[:, :, pl.ds(0, 192)], held, load_sem.at[0])
    map_copy.start()
    deep = (early - 192) if early > 192 else 0
    for chip in range(4 * layers):
        pltpu.make_async_copy(
            full.at[chip // 4, chip % 4, pl.ds(192, deep)], rel_map.at[pl.ds(chip * deep, deep)], load_sem.at[1]
        ).start()

    def wait_row(step, carry):
        source = lax.rem(me - step + n, n)
        pltpu.make_async_copy(rows.at[source], rows.at[source], row_recv.at[source]).wait()
        return carry

    lax.fori_loop(1, n, wait_row, 0)
    slots = n * capacity
    seats = lax.broadcasted_iota(jnp.int32, (place.shape[0], slots), 1) == place[...]
    target = dot_nn(jnp.where(seats, 1.0, 0.0).astype(low), rows[...].reshape(slots, -1))
    target_out[...] = target
    mask_owner, mask_slot = mask_token // rows_own, capacity - 1
    mask_row = rows[mask_owner, mask_slot : mask_slot + 1].astype(jnp.float32)
    entry = jnp.where(mask_col[...] == 1.0, mask_row, target)
    map_copy.wait()
    model = target.shape[1]

    def weight(at):
        return held[:, :, at : at + 48].reshape(-1, model)

    embedded = entry + dot_nt(boxes, weight(0))
    normed, white, scale = layer_norm(embedded, gains[0:1], gains[1:2])
    normed_out[...], white_out[...], scale_out[...] = normed, white, scale
    normed = normed.astype(low)
    low_out[...] = normed
    for third, ref in enumerate((q, k, v)):
        ref[...] = dot_nn(normed, weight(48 + 48 * third)).astype(low)
    rest[5]()
    pltpu.make_async_copy(rel_map, rel_map, load_sem.at[1]).wait()
    pairs = model // (2 * HD)
    turns = [[] for _ in range(pairs)]
    for at, which in zip((0, 1, 2, 3, 5), (7, 3, 6, 8, 9)):
        turns[min(at, pairs - 1)].append(rest[which])

    def shares_copy(pair):
        slot = lax.rem(pair, 2)
        return pltpu.make_async_copy(shares.at[slot], probs.at[pl.ds(2 * pair, 2)], out_sem.at[slot])

    def attend(pair, carry):
        for turn in range(pairs):

            @pl.when(pair == turn)
            def _():
                for step in turns[turn]:
                    step()

        @pl.when(pair >= 2)
        def _():
            shares_copy(pair - 2).wait()

        lanes = pl.ds(pl.multiple_of(pair * 2 * HD, 2 * HD), 2 * HD)
        band = pl.ds(pl.multiple_of(pair * 2 * HD, 2 * HD), 2 * HD)
        other = pl.ds(pl.multiple_of(model + pair * 2 * HD, 2 * HD), 2 * HD)
        slot = lax.rem(pair, 2)
        result = attend_pair(
            q[:, lanes], k[:, lanes], v[:, lanes], rel_map.at[band], rel_map.at[other],
            sines, cosines, bases[...], shares.at[slot],
        )
        attended[:, lanes] = result
        shares_copy(pair).start()
        return carry

    lax.fori_loop(0, pairs, attend, 0)
    shares_copy(pairs - 2).wait()
    shares_copy(pairs - 1).wait()
    rest[10]()
    gathered(1)

    def finish(level, carry):
        for g in range(2):
            for index in (spot, spot_a, spot_b, spot_ab):
                core_hop(g, level, index).wait_send()
            a_hop(g, level).wait_send()
            b_hop(g, 0, level).wait_send()
            b_hop(g, 1, level).wait_send()

            @pl.when((level <= layer) & high_z)
            def _():
                z_hop(g, 0, level).wait_send()

            @pl.when((level >= layer) & low_z)
            def _():
                z_hop(g, 1, level).wait_send()

        return carry

    lax.fori_loop(0, layers, finish, 0)
    for copy in swaps:
        copy.wait_send()

    def finish_rows(step, carry):
        peer = lax.rem(me + step, n)
        pltpu.make_async_copy(answers.at[peer], answers.at[peer], row_send.at[peer]).wait()
        return carry

    lax.fori_loop(1, n, finish_rows, 0)


def ahead(lists, vocabulary, pages, positions, place, mask_col, weights, layout, early, n, capacity, ident):
    model = vocabulary.shape[1]
    size = place.shape[0]
    layers = n // 8
    waves = model // 4
    omegas = jnp.power(10000.0, -jnp.arange(waves).astype(jnp.float32) / waves)
    omegas = jnp.concatenate([omegas, omegas])[None]
    swap = 24 * sum(unit for _, _, unit in layout)
    chip = 2 * (swap + pages.shape[0])
    low, wide = jnp.bfloat16, jnp.float32
    dma = pltpu.SemaphoreType.DMA
    vmem = pl.BlockSpec(memory_space=pltpu.VMEM)
    anywhere = pl.BlockSpec(memory_space=pl.ANY)
    shape = jax.ShapeDtypeStruct
    rows = lambda kind: shape((size, model), kind)
    heads = model // HD
    return pl.pallas_call(
        partial(ahead_kernel, n, layout, early, capacity),
        name="ahead",
        out_shape=(
            shape(lists.shape, lists.dtype),
            shape((layers, 4, chip, model), low),
            shape((heads, size, size), low),
            shape((size, 2 * waves), wide),
            shape((size, 2 * waves), wide),
            rows(low),
            rows(wide),
            rows(wide),
            rows(wide),
            shape((size, 1), wide),
            rows(low),
            rows(low),
            rows(low),
            rows(low),
            rows(low),
            shape((8, model), wide),
        ),
        in_specs=[vmem] * (7 + len(weights)),
        out_specs=(vmem, anywhere, anywhere) + (vmem,) * 13,
        scratch_shapes=[
            pltpu.VMEM((swap, model // 2), wide),
            pltpu.VMEM((swap, model // 2), wide),
            pltpu.VMEM((chip, model // 2), low),
            pltpu.VMEM((n, capacity, model), low),
            pltpu.VMEM((n, capacity, model), low),
            pltpu.VMEM((layers, 4, 192, model), low),
            pltpu.VMEM((2 * model, model), low),
            pltpu.VMEM((2, 2, size, size), low),
            pltpu.VMEM((weights[0].shape[0] + weights[1].shape[0], model), wide),
            dma((n,)),
            dma((n,)),
            dma((n,)),
            dma((n,)),
            dma((2,)),
            dma((2,)),
            dma((2,)),
            dma((2, layers, 4)),
            dma((2, layers, 4)),
            dma((2, layers, 4)),
            dma((2, 2, layers)),
            dma((2, layers)),
            dma((2, 2, layers)),
            dma((2,)),
            dma((2,)),
        ],
        compiler_params=pltpu.CompilerParams(
            collective_id=ident, has_side_effects=True, vmem_limit_bytes=62 * 2**20
        ),
        cost_estimate=pl.CostEstimate(
            flops=13 * 10**9, bytes_accessed=100 * 2**20, transcendentals=0
        ),
    )(lists, vocabulary, pages, positions, omegas, place, mask_col, *weights)


def behind_kernel(n, early, pieces, fold, fixed, *refs):
    full, upper, probs, d_lower, white, q_in, k_in, v_in, d_attended, sines, cosines, bases = refs[:12]
    scale, gains, normed, mask_col, pos_rows, place, upper_norms, asked, loss_part = refs[12:21]
    out, table, norm_piece, totals = refs[21:25]
    rel_map, low_grads, shares, q, k, v, sent, small = refs[25:33]
    own, par, par_low, from_b, from_a, from_z, chained, mine, gone, back = refs[33:43]
    came, small_came, message, told = refs[43:47]
    row_send, row_recv, load_sem, pair_send, pair_recv, local_sem, share_sem = refs[47:54]
    b_send, b_recv, a_send, a_recv, z_send, z_recv, c_send, c_recv, f_send, f_recv, t_send, t_recv = refs[54:]
    low, wide = jnp.bfloat16, jnp.float32
    layers = n // 8
    me = lax.axis_index("dp")
    core, spot, layer, step_a, step_b = place_of(me)
    half = own.shape[3]
    model = 2 * half
    size = normed.shape[0]
    here = pl.ds(pl.multiple_of(core * half, 128), half)
    there = pl.ds(pl.multiple_of((1 - core) * half, 128), half)
    partner = me + 1 - 2 * core
    to_a, to_b = me + 2 * step_a, me + 2 * step_b
    spot_a, spot_b, spot_ab = spot + step_a, spot + step_b, spot + step_a + step_b
    low_z, high_z = layer > 0, layer < layers - 1
    bulk = own.shape[2]
    chunk = 144
    parts = (bulk // chunk, early // chunk)
    pairs = model // (2 * HD)
    deep = early - 192

    for chip in range(4 * layers):
        pltpu.make_async_copy(
            full.at[chip // 4, chip % 4, pl.ds(192, deep)], rel_map.at[pl.ds(chip * deep, deep)], local_sem.at[0]
        ).start()
    joined = [
        pltpu.make_async_copy(src, dst, local_sem.at[1 + j])
        for j, (src, dst) in enumerate(((q_in, q), (k_in, k), (v_in, v)))
    ]
    mixing = pltpu.make_async_copy(
        full.at[:, :, pl.ds(48, 144)], low_grads.at[:, :, pl.ds(48, 144)], local_sem.at[4]
    )
    rest = size - (table.shape[0] - size)
    kept = [
        pltpu.make_async_copy(d_lower, table.at[pl.ds(0, size)], local_sem.at[5]),
        pltpu.make_async_copy(
            white.at[pl.ds(0, size - rest)], table.at[pl.ds(size, size - rest)], local_sem.at[6]
        ),
        pltpu.make_async_copy(white.at[pl.ds(size - rest, rest)], out.at[pl.ds(0, rest)], local_sem.at[7]),
    ]

    def shares_copy(pair):
        slot = lax.rem(pair, 2)
        return pltpu.make_async_copy(probs.at[pl.ds(2 * pair, 2)], shares.at[slot], share_sem.at[slot])

    for copy in (*joined, shares_copy(0), shares_copy(1), mixing, *kept):
        copy.start()

    greet_everyone(me, n)

    def pair_copy(g, index):
        if g == 0:
            src, dst = upper.at[:, index, :, there], par.at[:, index]
        else:
            src, dst = low_grads.at[:, index, :, there], par_low.at[:, index]
        return remote_copy(src, dst, pair_send.at[g, index], pair_recv.at[g, index], partner)

    def load_copy(index):
        return pltpu.make_async_copy(upper.at[:, index, :, here], own.at[:, index], load_sem.at[index])

    for index in (spot_ab, spot_a, spot_b, spot):
        pair_copy(0, index).start()
    for index in (spot_ab, spot_b, spot_a, spot):
        load_copy(index).start()

    def arrived(g, index):
        if g == 0:
            load_copy(index).wait()
        pair_copy(g, index).wait_recv()

    def total(*views):
        return sum(view[...].astype(wide) for view in views)

    def mine_at(g, level, index, part):
        cut = pl.ds(part * chunk, chunk)
        return own.at[level, index, cut] if g == 0 else low_grads.at[level, index, cut, here]

    def par_at(g, level, index, part):
        cut = pl.ds(part * chunk, chunk)
        return (par if g == 0 else par_low).at[level, index, cut]

    def cut_of(g, part):
        return pl.ds(g * bulk + part * chunk, chunk)

    def b_copy(g, kind, level, part):
        return remote_copy(
            mine_at(g, level, spot_ab if kind == 0 else spot_b, part),
            from_b.at[kind, level, cut_of(g, part)],
            b_send.at[g, kind, level, part], b_recv.at[g, kind, level, part], to_b,
        )

    def a_copy(g, level, part):
        return remote_copy(
            mine_at(g, level, spot_a, part), from_a.at[level, cut_of(g, part)],
            a_send.at[g, level, part], a_recv.at[g, level, part], to_a,
        )

    def z_copy(level, part):
        return remote_copy(
            mine_at(1, level, spot, part), from_z.at[layer, pl.ds(part * chunk, chunk)],
            z_send.at[level, part], z_recv.at[layer, part], me + 8 * (level - layer),
        )

    def chain_copy(way, gap, level, part):
        place = layers if way == 1 and gap == 1 else level
        return remote_copy(
            mine_at(0, level, spot, part), chained.at[place, pl.ds(part * chunk, chunk)],
            c_send.at[level, part], c_recv.at[place, part], me + (8 if way == 0 else -8),
        )

    def chain_part(place, part):
        view = chained.at[place, pl.ds(part * chunk, chunk)]
        pltpu.make_async_copy(view, view, c_recv.at[place, part]).wait()
        return total(view)

    def cross_b(g, kind):
        index = spot_ab if kind == 0 else spot_b

        def step(turn, carry):
            part, level = lax.div(turn, layers), lax.rem(turn, layers)
            view = mine_at(g, level, index, part)
            view[...] = total(view, par_at(g, level, index, part)).astype(low)
            b_copy(g, kind, level, part).start()
            return carry

        lax.fori_loop(0, layers * parts[g], step, 0)

    def cross_a(g, part):
        def step(level, carry):
            b_copy(g, 0, level, part).wait_recv()
            view = mine_at(g, level, spot_a, part)
            view[...] = total(
                view, par_at(g, level, spot_a, part), from_b.at[0, level, cut_of(g, part)]
            ).astype(low)
            a_copy(g, level, part).start()
            return carry

        lax.fori_loop(0, layers, step, 0)

    def column(g, level, part):
        b_copy(g, 1, level, part).wait_recv()
        a_copy(g, level, part).wait_recv()
        cut = cut_of(g, part)
        return total(
            mine_at(g, level, spot, part), par_at(g, level, spot, part),
            from_b.at[1, level, cut], from_a.at[level, cut],
        )

    def chain(gap):
        for way, guard, further, level in (
            (0, layer + gap < layers, low_z, layer + gap),
            (1, layer - gap >= 0, high_z, layer - gap),
        ):

            def step(part, carry, way=way, level=level, further=further):
                view = mine_at(0, level, spot, part)
                value = column(0, level, part)

                @pl.when(further)
                def _():
                    view[...] = (value + chain_part(level, part)).astype(low)

                @pl.when(jnp.logical_not(further))
                def _():
                    view[...] = value.astype(low)

                chain_copy(way, gap, level, part).start()
                return carry

            @pl.when(guard)
            def _():
                lax.fori_loop(0, parts[0], step, 0)

    def chain_end():
        def step(part, carry):
            cut = pl.ds(part * chunk, chunk)
            mine[cut] = column(0, layer, part)

            @pl.when(low_z)
            def _():
                mine[cut] += chain_part(layer, part)

            @pl.when(high_z)
            def _():
                mine[cut] += chain_part(layers, part)

            return carry

        lax.fori_loop(0, parts[0], step, 0)

    def cross_z(part):
        def step(gap, carry):
            level = lax.rem(layer + gap, layers)
            view = mine_at(1, level, spot, part)
            view[...] = column(1, level, part).astype(low)
            z_copy(level, part).start()
            return carry

        lax.fori_loop(1, layers, step, 0)
        mine[cut_of(1, part)] = column(1, layer, part)

    def last_z(part):
        def step(gap, carry):
            level = lax.rem(layer + gap, layers)
            view = from_z.at[level, pl.ds(part * chunk, chunk)]
            pltpu.make_async_copy(view, view, z_recv.at[level, part]).wait()
            mine[cut_of(1, part)] += total(view)
            return carry

        lax.fori_loop(1, layers, step, 0)

    for copy in joined:
        copy.wait()
    pltpu.make_async_copy(rel_map, rel_map, local_sem.at[0]).wait()

    def first_cross():
        arrived(0, spot_ab)
        cross_b(0, 0)

    def second_cross():
        arrived(0, spot_b)
        cross_b(0, 1)
        arrived(0, spot_a)
        arrived(0, spot)

    turns = [[] for _ in range(pairs)]
    turns[1], turns[2] = [first_cross], [second_cross]
    for part in range(parts[0]):
        turns[min(3 + part, pairs - 1)].append(lambda part=part: cross_a(0, part))

    def attend_turn(pair, carry):
        for at in range(pairs):

            @pl.when(pair == at)
            def _():
                for step in turns[at]:
                    step()

        shares_copy(pair).wait()
        start = pl.multiple_of(pair * 2 * HD, 2 * HD)
        lanes = pl.ds(start, 2 * HD)
        other = pl.ds(pl.multiple_of(model + start, 2 * HD), 2 * HD)
        dq, dk, dv, text_sum, box_sum = attend_back_pair(
            d_attended[:, lanes], q[:, lanes], k[:, lanes], v[:, lanes],
            rel_map.at[pl.ds(start, 2 * HD)], rel_map.at[other], shares.at[lax.rem(pair, 2)],
            sines, cosines, bases[...],
        )
        q[:, lanes], k[:, lanes], v[:, lanes] = dq, dk, dv
        for first, rows in ((0, text_sum), (model, box_sum)):
            for j in range(0, 2 * HD, 32):
                row = first + pair * 2 * HD + j
                chip = lax.div(row, deep)
                at = pl.multiple_of(192 + lax.rem(row, deep), 32)
                low_grads[lax.div(chip, 4), lax.rem(chip, 4), pl.ds(at, 32)] = rows[j : j + 32].astype(low)

        @pl.when(pair + 2 < pairs)
        def _():
            shares_copy(pair + 2).start()

        return carry

    lax.fori_loop(0, pairs, attend_turn, 0)

    mixing.wait()
    for copy in kept:
        copy.wait()
    d_first = table[0:size]
    for third, ref in enumerate((q, k, v)):
        at = 48 + 48 * third
        upstream = ref[...]
        d_first = d_first + dot_nt(upstream, low_grads[:, :, at : at + 48].reshape(-1, model))
        grad = dot_tn(normed[...], upstream).astype(low)
        low_grads[:, :, at : at + 48] = grad.reshape(layers, 4, 48, model)
    whitened = jnp.concatenate([table[size : 2 * size - rest], out[0:rest]], 0)
    d_rows, gain, bias = norm_back(d_first, whitened, scale[...], gains[0:1])
    mask = mask_col[...]
    token_grads = jnp.where(mask == 1.0, pos_rows[...].astype(wide), d_rows).astype(low)
    mask_grad = jnp.sum(mask * d_rows, 0, keepdims=True)
    slots = sent.shape[0] * sent.shape[1]
    seats = lax.broadcasted_iota(jnp.int32, (size, slots), 1) == place[...]
    found = dot_tn(jnp.where(seats, 1.0, 0.0).astype(low), token_grads)
    line = lax.broadcasted_iota(jnp.int32, (slots, 1), 0)
    sent[...] = jnp.where(line == fixed, mask_grad, found).astype(low).reshape(sent.shape)
    lines = jnp.concatenate([gain, bias, upper_norms[...]], 0)
    cols = model // n
    small[...] = jnp.zeros_like(small)
    for owner in range(n):
        small[owner, 0:6, 0:cols] = lines[:, owner * cols : (owner + 1) * cols]

    def row_copies(step):
        peer = lax.rem(me + step, n)
        return [
            remote_copy(src.at[peer], dst.at[me], row_send.at[j, step], row_recv.at[j, step], peer)
            for j, (src, dst) in enumerate(((sent, came), (small, small_came)))
        ]

    def start_rows(step, carry):
        for copy in row_copies(step):
            copy.start()
        return carry

    def finish_rows(step, carry):
        for copy in row_copies(step):
            copy.wait()
        return carry

    came[me] = sent[me]
    small_came[me] = small[me]

    lax.fori_loop(1, n, start_rows, 0)
    boxes = jnp.concatenate([sines[...], cosines[...]], 1).astype(low)
    grad = dot_tn(d_rows.astype(low), boxes).astype(low)
    low_grads[:, :, 0:48] = grad.reshape(layers, 4, 48, model)
    for index in (spot_ab, spot_a, spot_b, spot):
        pair_copy(1, index).start()

    arrived(1, spot_ab)
    cross_b(1, 0)
    arrived(1, spot_b)
    cross_b(1, 1)
    chain(layers - 1)
    for gap in range(layers - 2, 0, -1):
        chain(gap)
    arrived(1, spot_a)
    arrived(1, spot)
    for part in range(parts[1]):
        cross_a(1, part)
    chain_end()
    for part in range(parts[1]):
        cross_z(part)
    lax.fori_loop(1, n, finish_rows, 0)
    wanted = lax.broadcasted_iota(jnp.int32, (table.shape[0], 128), 0) + 1
    group = 128 // sent.shape[1]
    for turn in range(n // fold):
        ids = asked[turn * fold]
        for j in range(1, fold):
            ids = ids + asked[turn * fold + j]
        picks = jnp.where(ids[6:7].astype(jnp.int32) == wanted, 1.0, 0.0).astype(low)
        found = dot_nn(picks, came[turn * group : (turn + 1) * group].reshape(128, model))
        if turn == 0:
            table[...] = found
        else:
            table[...] += found
    squares = jnp.zeros((1, 1), wide)
    for part in range(4):
        rows = table.shape[0] // 4
        piece = table[part * rows : (part + 1) * rows]
        squares = squares + jnp.sum(piece * piece, keepdims=True)
    norm = small_came[0]
    for j in range(1, n):
        norm = norm + small_came[j]
    norm_piece[...] = norm
    squares = squares + jnp.sum(norm * norm, keepdims=True)
    for part in range(parts[1]):
        last_z(part)

    at = 0
    for piece in pieces:
        offset, rows = 2 * at, 24 * piece
        gone[pl.ds(at, rows)] = mine[pl.ds(pl.multiple_of(offset + (1 - core) * rows, 8), rows)]
        out[pl.ds(at, rows), here] = mine[pl.ds(pl.multiple_of(offset + core * rows, 8), rows)]
        at += rows
    last = remote_copy(gone, back, f_send, f_recv, partner)
    last.start()
    squares = squares + jnp.sum(out[:, here] * out[:, here], keepdims=True)
    last.wait()
    out[:, there] = back[...]
    squares = squares + jnp.sum(back[...] * back[...], keepdims=True)
    lane = lax.broadcasted_iota(jnp.int32, message.shape, 1)
    message[...] = jnp.where(lane == 0, squares, jnp.where(lane == 1, loss_part[...], 0.0))

    def tell(step):
        peer = lax.rem(me + step, n)
        return remote_copy(message, told.at[me], t_send.at[step], t_recv.at[step], peer)

    def start_told(step, carry):
        tell(step).start()
        return carry

    def wait_told(step, carry):
        tell(step).wait()
        return carry

    lax.fori_loop(1, n, start_told, 0)
    told[me] = message[...]
    for g in range(2):
        for index in range(4):
            pair_copy(g, index).wait_send()

        def settle(turn, carry, g=g):
            part, level = lax.div(turn, layers), lax.rem(turn, layers)
            b_copy(g, 0, level, part).wait_send()
            b_copy(g, 1, level, part).wait_send()
            a_copy(g, level, part).wait_send()

            @pl.when(level != layer)
            def _():
                if g == 0:
                    chain_copy(0, 2, level, part).wait_send()
                else:
                    z_copy(level, part).wait_send()

            return carry

        lax.fori_loop(0, layers * parts[g], settle, 0)
    lax.fori_loop(1, n, wait_told, 0)
    total_line = told[0]
    for j in range(1, n):
        total_line = total_line + told[j]
    totals[...] = total_line


def behind(in_hbm, in_vmem, rows_own, early, pieces, capacity, fold, fixed, n, ident):
    size, model = in_vmem[0].shape
    layers = n // 8
    bulk = in_hbm[1].shape[2]
    rows = bulk + early
    half = model // 2
    most = max(bulk, early) // 144
    low, wide = jnp.bfloat16, jnp.float32
    dma = pltpu.SemaphoreType.DMA
    vmem = pl.BlockSpec(memory_space=pltpu.VMEM)
    anywhere = pl.BlockSpec(memory_space=pl.ANY)
    shape = jax.ShapeDtypeStruct
    tile = shape((8, 128), wide)
    return pl.pallas_call(
        partial(behind_kernel, n, early, pieces, fold, fixed),
        name="behind",
        out_shape=(shape((rows // 2, model), wide), shape((rows_own, model), wide), tile, tile),
        in_specs=[anywhere] * len(in_hbm) + [vmem] * len(in_vmem),
        out_specs=(vmem,) * 4,
        scratch_shapes=[
            pltpu.VMEM((2 * model, model), low),
            pltpu.VMEM((layers, 4, early, model), low),
            pltpu.VMEM((2, 2, size, size), low),
            pltpu.VMEM((size, model), low),
            pltpu.VMEM((size, model), low),
            pltpu.VMEM((size, model), low),
            pltpu.VMEM((n, capacity, model), low),
            pltpu.VMEM((n, 8, 128), wide),
            pltpu.VMEM((layers, 4, bulk, half), low),
            pltpu.VMEM((layers, 4, bulk, half), low),
            pltpu.VMEM((layers, 4, early, half), low),
            pltpu.VMEM((2, layers, rows, half), low),
            pltpu.VMEM((layers, rows, half), low),
            pltpu.VMEM((layers, early, half), low),
            pltpu.VMEM((layers + 1, bulk, half), low),
            pltpu.VMEM((rows, half), wide),
            pltpu.VMEM((rows // 2, half), wide),
            pltpu.VMEM((rows // 2, half), wide),
            pltpu.VMEM((n, capacity, model), low),
            pltpu.VMEM((n, 8, 128), wide),
            pltpu.VMEM((8, 128), wide),
            pltpu.VMEM((n, 8, 128), wide),
            dma((2, n)),
            dma((2, n)),
            dma((4,)),
            dma((2, 4)),
            dma((2, 4)),
            dma((8,)),
            dma((2,)),
            dma((2, 2, layers, most)),
            dma((2, 2, layers, most)),
            dma((2, layers, most)),
            dma((2, layers, most)),
            dma((layers, most)),
            dma((layers, most)),
            dma((layers, most)),
            dma((layers + 1, most)),
            dma,
            dma,
            dma((n,)),
            dma((n,)),
        ],
        compiler_params=pltpu.CompilerParams(
            collective_id=ident, has_side_effects=True, vmem_limit_bytes=64 * 2**20 - 2**17
        ),
        cost_estimate=pl.CostEstimate(
            flops=20 * 10**9, bytes_accessed=100 * 2**20, transcendentals=0
        ),
    )(*in_hbm, *in_vmem)


def forward(weights, rows, positions):
    box_map, mix_map, rel_map, out_map, up_map, down_map, norm_rows = weights
    gains = norm_rows.astype(jnp.float32)
    sin_count = box_map.shape[1]
    sin_x, cos_x, sin_y, cos_y = sinusoids(positions, sin_count // 4)
    sines = jnp.concatenate([sin_x, sin_y], -1)
    cosines = jnp.concatenate([cos_x, cos_y], -1)
    boxes = jnp.concatenate([sines, cosines], -1).astype(jnp.bfloat16)
    bases = jnp.concatenate([cosines, sines], -1).astype(jnp.bfloat16)
    embedded = rows + dot_nt(boxes, box_map)
    first = layer_norm(embedded, gains[0], gains[1])
    normed = first[0].astype(jnp.bfloat16)
    joined = [dot_nn(normed, part).astype(jnp.bfloat16) for part in mix_map]
    attended, probs = attend(joined, rel_map, sines, cosines, bases)
    second = layer_norm(first[0] + dot_nn(attended, out_map), gains[2], gains[3])
    middle = second[0].astype(jnp.bfloat16)
    hidden_pre = [dot_nn(middle, part) for part in up_map]
    hidden = [jax.nn.gelu(part, approximate=False).astype(jnp.bfloat16) for part in hidden_pre]
    lowered = sum(dot_nn(part, weight) for part, weight in zip(hidden, down_map))
    third = layer_norm(second[0] + lowered, gains[4], gains[5])
    return {
        "sines": sines,
        "cosines": cosines,
        "boxes": boxes,
        "bases": bases,
        "first": first,
        "normed": normed,
        "joined": joined,
        "probs": probs,
        "attended": attended,
        "second": second,
        "middle": middle,
        "hidden_pre": hidden_pre,
        "hidden": hidden,
        "third": third,
    }


def backward_upper(weights, cache, d_states):
    _, _, _, out_map, up_map, down_map, norm_rows = weights
    gains = norm_rows.astype(jnp.float32)
    d_mid, gain_last, bias_last = norm_back(
        d_states, cache["third"][1], cache["third"][2], gains[4]
    )
    d_down = d_mid.astype(jnp.bfloat16)
    gelu_exact = partial(jax.nn.gelu, approximate=False)
    grad_down, grad_up, d_second = [], [], d_mid
    for pre, hidden, up, down in zip(cache["hidden_pre"], cache["hidden"], up_map, down_map):
        grad_down.append(dot_tn(hidden, d_down))
        d_pre = jax.vjp(gelu_exact, pre)[1](dot_nt(d_down, down))[0].astype(jnp.bfloat16)
        grad_up.append(dot_tn(cache["middle"], d_pre))
        d_second = d_second + dot_nt(d_pre, up)
    d_lower, gain_mid, bias_mid = norm_back(
        d_second, cache["second"][1], cache["second"][2], gains[2]
    )
    d_attn = d_lower.astype(jnp.bfloat16)
    grad_out = dot_tn(cache["attended"], d_attn)
    d_attended = dot_nt(d_attn, out_map).astype(jnp.bfloat16)
    return d_lower, d_attended, grad_out, grad_up, grad_down, [gain_mid, bias_mid, gain_last, bias_last]


def backward_lower(weights, cache, d_lower, d_attended):
    box_map, mix_map, rel_map, _, _, _, norm_rows = weights
    gains = norm_rows.astype(jnp.float32)
    *d_joined, grad_rel = attend_back(
        d_attended,
        cache["joined"],
        rel_map,
        cache["probs"],
        cache["sines"],
        cache["cosines"],
        cache["bases"],
    )
    grad_mix = [dot_tn(cache["normed"], part) for part in d_joined]
    d_first = d_lower + sum(dot_nt(part, weight) for part, weight in zip(d_joined, mix_map))
    d_embedded, gain_low, bias_low = norm_back(
        d_first, cache["first"][1], cache["first"][2], gains[0]
    )
    grad_box = dot_tn(d_embedded.astype(jnp.bfloat16), cache["boxes"])
    return d_embedded, grad_box, grad_mix, grad_rel, [gain_low, bias_low]


def per_device(
    n,
    tokens,
    positions,
    documents,
    masking,
    negative_page,
    negative_row,
    pages,
    vocabulary,
    geometry,
    mixing,
    relative,
    merging,
    widening,
    narrowing,
    scaling,
    moment_vocabulary,
    moment_geometry,
    moment_mixing,
    moment_relative,
    moment_merging,
    moment_widening,
    moment_narrowing,
    moment_scaling,
    average_vocabulary,
    average_geometry,
    average_mixing,
    average_relative,
    average_merging,
    average_widening,
    average_narrowing,
    average_scaling,
):
    size = tokens.shape[0]
    rows_own, model = vocabulary.shape
    page_rows = pages.shape[1]
    mask_float = masking.astype(jnp.float32)
    mask_col = mask_float[:, None]
    low = jnp.bfloat16
    blocks = widening.shape[1] // model
    decay = min(average_cap, (1.0 + STEP) / (10.0 + STEP))
    masters = (vocabulary, geometry, mixing, relative, merging, widening, narrowing, scaling)
    moments = (
        moment_vocabulary,
        moment_geometry,
        moment_mixing,
        moment_relative,
        moment_merging,
        moment_widening,
        moment_narrowing,
        moment_scaling,
    )
    averages = (
        average_vocabulary,
        average_geometry,
        average_mixing,
        average_relative,
        average_merging,
        average_widening,
        average_narrowing,
        average_scaling,
    )
    pieces = [
        swap_middle(geometry).T,
        *[mixing[:, k * model : (k + 1) * model] for k in range(3)],
        swap_middle(relative).T,
        merging,
        *[widening[:, k * model : (k + 1) * model] for k in range(blocks)],
        narrowing,
    ]
    bank_piece = pages.reshape(-1, model)

    def step(master, moment, average, piece, rate, factor):
        clipped = piece * factor
        velocity = momentum_decay * moment + clipped
        updated = master - rate * (clipped + momentum_decay * velocity)
        return updated, velocity, decay * average + (1.0 - decay) * updated

    def dense():
        chosen = (documents[0] == jnp.arange(DOCS)).astype(jnp.float32)
        counts = lax.psum(chosen * jnp.sum(mask_float), "dp")
        share = jnp.sum(chosen / (DOCS * jnp.maximum(counts, 1.0)))
        cast = [piece.astype(low) for piece in pieces] + [bank_piece]
        joined = lax.all_gather(jnp.concatenate(cast, 0), "dp", axis=0, tiled=False)
        weights, at = [], 0
        for piece in cast:
            weights.append(joined[:, at : at + piece.shape[0]].reshape(-1, model))
            at += piece.shape[0]
        norm_rows = lax.all_gather(scaling.astype(low), "dp", axis=1, tiled=True)
        entry = jnp.where(masking == 1, mask_token, tokens)
        lanes = 4

        def split(rows):
            return rows.reshape(rows.shape[0], lanes, -1).transpose(1, 0, 2)

        def join(rows):
            return rows.transpose(1, 0, 2).reshape(rows.shape[1], -1)

        def named_rows(part):
            table = lax.all_gather(part, "dp", axis=0, tiled=True)
            return table[tokens], table[entry]

        found = lax.map(named_rows, split(vocabulary.astype(low)))
        target_rows, entry_rows = [join(rows).astype(jnp.float32) for rows in found]
        box_map, mix_map, rel_map, out_map = weights[0], weights[1:4], weights[4], weights[5]
        up_map, down_full, bank = weights[6:-2], weights[-2], weights[-1]
        ff = len(up_map)
        down_map = [down_full[k * model : (k + 1) * model] for k in range(ff)]
        weights = (box_map, mix_map, rel_map, out_map, up_map, down_map, norm_rows)
        cache = forward(weights, entry_rows, positions)

        states_low = cache["third"][0].astype(low)
        inv_root = model ** (-0.5)
        positive = jnp.sum(states_low.astype(jnp.float32) * target_rows, -1, keepdims=True) * inv_root
        flat_index = (negative_page * page_rows + negative_row).T
        count_neg = flat_index.shape[1]
        width = bank.shape[0]
        repeated = jnp.tile(flat_index, (1, width // count_neg))
        chosen = repeated == jnp.arange(width)[None, :]
        logits = jnp.where(chosen, dot_nt(states_low, bank) * inv_root, -jnp.inf)
        highest = jnp.maximum(jnp.max(logits, -1, keepdims=True), positive)
        powers = jnp.exp(logits - highest)
        lead = jnp.exp(positive - highest)
        total = jnp.sum(powers, -1, keepdims=True) + lead
        per_token = highest + jnp.log(total) - positive
        loss_part = share * jnp.sum(mask_col * per_token)
        weight_map = (powers * (share * mask_col / total) * inv_root).astype(low)
        positive_grad = share * mask_col * (lead / total - 1.0) * inv_root
        d_states = positive_grad * target_rows + dot_nn(weight_map, bank)

        d_lower, d_attended, grad_out, grad_up, grad_down, upper_norms = backward_upper(
            weights, cache, d_states
        )
        d_embedded, grad_box, grad_mix, grad_rel, lower_norms = backward_lower(
            weights, cache, d_lower, d_attended
        )
        grad_norms = jnp.concatenate(lower_norms + upper_norms, 0)
        positive_rows = positive_grad * states_low.astype(jnp.float32)

        def summed_rows(parts):
            whole = jnp.zeros((rows_own * n, model // lanes), jnp.float32)
            whole = whole.at[entry].add(parts[0]).at[tokens].add(parts[1])
            return lax.psum_scatter(whole, "dp", scatter_dimension=0, tiled=True)

        table_piece = join(lax.map(summed_rows, (split(d_embedded), split(positive_rows))))
        norm_piece = lax.psum_scatter(grad_norms, "dp", scatter_dimension=1, tiled=True)
        grads = [grad_box, *grad_mix, grad_rel.reshape(-1, model), grad_out, *grad_up]
        grads = [grad.astype(low) for grad in [*grads, jnp.concatenate(grad_down, 0)]]
        sums = scatter(grads, n)
        reduced = (
            table_piece,
            swap_middle(sums[0].T),
            jnp.concatenate(sums[1:4], 1),
            swap_middle(sums[4].T),
            sums[5],
            jnp.concatenate(sums[6:-1], 1),
            sums[-1],
            norm_piece,
        )
        square = lax.psum(sum(jnp.sum(piece * piece) for piece in reduced), "dp")
        grad_norm = jnp.sqrt(square)
        factor = clip_limit / jnp.maximum(grad_norm, clip_limit)
        rates = (table_rate,) + (learn_rate,) * 7
        done = [step(*group, factor) for group in zip(masters, moments, averages, reduced, rates)]
        return (lax.psum(loss_part, "dp"), grad_norm) + sum(zip(*done), ())

    if n // 8 != 4 or n % 8 != 0 or merging.shape[0] != 24 or page_rows % 16 != 0 or size % 128 != 0:
        return dense()

    capacity = max(16, -(-2 * size // n) // 16 * 16)
    slots = n * capacity
    fold = 128 // capacity
    cols = scaling.shape[1]
    info = jnp.pad(scaling, ((0, 2), (0, 128 - cols)))
    lists, place, mask_col = make_plan(tokens, masking, documents, info, n, rows_own, capacity, fold)
    early = 48 * (1 + 3 + relative.shape[1] // 24)
    (
        asked,
        full,
        probs,
        sines,
        cosines,
        bases,
        target,
        normed,
        white,
        scale,
        normed_low,
        *joined,
        attended,
        gains,
    ) = ahead(
        lists,
        vocabulary,
        bank_piece,
        positions,
        place,
        mask_col,
        (geometry.T, relative.T, mixing, merging, widening, narrowing),
        (
            (0, 0, 1),
            *[(2, k * model, 1) for k in range(3)],
            (1, 0, relative.shape[1] // 24),
            (3, 0, 1),
            *[(4, k * model, 1) for k in range(blocks)],
            (5, 0, narrowing.shape[0] // 24),
        ),
        early,
        n,
        capacity,
        1,
    )
    upper_grads, d_attended, d_lower, positive_rows, upper_norms, loss_part = upper(
        full.reshape(-1, *full.shape[2:]),
        attended,
        normed,
        target,
        mask_col,
        negative_page,
        negative_row,
        asked,
        documents,
        gains,
        blocks,
        page_rows,
    )
    fixed = (mask_token // rows_own) * capacity + capacity - 1
    sums, table_piece, norm_piece, totals = behind(
        (
            full,
            upper_grads.reshape(*full.shape[:2], -1, model),
            probs,
            d_lower,
            white,
            *joined,
        ),
        (
            d_attended,
            sines,
            cosines,
            bases,
            scale,
            gains,
            normed_low,
            mask_col,
            positive_rows,
            place,
            upper_norms,
            asked,
            loss_part,
        ),
        rows_own,
        early,
        (1,) + (1,) * blocks + (narrowing.shape[0] // 24, 1, 1, 1, 1, 2),
        capacity,
        fold,
        fixed,
        n,
        2,
    )

    def finish():
        grad_norm = jnp.sqrt(totals[0, 0])
        factor = clip_limit / jnp.maximum(grad_norm, clip_limit)
        last = step(
            scaling, moment_scaling, average_scaling, norm_piece[:6, :cols], learn_rate, factor
        )
        row = 24 * (1 + blocks) + narrowing.shape[0]
        layout = (
            (1, row, 1, 24, True),
            (2, row + 24, 3, 24, False),
            (3, row + 96, 1, 48, True),
            (4, 0, 1, 24, False),
            (5, 24, blocks, 24, False),
            (6, 24 * (1 + blocks), 1, narrowing.shape[0], False),
        )
        lay = lambda group: [group[0], group[1].T, group[2], group[3].T, *group[4:7]]
        groups = [lay(group) for group in (masters, moments, averages)]
        done = update_all(factor.reshape(1, 1), table_piece, sums, *groups, decay, layout)
        results = [totals[0, 1], grad_norm]
        for at, tail in zip((0, 7, 14), last):
            results += [*lay(done[at : at + 7]), tail]
        return tuple(results)

    overflow = jnp.max(asked[:, 7, 2]) > 0.0
    return lax.cond(overflow, dense, finish)


ROWS = P("dp", None)
COLS = P(None, "dp")
WEIGHTS = (ROWS, COLS, ROWS, COLS, ROWS, ROWS, ROWS, COLS)


def solution(mesh):
    return jax.shard_map(
        partial(per_device, mesh.shape["dp"]),
        mesh=mesh,
        in_specs=(P("dp"), COLS, P("dp"), P("dp"), COLS, COLS, P("dp", None, None)) + 3 * WEIGHTS,
        out_specs=(P(), P()) + 3 * WEIGHTS,
        check_vma=False,
    )
```

```python
from functools import partial

import jax
import jax.numpy as jnp
from jax import lax
from jax.experimental import pallas as pl
from jax.experimental.pallas import tpu as pltpu
from jax.sharding import PartitionSpec as P

HD = 64
DOCS = 8
STEP = 10
MESH = pl.DeviceIdType.MESH

mask_token = 103
ln_epsilon = 1e-06
momentum_decay = 0.9
learn_rate = 5000.0
table_rate = 1000000.0
clip_limit = 0.01
average_cap = 0.999


def sinusoids(positions, count):
    ranks = jnp.arange(count).astype(jnp.float32)
    omegas = jnp.power(10000.0, -ranks / count)
    angle_x = positions[0].astype(jnp.float32)[:, None] * omegas[None, :]
    angle_y = positions[1].astype(jnp.float32)[:, None] * omegas[None, :]
    return (jnp.sin(angle_x), jnp.cos(angle_x), jnp.sin(angle_y), jnp.cos(angle_y))


def layer_norm(rows, gain, bias):
    centred = rows - jnp.mean(rows, -1, keepdims=True)
    rescale = lax.rsqrt(jnp.mean(centred * centred, -1, keepdims=True) + ln_epsilon)
    whitened = centred * rescale
    return (whitened * gain + bias, whitened, rescale)


def norm_back(upstream, whitened, rescale, gain):
    scaled = upstream * gain
    inner = (
        scaled
        - jnp.mean(scaled, -1, keepdims=True)
        - whitened * jnp.mean(scaled * whitened, -1, keepdims=True)
    )
    return (
        rescale * inner,
        jnp.sum(upstream * whitened, 0, keepdims=True),
        jnp.sum(upstream, 0, keepdims=True),
    )


def swap_middle(rows, axis=0):
    count = rows.shape[axis] // 4
    cuts = [lax.slice_in_dim(rows, k * count, (k + 1) * count, axis=axis) for k in (0, 2, 1, 3)]
    return jnp.concatenate(cuts, axis)


def dot_nn(left, right):
    return lax.dot_general(
        left, right, (((1,), (0,)), ((), ())), preferred_element_type=jnp.float32
    )


def dot_tn(left, right):
    return lax.dot_general(
        left, right, (((0,), (0,)), ((), ())), preferred_element_type=jnp.float32
    )


def dot_nt(left, right):
    return lax.dot_general(
        left, right, (((1,), (1,)), ((), ())), preferred_element_type=jnp.float32
    )


def plan_kernel(
    n, rows_own, capacity, fold, tok_row, mask_row, own, info, lists, place, mask_col
):
    size = tok_row.shape[1]
    ids_row = tok_row[...]
    line = lax.broadcasted_iota(jnp.int32, (8, size), 0)
    columns = jnp.where(line == 0, ids_row, mask_row[...]).astype(jnp.float32).T
    ids_col = columns[:, 0:1].astype(jnp.int32)
    mask_col[...] = columns[:, 1:2]
    owner_col = lax.div(ids_col, rows_own)
    owner_row = lax.div(ids_row, rows_own)
    at_col = lax.broadcasted_iota(jnp.int32, (size, size), 0)
    at_row = lax.broadcasted_iota(jnp.int32, (size, size), 1)
    same = ids_col == ids_row
    first_col = jnp.min(jnp.where(same, at_row, size), 1, keepdims=True)
    first_row = jnp.min(jnp.where(same, at_col, size), 0, keepdims=True)
    leads_row = first_row == lax.broadcasted_iota(jnp.int32, (1, size), 1)
    leads_col = first_col == lax.broadcasted_iota(jnp.int32, (size, 1), 0)
    ahead = (owner_col == owner_row) & leads_row & (at_row < first_col)
    slot = jnp.sum(jnp.where(ahead, 1.0, 0.0), 1, keepdims=True).astype(jnp.int32)
    fits = slot < capacity - 1
    place[...] = jnp.where(fits, owner_col * capacity + slot, -1)
    over = jnp.max(jnp.where(fits, 0.0, 1.0), keepdims=True)
    local = ids_col - owner_col * rows_own + 1
    high = lax.div(local, 128)
    to_owner = lax.broadcasted_iota(jnp.int32, (size, n), 1) == owner_col
    to_owner = to_owner & leads_col & fits
    shift = capacity * lax.rem(own[1], fold)
    in_slot = lax.broadcasted_iota(jnp.int32, (size, 128), 1) == slot + shift
    in_slot = jnp.where(in_slot, 1.0, 0.0).astype(jnp.bfloat16)
    high_part = jnp.where(to_owner, high.astype(jnp.float32), 0.0).astype(jnp.bfloat16)
    low_part = jnp.where(to_owner, (local - high * 128).astype(jnp.float32), 0.0)
    table = dot_tn(high_part, in_slot) * 128.0 + dot_tn(low_part.astype(jnp.bfloat16), in_slot)
    lane = lax.broadcasted_iota(jnp.int32, (n, 128), 1)
    line = lax.broadcasted_iota(jnp.int32, (n, 128), 0)
    fixed = (line == mask_token // rows_own) & (lane == capacity - 1 + shift)
    table = jnp.where(fixed, float(mask_token % rows_own + 1), table)
    count = jnp.sum(mask_row[...].astype(jnp.float32), keepdims=True)
    lane = lax.broadcasted_iota(jnp.int32, (8, 128), 1)
    line = lax.broadcasted_iota(jnp.int32, (8, 128), 0)
    extra = jnp.where(lane == 0, count, jnp.where(lane == 1, own[0].astype(jnp.float32), over))
    extra = jnp.where(line == 7, extra, info[...])
    line = lax.broadcasted_iota(jnp.int32, lists.shape, 1)
    lists[...] = jnp.where(line == 6, table[:, None, :], extra[None])


def make_plan(tokens, masking, documents, info, n, rows_own, capacity, fold):
    size = tokens.shape[0]
    vmem = pl.BlockSpec(memory_space=pltpu.VMEM)
    return pl.pallas_call(
        partial(plan_kernel, n, rows_own, capacity, fold),
        name="plan",
        out_shape=(
            jax.ShapeDtypeStruct((n, 8, 128), jnp.float32),
            jax.ShapeDtypeStruct((size, 1), jnp.int32),
            jax.ShapeDtypeStruct((size, 1), jnp.float32),
        ),
        in_specs=[vmem, vmem, pl.BlockSpec(memory_space=pltpu.SMEM), vmem],
        out_specs=(vmem,) * 3,
        compiler_params=pltpu.CompilerParams(vmem_limit_bytes=32 * 2**20),
    )(
        tokens[None, :],
        masking[None, :],
        jnp.stack([documents[0], lax.axis_index("dp")]),
        info,
    )


def place_of(me):
    core = lax.rem(me, 2)
    chip = lax.div(me, 2)
    spot = lax.rem(chip, 4)
    layer = lax.div(chip, 4)
    along_a = 1 + core
    along_b = 2 - core
    step_a = along_a * (1 - 2 * lax.rem(lax.div(spot, along_a), 2))
    step_b = along_b * (1 - 2 * lax.rem(lax.div(spot, along_b), 2))
    return core, spot, layer, step_a, step_b


def remote_copy(src, dst, send, recv, device):
    return pltpu.make_async_remote_copy(
        src_ref=src, dst_ref=dst, send_sem=send, recv_sem=recv, device_id=(device,), device_id_type=MESH
    )


def greet_everyone(me, n):
    barrier = pltpu.get_barrier_semaphore()

    def greet(step, carry):
        pl.semaphore_signal(
            barrier, inc=1, device_id=(lax.rem(me + step, n),), device_id_type=MESH
        )
        return carry

    lax.fori_loop(1, n, greet, 0)
    pl.semaphore_wait(barrier, n - 1)


def flat(rows):
    return rows.reshape(-1, rows.shape[-1])


def upper_kernel(
    page_rows, full, attended, normed, target, mask_col, page, row, asked, doc, gains,
    grads, d_attended, d_lower, pos_rows, norms, loss_part,
    held, bank, slopes, hidden, scores, load_sem, store_sem,
):
    low = jnp.bfloat16
    chips, used, model = held.shape
    size = attended.shape[0]
    blocks = hidden.shape[0]
    first_row = 288
    span = model // (used - 48 - 48 * blocks)
    down_at = 48 + 48 * blocks
    loads = [
        pltpu.make_async_copy(full.at[:, pl.ds(first_row + at, many)], held.at[:, pl.ds(at, many)], load_sem.at[k])
        for k, (at, many) in enumerate(((0, 48), (48, 48 * blocks), (down_at, used - down_at)))
    ]
    loads.append(
        pltpu.make_async_copy(full.at[:, pl.ds(first_row + used, bank.shape[1])], bank, load_sem.at[3])
    )
    for copy in loads:
        copy.start()

    def up_map(k):
        return flat(held[:, 48 + 48 * k : 96 + 48 * k])

    def down_map(k):
        return flat(held[span * k : span * (k + 1), down_at:])

    loads[0].wait()
    second, white_mid, scale_mid = layer_norm(
        normed[...] + dot_nn(attended[...], flat(held[:, 0:48])), gains[2:3], gains[3:4]
    )
    middle = second.astype(low)
    loads[1].wait()
    for k in range(blocks):
        pre = dot_nn(middle, up_map(k))
        normal = 0.5 + 0.5 * lax.erf(pre * (0.5**0.5))
        active = (pre * normal).astype(low)
        slopes[k] = normal + pre * (jnp.exp(-0.5 * pre * pre) * 0.3989422804014327)
        hidden[k] = active
        if k == 0:
            loads[2].wait()
        part = dot_nn(active, down_map(k))
        lowered = part if k == 0 else lowered + part
    states, white_last, scale_last = layer_norm(second + lowered, gains[4:5], gains[5:6])
    states = states.astype(low)

    inv_root = model ** (-0.5)
    positive = jnp.sum(states.astype(jnp.float32) * target[...], -1, keepdims=True) * inv_root
    many = page.shape[0]
    seat = lax.broadcasted_iota(jnp.int32, (many, 128), 0)
    lane = lax.broadcasted_iota(jnp.int32, (many, 128), 1)
    spread = jnp.where(lax.rem(lane, many) == seat, 1.0, 0.0).astype(low)
    wanted = page_rows * dot_tn(page[...].astype(jnp.float32).astype(low), spread) + dot_tn(
        row[...].astype(jnp.float32).astype(low), spread
    )
    wanted = jnp.concatenate([wanted.astype(jnp.int32)] * 4, 1)
    column = lax.broadcasted_iota(jnp.int32, wanted.shape, 1)
    width = wanted.shape[1]
    per = width // bank.shape[1]
    parts = chips // per
    loads[3].wait()
    highest = positive
    for c in range(parts):
        raw = dot_nt(states, flat(bank[per * c : per * (c + 1)])) * inv_root
        raw = jnp.where(wanted == column + c * width, raw, -jnp.inf)
        scores[:, c * width : (c + 1) * width] = raw
        highest = jnp.maximum(highest, jnp.max(raw, -1, keepdims=True))
    lead = jnp.exp(positive - highest)
    total = lead
    for c in range(parts):
        powers = jnp.exp(scores[:, c * width : (c + 1) * width] - highest)
        scores[:, c * width : (c + 1) * width] = powers
        total = total + jnp.sum(powers, -1, keepdims=True)
    mask = mask_col[...]
    facts = asked[:, 7, :]
    counted = jnp.where(facts[:, 1:2] == doc[0].astype(jnp.float32), facts[:, 0:1], 0.0)
    share = 1.0 / (DOCS * jnp.maximum(jnp.sum(counted, keepdims=True), 1.0))
    loss_part[...] = share * jnp.sum(
        mask * (highest + jnp.log(total) - positive), keepdims=True
    )
    factor = share * mask * inv_root
    positive_grad = factor * (lead / total - 1.0)
    factor = factor / total
    pos_rows[...] = (positive_grad * states.astype(jnp.float32)).astype(pos_rows.dtype)
    d_states = positive_grad * target[...]
    for c in range(parts):
        weights = (scores[:, c * width : (c + 1) * width] * factor).astype(low)
        d_states = d_states + dot_nn(weights, flat(bank[per * c : per * (c + 1)]))

    d_mid, gain_last, bias_last = norm_back(d_states, white_last, scale_last, gains[4:5])
    d_down = d_mid.astype(low)
    d_second = d_mid
    stores = []
    for k in range(blocks):
        d_pre = (dot_nt(d_down, down_map(k)) * slopes[k]).astype(low)
        d_second = d_second + dot_nt(d_pre, up_map(k))
        grad = dot_tn(hidden[k], d_down).astype(low)
        held[span * k : span * (k + 1), down_at:] = grad.reshape(span, -1, model)
        grad = dot_tn(middle, d_pre).astype(low)
        held[:, 48 + 48 * k : 96 + 48 * k] = grad.reshape(chips, 48, model)
        for j, cut in enumerate(
            (
                (pl.ds(span * k, span), pl.ds(down_at, used - down_at)),
                (pl.ds(0, chips), pl.ds(48 + 48 * k, 48)),
            )
        ):
            stores.append(pltpu.make_async_copy(held.at[cut], grads.at[cut], store_sem.at[2 * k + j]))
            stores[-1].start()
    d_low, gain_mid, bias_mid = norm_back(d_second, white_mid, scale_mid, gains[2:3])
    d_lower[...] = d_low
    d_attn = d_low.astype(low)
    d_attended[...] = dot_nt(d_attn, flat(held[:, 0:48])).astype(low)
    held[:, 0:48] = dot_tn(attended[...], d_attn).astype(low).reshape(chips, 48, model)
    cut = (pl.ds(0, chips), pl.ds(0, 48))
    stores.append(pltpu.make_async_copy(held.at[cut], grads.at[cut], store_sem.at[2 * blocks]))
    stores[-1].start()
    for at, line in enumerate((gain_mid, bias_mid, gain_last, bias_last)):
        norms[at : at + 1] = line
    for copy in stores:
        copy.wait()


def upper(full, attended, normed, target, mask_col, page, row, asked, doc, gains, blocks, page_rows):
    size, model = normed.shape
    chips = full.shape[0]
    used = full.shape[1] - 288 - 2 * page_rows
    low, wide = jnp.bfloat16, jnp.float32
    vmem = pl.BlockSpec(memory_space=pltpu.VMEM)
    anywhere = pl.BlockSpec(memory_space=pl.ANY)
    shape = jax.ShapeDtypeStruct
    return pl.pallas_call(
        partial(upper_kernel, page_rows),
        name="upper",
        out_shape=(
            shape((chips, used, model), low),
            shape((size, model), low),
            shape((size, model), wide),
            shape((size, model), low),
            shape((4, model), wide),
            shape((1, 1), wide),
        ),
        in_specs=[anywhere]
        + [vmem] * 7
        + [pl.BlockSpec(memory_space=pltpu.SMEM), vmem],
        out_specs=(anywhere,) + (vmem,) * 5,
        scratch_shapes=[
            pltpu.VMEM((chips, used, model), low),
            pltpu.VMEM((chips, 2 * page_rows, model), low),
            pltpu.VMEM((blocks, size, model), wide),
            pltpu.VMEM((blocks, size, model), low),
            pltpu.VMEM((size, chips * 2 * page_rows), wide),
            pltpu.SemaphoreType.DMA((4,)),
            pltpu.SemaphoreType.DMA((2 * blocks + 1,)),
        ],
        compiler_params=pltpu.CompilerParams(vmem_limit_bytes=63 * 2**20),
        cost_estimate=pl.CostEstimate(
            flops=20 * 10**9, bytes_accessed=32 * 2**20, transcendentals=4 * size * model * 2
        ),
    )(full, attended, normed, target, mask_col, page, row, asked, doc, gains)


def update_kernel(decay, layout, factor, table, sums, *refs):
    masters, moments, averages = refs[0:7], refs[7:14], refs[14:21]
    fresh, speeds, smooths = refs[21:28], refs[28:35], refs[35:42]
    scale = factor[0, 0]

    def update(k, piece, rate, cut):
        clipped = piece * scale
        velocity = momentum_decay * moments[k][cut] + clipped
        updated = masters[k][cut] - rate * (clipped + momentum_decay * velocity)
        fresh[k][cut] = updated
        speeds[k][cut] = velocity
        smooths[k][cut] = decay * averages[k][cut] + (1.0 - decay) * updated

    update(0, table[...], table_rate, (slice(None), slice(None)))

    @pl.when(pl.program_id(0) == 0)
    def _():
        model = sums.shape[1]
        for k, at, blocks, rows, turned in layout:
            for block in range(blocks):
                piece = sums[at + block * rows : at + (block + 1) * rows]
                if turned:
                    update(k, swap_middle(piece, 1), learn_rate, (slice(None), slice(None)))
                else:
                    cut = (slice(None), slice(block * model, (block + 1) * model))
                    update(k, piece, learn_rate, cut)


def update_all(factor, table, sums, masters, moments, averages, decay, layout):
    steps = 4
    rows, model = table.shape
    banded = pl.BlockSpec((rows // steps, model), lambda i: (i, 0))
    whole = lambda array: pl.BlockSpec(array.shape, lambda i: (0, 0))
    group = lambda arrays: [banded] + [whole(array) for array in arrays[1:]]
    shapes = tuple(jax.ShapeDtypeStruct(array.shape, jnp.float32) for array in masters)
    return pl.pallas_call(
        partial(update_kernel, decay, layout),
        name="update",
        grid=(steps,),
        out_shape=shapes * 3,
        in_specs=[pl.BlockSpec(memory_space=pltpu.SMEM), banded, whole(sums)]
        + group(masters)
        + group(moments)
        + group(averages),
        out_specs=tuple(group(masters) * 3),
        compiler_params=pltpu.CompilerParams(vmem_limit_bytes=56 * 2**20),
        cost_estimate=pl.CostEstimate(flops=0, bytes_accessed=28 * 2**20, transcendentals=0),
    )(factor, table, sums, *masters, *moments, *averages)


def split_rows(packed, grads, n):
    out, at = [], 0
    for grad in grads:
        count = grad.shape[0] // n
        out.append(packed[at : at + count])
        at += count
    return out


def scatter(grads, n):
    model = grads[0].shape[1]
    joined = jnp.concatenate([grad.reshape(n, -1, model) for grad in grads], 1)
    joined = joined.reshape(-1, model)
    mine = lax.psum_scatter(joined, "dp", scatter_dimension=0, tiled=True)
    return split_rows(mine.astype(jnp.float32), grads, n)


def masked(rows, half):
    lane = lax.broadcasted_iota(jnp.int32, rows.shape, 1)
    keep = (lane < HD) if half == 0 else (lane >= HD)
    return jnp.where(keep, rows, jnp.zeros_like(rows))


def turn(terms, sines, cosines):
    half = sines.shape[1]
    sine, cosine = terms[:, :half], terms[:, half:]
    return jnp.concatenate(
        [sine * sines + cosine * cosines, cosine * sines - sine * cosines], 1
    ).astype(jnp.bfloat16)


def turn_back(upstream, sines, cosines):
    half = sines.shape[1]
    first, second = upstream[:, :half], upstream[:, half:]
    return jnp.concatenate(
        [first * sines - second * cosines, first * cosines + second * sines], 1
    ).astype(jnp.bfloat16)


def pick_halves(low_half, high_half):
    lane = lax.broadcasted_iota(jnp.int32, low_half.shape, 1)
    return jnp.where(lane < HD, low_half, high_half)


def attend_pair(queries, keys, values, rel_text, rel_box, sines, cosines, spread, probs):
    results = []
    for half in range(2):
        mine = masked(queries, half)
        terms = dot_nn(masked(keys, half), rel_box[...])
        box_rot = turn(terms, sines[...], cosines[...])
        terms = dot_nn(mine, rel_text[...])
        text_rot = turn(terms, sines[...], cosines[...])
        scores = dot_nt(mine, keys) + dot_nt(text_rot, spread) + dot_nt(spread, box_rot)
        scores = scores * HD ** (-0.5)
        powers = jnp.exp(scores - jnp.max(scores, -1, keepdims=True))
        shares = powers * (1.0 / jnp.sum(powers, -1, keepdims=True))
        probs[half] = shares.astype(probs.dtype)
        results.append(dot_nn(shares.astype(jnp.bfloat16), values))
    return pick_halves(*results).astype(jnp.bfloat16)


def attend_kernel(q, k, v, rel_text, rel_box, sines, cosines, bases, attended, probs):
    attended[...] = attend_pair(
        q[...], k[...], v[...], rel_text, rel_box, sines, cosines, bases[...], probs
    )


def attend(joined, rel_map, sines, cosines, bases):
    size, model = bases.shape
    pairs = model // (2 * HD)
    lanes = 2 * HD
    whole = lambda rows: pl.BlockSpec(rows.shape, lambda i: (0, 0))
    column = pl.BlockSpec((size, lanes), lambda i: (0, i))
    band = lambda part: pl.BlockSpec((lanes, model), lambda i: (i + part * pairs, 0))
    return pl.pallas_call(
        attend_kernel,
        name="attend",
        grid=(pairs,),
        out_shape=(
            jax.ShapeDtypeStruct((size, model), jnp.bfloat16),
            jax.ShapeDtypeStruct((2 * pairs, size, size), jnp.float32),
        ),
        in_specs=[column, column, column, band(0), band(1)]
        + [whole(sines), whole(cosines), whole(bases)],
        out_specs=(
            column,
            pl.BlockSpec((2, size, size), lambda i: (i, 0, 0)),
        ),
        compiler_params=pltpu.CompilerParams(vmem_limit_bytes=56 * 2**20),
        cost_estimate=pl.CostEstimate(
            flops=2 * 12 * size * (size * 1700 + 2 * 64 * 768),
            bytes_accessed=20 * 2**20,
            transcendentals=12 * size * size,
        ),
    )(*joined, rel_map, rel_map, sines, cosines, bases)


def attend_back_pair(upstream, queries, keys, values, rel_text, rel_box, probs, sines, cosines, spread):
    scale = HD ** (-0.5)
    low = jnp.bfloat16
    got = [[], [], []]
    for half in range(2):
        shares = probs[half].astype(jnp.float32)
        d_probs = dot_nt(masked(upstream, half), values)
        got[2].append(dot_tn(shares.astype(low), upstream))
        inner = jnp.sum(d_probs * shares, -1, keepdims=True)
        d_scores = (shares * (d_probs - inner)).astype(low)
        d_text = turn_back(dot_nn(d_scores, spread) * scale, sines[...], cosines[...])
        got[0].append(dot_nn(d_scores, keys) * scale + dot_nt(d_text, rel_text[...]))
        part = dot_tn(masked(queries, half), d_text)
        text_sum = part if half == 0 else text_sum + part
        turned = d_scores.T
        d_box = turn_back(dot_nn(turned, spread) * scale, sines[...], cosines[...])
        got[1].append(dot_nn(turned, queries) * scale + dot_nt(d_box, rel_box[...]))
        part = dot_tn(masked(keys, half), d_box)
        box_sum = part if half == 0 else box_sum + part
    return (*[pick_halves(*halves).astype(low) for halves in got], text_sum, box_sum)


def attend_back_kernel(
    d_out, q, k, v, rel_text, rel_box, probs, sines, cosines, bases, dq, dk, dv, g_rel
):
    dq[...], dk[...], dv[...], text_sum, box_sum = attend_back_pair(
        d_out[...], q[...], k[...], v[...], rel_text, rel_box, probs, sines, cosines, bases[...]
    )
    g_rel[0] = text_sum.astype(jnp.bfloat16)
    g_rel[1] = box_sum.astype(jnp.bfloat16)


def attend_back(d_attended, joined, rel_map, probs, sines, cosines, bases):
    size, model = bases.shape
    pairs = model // (2 * HD)
    lanes = 2 * HD
    low = jnp.bfloat16
    whole = lambda rows: pl.BlockSpec(rows.shape, lambda i: (0, 0))
    column = pl.BlockSpec((size, lanes), lambda i: (0, i))
    band = lambda part: pl.BlockSpec((lanes, model), lambda i: (i + part * pairs, 0))
    return pl.pallas_call(
        attend_back_kernel,
        name="attend_back",
        grid=(pairs,),
        out_shape=(jax.ShapeDtypeStruct((size, model), low),) * 3
        + (jax.ShapeDtypeStruct((2, model, model), low),),
        in_specs=[column, column, column, column, band(0), band(1)]
        + [pl.BlockSpec((2, size, size), lambda i: (i, 0, 0))]
        + [whole(sines), whole(cosines), whole(bases)],
        out_specs=(column,) * 3 + (pl.BlockSpec((2, lanes, model), lambda i: (0, i, 0)),),
        compiler_params=pltpu.CompilerParams(vmem_limit_bytes=56 * 2**20),
        cost_estimate=pl.CostEstimate(
            flops=2 * 12 * size * (size * 1800 + 4 * 64 * 768),
            bytes_accessed=25 * 2**20,
            transcendentals=0,
        ),
    )(d_attended, *joined, rel_map, rel_map, probs, sines, cosines, bases)


def ahead_kernel(n, layout, early, capacity, *refs):
    count = 1 + max(source for source, _, _ in layout)
    lists, vocabulary, pages, positions, omegas, place, mask_col = refs[:7]
    weights = refs[7 : 7 + count]
    outs = refs[7 + count : 23 + count]
    asked, full, probs, sines, cosines, bases, target_out, normed_out, white_out, scale_out, low_out = outs[:11]
    q, k, v, attended, gains = outs[11:]
    swap_out, swap_in, chip_rows, answers, rows, held, rel_map, shares, turned = refs[23 + count : 32 + count]
    ask_send, ask_recv, row_send, row_recv, own_sem, swap_send, swap_recv = refs[32 + count : 39 + count]
    hop_recv, core_recv, core_send, z_send, a_send, b_send, load_sem, out_sem = refs[39 + count :]
    low = jnp.bfloat16
    me = lax.axis_index("dp")
    core, spot, layer, step_a, step_b = place_of(me)
    layers = n // 8
    half = chip_rows.shape[1]
    page_rows = pages.shape[0]
    here = pl.ds(pl.multiple_of(core * half, 128), half)
    there = pl.ds(pl.multiple_of((1 - core) * half, 128), half)
    partner = me + 1 - 2 * core
    to_a, to_b, up, down = me + 2 * step_a, me + 2 * step_b, me + 8, me - 8
    spot_a, spot_b, spot_ab = spot + step_a, spot + step_b, spot + step_a + step_b
    low_z, high_z = layer > 0, layer < layers - 1
    cuts = (pl.ds(0, early), pl.ds(early, chip_rows.shape[0] - early))

    high = weights[0].shape[0]
    turned[0:high] = swap_middle(weights[0][...], 1)
    turned[high:] = swap_middle(weights[1][...], 1)

    def piece(source, column, side):
        lanes = pl.ds(pl.multiple_of(column + side * half, 128), half)
        if source == 0:
            return turned[0:high, lanes]
        return turned[high:, lanes] if source == 1 else weights[source][:, lanes]

    at = 0
    for source, column, unit in layout:
        swap_out[pl.ds(at, 24 * unit)] = piece(source, column, 1 - core)
        at += 24 * unit
    greet_everyone(me, n)
    swaps = [
        remote_copy(swap_out, swap_in, swap_send.at[0], swap_recv.at[0], partner),
        remote_copy(
            pages.at[:, there],
            chip_rows.at[pl.ds(2 * at + core * page_rows, page_rows)],
            swap_send.at[1],
            swap_recv.at[1],
            partner,
        ),
    ]
    for copy in swaps:
        copy.start()

    def ask(step):
        peer = lax.rem(me + step, n)
        return remote_copy(lists.at[peer], asked.at[me], ask_send.at[step], ask_recv.at[step], peer)

    def start_ask(step, carry):
        ask(step).start()
        return carry

    def wait_ask(step, carry):
        ask(step).wait()
        return carry

    lax.fori_loop(1, n, start_ask, 0)
    asked[me] = lists[me]
    chip_rows[pl.ds(2 * at + pl.multiple_of(core * page_rows, page_rows), page_rows)] = pages[:, here]
    for copy in swaps:
        copy.wait_recv()
    at = 0
    for source, column, unit in layout:
        mine, other = piece(source, column, core), swap_in[pl.ds(at, 24 * unit)]
        ordered = jnp.where(
            core == 0, jnp.concatenate([mine, other], 0), jnp.concatenate([other, mine], 0)
        )
        chip_rows[pl.ds(2 * at, 48 * unit)] = ordered.astype(low)
        at += 24 * unit

    def block(g, level, index):
        return full.at[level, index, cuts[g], here]

    def z_hop(g, way, level, src=None):
        return remote_copy(
            block(g, level, spot) if src is None else src, block(g, level, spot),
            z_send.at[g, way, level], hop_recv.at[g, level, spot], up if way == 0 else down,
        )

    def a_hop(g, level, src=None):
        return remote_copy(
            block(g, level, spot) if src is None else src, block(g, level, spot),
            a_send.at[g, level], hop_recv.at[g, level, spot], to_a,
        )

    def b_hop(g, kind, level, src=None):
        index = spot if kind == 0 else spot_a
        return remote_copy(
            block(g, level, index) if src is None else src, block(g, level, index),
            b_send.at[g, kind, level], hop_recv.at[g, level, index], to_b,
        )

    def core_hop(g, level, index, src=None):
        return remote_copy(
            block(g, level, index) if src is None else src, block(g, level, index),
            core_send.at[g, level, index], core_recv.at[g, level, index], partner,
        )

    def arrived(g, level, index):
        view = block(g, level, index)
        pltpu.make_async_copy(view, view, hop_recv.at[g, level, index]).wait()

    def own_copy(g):
        return pltpu.make_async_copy(chip_rows.at[cuts[g]], block(g, layer, spot), own_sem.at[g])

    def send_own(g):
        src = chip_rows.at[cuts[g]]

        @pl.when(high_z)
        def _():
            z_hop(g, 0, layer, src).start()

        @pl.when(low_z)
        def _():
            z_hop(g, 1, layer, src).start()

        a_hop(g, layer, src).start()
        b_hop(g, 0, layer, src).start()
        core_hop(g, layer, spot, src).start()
        own_copy(g).start()

    def relay_column(g, gap):
        for way, level, there_is, further in (
            (0, layer - gap, layer - gap >= 0, high_z),
            (1, layer + gap, layer + gap < layers, low_z),
        ):

            @pl.when(there_is)
            def _():
                arrived(g, level, spot)

                @pl.when(further)
                def _():
                    z_hop(g, way, level).start()

                a_hop(g, level).start()
                b_hop(g, 0, level).start()
                core_hop(g, level, spot).start()

    def at_gap(gap, visit):
        if gap == 0:
            visit(layer)
            return

        @pl.when(layer - gap >= 0)
        def _():
            visit(layer - gap)

        @pl.when(layer + gap < layers)
        def _():
            visit(layer + gap)

    def relay_a(g, gap):
        def visit(level):
            arrived(g, level, spot_a)
            b_hop(g, 1, level).start()
            core_hop(g, level, spot_a).start()

        at_gap(gap, visit)

    def relay_b(g, gap):
        for index in (spot_b, spot_ab):

            def visit(level):
                arrived(g, level, index)
                core_hop(g, level, index).start()

            at_gap(gap, visit)

    def relays(g):
        steps = [lambda: relay_a(g, 0)]
        for gap in range(1, layers):
            steps.append(lambda gap=gap: relay_column(g, gap))
            steps.append(lambda gap=gap: relay_a(g, gap))
            steps.append(lambda gap=gap: relay_b(g, gap - 1))
        steps.append(lambda: relay_b(g, layers - 1))
        return steps

    def gathered(g):
        def wait(level, carry):
            for index in range(4):
                view = full.at[level, index, cuts[g], there]
                pltpu.make_async_copy(view, view, core_recv.at[g, level, index]).wait()
            return carry

        lax.fori_loop(0, layers, wait, 0)
        own_copy(g).wait()

    send_own(0)

    lax.fori_loop(1, n, wait_ask, 0)
    rows_own = vocabulary.shape[0]
    table = vocabulary[...].astype(low)
    group = 128 // capacity

    def row_copy(peer):
        return remote_copy(
            answers.at[peer], rows.at[me], row_send.at[peer], row_recv.at[me], peer
        )

    def answer(turn, carry):
        ids = jnp.zeros((8, 128), jnp.float32)
        for j in range(group):
            ids = ids + asked[turn * group + j]
        ids = ids.T[:, 6:7]
        wanted = lax.broadcasted_iota(jnp.int32, (128, rows_own), 1) + 1
        picks = jnp.where(ids.astype(jnp.int32) == wanted, 1.0, 0.0).astype(low)
        found = dot_nn(picks, table).astype(low)
        for j in range(group):
            peer = turn * group + j
            answers[peer] = found[j * capacity : (j + 1) * capacity]

            @pl.when(peer != me)
            def _():
                row_copy(peer).start()

        return carry

    lax.fori_loop(0, n // group, answer, 0)
    first = relays(0)
    rest = relays(1)
    for step in first[:2]:
        step()
    send_own(1)
    rows[me] = answers[me]
    cols = gains.shape[1] // n
    for source in range(n):
        gains[:, source * cols : (source + 1) * cols] = (
            asked[source, :, 0:cols].astype(low).astype(jnp.float32)
        )
    lane = lax.broadcasted_iota(jnp.int32, sines.shape, 1)
    line = lax.broadcasted_iota(jnp.int32, (8, sines.shape[0]), 0)
    points = jnp.where(line == 0, positions[0:1], positions[1:2]).astype(jnp.float32).T
    angles = jnp.where(lane < sines.shape[1] // 2, points[:, 0:1], points[:, 1:2]) * omegas[...]
    sines[...] = jnp.sin(angles)
    cosines[...] = jnp.cos(angles)
    boxes = jnp.concatenate([sines[...], cosines[...]], 1).astype(low)
    bases[...] = jnp.concatenate([cosines[...], sines[...]], 1).astype(low)
    for step in (*first[2:6], *rest[:2], *first[6:9], *rest[2:3], *first[9:], rest[4]):
        step()
    gathered(0)
    map_copy = pltpu.make_async_copy(full.at[:, :, pl.ds(0, 192)], held, load_sem.at[0])
    map_copy.start()
    deep = (early - 192) if early > 192 else 0
    for chip in range(4 * layers):
        pltpu.make_async_copy(
            full.at[chip // 4, chip % 4, pl.ds(192, deep)], rel_map.at[pl.ds(chip * deep, deep)], load_sem.at[1]
        ).start()

    def wait_row(step, carry):
        source = lax.rem(me - step + n, n)
        pltpu.make_async_copy(rows.at[source], rows.at[source], row_recv.at[source]).wait()
        return carry

    lax.fori_loop(1, n, wait_row, 0)
    slots = n * capacity
    seats = lax.broadcasted_iota(jnp.int32, (place.shape[0], slots), 1) == place[...]
    target = dot_nn(jnp.where(seats, 1.0, 0.0).astype(low), rows[...].reshape(slots, -1))
    target_out[...] = target
    mask_owner, mask_slot = mask_token // rows_own, capacity - 1
    mask_row = rows[mask_owner, mask_slot : mask_slot + 1].astype(jnp.float32)
    entry = jnp.where(mask_col[...] == 1.0, mask_row, target)
    map_copy.wait()
    model = target.shape[1]

    def weight(at):
        return held[:, :, at : at + 48].reshape(-1, model)

    embedded = entry + dot_nt(boxes, weight(0))
    normed, white, scale = layer_norm(embedded, gains[0:1], gains[1:2])
    normed_out[...], white_out[...], scale_out[...] = normed, white, scale
    normed = normed.astype(low)
    low_out[...] = normed
    for third, ref in enumerate((q, k, v)):
        ref[...] = dot_nn(normed, weight(48 + 48 * third)).astype(low)
    rest[5]()
    pltpu.make_async_copy(rel_map, rel_map, load_sem.at[1]).wait()
    pairs = model // (2 * HD)
    turns = [[] for _ in range(pairs)]
    for at, which in zip((0, 1, 2, 3, 5), (7, 3, 6, 8, 9)):
        turns[min(at, pairs - 1)].append(rest[which])

    def shares_copy(pair):
        slot = lax.rem(pair, 2)
        return pltpu.make_async_copy(shares.at[slot], probs.at[pl.ds(2 * pair, 2)], out_sem.at[slot])

    def attend(pair, carry):
        for turn in range(pairs):

            @pl.when(pair == turn)
            def _():
                for step in turns[turn]:
                    step()

        @pl.when(pair >= 2)
        def _():
            shares_copy(pair - 2).wait()

        lanes = pl.ds(pl.multiple_of(pair * 2 * HD, 2 * HD), 2 * HD)
        band = pl.ds(pl.multiple_of(pair * 2 * HD, 2 * HD), 2 * HD)
        other = pl.ds(pl.multiple_of(model + pair * 2 * HD, 2 * HD), 2 * HD)
        slot = lax.rem(pair, 2)
        result = attend_pair(
            q[:, lanes], k[:, lanes], v[:, lanes], rel_map.at[band], rel_map.at[other],
            sines, cosines, bases[...], shares.at[slot],
        )
        attended[:, lanes] = result
        shares_copy(pair).start()
        return carry

    lax.fori_loop(0, pairs, attend, 0)
    shares_copy(pairs - 2).wait()
    shares_copy(pairs - 1).wait()
    rest[10]()
    gathered(1)

    def finish(level, carry):
        for g in range(2):
            for index in (spot, spot_a, spot_b, spot_ab):
                core_hop(g, level, index).wait_send()
            a_hop(g, level).wait_send()
            b_hop(g, 0, level).wait_send()
            b_hop(g, 1, level).wait_send()

            @pl.when((level <= layer) & high_z)
            def _():
                z_hop(g, 0, level).wait_send()

            @pl.when((level >= layer) & low_z)
            def _():
                z_hop(g, 1, level).wait_send()

        return carry

    lax.fori_loop(0, layers, finish, 0)
    for copy in swaps:
        copy.wait_send()

    def finish_rows(step, carry):
        peer = lax.rem(me + step, n)
        pltpu.make_async_copy(answers.at[peer], answers.at[peer], row_send.at[peer]).wait()
        return carry

    lax.fori_loop(1, n, finish_rows, 0)


def ahead(lists, vocabulary, pages, positions, place, mask_col, weights, layout, early, n, capacity, ident):
    model = vocabulary.shape[1]
    size = place.shape[0]
    layers = n // 8
    waves = model // 4
    omegas = jnp.power(10000.0, -jnp.arange(waves).astype(jnp.float32) / waves)
    omegas = jnp.concatenate([omegas, omegas])[None]
    swap = 24 * sum(unit for _, _, unit in layout)
    chip = 2 * (swap + pages.shape[0])
    low, wide = jnp.bfloat16, jnp.float32
    dma = pltpu.SemaphoreType.DMA
    vmem = pl.BlockSpec(memory_space=pltpu.VMEM)
    anywhere = pl.BlockSpec(memory_space=pl.ANY)
    shape = jax.ShapeDtypeStruct
    rows = lambda kind: shape((size, model), kind)
    heads = model // HD
    return pl.pallas_call(
        partial(ahead_kernel, n, layout, early, capacity),
        name="ahead",
        out_shape=(
            shape(lists.shape, lists.dtype),
            shape((layers, 4, chip, model), low),
            shape((heads, size, size), low),
            shape((size, 2 * waves), wide),
            shape((size, 2 * waves), wide),
            rows(low),
            rows(wide),
            rows(wide),
            rows(wide),
            shape((size, 1), wide),
            rows(low),
            rows(low),
            rows(low),
            rows(low),
            rows(low),
            shape((8, model), wide),
        ),
        in_specs=[vmem] * (7 + len(weights)),
        out_specs=(vmem, anywhere, anywhere) + (vmem,) * 13,
        scratch_shapes=[
            pltpu.VMEM((swap, model // 2), wide),
            pltpu.VMEM((swap, model // 2), wide),
            pltpu.VMEM((chip, model // 2), low),
            pltpu.VMEM((n, capacity, model), low),
            pltpu.VMEM((n, capacity, model), low),
            pltpu.VMEM((layers, 4, 192, model), low),
            pltpu.VMEM((2 * model, model), low),
            pltpu.VMEM((2, 2, size, size), low),
            pltpu.VMEM((weights[0].shape[0] + weights[1].shape[0], model), wide),
            dma((n,)),
            dma((n,)),
            dma((n,)),
            dma((n,)),
            dma((2,)),
            dma((2,)),
            dma((2,)),
            dma((2, layers, 4)),
            dma((2, layers, 4)),
            dma((2, layers, 4)),
            dma((2, 2, layers)),
            dma((2, layers)),
            dma((2, 2, layers)),
            dma((2,)),
            dma((2,)),
        ],
        compiler_params=pltpu.CompilerParams(
            collective_id=ident, has_side_effects=True, vmem_limit_bytes=62 * 2**20
        ),
        cost_estimate=pl.CostEstimate(
            flops=13 * 10**9, bytes_accessed=100 * 2**20, transcendentals=0
        ),
    )(lists, vocabulary, pages, positions, omegas, place, mask_col, *weights)


def behind_kernel(n, early, pieces, fold, fixed, *refs):
    full, upper, probs, d_lower, white, q_in, k_in, v_in, d_attended, sines, cosines, bases = refs[:12]
    scale, gains, normed, mask_col, pos_rows, place, upper_norms, asked, loss_part = refs[12:21]
    out, table, norm_piece, totals = refs[21:25]
    rel_map, low_grads, shares, q, k, v, sent, small = refs[25:33]
    own, par, par_low, from_b, from_a, from_z, chained, mine, gone, back = refs[33:43]
    came, small_came, message, told = refs[43:47]
    row_send, row_recv, load_sem, pair_send, pair_recv, local_sem, share_sem = refs[47:54]
    b_send, b_recv, a_send, a_recv, z_send, z_recv, c_send, c_recv, f_send, f_recv, t_send, t_recv = refs[54:]
    low, wide = jnp.bfloat16, jnp.float32
    layers = n // 8
    me = lax.axis_index("dp")
    core, spot, layer, step_a, step_b = place_of(me)
    half = own.shape[3]
    model = 2 * half
    size = normed.shape[0]
    here = pl.ds(pl.multiple_of(core * half, 128), half)
    there = pl.ds(pl.multiple_of((1 - core) * half, 128), half)
    partner = me + 1 - 2 * core
    to_a, to_b = me + 2 * step_a, me + 2 * step_b
    spot_a, spot_b, spot_ab = spot + step_a, spot + step_b, spot + step_a + step_b
    low_z, high_z = layer > 0, layer < layers - 1
    bulk = own.shape[2]
    chunk = 144
    parts = (bulk // chunk, early // chunk)
    pairs = model // (2 * HD)
    deep = early - 192

    for chip in range(4 * layers):
        pltpu.make_async_copy(
            full.at[chip // 4, chip % 4, pl.ds(192, deep)], rel_map.at[pl.ds(chip * deep, deep)], local_sem.at[0]
        ).start()
    joined = [
        pltpu.make_async_copy(src, dst, local_sem.at[1 + j])
        for j, (src, dst) in enumerate(((q_in, q), (k_in, k), (v_in, v)))
    ]
    mixing = pltpu.make_async_copy(
        full.at[:, :, pl.ds(48, 144)], low_grads.at[:, :, pl.ds(48, 144)], local_sem.at[4]
    )
    rest = size - (table.shape[0] - size)
    kept = [
        pltpu.make_async_copy(d_lower, table.at[pl.ds(0, size)], local_sem.at[5]),
        pltpu.make_async_copy(
            white.at[pl.ds(0, size - rest)], table.at[pl.ds(size, size - rest)], local_sem.at[6]
        ),
        pltpu.make_async_copy(white.at[pl.ds(size - rest, rest)], out.at[pl.ds(0, rest)], local_sem.at[7]),
    ]

    def shares_copy(pair):
        slot = lax.rem(pair, 2)
        return pltpu.make_async_copy(probs.at[pl.ds(2 * pair, 2)], shares.at[slot], share_sem.at[slot])

    for copy in (*joined, shares_copy(0), shares_copy(1), mixing, *kept):
        copy.start()

    greet_everyone(me, n)

    def pair_copy(g, index):
        if g == 0:
            src, dst = upper.at[:, index, :, there], par.at[:, index]
        else:
            src, dst = low_grads.at[:, index, :, there], par_low.at[:, index]
        return remote_copy(src, dst, pair_send.at[g, index], pair_recv.at[g, index], partner)

    def load_copy(index):
        return pltpu.make_async_copy(upper.at[:, index, :, here], own.at[:, index], load_sem.at[index])

    for index in (spot_ab, spot_a, spot_b, spot):
        pair_copy(0, index).start()
    for index in (spot_ab, spot_b, spot_a, spot):
        load_copy(index).start()

    def arrived(g, index):
        if g == 0:
            load_copy(index).wait()
        pair_copy(g, index).wait_recv()

    def total(*views):
        return sum(view[...].astype(wide) for view in views)

    def mine_at(g, level, index, part):
        cut = pl.ds(part * chunk, chunk)
        return own.at[level, index, cut] if g == 0 else low_grads.at[level, index, cut, here]

    def par_at(g, level, index, part):
        cut = pl.ds(part * chunk, chunk)
        return (par if g == 0 else par_low).at[level, index, cut]

    def cut_of(g, part):
        return pl.ds(g * bulk + part * chunk, chunk)

    def b_copy(g, kind, level, part):
        return remote_copy(
            mine_at(g, level, spot_ab if kind == 0 else spot_b, part),
            from_b.at[kind, level, cut_of(g, part)],
            b_send.at[g, kind, level, part], b_recv.at[g, kind, level, part], to_b,
        )

    def a_copy(g, level, part):
        return remote_copy(
            mine_at(g, level, spot_a, part), from_a.at[level, cut_of(g, part)],
            a_send.at[g, level, part], a_recv.at[g, level, part], to_a,
        )

    def z_copy(level, part):
        return remote_copy(
            mine_at(1, level, spot, part), from_z.at[layer, pl.ds(part * chunk, chunk)],
            z_send.at[level, part], z_recv.at[layer, part], me + 8 * (level - layer),
        )

    def chain_copy(way, gap, level, part):
        place = layers if way == 1 and gap == 1 else level
        return remote_copy(
            mine_at(0, level, spot, part), chained.at[place, pl.ds(part * chunk, chunk)],
            c_send.at[level, part], c_recv.at[place, part], me + (8 if way == 0 else -8),
        )

    def chain_part(place, part):
        view = chained.at[place, pl.ds(part * chunk, chunk)]
        pltpu.make_async_copy(view, view, c_recv.at[place, part]).wait()
        return total(view)

    def cross_b(g, kind):
        index = spot_ab if kind == 0 else spot_b

        def step(turn, carry):
            part, level = lax.div(turn, layers), lax.rem(turn, layers)
            view = mine_at(g, level, index, part)
            view[...] = total(view, par_at(g, level, index, part)).astype(low)
            b_copy(g, kind, level, part).start()
            return carry

        lax.fori_loop(0, layers * parts[g], step, 0)

    def cross_a(g, part):
        def step(level, carry):
            b_copy(g, 0, level, part).wait_recv()
            view = mine_at(g, level, spot_a, part)
            view[...] = total(
                view, par_at(g, level, spot_a, part), from_b.at[0, level, cut_of(g, part)]
            ).astype(low)
            a_copy(g, level, part).start()
            return carry

        lax.fori_loop(0, layers, step, 0)

    def column(g, level, part):
        b_copy(g, 1, level, part).wait_recv()
        a_copy(g, level, part).wait_recv()
        cut = cut_of(g, part)
        return total(
            mine_at(g, level, spot, part), par_at(g, level, spot, part),
            from_b.at[1, level, cut], from_a.at[level, cut],
        )

    def chain(gap):
        for way, guard, further, level in (
            (0, layer + gap < layers, low_z, layer + gap),
            (1, layer - gap >= 0, high_z, layer - gap),
        ):

            def step(part, carry, way=way, level=level, further=further):
                view = mine_at(0, level, spot, part)
                value = column(0, level, part)

                @pl.when(further)
                def _():
                    view[...] = (value + chain_part(level, part)).astype(low)

                @pl.when(jnp.logical_not(further))
                def _():
                    view[...] = value.astype(low)

                chain_copy(way, gap, level, part).start()
                return carry

            @pl.when(guard)
            def _():
                lax.fori_loop(0, parts[0], step, 0)

    def chain_end():
        def step(part, carry):
            cut = pl.ds(part * chunk, chunk)
            mine[cut] = column(0, layer, part)

            @pl.when(low_z)
            def _():
                mine[cut] += chain_part(layer, part)

            @pl.when(high_z)
            def _():
                mine[cut] += chain_part(layers, part)

            return carry

        lax.fori_loop(0, parts[0], step, 0)

    def cross_z(part):
        def step(gap, carry):
            level = lax.rem(layer + gap, layers)
            view = mine_at(1, level, spot, part)
            view[...] = column(1, level, part).astype(low)
            z_copy(level, part).start()
            return carry

        lax.fori_loop(1, layers, step, 0)
        mine[cut_of(1, part)] = column(1, layer, part)

    def last_z(part):
        def step(gap, carry):
            level = lax.rem(layer + gap, layers)
            view = from_z.at[level, pl.ds(part * chunk, chunk)]
            pltpu.make_async_copy(view, view, z_recv.at[level, part]).wait()
            mine[cut_of(1, part)] += total(view)
            return carry

        lax.fori_loop(1, layers, step, 0)

    for copy in joined:
        copy.wait()
    pltpu.make_async_copy(rel_map, rel_map, local_sem.at[0]).wait()

    def first_cross():
        arrived(0, spot_ab)
        cross_b(0, 0)

    def second_cross():
        arrived(0, spot_b)
        cross_b(0, 1)
        arrived(0, spot_a)
        arrived(0, spot)

    turns = [[] for _ in range(pairs)]
    turns[1], turns[2] = [first_cross], [second_cross]
    for part in range(parts[0]):
        turns[min(3 + part, pairs - 1)].append(lambda part=part: cross_a(0, part))

    def attend_turn(pair, carry):
        for at in range(pairs):

            @pl.when(pair == at)
            def _():
                for step in turns[at]:
                    step()

        shares_copy(pair).wait()
        start = pl.multiple_of(pair * 2 * HD, 2 * HD)
        lanes = pl.ds(start, 2 * HD)
        other = pl.ds(pl.multiple_of(model + start, 2 * HD), 2 * HD)
        dq, dk, dv, text_sum, box_sum = attend_back_pair(
            d_attended[:, lanes], q[:, lanes], k[:, lanes], v[:, lanes],
            rel_map.at[pl.ds(start, 2 * HD)], rel_map.at[other], shares.at[lax.rem(pair, 2)],
            sines, cosines, bases[...],
        )
        q[:, lanes], k[:, lanes], v[:, lanes] = dq, dk, dv
        for first, rows in ((0, text_sum), (model, box_sum)):
            for j in range(0, 2 * HD, 32):
                row = first + pair * 2 * HD + j
                chip = lax.div(row, deep)
                at = pl.multiple_of(192 + lax.rem(row, deep), 32)
                low_grads[lax.div(chip, 4), lax.rem(chip, 4), pl.ds(at, 32)] = rows[j : j + 32].astype(low)

        @pl.when(pair + 2 < pairs)
        def _():
            shares_copy(pair + 2).start()

        return carry

    lax.fori_loop(0, pairs, attend_turn, 0)

    mixing.wait()
    for copy in kept:
        copy.wait()
    d_first = table[0:size]
    for third, ref in enumerate((q, k, v)):
        at = 48 + 48 * third
        upstream = ref[...]
        d_first = d_first + dot_nt(upstream, low_grads[:, :, at : at + 48].reshape(-1, model))
        grad = dot_tn(normed[...], upstream).astype(low)
        low_grads[:, :, at : at + 48] = grad.reshape(layers, 4, 48, model)
    whitened = jnp.concatenate([table[size : 2 * size - rest], out[0:rest]], 0)
    d_rows, gain, bias = norm_back(d_first, whitened, scale[...], gains[0:1])
    mask = mask_col[...]
    token_grads = jnp.where(mask == 1.0, pos_rows[...].astype(wide), d_rows).astype(low)
    mask_grad = jnp.sum(mask * d_rows, 0, keepdims=True)
    slots = sent.shape[0] * sent.shape[1]
    seats = lax.broadcasted_iota(jnp.int32, (size, slots), 1) == place[...]
    found = dot_tn(jnp.where(seats, 1.0, 0.0).astype(low), token_grads)
    line = lax.broadcasted_iota(jnp.int32, (slots, 1), 0)
    sent[...] = jnp.where(line == fixed, mask_grad, found).astype(low).reshape(sent.shape)
    lines = jnp.concatenate([gain, bias, upper_norms[...]], 0)
    cols = model // n
    small[...] = jnp.zeros_like(small)
    for owner in range(n):
        small[owner, 0:6, 0:cols] = lines[:, owner * cols : (owner + 1) * cols]

    def row_copies(step):
        peer = lax.rem(me + step, n)
        return [
            remote_copy(src.at[peer], dst.at[me], row_send.at[j, step], row_recv.at[j, step], peer)
            for j, (src, dst) in enumerate(((sent, came), (small, small_came)))
        ]

    def start_rows(step, carry):
        for copy in row_copies(step):
            copy.start()
        return carry

    def finish_rows(step, carry):
        for copy in row_copies(step):
            copy.wait()
        return carry

    came[me] = sent[me]
    small_came[me] = small[me]

    lax.fori_loop(1, n, start_rows, 0)
    boxes = jnp.concatenate([sines[...], cosines[...]], 1).astype(low)
    grad = dot_tn(d_rows.astype(low), boxes).astype(low)
    low_grads[:, :, 0:48] = grad.reshape(layers, 4, 48, model)
    for index in (spot_ab, spot_a, spot_b, spot):
        pair_copy(1, index).start()

    arrived(1, spot_ab)
    cross_b(1, 0)
    arrived(1, spot_b)
    cross_b(1, 1)
    chain(layers - 1)
    for gap in range(layers - 2, 0, -1):
        chain(gap)
    arrived(1, spot_a)
    arrived(1, spot)
    for part in range(parts[1]):
        cross_a(1, part)
    chain_end()
    for part in range(parts[1]):
        cross_z(part)
    lax.fori_loop(1, n, finish_rows, 0)
    wanted = lax.broadcasted_iota(jnp.int32, (table.shape[0], 128), 0) + 1
    group = 128 // sent.shape[1]
    for turn in range(n // fold):
        ids = asked[turn * fold]
        for j in range(1, fold):
            ids = ids + asked[turn * fold + j]
        picks = jnp.where(ids[6:7].astype(jnp.int32) == wanted, 1.0, 0.0).astype(low)
        found = dot_nn(picks, came[turn * group : (turn + 1) * group].reshape(128, model))
        if turn == 0:
            table[...] = found
        else:
            table[...] += found
    squares = jnp.zeros((1, 1), wide)
    for part in range(4):
        rows = table.shape[0] // 4
        piece = table[part * rows : (part + 1) * rows]
        squares = squares + jnp.sum(piece * piece, keepdims=True)
    norm = small_came[0]
    for j in range(1, n):
        norm = norm + small_came[j]
    norm_piece[...] = norm
    squares = squares + jnp.sum(norm * norm, keepdims=True)
    for part in range(parts[1]):
        last_z(part)

    at = 0
    for piece in pieces:
        offset, rows = 2 * at, 24 * piece
        gone[pl.ds(at, rows)] = mine[pl.ds(pl.multiple_of(offset + (1 - core) * rows, 8), rows)]
        out[pl.ds(at, rows), here] = mine[pl.ds(pl.multiple_of(offset + core * rows, 8), rows)]
        at += rows
    last = remote_copy(gone, back, f_send, f_recv, partner)
    last.start()
    squares = squares + jnp.sum(out[:, here] * out[:, here], keepdims=True)
    last.wait()
    out[:, there] = back[...]
    squares = squares + jnp.sum(back[...] * back[...], keepdims=True)
    lane = lax.broadcasted_iota(jnp.int32, message.shape, 1)
    message[...] = jnp.where(lane == 0, squares, jnp.where(lane == 1, loss_part[...], 0.0))

    def tell(step):
        peer = lax.rem(me + step, n)
        return remote_copy(message, told.at[me], t_send.at[step], t_recv.at[step], peer)

    def start_told(step, carry):
        tell(step).start()
        return carry

    def wait_told(step, carry):
        tell(step).wait()
        return carry

    lax.fori_loop(1, n, start_told, 0)
    told[me] = message[...]
    for g in range(2):
        for index in range(4):
            pair_copy(g, index).wait_send()

        def settle(turn, carry, g=g):
            part, level = lax.div(turn, layers), lax.rem(turn, layers)
            b_copy(g, 0, level, part).wait_send()
            b_copy(g, 1, level, part).wait_send()
            a_copy(g, level, part).wait_send()

            @pl.when(level != layer)
            def _():
                if g == 0:
                    chain_copy(0, 2, level, part).wait_send()
                else:
                    z_copy(level, part).wait_send()

            return carry

        lax.fori_loop(0, layers * parts[g], settle, 0)
    lax.fori_loop(1, n, wait_told, 0)
    total_line = told[0]
    for j in range(1, n):
        total_line = total_line + told[j]
    over = jnp.max(jnp.max(asked[:, 7, :], 0, keepdims=True)[:, 2:3], keepdims=True)
    totals[...] = jnp.where(lane == 2, over, total_line)


def behind(in_hbm, in_vmem, rows_own, early, pieces, capacity, fold, fixed, n, ident):
    size, model = in_vmem[0].shape
    layers = n // 8
    bulk = in_hbm[1].shape[2]
    rows = bulk + early
    half = model // 2
    most = max(bulk, early) // 144
    low, wide = jnp.bfloat16, jnp.float32
    dma = pltpu.SemaphoreType.DMA
    vmem = pl.BlockSpec(memory_space=pltpu.VMEM)
    anywhere = pl.BlockSpec(memory_space=pl.ANY)
    shape = jax.ShapeDtypeStruct
    tile = shape((8, 128), wide)
    return pl.pallas_call(
        partial(behind_kernel, n, early, pieces, fold, fixed),
        name="behind",
        out_shape=(shape((rows // 2, model), wide), shape((rows_own, model), wide), tile, tile),
        in_specs=[anywhere] * len(in_hbm) + [vmem] * len(in_vmem),
        out_specs=(vmem,) * 4,
        scratch_shapes=[
            pltpu.VMEM((2 * model, model), low),
            pltpu.VMEM((layers, 4, early, model), low),
            pltpu.VMEM((2, 2, size, size), low),
            pltpu.VMEM((size, model), low),
            pltpu.VMEM((size, model), low),
            pltpu.VMEM((size, model), low),
            pltpu.VMEM((n, capacity, model), low),
            pltpu.VMEM((n, 8, 128), wide),
            pltpu.VMEM((layers, 4, bulk, half), low),
            pltpu.VMEM((layers, 4, bulk, half), low),
            pltpu.VMEM((layers, 4, early, half), low),
            pltpu.VMEM((2, layers, rows, half), low),
            pltpu.VMEM((layers, rows, half), low),
            pltpu.VMEM((layers, early, half), low),
            pltpu.VMEM((layers + 1, bulk, half), low),
            pltpu.VMEM((rows, half), wide),
            pltpu.VMEM((rows // 2, half), wide),
            pltpu.VMEM((rows // 2, half), wide),
            pltpu.VMEM((n, capacity, model), low),
            pltpu.VMEM((n, 8, 128), wide),
            pltpu.VMEM((8, 128), wide),
            pltpu.VMEM((n, 8, 128), wide),
            dma((2, n)),
            dma((2, n)),
            dma((4,)),
            dma((2, 4)),
            dma((2, 4)),
            dma((8,)),
            dma((2,)),
            dma((2, 2, layers, most)),
            dma((2, 2, layers, most)),
            dma((2, layers, most)),
            dma((2, layers, most)),
            dma((layers, most)),
            dma((layers, most)),
            dma((layers, most)),
            dma((layers + 1, most)),
            dma,
            dma,
            dma((n,)),
            dma((n,)),
        ],
        compiler_params=pltpu.CompilerParams(
            collective_id=ident, has_side_effects=True, vmem_limit_bytes=64 * 2**20 - 2**17
        ),
        cost_estimate=pl.CostEstimate(
            flops=20 * 10**9, bytes_accessed=100 * 2**20, transcendentals=0
        ),
    )(*in_hbm, *in_vmem)


def forward(weights, rows, positions):
    box_map, mix_map, rel_map, out_map, up_map, down_map, norm_rows = weights
    gains = norm_rows.astype(jnp.float32)
    sin_count = box_map.shape[1]
    sin_x, cos_x, sin_y, cos_y = sinusoids(positions, sin_count // 4)
    sines = jnp.concatenate([sin_x, sin_y], -1)
    cosines = jnp.concatenate([cos_x, cos_y], -1)
    boxes = jnp.concatenate([sines, cosines], -1).astype(jnp.bfloat16)
    bases = jnp.concatenate([cosines, sines], -1).astype(jnp.bfloat16)
    embedded = rows + dot_nt(boxes, box_map)
    first = layer_norm(embedded, gains[0], gains[1])
    normed = first[0].astype(jnp.bfloat16)
    joined = [dot_nn(normed, part).astype(jnp.bfloat16) for part in mix_map]
    attended, probs = attend(joined, rel_map, sines, cosines, bases)
    second = layer_norm(first[0] + dot_nn(attended, out_map), gains[2], gains[3])
    middle = second[0].astype(jnp.bfloat16)
    hidden_pre = [dot_nn(middle, part) for part in up_map]
    hidden = [jax.nn.gelu(part, approximate=False).astype(jnp.bfloat16) for part in hidden_pre]
    lowered = sum(dot_nn(part, weight) for part, weight in zip(hidden, down_map))
    third = layer_norm(second[0] + lowered, gains[4], gains[5])
    return {
        "sines": sines,
        "cosines": cosines,
        "boxes": boxes,
        "bases": bases,
        "first": first,
        "normed": normed,
        "joined": joined,
        "probs": probs,
        "attended": attended,
        "second": second,
        "middle": middle,
        "hidden_pre": hidden_pre,
        "hidden": hidden,
        "third": third,
    }


def backward_upper(weights, cache, d_states):
    _, _, _, out_map, up_map, down_map, norm_rows = weights
    gains = norm_rows.astype(jnp.float32)
    d_mid, gain_last, bias_last = norm_back(
        d_states, cache["third"][1], cache["third"][2], gains[4]
    )
    d_down = d_mid.astype(jnp.bfloat16)
    gelu_exact = partial(jax.nn.gelu, approximate=False)
    grad_down, grad_up, d_second = [], [], d_mid
    for pre, hidden, up, down in zip(cache["hidden_pre"], cache["hidden"], up_map, down_map):
        grad_down.append(dot_tn(hidden, d_down))
        d_pre = jax.vjp(gelu_exact, pre)[1](dot_nt(d_down, down))[0].astype(jnp.bfloat16)
        grad_up.append(dot_tn(cache["middle"], d_pre))
        d_second = d_second + dot_nt(d_pre, up)
    d_lower, gain_mid, bias_mid = norm_back(
        d_second, cache["second"][1], cache["second"][2], gains[2]
    )
    d_attn = d_lower.astype(jnp.bfloat16)
    grad_out = dot_tn(cache["attended"], d_attn)
    d_attended = dot_nt(d_attn, out_map).astype(jnp.bfloat16)
    return d_lower, d_attended, grad_out, grad_up, grad_down, [gain_mid, bias_mid, gain_last, bias_last]


def backward_lower(weights, cache, d_lower, d_attended):
    box_map, mix_map, rel_map, _, _, _, norm_rows = weights
    gains = norm_rows.astype(jnp.float32)
    *d_joined, grad_rel = attend_back(
        d_attended,
        cache["joined"],
        rel_map,
        cache["probs"],
        cache["sines"],
        cache["cosines"],
        cache["bases"],
    )
    grad_mix = [dot_tn(cache["normed"], part) for part in d_joined]
    d_first = d_lower + sum(dot_nt(part, weight) for part, weight in zip(d_joined, mix_map))
    d_embedded, gain_low, bias_low = norm_back(
        d_first, cache["first"][1], cache["first"][2], gains[0]
    )
    grad_box = dot_tn(d_embedded.astype(jnp.bfloat16), cache["boxes"])
    return d_embedded, grad_box, grad_mix, grad_rel, [gain_low, bias_low]


def per_device(
    n,
    tokens,
    positions,
    documents,
    masking,
    negative_page,
    negative_row,
    pages,
    vocabulary,
    geometry,
    mixing,
    relative,
    merging,
    widening,
    narrowing,
    scaling,
    moment_vocabulary,
    moment_geometry,
    moment_mixing,
    moment_relative,
    moment_merging,
    moment_widening,
    moment_narrowing,
    moment_scaling,
    average_vocabulary,
    average_geometry,
    average_mixing,
    average_relative,
    average_merging,
    average_widening,
    average_narrowing,
    average_scaling,
):
    size = tokens.shape[0]
    rows_own, model = vocabulary.shape
    page_rows = pages.shape[1]
    mask_float = masking.astype(jnp.float32)
    mask_col = mask_float[:, None]
    low = jnp.bfloat16
    blocks = widening.shape[1] // model
    decay = min(average_cap, (1.0 + STEP) / (10.0 + STEP))
    masters = (vocabulary, geometry, mixing, relative, merging, widening, narrowing, scaling)
    moments = (
        moment_vocabulary,
        moment_geometry,
        moment_mixing,
        moment_relative,
        moment_merging,
        moment_widening,
        moment_narrowing,
        moment_scaling,
    )
    averages = (
        average_vocabulary,
        average_geometry,
        average_mixing,
        average_relative,
        average_merging,
        average_widening,
        average_narrowing,
        average_scaling,
    )
    pieces = [
        swap_middle(geometry).T,
        *[mixing[:, k * model : (k + 1) * model] for k in range(3)],
        swap_middle(relative).T,
        merging,
        *[widening[:, k * model : (k + 1) * model] for k in range(blocks)],
        narrowing,
    ]
    bank_piece = pages.reshape(-1, model)

    def step(master, moment, average, piece, rate, factor):
        clipped = piece * factor
        velocity = momentum_decay * moment + clipped
        updated = master - rate * (clipped + momentum_decay * velocity)
        return updated, velocity, decay * average + (1.0 - decay) * updated

    def dense():
        chosen = (documents[0] == jnp.arange(DOCS)).astype(jnp.float32)
        counts = lax.psum(chosen * jnp.sum(mask_float), "dp")
        share = jnp.sum(chosen / (DOCS * jnp.maximum(counts, 1.0)))
        cast = [piece.astype(low) for piece in pieces] + [bank_piece]
        joined = lax.all_gather(jnp.concatenate(cast, 0), "dp", axis=0, tiled=False)
        weights, at = [], 0
        for piece in cast:
            weights.append(joined[:, at : at + piece.shape[0]].reshape(-1, model))
            at += piece.shape[0]
        norm_rows = lax.all_gather(scaling.astype(low), "dp", axis=1, tiled=True)
        entry = jnp.where(masking == 1, mask_token, tokens)
        lanes = 4

        def split(rows):
            return rows.reshape(rows.shape[0], lanes, -1).transpose(1, 0, 2)

        def join(rows):
            return rows.transpose(1, 0, 2).reshape(rows.shape[1], -1)

        def named_rows(part):
            table = lax.all_gather(part, "dp", axis=0, tiled=True)
            return table[tokens], table[entry]

        found = lax.map(named_rows, split(vocabulary.astype(low)))
        target_rows, entry_rows = [join(rows).astype(jnp.float32) for rows in found]
        box_map, mix_map, rel_map, out_map = weights[0], weights[1:4], weights[4], weights[5]
        up_map, down_full, bank = weights[6:-2], weights[-2], weights[-1]
        ff = len(up_map)
        down_map = [down_full[k * model : (k + 1) * model] for k in range(ff)]
        weights = (box_map, mix_map, rel_map, out_map, up_map, down_map, norm_rows)
        cache = forward(weights, entry_rows, positions)

        states_low = cache["third"][0].astype(low)
        inv_root = model ** (-0.5)
        positive = jnp.sum(states_low.astype(jnp.float32) * target_rows, -1, keepdims=True) * inv_root
        flat_index = (negative_page * page_rows + negative_row).T
        count_neg = flat_index.shape[1]
        width = bank.shape[0]
        repeated = jnp.tile(flat_index, (1, width // count_neg))
        chosen = repeated == jnp.arange(width)[None, :]
        logits = jnp.where(chosen, dot_nt(states_low, bank) * inv_root, -jnp.inf)
        highest = jnp.maximum(jnp.max(logits, -1, keepdims=True), positive)
        powers = jnp.exp(logits - highest)
        lead = jnp.exp(positive - highest)
        total = jnp.sum(powers, -1, keepdims=True) + lead
        per_token = highest + jnp.log(total) - positive
        loss_part = share * jnp.sum(mask_col * per_token)
        weight_map = (powers * (share * mask_col / total) * inv_root).astype(low)
        positive_grad = share * mask_col * (lead / total - 1.0) * inv_root
        d_states = positive_grad * target_rows + dot_nn(weight_map, bank)

        d_lower, d_attended, grad_out, grad_up, grad_down, upper_norms = backward_upper(
            weights, cache, d_states
        )
        d_embedded, grad_box, grad_mix, grad_rel, lower_norms = backward_lower(
            weights, cache, d_lower, d_attended
        )
        grad_norms = jnp.concatenate(lower_norms + upper_norms, 0)
        positive_rows = positive_grad * states_low.astype(jnp.float32)

        def summed_rows(parts):
            whole = jnp.zeros((rows_own * n, model // lanes), jnp.float32)
            whole = whole.at[entry].add(parts[0]).at[tokens].add(parts[1])
            return lax.psum_scatter(whole, "dp", scatter_dimension=0, tiled=True)

        table_piece = join(lax.map(summed_rows, (split(d_embedded), split(positive_rows))))
        norm_piece = lax.psum_scatter(grad_norms, "dp", scatter_dimension=1, tiled=True)
        grads = [grad_box, *grad_mix, grad_rel.reshape(-1, model), grad_out, *grad_up]
        grads = [grad.astype(low) for grad in [*grads, jnp.concatenate(grad_down, 0)]]
        sums = scatter(grads, n)
        reduced = (
            table_piece,
            swap_middle(sums[0].T),
            jnp.concatenate(sums[1:4], 1),
            swap_middle(sums[4].T),
            sums[5],
            jnp.concatenate(sums[6:-1], 1),
            sums[-1],
            norm_piece,
        )
        square = lax.psum(sum(jnp.sum(piece * piece) for piece in reduced), "dp")
        grad_norm = jnp.sqrt(square)
        factor = clip_limit / jnp.maximum(grad_norm, clip_limit)
        rates = (table_rate,) + (learn_rate,) * 7
        done = [step(*group, factor) for group in zip(masters, moments, averages, reduced, rates)]
        return (lax.psum(loss_part, "dp"), grad_norm) + sum(zip(*done), ())

    if n // 8 != 4 or n % 8 != 0 or merging.shape[0] != 24 or page_rows % 16 != 0 or size % 128 != 0:
        return dense()

    capacity = max(16, -(-2 * size // n) // 16 * 16)
    slots = n * capacity
    fold = 128 // capacity
    cols = scaling.shape[1]
    info = jnp.pad(scaling, ((0, 2), (0, 128 - cols)))
    lists, place, mask_col = make_plan(tokens, masking, documents, info, n, rows_own, capacity, fold)
    early = 48 * (1 + 3 + relative.shape[1] // 24)
    (
        asked,
        full,
        probs,
        sines,
        cosines,
        bases,
        target,
        normed,
        white,
        scale,
        normed_low,
        *joined,
        attended,
        gains,
    ) = ahead(
        lists,
        vocabulary,
        bank_piece,
        positions,
        place,
        mask_col,
        (geometry.T, relative.T, mixing, merging, widening, narrowing),
        (
            (0, 0, 1),
            *[(2, k * model, 1) for k in range(3)],
            (1, 0, relative.shape[1] // 24),
            (3, 0, 1),
            *[(4, k * model, 1) for k in range(blocks)],
            (5, 0, narrowing.shape[0] // 24),
        ),
        early,
        n,
        capacity,
        1,
    )
    upper_grads, d_attended, d_lower, positive_rows, upper_norms, loss_part = upper(
        full.reshape(-1, *full.shape[2:]),
        attended,
        normed,
        target,
        mask_col,
        negative_page,
        negative_row,
        asked,
        documents,
        gains,
        blocks,
        page_rows,
    )
    fixed = (mask_token // rows_own) * capacity + capacity - 1
    sums, table_piece, norm_piece, totals = behind(
        (
            full,
            upper_grads.reshape(*full.shape[:2], -1, model),
            probs,
            d_lower,
            white,
            *joined,
        ),
        (
            d_attended,
            sines,
            cosines,
            bases,
            scale,
            gains,
            normed_low,
            mask_col,
            positive_rows,
            place,
            upper_norms,
            asked,
            loss_part,
        ),
        rows_own,
        early,
        (1,) + (1,) * blocks + (narrowing.shape[0] // 24, 1, 1, 1, 1, 2),
        capacity,
        fold,
        fixed,
        n,
        2,
    )

    def finish():
        grad_norm = jnp.sqrt(totals[0, 0])
        factor = clip_limit / jnp.maximum(grad_norm, clip_limit)
        last = step(
            scaling, moment_scaling, average_scaling, norm_piece[:6, :cols], learn_rate, factor
        )
        row = 24 * (1 + blocks) + narrowing.shape[0]
        layout = (
            (1, row, 1, 24, True),
            (2, row + 24, 3, 24, False),
            (3, row + 96, 1, 48, True),
            (4, 0, 1, 24, False),
            (5, 24, blocks, 24, False),
            (6, 24 * (1 + blocks), 1, narrowing.shape[0], False),
        )
        lay = lambda group: [group[0], group[1].T, group[2], group[3].T, *group[4:7]]
        groups = [lay(group) for group in (masters, moments, averages)]
        done = update_all(factor.reshape(1, 1), table_piece, sums, *groups, decay, layout)
        results = [totals[0, 1], grad_norm]
        for at, tail in zip((0, 7, 14), last):
            results += [*lay(done[at : at + 7]), tail]
        return tuple(results)

    overflow = totals[0, 2] > 0.0
    return lax.cond(overflow, dense, finish)


ROWS = P("dp", None)
COLS = P(None, "dp")
WEIGHTS = (ROWS, COLS, ROWS, COLS, ROWS, ROWS, ROWS, COLS)


def solution(mesh):
    return jax.shard_map(
        partial(per_device, mesh.shape["dp"]),
        mesh=mesh,
        in_specs=(P("dp"), COLS, P("dp"), P("dp"), COLS, COLS, P("dp", None, None)) + 3 * WEIGHTS,
        out_specs=(P(), P()) + 3 * WEIGHTS,
        check_vma=False,
    )
```
